32 devices in a mesh: seq: 8 (over z, y), grp: 4 (over x, core).
Axes of the slice: x: 2, y: 2, z: 4, core: 2. Of those that a mesh axis runs over, the one named last changes fastest.
Arguments:
- tokens_in: bfloat16 [65536, 512], P(('seq', 'grp')), may hold values from -27 to 27, as said below
- seq_starts: int32 [8], replicated, may hold values from 0 to 64511, as said below
- norm_gain: float32 [2, 512], replicated, may hold values from 0.1 to 1.9
- norm_bias: float32 [2, 512], replicated, may hold values from -3 to 3
- decay_rate: float32 [2, 384], replicated, may hold values from 0 to 1, as said below
- step_log: float32 [2, 384], replicated, may hold values from -12 to 0
- frequency: float32 [2, 384], replicated, may hold values from -3 to 3
- in_proj: bfloat16 [2, 512, 768], replicated, may hold values from -0.25 to 0.25
- out_proj: bfloat16 [2, 768, 512], replicated, may hold values from -0.3125 to 0.3125
- skip_gain: float32 [2, 512], replicated, may hold values from -4 to 4
- gate_proj: bfloat16 [2, 512, 512], replicated, may hold values from -0.25 to 0.25
- grad_out: bfloat16 [65536, 512], P(('seq', 'grp')), may hold values from -6 to 6
Outputs:
- layer_out: float32 [65536, 512], P(('seq', 'grp'))
- grad_in: float32 [65536, 512], P(('seq', 'grp'))
- grad_gain: float32 [2, 512], replicated
- grad_bias: float32 [2, 512], replicated
- grad_rate: float32 [2, 384], replicated
- grad_step: float32 [2, 384], replicated
- grad_freq: float32 [2, 384], replicated
- grad_in_proj: float32 [2, 512, 768], replicated
- grad_out_proj: float32 [2, 768, 512], replicated
- grad_skip: float32 [2, 512], replicated
- grad_gate: float32 [2, 512, 512], replicated
The draws below stay inside these ranges and needn't reach their ends.
Inputs may be any that keep to these rules, and one draw needn't show every extreme that they name: tokens_in drawn in float32 and rounded. `seq_starts`: the first is 0; they increase, consecutive ones differ by more than 1024, and the last lies more than 1024 below 65536. `decay_rate`: positive.
All inputs are finite; a program needn't handle non-finite values.
Results may differ from the reference program's by a relative error of at most 0.02.
Values sent between devices are 32-bit elements; how exact they have to be, the bound alone decides.
No kernel may reach another device: no remote copies, remote signals or barrier semaphores. Data moves between devices by JAX's collectives and lax.ppermute only.
A program may use at most 256 MiB of HBM per device.

```python
import jax
import jax.numpy as jnp
from jax import lax

H = 512
P_SIZE = 384
LAYERS = 2
MINLEN = 1024
TOKENS = 65536
NSEQ = 8


def decay_pair(key, slow_share):
    pick = jax.random.uniform(jax.random.fold_in(key, 11), (LAYERS, P_SIZE))
    level = jax.random.uniform(jax.random.fold_in(key, 12), (LAYERS, P_SIZE))
    spread = jax.random.uniform(jax.random.fold_in(key, 13), (LAYERS, P_SIZE), minval=0.7, maxval=1.4)
    slow_log = jnp.log(0.3 / TOKENS) + level * jnp.log(6.0)
    fast_log = jnp.log(2.0 / TOKENS) + level * jnp.log(TOKENS / 60.0)
    per_step = jnp.exp(jnp.where(pick < slow_share, slow_log, fast_log))
    step_size = jnp.sqrt(2.0 * per_step) * spread
    return (per_step / step_size, step_size)


def draw_decay_rate(key, part):
    slow_share = 0.5
    rate_value, step_size = decay_pair(key, slow_share)
    return rate_value.astype(jnp.float32)


def draw_step_log(key, part):
    slow_share = 0.5
    rate_value, step_size = decay_pair(key, slow_share)
    return jnp.log(step_size).astype(jnp.float32)


def draw_tokens_in(key, part):
    key = jax.random.fold_in(key, 3)
    place = jnp.arange(TOKENS, dtype=jnp.float32)[:, None] / TOKENS
    noise = jnp.clip(jax.random.normal(key, (TOKENS, H)), -5.0, 5.0)
    return (noise * (1.0 + 2.0 * place)).astype(jnp.bfloat16)


def draw_seq_starts(key, part):
    key = jax.random.fold_in(key, 5)
    slot_count = TOKENS // (2 * MINLEN)
    if NSEQ == 1:
        return jnp.zeros((1,), jnp.int32)
    middle = jax.random.permutation(jax.random.fold_in(key, 1), max(slot_count - 2, 1)).astype(jnp.int32) + 1
    chosen = jnp.concatenate([jnp.sort(middle[:NSEQ - 2]), jnp.full((1,), slot_count - 1, jnp.int32)])
    offsets = jax.random.randint(jax.random.fold_in(key, 2), (NSEQ - 1,), 0, MINLEN).astype(jnp.int32)
    offsets = offsets.at[NSEQ - 2].set(MINLEN - 1)
    cuts = chosen * (2 * MINLEN) + offsets
    return jnp.concatenate([jnp.zeros((1,), jnp.int32), cuts.astype(jnp.int32)])


def steps_of(key, extent, shards, least, largest):
    factor_of = 1.0
    for dim, parts in shards:
        steps = jax.random.uniform(jax.random.fold_in(jax.random.fold_in(key, 6), dim), (parts,), jnp.float32, least / len(shards), largest / len(shards))
        factor_of = factor_of * jnp.repeat(jnp.exp(steps), extent[dim] // parts).reshape((-1,) + (1,) * (len(extent) - 1 - dim))
    return factor_of


def gaussian(stream_key, shape, scale, most, pieces=(), kind=jnp.bfloat16):
    values = scale * jax.random.normal(stream_key, shape, jnp.float32)
    if pieces:
        values = values * steps_of(stream_key, shape, pieces, -0.22, 0.18)
    return jnp.clip(values, -most, most).astype(kind)


def setup_inputs(seed: int = 0) -> dict:
    streams_of = jax.random.split(jax.random.key(seed), 13)
    return {
        "tokens_in": draw_tokens_in(jax.random.fold_in(streams_of[12], 71), 0),
        "seq_starts": draw_seq_starts(jax.random.fold_in(streams_of[12], 71), 0),
        "norm_gain": jnp.clip(1.0 + 0.18 * jax.random.normal(streams_of[2], (LAYERS, H), jnp.float32), 0.1, 1.9),
        "norm_bias": gaussian(streams_of[3], (LAYERS, H), 0.5, 3.0, (), jnp.float32),
        "decay_rate": draw_decay_rate(jax.random.fold_in(streams_of[12], 71), 0),
        "step_log": draw_step_log(jax.random.fold_in(streams_of[12], 71), 0),
        "frequency": jnp.clip(jax.random.uniform(streams_of[6], (LAYERS, P_SIZE), jnp.float32, -3.0, 3.0), -3.0, 3.0),
        "in_proj": gaussian(streams_of[7], (LAYERS, H, 2 * P_SIZE), H ** -0.5, 0.25),
        "out_proj": gaussian(streams_of[8], (LAYERS, 2 * P_SIZE, H), P_SIZE ** -0.5, 0.3125),
        "skip_gain": gaussian(streams_of[9], (LAYERS, H), 1.0, 4.0, (), jnp.float32),
        "gate_proj": gaussian(streams_of[10], (LAYERS, H, H), H ** -0.5, 0.25),
        "grad_out": gaussian(streams_of[11], (TOKENS, H), 1.0, 6.0, ((0, 32),)),
    }


EPSILON = 1e-05
HIGHEST = lax.Precision.HIGHEST

@jax.custom_vjp
def low(v):
    return lax.optimization_barrier(v.astype(jnp.bfloat16)).astype(jnp.float32)

@jax.custom_vjp
def low_back(v):
    return v

def low_keep(v):
    return (low(v), None)

def low_pass(kept, grad):
    return (grad,)

def back_keep(v):
    return (v, None)

def back_low(kept, grad):
    return (low(grad),)
low.defvjp(low_keep, low_pass)
low_back.defvjp(back_keep, back_low)

def halves(value):
    half_width = value.shape[-1] // 2
    return (value[..., :half_width], value[..., half_width:])

def complex_mul(left_side, right_side):
    left_real, left_imag = halves(left_side)
    right_real, right_imag = halves(right_side)
    return jnp.concatenate([left_real * right_real - left_imag * right_imag, left_real * right_imag + left_imag * right_real], axis=-1)

def discretize(decay_rate, step_log, frequency):
    step_size = jnp.exp(step_log)
    real_angle = -decay_rate * step_size
    imag_angle = frequency * step_size
    magnitude = jnp.exp(real_angle)
    cosine = jnp.cos(imag_angle)
    sine = jnp.sin(imag_angle)
    decay_row = jnp.concatenate([magnitude * cosine, magnitude * sine], axis=-1)
    minus_real = jnp.expm1(real_angle) * cosine - 2.0 * jnp.sin(0.5 * imag_angle) ** 2
    minus_imag = magnitude * sine
    modulus = decay_rate * decay_rate + frequency * frequency
    factor_real = (-decay_rate * minus_real + frequency * minus_imag) / modulus
    factor_imag = (-decay_rate * minus_imag - frequency * minus_real) / modulus
    return (decay_row, jnp.concatenate([factor_real, factor_imag], axis=-1))

def recurrence(decay_row, keep_mask, drive_in, backward_flag):

    def advance(state_now, row_pair):
        keep_now, input_now = row_pair
        state_next = keep_now * complex_mul(decay_row, state_now) + input_now
        return (state_next, state_next)
    initial = jnp.zeros((drive_in.shape[1],), jnp.float32)
    _, states = lax.scan(advance, initial, (keep_mask, drive_in), reverse=backward_flag)
    return states

def residual_layer(stream, keep_mask, backward_flag, picked):
    norm_gain, norm_bias, decay_rate, step_log, frequency, in_proj, out_proj, skip_gain, gate_proj = picked
    feature_mean = lax.optimization_barrier(jnp.mean(stream, axis=0))
    centered = stream - feature_mean
    variance = lax.optimization_barrier(jnp.mean(centered * centered, axis=0))
    normed = centered * lax.rsqrt(variance + EPSILON) * norm_gain + norm_bias
    low_normed = low(normed)
    drive_term = low_back(jnp.dot(low_normed, in_proj, precision=HIGHEST, preferred_element_type=jnp.float32))
    decay_row, factor = discretize(decay_rate, step_log, frequency)
    states = recurrence(decay_row, keep_mask, complex_mul(drive_term, factor[None, :]), backward_flag)
    projected = low_back(jnp.dot(low(states), out_proj, precision=HIGHEST, preferred_element_type=jnp.float32))
    mixed = projected + skip_gain * normed
    activation = jax.nn.gelu(mixed)
    logits = low_back(jnp.dot(low(activation), gate_proj, precision=HIGHEST, preferred_element_type=jnp.float32))
    return stream + activation * jax.nn.sigmoid(logits)

def reference(tokens_in, seq_starts, norm_gain, norm_bias, decay_rate, step_log, frequency, in_proj, out_proj, skip_gain, gate_proj, grad_out):
    position = jnp.arange(TOKENS, dtype=jnp.int32)
    begins = jnp.any(position[:, None] == seq_starts[None, :], axis=1)
    afters = jnp.any(position[:, None] + 1 == seq_starts[None, :], axis=1) | (position + 1 == TOKENS)
    keep_forward = 1.0 - begins.astype(jnp.float32)
    keep_backward = 1.0 - afters.astype(jnp.float32)
    weights = (norm_gain, norm_bias, decay_rate, step_log, frequency, in_proj.astype(jnp.float32), out_proj.astype(jnp.float32), skip_gain, gate_proj.astype(jnp.float32))

    def forward(stream, layer_weights):
        for layer_index in range(LAYERS):
            picked = tuple((weight[layer_index] for weight in layer_weights))
            backward_flag = layer_index % 2 == 1
            keep_mask = keep_backward if backward_flag else keep_forward
            stream = residual_layer(stream, keep_mask, backward_flag, picked)
        return stream
    layer_out, pullback = jax.vjp(forward, tokens_in.astype(jnp.float32), weights)
    grad_in, weight_grads = pullback(grad_out.astype(jnp.float32))
    return (layer_out, grad_in, weight_grads[0], weight_grads[1], weight_grads[2], weight_grads[3], weight_grads[4], weight_grads[5], weight_grads[6], weight_grads[7], weight_grads[8])
```

```python
import functools

import jax
import jax.numpy as jnp
from jax import lax
from jax.experimental import pallas as pl
from jax.experimental.pallas import tpu as pltpu
from jax.sharding import PartitionSpec as P

LAYERS = 2
EPSILON = 1e-05
LANES = 8
VMEM_LIMIT = 48 * 1024 * 1024
GELU_A = 0.7978845608028654
GELU_B = 0.044715
NT = (((1,), (1,)), ((), ()))
TN = (((0,), (0,)), ((), ()))
F32 = jnp.float32
BF16 = jnp.bfloat16


def discretize(decay_rate, step_log, frequency):
    step_size = jnp.exp(step_log)
    real_angle = -decay_rate * step_size
    imag_angle = frequency * step_size
    magnitude = jnp.exp(real_angle)
    cosine = jnp.cos(imag_angle)
    sine = jnp.sin(imag_angle)
    decay_row = jnp.concatenate([magnitude * cosine, magnitude * sine], axis=-1)
    minus_real = jnp.expm1(real_angle) * cosine - 2.0 * jnp.sin(0.5 * imag_angle) ** 2
    minus_imag = magnitude * sine
    modulus = decay_rate * decay_rate + frequency * frequency
    factor_real = (-decay_rate * minus_real + frequency * minus_imag) / modulus
    factor_imag = (-decay_rate * minus_imag - frequency * minus_real) / modulus
    return (decay_row, jnp.concatenate([factor_real, factor_imag], axis=-1))


def decay_power(decay_rate, step_log, frequency, count):
    step_size = jnp.exp(step_log)
    magnitude = jnp.exp(-(decay_rate * step_size) * count)
    angle = (frequency * step_size) * count
    return jnp.concatenate([magnitude * jnp.cos(angle), magnitude * jnp.sin(angle)], axis=-1)


def shifted(value, axis, count):
    size = lax.axis_size(axis)
    return lax.ppermute(value, axis, [(i, (i + count) % size) for i in range(size)])


def along(value, axis):
    return [value] + [shifted(value, axis, k) for k in range(1, lax.axis_size(axis))]


def gather_parts(row):
    return along(jnp.concatenate(along(row, "grp"), axis=0), "seq")


def sum_parts(value):
    parts = along(value, "grp")
    return along(functools.reduce(jnp.add, parts), "seq")


def cols(c):
    return slice(c * 128, (c + 1) * 128)


def chunk_count(ref):
    return ref.shape[-1] // 256


def rows_of(ref, at, chunks):
    half = chunks * 128
    re = [ref[at, c * 128 : (c + 1) * 128] for c in range(chunks)]
    im = [ref[at, half + c * 128 : half + (c + 1) * 128] for c in range(chunks)]
    return re, im


def put_rows(ref, at, re, im):
    chunks = len(re)
    half = chunks * 128
    for c in range(chunks):
        ref[at, c * 128 : (c + 1) * 128] = re[c]
        ref[at, half + c * 128 : half + (c + 1) * 128] = im[c]


def wide(rows):
    return [jnp.broadcast_to(v, (LANES, 128)) for v in rows]


def chain(ends_ref, jr_ref, power, carry, down, start_ref=None):
    chunks = len(power[0])
    pr, pi = power
    cr, ci = carry
    order = range(LANES - 1, -1, -1) if down else range(LANES)
    for s in order:
        at = slice(s, s + 1)
        if start_ref is not None:
            put_rows(start_ref, at, cr, ci)
        er, ei = rows_of(ends_ref, at, chunks)
        alive = (jr_ref[at, :] < 0).astype(F32)
        cr, ci = (
            [er[c] + alive * (pr[c] * cr[c] - pi[c] * ci[c]) for c in range(chunks)],
            [ei[c] + alive * (pr[c] * ci[c] + pi[c] * cr[c]) for c in range(chunks)],
        )
    return cr, ci


def carry_in(end_refs, table_ref, chunks):
    half = chunks * 128
    re = jnp.zeros((1, half), F32)
    im = jnp.zeros((1, half), F32)
    group = end_refs[0].shape[0]
    for k, ref in enumerate(end_refs):
        er, ei = ref[:, :half], ref[:, half:]
        tr = table_ref[k * group : (k + 1) * group, :half]
        ti = table_ref[k * group : (k + 1) * group, half:]
        re += jnp.sum(tr * er - ti * ei, axis=0, keepdims=True)
        im += jnp.sum(tr * ei + ti * er, axis=0, keepdims=True)
    return (
        [re[:, cols(c)] for c in range(chunks)],
        [im[:, cols(c)] for c in range(chunks)],
    )


def scan_tile(src_ref, st_ref, decay, jr_ref, first_step, steps, down, emit=None, unroll=4):
    chunks = chunk_count(src_ref)
    dr, di = wide(decay[0]), wide(decay[1])
    jr = jr_ref[...]
    re, im = rows_of(st_ref, slice(0, LANES), chunks)

    def one(step, re, im):
        at = pl.ds(pl.multiple_of(step * LANES, LANES), LANES)
        br, bi = rows_of(src_ref, at, chunks)
        live = jr != first_step + step
        nr, ni = [], []
        for c in range(chunks):
            xr = jnp.where(live, re[c], 0.0)
            xi = jnp.where(live, im[c], 0.0)
            nr.append(dr[c] * xr - di[c] * xi + br[c])
            ni.append(dr[c] * xi + di[c] * xr + bi[c])
        return nr, ni

    def body(i, carry):
        re, im = list(carry[:chunks]), list(carry[chunks : 2 * chunks])
        extra = carry[2 * chunks :]
        for q in range(unroll):
            n = 2 * (i * unroll + q)
            low_step = steps - 2 - n if down else n
            a, b = (low_step + 1, low_step) if down else (low_step, low_step + 1)
            r1, i1 = one(a, re, im)
            r2, i2 = one(b, r1, i1)
            if emit is not None:
                pair = ((r2, i2), (r1, i1)) if down else ((r1, i1), (r2, i2))
                extra = emit(low_step, pair, extra)
            re, im = r2, i2
        return tuple(re) + tuple(im) + tuple(extra)

    start = tuple(re) + tuple(im)
    if emit is not None:
        start = start + tuple(emit(None, None, None))
    out = lax.fori_loop(0, steps // (2 * unroll), body, start)
    put_rows(st_ref, slice(0, LANES), list(out[:chunks]), list(out[chunks : 2 * chunks]))
    return out[2 * chunks :]


def store_pair(ref, low_step, first, second):
    at = pl.ds(pl.multiple_of(low_step * LANES, 2 * LANES), 2 * LANES)
    re = [jnp.concatenate([p, q], axis=0).astype(BF16) for p, q in zip(first[0], second[0])]
    im = [jnp.concatenate([p, q], axis=0).astype(BF16) for p, q in zip(first[1], second[1])]
    put_rows(ref, at, re, im)


def disc_row(disc_ref, row, chunks, conj=False):
    re, im = rows_of(disc_ref, slice(row, row + 1), chunks)
    return (re, [-v for v in im]) if conj else (re, im)


def column_sum(value):
    rows, width = value.shape
    return jnp.sum(jnp.sum(value.reshape(rows // 8, 8, width), axis=0), axis=0, keepdims=True)


def permute_in(block, order_ref):
    runs, steps, width = block.shape
    span = order_ref.shape[0] // runs
    out = []
    for k in range(steps // span):
        part = block[:, k * span : (k + 1) * span, :].reshape(runs * span, width)
        out.append(jnp.dot(order_ref[...], part, preferred_element_type=F32))
    return out[0] if len(out) == 1 else jnp.concatenate(out, axis=0)


def permute_out(value, order_ref, out_ref):
    rows, width = value.shape
    size = order_ref.shape[0]
    span = size // LANES
    high = value.astype(BF16)
    low = (value - high.astype(F32)).astype(BF16)
    for k in range(rows // size):
        at = slice(k * size, (k + 1) * size)
        back = lax.dot_general(order_ref[...], high[at], TN, preferred_element_type=F32)
        back += lax.dot_general(order_ref[...], low[at], TN, preferred_element_type=F32)
        out_ref[:, k * span : (k + 1) * span, :] = back.reshape(LANES, span, width)


def stats_kernel(tok_ref, order_ref, u_ref, stats_ref):
    value = permute_in(tok_ref[...], order_ref)
    u_ref[...] = value.astype(BF16)
    add_stats(stats_ref, value)


def add_stats(stats_ref, value):
    part = jnp.concatenate([column_sum(value), column_sum(value * value)], axis=0)

    @pl.when(pl.program_id(0) == 0)
    def _():
        stats_ref[...] = part

    @pl.when(pl.program_id(0) != 0)
    def _():
        stats_ref[...] += part


def drive_kernel(parts, down, tokens, *refs):
    stat_refs = refs[:parts]
    (u_ref, prm_ref, win_ref, disc_ref, jr_ref, b_ref, end_ref, blk_ref, norm_ref) = refs[parts:]
    i, nt = pl.program_id(0), pl.num_programs(0)
    steps = u_ref.shape[0] // LANES
    chunks = chunk_count(b_ref)
    half = chunks * 128

    @pl.when(i == 0)
    def _():
        total = functools.reduce(jnp.add, [ref[...] for ref in stat_refs])
        mean = total[0:1] / tokens
        inv = lax.rsqrt(total[1:2] / tokens - mean * mean + EPSILON)
        norm_ref[0:1] = mean
        norm_ref[1:2] = inv
        norm_ref[2:3] = inv * prm_ref[0:1]
        norm_ref[3:4] = prm_ref[1:2]
        norm_ref[4:5] = prm_ref[2:3]
        norm_ref[5:8] = jnp.zeros((3, norm_ref.shape[1]), F32)
        blk_ref[...] = jnp.zeros_like(blk_ref)

    u = u_ref[...].astype(F32)
    normed = (u - norm_ref[0:1]) * norm_ref[2:3] + norm_ref[3:4]
    drive = jnp.dot(normed.astype(BF16), win_ref[...], preferred_element_type=F32)
    fr, fi = disc_ref[1:2, :half], disc_ref[1:2, half:]
    re, im = drive[:, :half], drive[:, half:]
    b_ref[:, :half] = re * fr - im * fi
    b_ref[:, half:] = re * fi + im * fr
    tile = nt - 1 - i if down else i
    scan_tile(b_ref, blk_ref, disc_row(disc_ref, 0, chunks), jr_ref, tile * steps, steps, down)

    @pl.when(i == nt - 1)
    def _():
        zero = [jnp.zeros((1, 128), F32)] * chunks
        cr, ci = chain(blk_ref, jr_ref, disc_row(disc_ref, 2, chunks), (zero, zero), down)
        put_rows(end_ref, slice(0, 1), cr, ci)


def states_of(parts_refs, table_ref, b_ref, blk_ref, disc_ref, jr_ref, low_ref, st_ref, down):
    i, nt = pl.program_id(0), pl.num_programs(0)
    chunks = chunk_count(b_ref)
    steps = b_ref.shape[0] // LANES

    @pl.when(i == 0)
    def _():
        carry = carry_in(parts_refs, table_ref, chunks)
        chain(blk_ref, jr_ref, disc_row(disc_ref, 2, chunks), carry, down, st_ref)

    def emit(low_step, pair, extra):
        if pair is None:
            return ()
        (first, second) = pair
        store_pair(low_ref, low_step, first, second)
        return ()

    tile = nt - 1 - i if down else i
    scan_tile(
        b_ref, st_ref, disc_row(disc_ref, 0, chunks), jr_ref, tile * steps, steps, down, emit
    )


def gelu_parts(mixed):
    square = mixed * mixed
    tanh = jnp.tanh(mixed * (GELU_A + (GELU_A * GELU_B) * square))
    half_up = 0.5 + 0.5 * tanh
    return square, tanh, half_up


def gelu_slope(mixed, square, tanh, half_up):
    return half_up + (mixed * (0.5 - 0.5 * tanh * tanh)) * (
        GELU_A + (3.0 * GELU_A * GELU_B) * square
    )


def sigmoid(value):
    return 0.5 + 0.5 * jnp.tanh(0.5 * value)


def forward_kernel(parts, down, *refs):
    parts_refs = refs[:parts]
    (
        table_ref, b_ref, blk_ref, disc_ref, jr_ref, u_ref, norm_ref, wout_ref, wgate_ref,
        next_ref, low_ref, mixed_ref, gate_ref, stats_ref, st_ref,
    ) = refs[parts:]
    states_of(parts_refs, table_ref, b_ref, blk_ref, disc_ref, jr_ref, low_ref, st_ref, down)
    u = u_ref[...].astype(F32)
    normed = (u - norm_ref[0:1]) * norm_ref[2:3] + norm_ref[3:4]
    mixed = jnp.dot(low_ref[...], wout_ref[...], preferred_element_type=F32)
    mixed += norm_ref[4:5] * normed
    _, _, half_up = gelu_parts(mixed)
    act = mixed * half_up
    gate = sigmoid(jnp.dot(act.astype(BF16), wgate_ref[...], preferred_element_type=F32))
    after = u + act * gate
    next_ref[...] = after
    mixed_ref[...] = mixed.astype(mixed_ref.dtype)
    gate_ref[...] = gate.astype(gate_ref.dtype)
    add_stats(stats_ref, after)


def accumulate(ref, value):
    @pl.when(pl.program_id(0) == 0)
    def _():
        ref[...] = value

    @pl.when(pl.program_id(0) != 0)
    def _():
        ref[...] += value


def gate_backward(g, mixed, gate, normed, low_ref, wout_ref, wgate_ref, outs, kept=None):
    pg_ref, sg_ref, gsum_ref, osum_ref, ssum_ref = outs
    square, tanh, half_up = gelu_parts(mixed) if kept is None else kept
    act = mixed * half_up
    g_gate = g * gate
    logit_grad = (g_gate * act * (1.0 - gate)).astype(BF16)
    accumulate(
        gsum_ref,
        lax.dot_general(act.astype(BF16), logit_grad, TN, preferred_element_type=F32),
    )
    act_grad = g_gate + lax.dot_general(
        logit_grad, wgate_ref[...], NT, preferred_element_type=F32
    )
    mixed_grad = act_grad * gelu_slope(mixed, square, tanh, half_up)
    accumulate(ssum_ref, column_sum(mixed_grad * normed))
    proj_grad = mixed_grad.astype(BF16)
    pg_ref[...] = proj_grad
    accumulate(osum_ref, lax.dot_general(low_ref[...], proj_grad, TN, preferred_element_type=F32))
    sg_ref[...] = lax.dot_general(proj_grad, wout_ref[...], NT, preferred_element_type=F32)


def turn_kernel(parts, down, *refs):
    parts_refs = refs[:parts]
    (
        table_ref, b_ref, blk_ref, disc_ref, jr_ref, jo_ref, u_ref, norm_ref, wout_ref, wgate_ref,
        gout_ref, order_ref,
        out_ref, low_ref, g_ref, pg_ref, sg_ref, gsum_ref, osum_ref, ssum_ref, end_ref, ablk_ref,
        st_ref, w_ref,
    ) = refs[parts:]
    i, nt = pl.program_id(0), pl.num_programs(0)
    chunks = chunk_count(b_ref)
    half = chunks * 128
    steps = b_ref.shape[0] // LANES
    tile = nt - 1 - i if down else i
    states_of(parts_refs, table_ref, b_ref, blk_ref, disc_ref, jr_ref, low_ref, st_ref, down)
    u = u_ref[...]
    normed = (u - norm_ref[0:1]) * norm_ref[2:3] + norm_ref[3:4]
    mixed = jnp.dot(low_ref[...], wout_ref[...], preferred_element_type=F32)
    mixed += norm_ref[4:5] * normed
    kept = gelu_parts(mixed)
    act = mixed * kept[2]
    gate = sigmoid(jnp.dot(act.astype(BF16), wgate_ref[...], preferred_element_type=F32))
    permute_out(u + act * gate, order_ref, out_ref)
    g = permute_in(gout_ref[...], order_ref)
    g_ref[...] = g.astype(BF16)
    gate_backward(
        g, mixed, gate, normed, low_ref, wout_ref, wgate_ref,
        (pg_ref, sg_ref, gsum_ref, osum_ref, ssum_ref), kept,
    )

    @pl.when(i == 0)
    def _():
        w_ref[:, :half] = jnp.ones((LANES, half), F32)
        w_ref[:, half:] = jnp.zeros((LANES, half), F32)
        ablk_ref[...] = jnp.zeros_like(ablk_ref)

    dr, di = disc_row(disc_ref, 0, chunks, conj=True)
    dr, di = wide(dr), wide(di)
    jo = jo_ref[...]
    unroll = 4

    def body(k, carry):
        wr, wi, ar, ai = (list(carry[n * chunks : (n + 1) * chunks]) for n in range(4))
        for q in range(unroll):
            n = k * unroll + q
            step = steps - 1 - n if down else n
            at = pl.ds(pl.multiple_of(step * LANES, LANES), LANES)
            sr, si = rows_of(sg_ref, at, chunks)
            live = jo != tile * steps + step
            for c in range(chunks):
                ar[c] = ar[c] + (wr[c] * sr[c] - wi[c] * si[c])
                ai[c] = ai[c] + (wr[c] * si[c] + wi[c] * sr[c])
                xr = jnp.where(live, wr[c], 0.0)
                xi = jnp.where(live, wi[c], 0.0)
                wr[c] = xr * dr[c] - xi * di[c]
                wi[c] = xr * di[c] + xi * dr[c]
        return tuple(wr) + tuple(wi) + tuple(ar) + tuple(ai)

    wr, wi = rows_of(w_ref, slice(0, LANES), chunks)
    ar, ai = rows_of(ablk_ref, slice(0, LANES), chunks)
    out = lax.fori_loop(
        0, steps // unroll, body, tuple(wr) + tuple(wi) + tuple(ar) + tuple(ai)
    )
    wr, wi, ar, ai = (list(out[n * chunks : (n + 1) * chunks]) for n in range(4))
    put_rows(w_ref, slice(0, LANES), wr, wi)
    put_rows(ablk_ref, slice(0, LANES), ar, ai)

    @pl.when(i == nt - 1)
    def _():
        zero = [jnp.zeros((1, 128), F32)] * chunks
        power = disc_row(disc_ref, 2, chunks, conj=True)
        cr, ci = chain(ablk_ref, jo_ref, power, (zero, zero), not down)
        put_rows(end_ref, slice(0, 1), cr, ci)


def adjoint_kernel(parts, down, unpermute, *refs):
    parts_refs = refs[:parts]
    (
        table_ref, sg_ref, ablk_ref, disc_ref, jr_ref, low_ref, u_ref, norm_ref, pg_ref, g_ref,
        win_ref, order_ref,
        res_ref, isum_ref, nsum_ref, dsum_ref, fsum_ref, st_ref, dg_ref, ax_ref,
    ) = refs[parts:]
    i, nt = pl.program_id(0), pl.num_programs(0)
    chunks = chunk_count(sg_ref)
    half = chunks * 128
    steps = sg_ref.shape[0] // LANES
    tile = nt - 1 - i if down else i

    @pl.when(i == 0)
    def _():
        carry = carry_in(parts_refs, table_ref, chunks)
        power = disc_row(disc_ref, 2, chunks, conj=True)
        chain(ablk_ref, jr_ref, power, carry, down, st_ref)
        ax_ref[...] = jnp.zeros_like(ax_ref)

    fr, fi = disc_row(disc_ref, 1, chunks)
    fr, fi = wide(fr), wide(fi)

    def emit(low_step, pair, extra):
        if pair is None:
            re, im = rows_of(ax_ref, slice(0, LANES), chunks)
            return tuple(re) + tuple(im)
        sums_r, sums_i = list(extra[:chunks]), list(extra[chunks:])
        at = pl.ds(pl.multiple_of(low_step * LANES, 2 * LANES), 2 * LANES)
        xr, xi = rows_of(low_ref, at, chunks)
        grads = []
        for which, (ar, ai) in enumerate(pair):
            gr, gi = [], []
            rows = slice(which * LANES, (which + 1) * LANES)
            for c in range(chunks):
                vr, vi = xr[c].astype(F32)[rows], xi[c].astype(F32)[rows]
                sums_r[c] = sums_r[c] + (ar[c] * vr + ai[c] * vi)
                sums_i[c] = sums_i[c] + (ai[c] * vr - ar[c] * vi)
                gr.append(ar[c] * fr[c] + ai[c] * fi[c])
                gi.append(ai[c] * fr[c] - ar[c] * fi[c])
            grads.append((gr, gi))
        store_pair(dg_ref, low_step, grads[0], grads[1])
        return tuple(sums_r) + tuple(sums_i)

    sums = scan_tile(
        sg_ref, st_ref, disc_row(disc_ref, 0, chunks, conj=True), jr_ref, tile * steps, steps,
        down, emit,
    )
    put_rows(ax_ref, slice(0, LANES), list(sums[:chunks]), list(sums[chunks:]))

    u = u_ref[...].astype(F32)
    centered = u - norm_ref[0:1]
    normed = (centered * norm_ref[2:3] + norm_ref[3:4]).astype(BF16)
    drive_grad = dg_ref[...]
    accumulate(isum_ref, lax.dot_general(normed, drive_grad, TN, preferred_element_type=F32))
    normed_grad = lax.dot_general(drive_grad, win_ref[...], NT, preferred_element_type=F32)
    normed_grad += norm_ref[4:5] * pg_ref[...].astype(F32)
    accumulate(
        nsum_ref,
        jnp.concatenate(
            [column_sum(normed_grad), column_sum(normed_grad * centered) * norm_ref[1:2]], axis=0
        ),
    )
    result = g_ref[...].astype(F32) + norm_ref[2:3] * normed_grad
    if unpermute:
        permute_out(result, order_ref, res_ref)
    else:
        res_ref[...] = result

    @pl.when(i == nt - 1)
    def _():
        dsum_ref[...] = jnp.sum(ax_ref[...], axis=0, keepdims=True)
        wr, wi = win_ref[:, :half].astype(F32), win_ref[:, half:].astype(F32)
        gr, gi = isum_ref[:, :half], isum_ref[:, half:]
        re = jnp.sum(wr * gr + wi * gi, axis=0, keepdims=True)
        im = jnp.sum(wr * gi - wi * gr, axis=0, keepdims=True)
        gr, gi = disc_ref[1:2, :half], disc_ref[1:2, half:]
        scale = 1.0 / (gr * gr + gi * gi)
        fsum_ref[:, :half] = (re * gr - im * gi) * scale
        fsum_ref[:, half:] = (re * gi + im * gr) * scale


def back_kernel(parts, down, tokens, *refs):
    parts_refs = refs[:parts]
    (
        r_ref, up_ref, up_norm_ref, mixed_ref, gate_ref, low_ref, u_ref, norm_ref, wout_ref,
        wgate_ref, disc_ref, jo_ref,
        g_ref, pg_ref, sg_ref, gsum_ref, osum_ref, ssum_ref, end_ref, ablk_ref, nsum_ref,
    ) = refs[parts:]
    i, nt = pl.program_id(0), pl.num_programs(0)
    chunks = chunk_count(sg_ref)
    steps = sg_ref.shape[0] // LANES
    tile = nt - 1 - i if down else i

    @pl.when(i == 0)
    def _():
        nsum_ref[...] = functools.reduce(jnp.add, [ref[...] for ref in parts_refs])
        ablk_ref[...] = jnp.zeros_like(ablk_ref)

    scale = up_norm_ref[2:3] * (-1.0 / tokens)
    standard = (up_ref[...] - up_norm_ref[0:1]) * (scale * up_norm_ref[1:2] * nsum_ref[1:2])
    g = r_ref[...] + (standard + scale * nsum_ref[0:1])
    g_ref[...] = g
    u = u_ref[...].astype(F32)
    normed = (u - norm_ref[0:1]) * norm_ref[2:3] + norm_ref[3:4]
    gate_backward(
        g, mixed_ref[...].astype(F32), gate_ref[...].astype(F32), normed, low_ref, wout_ref,
        wgate_ref, (pg_ref, sg_ref, gsum_ref, osum_ref, ssum_ref),
    )
    decay = disc_row(disc_ref, 0, chunks, conj=True)
    scan_tile(sg_ref, ablk_ref, decay, jo_ref, tile * steps, steps, down)

    @pl.when(i == nt - 1)
    def _():
        zero = [jnp.zeros((1, 128), F32)] * chunks
        power = disc_row(disc_ref, 2, chunks, conj=True)
        cr, ci = chain(ablk_ref, jo_ref, power, (zero, zero), down)
        put_rows(end_ref, slice(0, 1), cr, ci)


def whole(array):
    shape = array.shape
    return pl.BlockSpec(shape, lambda i: (0,) * len(shape))


def tile_spec(rows, width, nt, down):
    if down:
        return pl.BlockSpec((rows, width), lambda i: (nt - 1 - i, 0))
    return pl.BlockSpec((rows, width), lambda i: (i, 0))


def run_spec(steps, width, nt, down):
    if down:
        return pl.BlockSpec((LANES, steps, width), lambda i: (0, nt - 1 - i, 0))
    return pl.BlockSpec((LANES, steps, width), lambda i: (0, i, 0))


def call(kernel, nt, args, outs, scratch, flops, name):
    arrays = [a for a, _ in args]
    sizes = sum(a.size * a.dtype.itemsize for a in arrays)
    sizes += sum(a.size * a.dtype.itemsize for a, _ in outs)
    return pl.pallas_call(
        kernel,
        grid=(nt,),
        in_specs=[whole(a) if s is None else s for a, s in args],
        out_specs=[whole(a) if s is None else s for a, s in outs],
        out_shape=[a for a, _ in outs],
        scratch_shapes=scratch,
        compiler_params=pltpu.CompilerParams(
            vmem_limit_bytes=VMEM_LIMIT, dimension_semantics=("arbitrary",)
        ),
        cost_estimate=pl.CostEstimate(flops=flops, bytes_accessed=sizes, transcendentals=0),
        name=name,
    )(*arrays)


def shape(*dims, dtype=F32):
    return jax.ShapeDtypeStruct(dims, dtype)


def body(
    tokens_in,
    seq_starts,
    norm_gain,
    norm_bias,
    decay_rate,
    step_log,
    frequency,
    in_proj,
    out_proj,
    skip_gain,
    gate_proj,
    grad_out,
):
    rows, width = tokens_in.shape
    states = in_proj.shape[-1]
    seq_size, grp_size = lax.axis_size("seq"), lax.axis_size("grp")
    devices = seq_size * grp_size
    total = rows * devices
    tokens = float(total)
    run = rows // LANES
    steps = min(64, run)
    tile = steps * LANES
    nt = rows // tile
    seq_at, grp_at = lax.axis_index("seq"), lax.axis_index("grp")
    me = seq_at * grp_size + grp_at

    run_base = me * rows + run * jnp.arange(LANES, dtype=jnp.int32)
    rel = seq_starts[None, :] - run_base[:, None]
    cut_up = jnp.max(jnp.where((rel >= 0) & (rel < run), rel, -1), axis=1)
    ends = jnp.concatenate([seq_starts, jnp.full((1,), total, jnp.int32)])
    rel = ends[None, :] - 1 - run_base[:, None]
    cut_down = jnp.max(jnp.where((rel >= 0) & (rel < run), rel, -1), axis=1)
    cuts = (
        jnp.broadcast_to(cut_up[:, None], (LANES, 128)),
        jnp.broadcast_to(cut_down[:, None], (LANES, 128)),
    )

    from_seq = (seq_at - jnp.arange(seq_size, dtype=jnp.int32)) % seq_size
    from_grp = (grp_at - jnp.arange(grp_size, dtype=jnp.int32)) % grp_size
    source = (from_seq[:, None] * grp_size + from_grp[None, :]).reshape(-1)
    begin_up = ((source + 1) * rows)[:, None]
    cut = (seq_starts[None, :] >= begin_up) & (seq_starts[None, :] < me * rows)
    up_live = (source < me) & ~jnp.any(cut, axis=1)
    up_count = jnp.maximum(me - 1 - source, 0) * rows
    stop = (source * rows)[:, None]
    cut = (seq_starts[None, :] > (me + 1) * rows) & (seq_starts[None, :] <= stop)
    down_live = (source > me) & ~jnp.any(cut, axis=1)
    down_count = jnp.maximum(source - me - 1, 0) * rows
    lives, counts = (up_live, down_live), (up_count, down_count)
    flip = jnp.concatenate([jnp.ones((states // 2,), F32), -jnp.ones((states // 2,), F32)])

    span = min(32, steps)
    place = jnp.arange(span * LANES)
    order = (
        (place[:, None] % LANES) * span + place[:, None] // LANES == place[None, :]
    ).astype(BF16)

    discs, tables, prms = [], [], []
    for l in range(LAYERS):
        pick = (decay_rate[l], step_log[l], frequency[l])
        decay, factor = discretize(*pick)
        power = decay_power(*pick, float(run))
        discs.append(
            jnp.concatenate(
                [decay[None], factor[None], power[None], jnp.zeros((5, states), F32)], axis=0
            )
        )
        down = l % 2
        pair = []
        for way, sign in ((down, None), (1 - down, flip)):
            table = decay_power(
                pick[0][None], pick[1][None], pick[2][None], counts[way].astype(F32)[:, None]
            )
            table = jnp.where(lives[way][:, None], table, 0.0)
            pair.append(table if sign is None else table * sign[None])
        tables.append(pair)
        prms.append(jnp.stack([norm_gain[l], norm_bias[l], skip_gain[l]]))

    def tiles(array, down):
        return (array, tile_spec(tile, array.shape[-1], nt, down))

    def runs(array, down):
        return (array, run_spec(steps, array.shape[-1], nt, down))

    def full(array):
        return (array, None)

    tokens_run = tokens_in.reshape(LANES, run, width)
    grad_run = grad_out.reshape(LANES, run, width)
    state_scratch = pltpu.VMEM((LANES, states), F32)
    cost_in = 2 * rows * width * states
    cost_gate = 2 * rows * width * width

    u0, stats = call(
        stats_kernel, nt, [runs(tokens_run, 0), full(order)],
        [tiles(shape(rows, width, dtype=BF16), 0), full(shape(2, width))],
        [], rows * width * 8, "stats",
    )

    def drive(l, stream, stats):
        down = l % 2
        parts = sum_parts(stats)
        return call(
            functools.partial(drive_kernel, len(parts), bool(down), tokens), nt,
            [full(p) for p in parts]
            + [tiles(stream, down), full(prms[l]), full(in_proj[l]), full(discs[l]),
               full(cuts[down])],
            [tiles(shape(rows, states), down), full(shape(1, states)),
             full(shape(LANES, states)), full(shape(8, width))],
            [], cost_in, f"drive_{l}",
        )

    b0, end0, blk0, norm0 = drive(0, u0, stats)
    parts = gather_parts(end0)
    u1, low0, mixed0, gate0, stats = call(
        functools.partial(forward_kernel, len(parts), False), nt,
        [full(p) for p in parts]
        + [full(tables[0][0]), tiles(b0, 0), full(blk0), full(discs[0]), full(cuts[0]),
           tiles(u0, 0), full(norm0), full(out_proj[0]), full(gate_proj[0])],
        [tiles(shape(rows, width), 0), tiles(shape(rows, states, dtype=BF16), 0),
         tiles(shape(rows, width, dtype=BF16), 0), tiles(shape(rows, width, dtype=BF16), 0),
         full(shape(2, width))],
        [state_scratch], cost_in + cost_gate, "forward_0",
    )

    b1, end1, blk1, norm1 = drive(1, u1, stats)
    parts = gather_parts(end1)
    (
        out, low1, g1, pg1, sg1, gate_sum1, out_sum1, skip_sum1, aend1, ablk1
    ) = call(
        functools.partial(turn_kernel, len(parts), True), nt,
        [full(p) for p in parts]
        + [full(tables[1][0]), tiles(b1, 1), full(blk1), full(discs[1]), full(cuts[1]),
           full(cuts[0]), tiles(u1, 1), full(norm1), full(out_proj[1]), full(gate_proj[1]),
           runs(grad_run, 1), full(order)],
        [runs(shape(LANES, run, width), 1), tiles(shape(rows, states, dtype=BF16), 1),
         tiles(shape(rows, width, dtype=BF16), 1), tiles(shape(rows, width, dtype=BF16), 1),
         tiles(shape(rows, states), 1), full(shape(width, width)), full(shape(states, width)),
         full(shape(1, width)), full(shape(1, states)), full(shape(LANES, states))],
        [state_scratch, state_scratch], 3 * cost_in + 3 * cost_gate, "turn_1",
    )

    def adjoint(l, sg, ablk, aend, low, stream, norm, pg, g):
        down = 1 - l % 2
        parts = gather_parts(aend)
        last = l == 0
        return call(
            functools.partial(adjoint_kernel, len(parts), bool(down), last), nt,
            [full(p) for p in parts]
            + [full(tables[l][1]), tiles(sg, down), full(ablk), full(discs[l]), full(cuts[down]),
               tiles(low, down), tiles(stream, down), full(norm), tiles(pg, down),
               tiles(g, down), full(in_proj[l]), full(order)],
            [runs(shape(LANES, run, width), down) if last else tiles(shape(rows, width), down),
             full(shape(width, states)), full(shape(2, width)), full(shape(1, states)),
             full(shape(1, states))],
            [state_scratch, pltpu.VMEM((tile, states), BF16), state_scratch], 2 * cost_in,
            f"adjoint_{l}",
        )

    r1, in_sum1, norm_sum1, dsum1, fsum1 = adjoint(1, sg1, ablk1, aend1, low1, u1, norm1, pg1, g1)
    parts = sum_parts(norm_sum1)
    (
        g0, pg0, sg0, gate_sum0, out_sum0, skip_sum0, aend0, ablk0, norm_all1
    ) = call(
        functools.partial(back_kernel, len(parts), True, tokens), nt,
        [full(p) for p in parts]
        + [tiles(r1, 1), tiles(u1, 1), full(norm1), tiles(mixed0, 1), tiles(gate0, 1),
           tiles(low0, 1), tiles(u0, 1), full(norm0), full(out_proj[0]), full(gate_proj[0]),
           full(discs[0]), full(cuts[1])],
        [tiles(shape(rows, width), 1), tiles(shape(rows, width, dtype=BF16), 1),
         tiles(shape(rows, states), 1), full(shape(width, width)), full(shape(states, width)),
         full(shape(1, width)), full(shape(1, states)), full(shape(LANES, states)),
         full(shape(2, width))],
        [], 2 * cost_in + 2 * cost_gate, "back_0",
    )
    r0, in_sum0, norm_sum0, dsum0, fsum0 = adjoint(0, sg0, ablk0, aend0, low0, u0, norm0, pg0, g0)

    small = jnp.concatenate(
        [
            v.reshape(-1, 128)
            for v in (norm_sum0, skip_sum0, skip_sum1, dsum0, dsum1, fsum0, fsum1)
        ],
        axis=0,
    )
    small = functools.reduce(jnp.add, sum_parts(small)).reshape(-1)
    norm_all0 = small[: 2 * width].reshape(2, width)
    skip_grad = small[2 * width : 4 * width].reshape(LAYERS, width)
    dsum = small[4 * width : 4 * width + 2 * states].reshape(LAYERS, states)
    fsum = small[4 * width + 2 * states :].reshape(LAYERS, states)

    scale = norm0[2:3] * (-1.0 / tokens)
    grad_in = r0.reshape(rows, width) + (
        (tokens_in.astype(F32) - norm0[0:1]) * (scale * norm0[1:2] * norm_all0[1:2])
        + scale * norm_all0[0:1]
    )

    gate1, outp1, inp1 = lax.psum((gate_sum1, out_sum1, in_sum1), ("seq", "grp"))
    gate0g, outp0, inp0 = lax.psum((gate_sum0, out_sum0, in_sum0), ("seq", "grp"))

    (decay, factor), discrete_back = jax.vjp(
        jax.vmap(discretize), decay_rate, step_log, frequency
    )
    half = states // 2
    dr, di = decay[:, :half], decay[:, half:]
    fr, fi = factor[:, :half], factor[:, half:]
    sr, si = fsum[:, :half], fsum[:, half:]
    tr = dsum[:, :half] - (fr * sr + fi * si)
    ti = dsum[:, half:] - (fr * si - fi * sr)
    modulus = dr * dr + di * di
    decay_grad = jnp.concatenate(
        [(tr * dr - ti * di) / modulus, (tr * di + ti * dr) / modulus], axis=-1
    )
    rate_grad, step_grad, freq_grad = discrete_back((decay_grad, fsum))
    return (
        out.reshape(rows, width),
        grad_in,
        jnp.stack([norm_all0[1], norm_all1[1]]),
        jnp.stack([norm_all0[0], norm_all1[0]]),
        rate_grad,
        step_grad,
        freq_grad,
        jnp.stack([inp0, inp1]),
        jnp.stack([outp0, outp1]),
        skip_grad,
        jnp.stack([gate0g, gate1]),
    )


def solution(mesh):
    rows = P(("seq", "grp"), None)
    return jax.shard_map(
        body,
        mesh=mesh,
        in_specs=(rows,) + (P(),) * 10 + (rows,),
        out_specs=(rows, rows) + (P(),) * 9,
        check_vma=False,
    )
```

```python
import functools

import jax
import jax.numpy as jnp
from jax import lax
from jax.experimental import pallas as pl
from jax.experimental.pallas import tpu as pltpu
from jax.sharding import PartitionSpec as P

LAYERS = 2
EPSILON = 1e-05
LANES = 8
VMEM_LIMIT = 36 * 1024 * 1024
GELU_A = 0.7978845608028654
GELU_B = 0.044715
NT = (((1,), (1,)), ((), ()))
TN = (((0,), (0,)), ((), ()))
F32 = jnp.float32
BF16 = jnp.bfloat16


def discretize(decay_rate, step_log, frequency):
    step_size = jnp.exp(step_log)
    real_angle = -decay_rate * step_size
    imag_angle = frequency * step_size
    magnitude = jnp.exp(real_angle)
    cosine = jnp.cos(imag_angle)
    sine = jnp.sin(imag_angle)
    decay_row = jnp.concatenate([magnitude * cosine, magnitude * sine], axis=-1)
    minus_real = jnp.expm1(real_angle) * cosine - 2.0 * jnp.sin(0.5 * imag_angle) ** 2
    minus_imag = magnitude * sine
    modulus = decay_rate * decay_rate + frequency * frequency
    factor_real = (-decay_rate * minus_real + frequency * minus_imag) / modulus
    factor_imag = (-decay_rate * minus_imag - frequency * minus_real) / modulus
    return (decay_row, jnp.concatenate([factor_real, factor_imag], axis=-1))


def swapped(value, axis, mask):
    size = lax.axis_size(axis)
    return lax.ppermute(value, axis, [(i, i ^ mask) for i in range(size)])


def axis_phases(axis, radix):
    size, at, out = lax.axis_size(axis), 1, []
    while at < size:
        reach = min(radix, size // at)
        out.append((axis, [at * k for k in range(1, reach)]))
        at *= reach
    return out


def phases(grp_radix, seq_radix):
    return axis_phases("grp", grp_radix) + axis_phases("seq", seq_radix)


def received(value, plan):
    axis, masks = plan
    return [value] + [swapped(value, axis, mask) for mask in masks]


def gather_parts(row, plan):
    for step in plan[:-1]:
        row = jnp.concatenate(received(row, step), axis=0)
    return received(row, plan[-1])


def sum_parts(value, plan):
    for step in plan[:-1]:
        value = functools.reduce(jnp.add, received(value, step))
    return received(value, plan[-1])


def gather_all(row):
    devices = lax.axis_size("seq") * lax.axis_size("grp")
    copies = jnp.broadcast_to(row, (devices,) + row.shape[1:])
    return [lax.all_to_all(copies, ("seq", "grp"), 0, 0, tiled=True)]


def cols(c):
    return slice(c * 128, (c + 1) * 128)


def chunk_count(ref):
    return ref.shape[-1] // 256


def rows_of(ref, at, chunks):
    half = chunks * 128
    re = [ref[at, c * 128 : (c + 1) * 128] for c in range(chunks)]
    im = [ref[at, half + c * 128 : half + (c + 1) * 128] for c in range(chunks)]
    return re, im


def put_rows(ref, at, re, im):
    chunks = len(re)
    half = chunks * 128
    for c in range(chunks):
        ref[at, c * 128 : (c + 1) * 128] = re[c]
        ref[at, half + c * 128 : half + (c + 1) * 128] = im[c]


def wide(rows):
    return [jnp.broadcast_to(v, (LANES, 128)) for v in rows]


def chain(ends_ref, jr_ref, power, carry, down, start_ref=None):
    chunks = len(power[0])
    pr, pi = power
    cr, ci = carry
    order = range(LANES - 1, -1, -1) if down else range(LANES)
    for s in order:
        at = slice(s, s + 1)
        if start_ref is not None:
            put_rows(start_ref, at, cr, ci)
        er, ei = rows_of(ends_ref, at, chunks)
        alive = (jr_ref[at, :] < 0).astype(F32)
        cr, ci = (
            [er[c] + alive * (pr[c] * cr[c] - pi[c] * ci[c]) for c in range(chunks)],
            [ei[c] + alive * (pr[c] * ci[c] + pi[c] * cr[c]) for c in range(chunks)],
        )
    return cr, ci


def carry_in(end_refs, table_ref, chunks):
    half = chunks * 128
    re = jnp.zeros((1, half), F32)
    im = jnp.zeros((1, half), F32)
    group = end_refs[0].shape[0]
    for k, ref in enumerate(end_refs):
        er, ei = ref[:, :half], ref[:, half:]
        tr = table_ref[k * group : (k + 1) * group, :half]
        ti = table_ref[k * group : (k + 1) * group, half:]
        re += jnp.sum(tr * er - ti * ei, axis=0, keepdims=True)
        im += jnp.sum(tr * ei + ti * er, axis=0, keepdims=True)
    return (
        [re[:, cols(c)] for c in range(chunks)],
        [im[:, cols(c)] for c in range(chunks)],
    )


def scan_tile(src_ref, st_ref, decay, jr_ref, first_step, steps, down, emit=None, unroll=4):
    chunks = chunk_count(src_ref)
    dr, di = wide(decay[0]), wide(decay[1])
    jr = jr_ref[...]
    re, im = rows_of(st_ref, slice(0, LANES), chunks)

    def one(step, re, im):
        at = pl.ds(pl.multiple_of(step * LANES, LANES), LANES)
        br, bi = rows_of(src_ref, at, chunks)
        live = jr != first_step + step
        nr, ni = [], []
        for c in range(chunks):
            xr = jnp.where(live, re[c], 0.0)
            xi = jnp.where(live, im[c], 0.0)
            nr.append(dr[c] * xr - di[c] * xi + br[c])
            ni.append(dr[c] * xi + di[c] * xr + bi[c])
        return nr, ni

    def body(i, carry):
        re, im = list(carry[:chunks]), list(carry[chunks : 2 * chunks])
        extra = carry[2 * chunks :]
        for q in range(unroll):
            n = 2 * (i * unroll + q)
            low_step = steps - 2 - n if down else n
            a, b = (low_step + 1, low_step) if down else (low_step, low_step + 1)
            r1, i1 = one(a, re, im)
            r2, i2 = one(b, r1, i1)
            if emit is not None:
                pair = ((r2, i2), (r1, i1)) if down else ((r1, i1), (r2, i2))
                extra = emit(low_step, pair, extra)
            re, im = r2, i2
        return tuple(re) + tuple(im) + tuple(extra)

    start = tuple(re) + tuple(im)
    if emit is not None:
        start = start + tuple(emit(None, None, None))
    out = lax.fori_loop(0, steps // (2 * unroll), body, start)
    put_rows(st_ref, slice(0, LANES), list(out[:chunks]), list(out[chunks : 2 * chunks]))
    return out[2 * chunks :]


def store_pair(ref, low_step, first, second):
    at = pl.ds(pl.multiple_of(low_step * LANES, 2 * LANES), 2 * LANES)
    re = [jnp.concatenate([p, q], axis=0).astype(BF16) for p, q in zip(first[0], second[0])]
    im = [jnp.concatenate([p, q], axis=0).astype(BF16) for p, q in zip(first[1], second[1])]
    put_rows(ref, at, re, im)


def disc_row(disc_ref, row, chunks, conj=False):
    re, im = rows_of(disc_ref, slice(row, row + 1), chunks)
    return (re, [-v for v in im]) if conj else (re, im)


def column_sum(value):
    rows, width = value.shape
    return jnp.sum(jnp.sum(value.reshape(rows // 8, 8, width), axis=0), axis=0, keepdims=True)


def permute_in(block, order_ref):
    runs, steps, width = block.shape
    span = order_ref.shape[0] // runs
    out = []
    for k in range(steps // span):
        part = block[:, k * span : (k + 1) * span, :].reshape(runs * span, width)
        out.append(jnp.dot(order_ref[...], part, preferred_element_type=F32))
    return out[0] if len(out) == 1 else jnp.concatenate(out, axis=0)


def permute_out(value, order_ref, out_ref):
    rows, width = value.shape
    size = order_ref.shape[0]
    span = size // LANES
    high = value.astype(BF16)
    low = (value - high.astype(F32)).astype(BF16)
    for k in range(rows // size):
        at = slice(k * size, (k + 1) * size)
        back = lax.dot_general(order_ref[...], high[at], TN, preferred_element_type=F32)
        back += lax.dot_general(order_ref[...], low[at], TN, preferred_element_type=F32)
        out_ref[:, k * span : (k + 1) * span, :] = back.reshape(LANES, span, width)


def expm1(value):
    acc = jnp.full_like(value, 1.0 / 479001600.0)
    for n in (39916800.0, 3628800.0, 362880.0, 40320.0, 5040.0, 720.0, 120.0, 24.0, 6.0, 2.0, 1.0):
        acc = acc * value + 1.0 / n
    return jnp.where(value > -1.0, acc * value, jnp.exp(value) - 1.0)


def prep_kernel(
    rows, sizes, absolute, starts_ref, rate_ref, step_ref, freq_ref,
    disc_ref, table_ref, cut_ref, order_ref,
):
    seq_size, grp_size = sizes
    devices = seq_size * grp_size
    total = rows * devices
    run = rows // LANES
    half = rate_ref.shape[-1]
    seq_at, grp_at = lax.axis_index("seq"), lax.axis_index("grp")
    me = seq_at * grp_size + grp_at
    starts = [starts_ref[k] for k in range(starts_ref.shape[0])]

    base = me * rows + run * lax.broadcasted_iota(jnp.int32, (LANES, 128), 0)
    up = jnp.full((LANES, 128), -1, jnp.int32)
    down = up
    for begin in starts + [total]:
        rel = begin - base
        up = jnp.maximum(up, jnp.where((rel >= 0) & (rel < run), rel, -1))
        down = jnp.maximum(down, jnp.where((rel >= 1) & (rel <= run), rel - 1, -1))
    cut_ref[0] = up
    cut_ref[1] = down

    size = order_ref.shape[0]
    span = size // LANES
    to = lax.broadcasted_iota(jnp.int32, (size, size), 0)
    back = lax.broadcasted_iota(jnp.int32, (size, size), 1)
    order_ref[...] = ((to % LANES) * span + to // LANES == back).astype(F32).astype(BF16)

    place = lax.broadcasted_iota(jnp.int32, (devices, half), 0)
    near = ((place // grp_size) ^ seq_at) * grp_size + ((place % grp_size) ^ grp_at)
    for l in range(LAYERS):
        at = slice(l, l + 1)
        rate, freq = rate_ref[at], freq_ref[at]
        step_size = jnp.exp(step_ref[at])
        real_angle = -rate * step_size
        imag_angle = freq * step_size
        magnitude = jnp.exp(real_angle)
        cosine, sine = jnp.cos(imag_angle), jnp.sin(imag_angle)
        minus_real = expm1(real_angle) * cosine - 2.0 * jnp.sin(0.5 * imag_angle) ** 2
        minus_imag = magnitude * sine
        modulus = rate * rate + freq * freq
        disc_ref[l, 0:1, :half] = magnitude * cosine
        disc_ref[l, 0:1, half:] = minus_imag
        disc_ref[l, 1:2, :half] = (-rate * minus_real + freq * minus_imag) / modulus
        disc_ref[l, 1:2, half:] = (-rate * minus_imag - freq * minus_real) / modulus
        magnitude = jnp.exp(real_angle * float(run))
        disc_ref[l, 2:3, :half] = magnitude * jnp.cos(imag_angle * float(run))
        disc_ref[l, 2:3, half:] = magnitude * jnp.sin(imag_angle * float(run))
        disc_ref[l, 3:8] = jnp.zeros((5, 2 * half), F32)
        for back in range(2):
            source = place if absolute[l][back] else near
            going_down = (l + back) % 2 == 1
            if going_down:
                live, count = source > me, source - me - 1
            else:
                live, count = source < me, me - 1 - source
            for begin in starts:
                if going_down:
                    cut = ((begin > (me + 1) * rows).astype(jnp.int32) > 0) & (
                        source * rows >= begin
                    )
                else:
                    cut = ((begin < me * rows).astype(jnp.int32) > 0) & (
                        (source + 1) * rows <= begin
                    )
                live &= ~cut
            count = (jnp.maximum(count, 0) * rows).astype(F32)
            magnitude = jnp.where(live, jnp.exp(real_angle * count), 0.0)
            angle = imag_angle * count
            table_ref[2 * l + back, :, :half] = magnitude * jnp.cos(angle)
            imag = magnitude * jnp.sin(angle)
            table_ref[2 * l + back, :, half:] = -imag if back else imag


def stats_kernel(tok_ref, order_ref, u_ref, stats_ref):
    value = permute_in(tok_ref[...], order_ref)
    u_ref[...] = value.astype(BF16)
    add_stats(stats_ref, value)


def add_stats(stats_ref, value):
    part = jnp.concatenate([column_sum(value), column_sum(value * value)], axis=0)

    @pl.when(pl.program_id(0) == 0)
    def _():
        stats_ref[...] = part

    @pl.when(pl.program_id(0) != 0)
    def _():
        stats_ref[...] += part


def summed(refs):
    total = functools.reduce(jnp.add, [ref[...] for ref in refs])
    if total.shape[0] == 2:
        return total
    total = jnp.sum(total, axis=0, keepdims=True)
    width = total.shape[1] // 2
    return jnp.concatenate([total[:, :width], total[:, width:]], axis=0)


def drive_kernel(parts, layer, down, tokens, *refs):
    stat_refs = refs[:parts]
    (
        u_ref, gain_ref, bias_ref, skip_ref, win_ref, disc_ref, jr_ref,
        b_ref, end_ref, blk_ref, norm_ref,
    ) = refs[parts:]
    i, nt = pl.program_id(0), pl.num_programs(0)
    steps = u_ref.shape[0] // LANES
    chunks = chunk_count(b_ref)
    half = chunks * 128

    @pl.when(i == 0)
    def _():
        total = summed(stat_refs)
        row = slice(layer, layer + 1)
        mean = total[0:1] / tokens
        inv = lax.rsqrt(total[1:2] / tokens - mean * mean + EPSILON)
        norm_ref[0:1] = mean
        norm_ref[1:2] = inv
        norm_ref[2:3] = inv * gain_ref[row]
        norm_ref[3:4] = bias_ref[row]
        norm_ref[4:5] = skip_ref[row]
        norm_ref[5:8] = jnp.zeros((3, norm_ref.shape[1]), F32)
        blk_ref[...] = jnp.zeros_like(blk_ref)

    u = u_ref[...].astype(F32)
    normed = (u - norm_ref[0:1]) * norm_ref[2:3] + norm_ref[3:4]
    drive = jnp.dot(normed.astype(BF16), win_ref[...], preferred_element_type=F32)
    fr, fi = disc_ref[1:2, :half], disc_ref[1:2, half:]
    re, im = drive[:, :half], drive[:, half:]
    b_ref[:, :half] = re * fr - im * fi
    b_ref[:, half:] = re * fi + im * fr
    tile = nt - 1 - i if down else i
    scan_tile(b_ref, blk_ref, disc_row(disc_ref, 0, chunks), jr_ref, tile * steps, steps, down)

    @pl.when(i == nt - 1)
    def _():
        zero = [jnp.zeros((1, 128), F32)] * chunks
        cr, ci = chain(blk_ref, jr_ref, disc_row(disc_ref, 2, chunks), (zero, zero), down)
        put_rows(end_ref, slice(0, 1), cr, ci)


def states_of(parts_refs, table_ref, b_ref, blk_ref, disc_ref, jr_ref, low_ref, st_ref, down):
    i, nt = pl.program_id(0), pl.num_programs(0)
    chunks = chunk_count(b_ref)
    steps = b_ref.shape[0] // LANES

    @pl.when(i == 0)
    def _():
        carry = carry_in(parts_refs, table_ref, chunks)
        chain(blk_ref, jr_ref, disc_row(disc_ref, 2, chunks), carry, down, st_ref)

    def emit(low_step, pair, extra):
        if pair is None:
            return ()
        (first, second) = pair
        store_pair(low_ref, low_step, first, second)
        return ()

    tile = nt - 1 - i if down else i
    scan_tile(
        b_ref, st_ref, disc_row(disc_ref, 0, chunks), jr_ref, tile * steps, steps, down, emit
    )


def gelu_parts(mixed):
    square = mixed * mixed
    tanh = jnp.tanh(mixed * (GELU_A + (GELU_A * GELU_B) * square))
    half_up = 0.5 + 0.5 * tanh
    return square, tanh, half_up


def gelu_slope(mixed, square, tanh, half_up):
    return half_up + (mixed * (0.5 - 0.5 * tanh * tanh)) * (
        GELU_A + (3.0 * GELU_A * GELU_B) * square
    )


def sigmoid(value):
    return 0.5 + 0.5 * jnp.tanh(0.5 * value)


def forward_kernel(parts, down, *refs):
    parts_refs = refs[:parts]
    (
        table_ref, b_ref, blk_ref, disc_ref, jr_ref, u_ref, norm_ref, wout_ref, wgate_ref,
        next_ref, low_ref, mixed_ref, gate_ref, stats_ref, st_ref,
    ) = refs[parts:]
    states_of(parts_refs, table_ref, b_ref, blk_ref, disc_ref, jr_ref, low_ref, st_ref, down)
    u = u_ref[...].astype(F32)
    normed = (u - norm_ref[0:1]) * norm_ref[2:3] + norm_ref[3:4]
    mixed = jnp.dot(low_ref[...], wout_ref[...], preferred_element_type=F32)
    mixed += norm_ref[4:5] * normed
    _, _, half_up = gelu_parts(mixed)
    act = mixed * half_up
    gate = sigmoid(jnp.dot(act.astype(BF16), wgate_ref[...], preferred_element_type=F32))
    after = u + act * gate
    next_ref[...] = after
    mixed_ref[...] = mixed.astype(mixed_ref.dtype)
    gate_ref[...] = gate.astype(gate_ref.dtype)
    add_stats(stats_ref, after)


def accumulate(ref, value):
    @pl.when(pl.program_id(0) == 0)
    def _():
        ref[...] = value

    @pl.when(pl.program_id(0) != 0)
    def _():
        ref[...] += value


def gate_backward(g, mixed, gate, normed, low_ref, wout_ref, wgate_ref, outs, kept=None):
    pg_ref, sg_ref, wsum_ref, ssum_ref = outs
    width = g.shape[1]
    square, tanh, half_up = gelu_parts(mixed) if kept is None else kept
    act = mixed * half_up
    g_gate = g * gate
    logit_grad = (g_gate * act * (1.0 - gate)).astype(BF16)
    accumulate(
        wsum_ref.at[:width],
        lax.dot_general(act.astype(BF16), logit_grad, TN, preferred_element_type=F32),
    )
    act_grad = g_gate + lax.dot_general(
        logit_grad, wgate_ref[...], NT, preferred_element_type=F32
    )
    mixed_grad = act_grad * gelu_slope(mixed, square, tanh, half_up)
    accumulate(ssum_ref, column_sum(mixed_grad * normed))
    proj_grad = mixed_grad.astype(BF16)
    pg_ref[...] = proj_grad
    accumulate(
        wsum_ref.at[width:],
        lax.dot_general(low_ref[...], proj_grad, TN, preferred_element_type=F32),
    )
    sg_ref[...] = lax.dot_general(proj_grad, wout_ref[...], NT, preferred_element_type=F32)


def turn_kernel(parts, down, *refs):
    parts_refs = refs[:parts]
    (
        table_ref, b_ref, blk_ref, disc_ref, jr_ref, jo_ref, u_ref, norm_ref, wout_ref, wgate_ref,
        gout_ref, order_ref,
        out_ref, low_ref, g_ref, pg_ref, sg_ref, wsum_ref, ssum_ref, end_ref, ablk_ref,
        st_ref, w_ref,
    ) = refs[parts:]
    i, nt = pl.program_id(0), pl.num_programs(0)
    chunks = chunk_count(b_ref)
    half = chunks * 128
    steps = b_ref.shape[0] // LANES
    tile = nt - 1 - i if down else i
    states_of(parts_refs, table_ref, b_ref, blk_ref, disc_ref, jr_ref, low_ref, st_ref, down)
    u = u_ref[...]
    normed = (u - norm_ref[0:1]) * norm_ref[2:3] + norm_ref[3:4]
    mixed = jnp.dot(low_ref[...], wout_ref[...], preferred_element_type=F32)
    mixed += norm_ref[4:5] * normed
    kept = gelu_parts(mixed)
    act = mixed * kept[2]
    gate = sigmoid(jnp.dot(act.astype(BF16), wgate_ref[...], preferred_element_type=F32))
    permute_out(u + act * gate, order_ref, out_ref)
    g = permute_in(gout_ref[...], order_ref)
    g_ref[...] = g.astype(BF16)
    gate_backward(
        g, mixed, gate, normed, low_ref, wout_ref, wgate_ref,
        (pg_ref, sg_ref, wsum_ref, ssum_ref), kept,
    )

    @pl.when(i == 0)
    def _():
        w_ref[:, :half] = jnp.ones((LANES, half), F32)
        w_ref[:, half:] = jnp.zeros((LANES, half), F32)
        ablk_ref[...] = jnp.zeros_like(ablk_ref)

    dr, di = disc_row(disc_ref, 0, chunks, conj=True)
    dr, di = wide(dr), wide(di)
    jo = jo_ref[...]
    unroll = 4

    def body(k, carry):
        wr, wi, ar, ai = (list(carry[n * chunks : (n + 1) * chunks]) for n in range(4))
        for q in range(unroll):
            n = k * unroll + q
            step = steps - 1 - n if down else n
            at = pl.ds(pl.multiple_of(step * LANES, LANES), LANES)
            sr, si = rows_of(sg_ref, at, chunks)
            live = jo != tile * steps + step
            for c in range(chunks):
                ar[c] = ar[c] + (wr[c] * sr[c] - wi[c] * si[c])
                ai[c] = ai[c] + (wr[c] * si[c] + wi[c] * sr[c])
                xr = jnp.where(live, wr[c], 0.0)
                xi = jnp.where(live, wi[c], 0.0)
                wr[c] = xr * dr[c] - xi * di[c]
                wi[c] = xr * di[c] + xi * dr[c]
        return tuple(wr) + tuple(wi) + tuple(ar) + tuple(ai)

    wr, wi = rows_of(w_ref, slice(0, LANES), chunks)
    ar, ai = rows_of(ablk_ref, slice(0, LANES), chunks)
    out = lax.fori_loop(
        0, steps // unroll, body, tuple(wr) + tuple(wi) + tuple(ar) + tuple(ai)
    )
    wr, wi, ar, ai = (list(out[n * chunks : (n + 1) * chunks]) for n in range(4))
    put_rows(w_ref, slice(0, LANES), wr, wi)
    put_rows(ablk_ref, slice(0, LANES), ar, ai)

    @pl.when(i == nt - 1)
    def _():
        zero = [jnp.zeros((1, 128), F32)] * chunks
        power = disc_row(disc_ref, 2, chunks, conj=True)
        cr, ci = chain(ablk_ref, jo_ref, power, (zero, zero), not down)
        put_rows(end_ref, slice(0, 1), cr, ci)


def adjoint_kernel(parts, down, unpermute, *refs):
    parts_refs = refs[:parts]
    (
        table_ref, sg_ref, ablk_ref, disc_ref, jr_ref, low_ref, u_ref, norm_ref, pg_ref, g_ref,
        win_ref, order_ref,
        res_ref, isum_ref, nsum_ref, dsum_ref, fsum_ref, st_ref, dg_ref, ax_ref,
    ) = refs[parts:]
    i, nt = pl.program_id(0), pl.num_programs(0)
    chunks = chunk_count(sg_ref)
    half = chunks * 128
    steps = sg_ref.shape[0] // LANES
    tile = nt - 1 - i if down else i

    @pl.when(i == 0)
    def _():
        carry = carry_in(parts_refs, table_ref, chunks)
        power = disc_row(disc_ref, 2, chunks, conj=True)
        chain(ablk_ref, jr_ref, power, carry, down, st_ref)
        ax_ref[...] = jnp.zeros_like(ax_ref)

    fr, fi = disc_row(disc_ref, 1, chunks)
    fr, fi = wide(fr), wide(fi)

    def emit(low_step, pair, extra):
        if pair is None:
            re, im = rows_of(ax_ref, slice(0, LANES), chunks)
            return tuple(re) + tuple(im)
        sums_r, sums_i = list(extra[:chunks]), list(extra[chunks:])
        at = pl.ds(pl.multiple_of(low_step * LANES, 2 * LANES), 2 * LANES)
        xr, xi = rows_of(low_ref, at, chunks)
        grads = []
        for which, (ar, ai) in enumerate(pair):
            gr, gi = [], []
            rows = slice(which * LANES, (which + 1) * LANES)
            for c in range(chunks):
                vr, vi = xr[c].astype(F32)[rows], xi[c].astype(F32)[rows]
                sums_r[c] = sums_r[c] + (ar[c] * vr + ai[c] * vi)
                sums_i[c] = sums_i[c] + (ai[c] * vr - ar[c] * vi)
                gr.append(ar[c] * fr[c] + ai[c] * fi[c])
                gi.append(ai[c] * fr[c] - ar[c] * fi[c])
            grads.append((gr, gi))
        store_pair(dg_ref, low_step, grads[0], grads[1])
        return tuple(sums_r) + tuple(sums_i)

    sums = scan_tile(
        sg_ref, st_ref, disc_row(disc_ref, 0, chunks, conj=True), jr_ref, tile * steps, steps,
        down, emit,
    )
    put_rows(ax_ref, slice(0, LANES), list(sums[:chunks]), list(sums[chunks:]))

    u = u_ref[...].astype(F32)
    centered = u - norm_ref[0:1]
    normed = (centered * norm_ref[2:3] + norm_ref[3:4]).astype(BF16)
    drive_grad = dg_ref[...]
    accumulate(isum_ref, lax.dot_general(normed, drive_grad, TN, preferred_element_type=F32))
    normed_grad = lax.dot_general(drive_grad, win_ref[...], NT, preferred_element_type=F32)
    normed_grad += norm_ref[4:5] * pg_ref[...].astype(F32)
    accumulate(
        nsum_ref,
        jnp.concatenate(
            [column_sum(normed_grad), column_sum(normed_grad * centered) * norm_ref[1:2]], axis=0
        ),
    )
    result = g_ref[...].astype(F32) + norm_ref[2:3] * normed_grad
    if unpermute:
        permute_out(result, order_ref, res_ref)
    else:
        res_ref[...] = result

    @pl.when(i == nt - 1)
    def _():
        dsum_ref[...] = jnp.sum(ax_ref[...], axis=0, keepdims=True)
        wr, wi = win_ref[:, :half].astype(F32), win_ref[:, half:].astype(F32)
        gr, gi = isum_ref[:, :half], isum_ref[:, half:]
        re = jnp.sum(wr * gr + wi * gi, axis=0, keepdims=True)
        im = jnp.sum(wr * gi - wi * gr, axis=0, keepdims=True)
        gr, gi = disc_ref[1:2, :half], disc_ref[1:2, half:]
        scale = 1.0 / (gr * gr + gi * gi)
        fsum_ref[:, :half] = (re * gr - im * gi) * scale
        fsum_ref[:, half:] = (re * gi + im * gr) * scale


def back_kernel(parts, down, tokens, *refs):
    parts_refs = refs[:parts]
    (
        r_ref, up_ref, up_norm_ref, mixed_ref, gate_ref, low_ref, u_ref, norm_ref, wout_ref,
        wgate_ref, disc_ref, jo_ref,
        g_ref, pg_ref, sg_ref, wsum_ref, ssum_ref, end_ref, ablk_ref, nsum_ref,
    ) = refs[parts:]
    i, nt = pl.program_id(0), pl.num_programs(0)
    chunks = chunk_count(sg_ref)
    steps = sg_ref.shape[0] // LANES
    tile = nt - 1 - i if down else i

    @pl.when(i == 0)
    def _():
        nsum_ref[...] = summed(parts_refs)
        ablk_ref[...] = jnp.zeros_like(ablk_ref)

    scale = up_norm_ref[2:3] * (-1.0 / tokens)
    standard = (up_ref[...] - up_norm_ref[0:1]) * (scale * up_norm_ref[1:2] * nsum_ref[1:2])
    g = r_ref[...] + (standard + scale * nsum_ref[0:1])
    g_ref[...] = g
    u = u_ref[...].astype(F32)
    normed = (u - norm_ref[0:1]) * norm_ref[2:3] + norm_ref[3:4]
    gate_backward(
        g, mixed_ref[...].astype(F32), gate_ref[...].astype(F32), normed, low_ref, wout_ref,
        wgate_ref, (pg_ref, sg_ref, wsum_ref, ssum_ref),
    )
    decay = disc_row(disc_ref, 0, chunks, conj=True)
    scan_tile(sg_ref, ablk_ref, decay, jo_ref, tile * steps, steps, down)

    @pl.when(i == nt - 1)
    def _():
        zero = [jnp.zeros((1, 128), F32)] * chunks
        power = disc_row(disc_ref, 2, chunks, conj=True)
        cr, ci = chain(ablk_ref, jo_ref, power, (zero, zero), down)
        put_rows(end_ref, slice(0, 1), cr, ci)


def whole(array):
    shape = array.shape
    return pl.BlockSpec(shape, lambda i: (0,) * len(shape))


def tile_spec(rows, width, nt, down):
    if down:
        return pl.BlockSpec((rows, width), lambda i: (nt - 1 - i, 0))
    return pl.BlockSpec((rows, width), lambda i: (i, 0))


def run_spec(steps, width, nt, down):
    if down:
        return pl.BlockSpec((LANES, steps, width), lambda i: (0, nt - 1 - i, 0))
    return pl.BlockSpec((LANES, steps, width), lambda i: (0, i, 0))


def call(kernel, nt, args, outs, scratch, flops, name):
    arrays = [a for a, _ in args]
    sizes = sum(a.size * a.dtype.itemsize for a in arrays)
    sizes += sum(a.size * a.dtype.itemsize for a, _ in outs)
    return pl.pallas_call(
        kernel,
        grid=(nt,),
        in_specs=[whole(a) if s is None else s for a, s in args],
        out_specs=[whole(a) if s is None else s for a, s in outs],
        out_shape=[a for a, _ in outs],
        scratch_shapes=scratch,
        compiler_params=pltpu.CompilerParams(
            vmem_limit_bytes=VMEM_LIMIT, dimension_semantics=("arbitrary",)
        ),
        cost_estimate=pl.CostEstimate(flops=flops, bytes_accessed=sizes, transcendentals=0),
        name=name,
    )(*arrays)


def shape(*dims, dtype=F32):
    return jax.ShapeDtypeStruct(dims, dtype)


def body(
    tokens_in,
    seq_starts,
    norm_gain,
    norm_bias,
    decay_rate,
    step_log,
    frequency,
    in_proj,
    out_proj,
    skip_gain,
    gate_proj,
    grad_out,
):
    rows, width = tokens_in.shape
    states = in_proj.shape[-1]
    seq_size, grp_size = lax.axis_size("seq"), lax.axis_size("grp")
    devices = seq_size * grp_size
    total = rows * devices
    tokens = float(total)
    run = rows // LANES
    steps = min(64, run)
    tile = steps * LANES
    nt = rows // tile
    seq_at, grp_at = lax.axis_index("seq"), lax.axis_index("grp")
    me = seq_at * grp_size + grp_at

    span = min(32, steps)
    absolute = ((False, False), (False, True))
    discs, tables, cuts, order = pl.pallas_call(
        functools.partial(prep_kernel, rows, (seq_size, grp_size), absolute),
        in_specs=[pl.BlockSpec(memory_space=pltpu.SMEM)]
        + [pl.BlockSpec(memory_space=pltpu.VMEM)] * 3,
        out_specs=[pl.BlockSpec(memory_space=pltpu.VMEM)] * 4,
        out_shape=[
            shape(LAYERS, 8, states), shape(2 * LAYERS, devices, states),
            shape(2, LANES, 128, dtype=jnp.int32), shape(span * LANES, span * LANES, dtype=BF16),
        ],
        name="prep",
    )(seq_starts, decay_rate, step_log, frequency)

    def tiles(array, down):
        return (array, tile_spec(tile, array.shape[-1], nt, down))

    def runs(array, down):
        return (array, run_spec(steps, array.shape[-1], nt, down))

    def full(array):
        return (array, None)

    def of(array, l):
        size = array.shape[1:]
        return (array, pl.BlockSpec((None,) + size, lambda i: (l,) + (0,) * len(size)))

    tokens_run = tokens_in.reshape(LANES, run, width)
    grad_run = grad_out.reshape(LANES, run, width)
    state_scratch = pltpu.VMEM((LANES, states), F32)
    cost_in = 2 * rows * width * states
    cost_gate = 2 * rows * width * width

    u0, stats = call(
        stats_kernel, nt, [runs(tokens_run, 0), full(order)],
        [tiles(shape(rows, width, dtype=BF16), 0), full(shape(2, width))],
        [], rows * width * 8, "stats",
    )

    def drive(l, stream, parts):
        down = l % 2
        return call(
            functools.partial(drive_kernel, len(parts), l, bool(down), tokens), nt,
            [full(p) for p in parts]
            + [tiles(stream, down), full(norm_gain), full(norm_bias), full(skip_gain), of(in_proj, l), of(discs, l),
               of(cuts, down)],
            [tiles(shape(rows, states), down), full(shape(1, states)),
             full(shape(LANES, states)), full(shape(8, width))],
            [], cost_in, f"drive_{l}",
        )

    b0, end0, blk0, norm0 = drive(0, u0, gather_all(stats.reshape(1, 2 * width)))
    parts = gather_parts(end0, phases(2, 2))
    u1, low0, mixed0, gate0, stats = call(
        functools.partial(forward_kernel, len(parts), False), nt,
        [full(p) for p in parts]
        + [of(tables, 2 * 0 + 0), tiles(b0, 0), full(blk0), of(discs, 0), of(cuts, 0),
           tiles(u0, 0), full(norm0), of(out_proj, 0), of(gate_proj, 0)],
        [tiles(shape(rows, width), 0), tiles(shape(rows, states, dtype=BF16), 0),
         tiles(shape(rows, width, dtype=BF16), 0), tiles(shape(rows, width, dtype=BF16), 0),
         full(shape(2, width))],
        [state_scratch], cost_in + cost_gate, "forward_0",
    )

    b1, end1, blk1, norm1 = drive(1, u1, sum_parts(stats, phases(2, 2)))
    parts = gather_parts(end1, phases(4, 4))
    (
        out, low1, g1, pg1, sg1, w_sum1, skip_sum1, aend1, ablk1
    ) = call(
        functools.partial(turn_kernel, len(parts), True), nt,
        [full(p) for p in parts]
        + [of(tables, 2 * 1 + 0), tiles(b1, 1), full(blk1), of(discs, 1), of(cuts, 1),
           of(cuts, 0), tiles(u1, 1), full(norm1), of(out_proj, 1), of(gate_proj, 1),
           runs(grad_run, 1), full(order)],
        [runs(shape(LANES, run, width), 1), tiles(shape(rows, states, dtype=BF16), 1),
         tiles(shape(rows, width, dtype=BF16), 1), tiles(shape(rows, width, dtype=BF16), 1),
         tiles(shape(rows, states), 1), full(shape(width + states, width)),
         full(shape(1, width)), full(shape(1, states)), full(shape(LANES, states))],
        [state_scratch, state_scratch], 3 * cost_in + 3 * cost_gate, "turn_1",
    )

    def adjoint(l, sg, ablk, parts, low, stream, norm, pg, g):
        down = 1 - l % 2
        last = l == 0
        return call(
            functools.partial(adjoint_kernel, len(parts), bool(down), last), nt,
            [full(p) for p in parts]
            + [of(tables, 2 * l + 1), tiles(sg, down), full(ablk), of(discs, l), of(cuts, down),
               tiles(low, down), tiles(stream, down), full(norm), tiles(pg, down),
               tiles(g, down), of(in_proj, l), full(order)],
            [runs(shape(LANES, run, width), down) if last else tiles(shape(rows, width), down),
             full(shape(width, states)), full(shape(2, width)), full(shape(1, states)),
             full(shape(1, states))],
            [state_scratch, pltpu.VMEM((tile, states), BF16), state_scratch], 2 * cost_in,
            f"adjoint_{l}",
        )

    r1, in_sum1, norm_sum1, dsum1, fsum1 = adjoint(
        1, sg1, ablk1, gather_all(aend1), low1, u1, norm1, pg1, g1
    )
    parts = sum_parts(norm_sum1, phases(4, 4))
    (
        g0, pg0, sg0, w_sum0, skip_sum0, aend0, ablk0, norm_all1
    ) = call(
        functools.partial(back_kernel, len(parts), True, tokens), nt,
        [full(p) for p in parts]
        + [tiles(r1, 1), tiles(u1, 1), full(norm1), tiles(mixed0, 1), tiles(gate0, 1),
           tiles(low0, 1), tiles(u0, 1), full(norm0), of(out_proj, 0), of(gate_proj, 0),
           of(discs, 0), of(cuts, 1)],
        [tiles(shape(rows, width), 1), tiles(shape(rows, width, dtype=BF16), 1),
         tiles(shape(rows, states), 1), full(shape(width + states, width)),
         full(shape(1, width)), full(shape(1, states)), full(shape(LANES, states)),
         full(shape(2, width))],
        [], 2 * cost_in + 2 * cost_gate, "back_0",
    )
    r0, in_sum0, norm_sum0, dsum0, fsum0 = adjoint(
        0, sg0, ablk0, gather_parts(aend0, phases(4, 2)), low0, u0, norm0, pg0, g0
    )

    small = jnp.concatenate(
        [
            v.reshape(-1, 128)
            for v in (norm_sum0, skip_sum0, skip_sum1, dsum0, dsum1, fsum0, fsum1)
        ],
        axis=0,
    )
    small = functools.reduce(jnp.add, sum_parts(small, phases(4, 2))).reshape(-1)
    norm_all0 = small[: 2 * width].reshape(2, width)
    skip_grad = small[2 * width : 4 * width].reshape(LAYERS, width)
    dsum = small[4 * width : 4 * width + 2 * states].reshape(LAYERS, states)
    fsum = small[4 * width + 2 * states :].reshape(LAYERS, states)

    scale = norm0[2:3] * (-1.0 / tokens)
    grad_in = r0.reshape(rows, width) + (
        (tokens_in.astype(F32) - norm0[0:1]) * (scale * norm0[1:2] * norm_all0[1:2])
        + scale * norm_all0[0:1]
    )

    both = ("seq", "grp")
    wide1 = lax.psum(w_sum1, both)
    in_sum1, wide1 = lax.optimization_barrier((in_sum1, wide1))
    inp1 = lax.psum(lax.psum(in_sum1, "grp"), "seq")
    w_sum0, inp1 = lax.optimization_barrier((w_sum0, inp1))
    wide0 = lax.psum(w_sum0, both)
    in_sum0, wide0 = lax.optimization_barrier((in_sum0, wide0))
    piece = lax.psum_scatter(in_sum0, "grp", scatter_dimension=0, tiled=True)
    inp0 = lax.all_gather(lax.psum(piece, "seq"), "grp", axis=0, tiled=True)

    (decay, factor), discrete_back = jax.vjp(
        jax.vmap(discretize), decay_rate, step_log, frequency
    )
    half = states // 2
    dr, di = decay[:, :half], decay[:, half:]
    fr, fi = factor[:, :half], factor[:, half:]
    sr, si = fsum[:, :half], fsum[:, half:]
    tr = dsum[:, :half] - (fr * sr + fi * si)
    ti = dsum[:, half:] - (fr * si - fi * sr)
    modulus = dr * dr + di * di
    decay_grad = jnp.concatenate(
        [(tr * dr - ti * di) / modulus, (tr * di + ti * dr) / modulus], axis=-1
    )
    rate_grad, step_grad, freq_grad = discrete_back((decay_grad, fsum))
    return (
        out.reshape(rows, width),
        grad_in,
        jnp.stack([norm_all0[1], norm_all1[1]]),
        jnp.stack([norm_all0[0], norm_all1[0]]),
        rate_grad,
        step_grad,
        freq_grad,
        jnp.stack([inp0, inp1]),
        jnp.stack([wide0[width:], wide1[width:]]),
        skip_grad,
        jnp.stack([wide0[:width], wide1[:width]]),
    )


def solution(mesh):
    rows = P(("seq", "grp"), None)
    return jax.shard_map(
        body,
        mesh=mesh,
        in_specs=(rows,) + (P(),) * 10 + (rows,),
        out_specs=(rows, rows) + (P(),) * 9,
        check_vma=False,
    )
```

```python
import functools

import jax
import jax.numpy as jnp
from jax import lax
from jax.experimental import pallas as pl
from jax.experimental.pallas import tpu as pltpu
from jax.sharding import PartitionSpec as P

LAYERS = 2
EPSILON = 1e-05
SLOT = 4
LANES = 8
VMEM_LIMIT = 60 * 1024 * 1024
GELU_A = 0.7978845608028654
GELU_B = 0.044715
NT = (((1,), (1,)), ((), ()))
TN = (((0,), (0,)), ((), ()))
F32 = jnp.float32
BF16 = jnp.bfloat16


def discretize(decay_rate, step_log, frequency):
    step_size = jnp.exp(step_log)
    real_angle = -decay_rate * step_size
    imag_angle = frequency * step_size
    magnitude = jnp.exp(real_angle)
    cosine = jnp.cos(imag_angle)
    sine = jnp.sin(imag_angle)
    decay_row = jnp.concatenate([magnitude * cosine, magnitude * sine], axis=-1)
    minus_real = jnp.expm1(real_angle) * cosine - 2.0 * jnp.sin(0.5 * imag_angle) ** 2
    minus_imag = magnitude * sine
    modulus = decay_rate * decay_rate + frequency * frequency
    factor_real = (-decay_rate * minus_real + frequency * minus_imag) / modulus
    factor_imag = (-decay_rate * minus_imag - frequency * minus_real) / modulus
    return (decay_row, jnp.concatenate([factor_real, factor_imag], axis=-1))


def gather_all(copies):
    return lax.all_to_all(copies, ("seq", "grp"), 0, 0)


def cols(c):
    return slice(c * 128, (c + 1) * 128)


def chunk_count(ref):
    return ref.shape[-1] // 256


def rows_of(ref, at, chunks):
    half = chunks * 128
    re = [ref[at, c * 128 : (c + 1) * 128] for c in range(chunks)]
    im = [ref[at, half + c * 128 : half + (c + 1) * 128] for c in range(chunks)]
    return re, im


def put_rows(ref, at, re, im):
    chunks = len(re)
    half = chunks * 128
    for c in range(chunks):
        ref[at, c * 128 : (c + 1) * 128] = re[c]
        ref[at, half + c * 128 : half + (c + 1) * 128] = im[c]


def put_copies(ref, re, im):
    ref[0] = jnp.zeros(ref.shape[1:], F32)
    for c in range(len(re)):
        ref[0, c : c + 1] = re[c]
        ref[0, SLOT + c : SLOT + c + 1] = im[c]
    ref[...] = jnp.broadcast_to(ref[0:1], ref.shape)


def wide(rows):
    return [jnp.broadcast_to(v, (LANES, 128)) for v in rows]


def chain(ends_ref, jr_ref, power, carry, down, start_ref=None):
    chunks = len(power[0])
    pr, pi = power
    cr, ci = carry
    order = range(LANES - 1, -1, -1) if down else range(LANES)
    for s in order:
        at = slice(s, s + 1)
        if start_ref is not None:
            put_rows(start_ref, at, cr, ci)
        er, ei = rows_of(ends_ref, at, chunks)
        alive = (jr_ref[at, :] < 0).astype(F32)
        cr, ci = (
            [er[c] + alive * (pr[c] * cr[c] - pi[c] * ci[c]) for c in range(chunks)],
            [ei[c] + alive * (pr[c] * ci[c] + pi[c] * cr[c]) for c in range(chunks)],
        )
    return cr, ci


def carry_in(ends_ref, table_ref, chunks):
    total = jnp.zeros((2 * SLOT, 128), F32)
    for e in range(ends_ref.shape[0]):
        end = ends_ref[e]
        turned = jnp.concatenate([end[SLOT:], end[:SLOT]], axis=0)
        total += table_ref[0, e] * end + table_ref[1, e] * turned
    return (
        [total[c : c + 1] for c in range(chunks)],
        [total[SLOT + c : SLOT + c + 1] for c in range(chunks)],
    )


def scan_tile(src_ref, st_ref, decay, jr_ref, first_step, steps, down, emit=None, unroll=4):
    chunks = chunk_count(src_ref)
    dr, di = wide(decay[0]), wide(decay[1])
    jr = jr_ref[...]
    re, im = rows_of(st_ref, slice(0, LANES), chunks)

    def one(step, re, im):
        at = pl.ds(pl.multiple_of(step * LANES, LANES), LANES)
        br, bi = rows_of(src_ref, at, chunks)
        live = jr != first_step + step
        nr, ni = [], []
        for c in range(chunks):
            xr = jnp.where(live, re[c], 0.0)
            xi = jnp.where(live, im[c], 0.0)
            nr.append(dr[c] * xr - di[c] * xi + br[c])
            ni.append(dr[c] * xi + di[c] * xr + bi[c])
        return nr, ni

    def body(i, carry):
        re, im = list(carry[:chunks]), list(carry[chunks : 2 * chunks])
        extra = carry[2 * chunks :]
        for q in range(unroll):
            n = 2 * (i * unroll + q)
            low_step = steps - 2 - n if down else n
            a, b = (low_step + 1, low_step) if down else (low_step, low_step + 1)
            r1, i1 = one(a, re, im)
            r2, i2 = one(b, r1, i1)
            if emit is not None:
                pair = ((r2, i2), (r1, i1)) if down else ((r1, i1), (r2, i2))
                extra = emit(low_step, pair, extra)
            re, im = r2, i2
        return tuple(re) + tuple(im) + tuple(extra)

    start = tuple(re) + tuple(im)
    if emit is not None:
        start = start + tuple(emit(None, None, None))
    out = lax.fori_loop(0, steps // (2 * unroll), body, start)
    put_rows(st_ref, slice(0, LANES), list(out[:chunks]), list(out[chunks : 2 * chunks]))
    return out[2 * chunks :]


def store_pair(ref, low_step, first, second):
    at = pl.ds(pl.multiple_of(low_step * LANES, 2 * LANES), 2 * LANES)
    re = [jnp.concatenate([p, q], axis=0).astype(BF16) for p, q in zip(first[0], second[0])]
    im = [jnp.concatenate([p, q], axis=0).astype(BF16) for p, q in zip(first[1], second[1])]
    put_rows(ref, at, re, im)


def disc_row(disc_ref, row, chunks, conj=False):
    re, im = rows_of(disc_ref, slice(row, row + 1), chunks)
    return (re, [-v for v in im]) if conj else (re, im)


def column_sum(value):
    rows, width = value.shape
    return jnp.sum(jnp.sum(value.reshape(rows // 8, 8, width), axis=0), axis=0, keepdims=True)


def permute_in(block, order_ref):
    runs, steps, width = block.shape
    span = order_ref.shape[0] // runs
    out = []
    for k in range(steps // span):
        part = block[:, k * span : (k + 1) * span, :].reshape(runs * span, width)
        out.append(jnp.dot(order_ref[...], part, preferred_element_type=F32))
    return out[0] if len(out) == 1 else jnp.concatenate(out, axis=0)


def permute_out(value, order_ref, out_ref):
    rows, width = value.shape
    size = order_ref.shape[0]
    span = size // LANES
    high = value.astype(BF16)
    low = (value - high.astype(F32)).astype(BF16)
    for k in range(rows // size):
        at = slice(k * size, (k + 1) * size)
        back = lax.dot_general(order_ref[...], high[at], TN, preferred_element_type=F32)
        back += lax.dot_general(order_ref[...], low[at], TN, preferred_element_type=F32)
        out_ref[:, k * span : (k + 1) * span, :] = back.reshape(LANES, span, width)


def expm1(value):
    acc = jnp.full_like(value, 1.0 / 479001600.0)
    for n in (39916800.0, 3628800.0, 362880.0, 40320.0, 5040.0, 720.0, 120.0, 24.0, 6.0, 2.0, 1.0):
        acc = acc * value + 1.0 / n
    return jnp.where(value > -1.0, acc * value, jnp.exp(value) - 1.0)


def prep_kernel(
    rows, sizes, starts_ref, rate_ref, step_ref, freq_ref,
    disc_ref, table_ref, cut_ref, order_ref,
):
    seq_size, grp_size = sizes
    devices = seq_size * grp_size
    total = rows * devices
    run = rows // LANES
    half = rate_ref.shape[-1]
    seq_at, grp_at = lax.axis_index("seq"), lax.axis_index("grp")
    me = seq_at * grp_size + grp_at
    starts = [starts_ref[k] for k in range(starts_ref.shape[0])]

    base = me * rows + run * lax.broadcasted_iota(jnp.int32, (LANES, 128), 0)
    up = jnp.full((LANES, 128), -1, jnp.int32)
    down = up
    for begin in starts + [total]:
        rel = begin - base
        up = jnp.maximum(up, jnp.where((rel >= 0) & (rel < run), rel, -1))
        down = jnp.maximum(down, jnp.where((rel >= 1) & (rel <= run), rel - 1, -1))
    cut_ref[0] = up
    cut_ref[1] = down

    size = order_ref.shape[0]
    span = size // LANES
    to = lax.broadcasted_iota(jnp.int32, (size, size), 0)
    back = lax.broadcasted_iota(jnp.int32, (size, size), 1)
    order_ref[...] = ((to % LANES) * span + to // LANES == back).astype(F32).astype(BF16)

    source = lax.broadcasted_iota(jnp.int32, (devices, half), 0)
    for l in range(LAYERS):
        row = slice(l, l + 1)
        rate, freq = rate_ref[row], freq_ref[row]
        step_size = jnp.exp(step_ref[row])
        real_angle = -rate * step_size
        imag_angle = freq * step_size
        magnitude = jnp.exp(real_angle)
        cosine, sine = jnp.cos(imag_angle), jnp.sin(imag_angle)
        minus_real = expm1(real_angle) * cosine - 2.0 * jnp.sin(0.5 * imag_angle) ** 2
        minus_imag = magnitude * sine
        modulus = rate * rate + freq * freq
        disc_ref[l, 0:1, :half] = magnitude * cosine
        disc_ref[l, 0:1, half:] = minus_imag
        disc_ref[l, 1:2, :half] = (-rate * minus_real + freq * minus_imag) / modulus
        disc_ref[l, 1:2, half:] = (-rate * minus_imag - freq * minus_real) / modulus
        magnitude = jnp.exp(real_angle * float(run))
        disc_ref[l, 2:3, :half] = magnitude * jnp.cos(imag_angle * float(run))
        disc_ref[l, 2:3, half:] = magnitude * jnp.sin(imag_angle * float(run))
        disc_ref[l, 3:8] = jnp.zeros((5, 2 * half), F32)
        for back in range(2):
            going_down = (l + back) % 2 == 1
            if going_down:
                live, count = source > me, source - me - 1
            else:
                live, count = source < me, me - 1 - source
            for begin in starts:
                if going_down:
                    cut = ((begin > (me + 1) * rows).astype(jnp.int32) > 0) & (
                        source * rows >= begin
                    )
                else:
                    cut = ((begin < me * rows).astype(jnp.int32) > 0) & (
                        (source + 1) * rows <= begin
                    )
                live &= ~cut
            count = (jnp.maximum(count, 0) * rows).astype(F32)
            magnitude = jnp.where(live, jnp.exp(real_angle * count), 0.0)
            angle = imag_angle * count
            real = magnitude * jnp.cos(angle)
            imag = magnitude * jnp.sin(angle)
            imag = -imag if back else imag
            at = 2 * l + back
            table_ref[at] = jnp.zeros(table_ref.shape[1:], F32)
            for c in range(half // 128):
                table_ref[at, 0, :, c, :] = real[:, cols(c)]
                table_ref[at, 0, :, SLOT + c, :] = real[:, cols(c)]
                table_ref[at, 1, :, c, :] = -imag[:, cols(c)]
                table_ref[at, 1, :, SLOT + c, :] = imag[:, cols(c)]


def stats_kernel(tok_ref, order_ref, u_ref, stats_ref):
    value = permute_in(tok_ref[...], order_ref)
    u_ref[...] = value.astype(BF16)
    add_stats(stats_ref, value)


def add_stats(stats_ref, value):
    add_rows(stats_ref, column_sum(value), column_sum(value * value))


def add_rows(copies_ref, first, second):
    i, nt = pl.program_id(0), pl.num_programs(0)
    chunks = first.shape[1] // 128

    @pl.when(i == 0)
    def _():
        copies_ref[0] = jnp.zeros(copies_ref.shape[1:], F32)

    for c in range(chunks):
        copies_ref[0, c : c + 1] += first[:, cols(c)]
        copies_ref[0, SLOT + c : SLOT + c + 1] += second[:, cols(c)]

    @pl.when(i == nt - 1)
    def _():
        copies_ref[...] = jnp.broadcast_to(copies_ref[0:1], copies_ref.shape)


def summed(ref):
    total = jnp.sum(ref[...], axis=0)
    return tuple(
        jnp.concatenate([total[SLOT * k + c : SLOT * k + c + 1] for c in range(SLOT)], axis=1)
        for k in range(2)
    )


def drive_kernel(layer, down, tokens, *refs):
    (
        stat_ref, u_ref, gain_ref, bias_ref, skip_ref, win_ref, disc_ref, jr_ref,
        b_ref, end_ref, blk_ref, norm_ref,
    ) = refs
    i, nt = pl.program_id(0), pl.num_programs(0)
    steps = u_ref.shape[0] // LANES
    chunks = chunk_count(b_ref)
    half = chunks * 128

    @pl.when(i == 0)
    def _():
        total, squares = summed(stat_ref)
        row = slice(layer, layer + 1)
        mean = total / tokens
        inv = lax.rsqrt(squares / tokens - mean * mean + EPSILON)
        norm_ref[0:1] = mean
        norm_ref[1:2] = inv
        norm_ref[2:3] = inv * gain_ref[row]
        norm_ref[3:4] = bias_ref[row]
        norm_ref[4:5] = skip_ref[row]
        norm_ref[5:8] = jnp.zeros((3, norm_ref.shape[1]), F32)
        blk_ref[...] = jnp.zeros_like(blk_ref)

    u = u_ref[...].astype(F32)
    normed = (u - norm_ref[0:1]) * norm_ref[2:3] + norm_ref[3:4]
    drive = jnp.dot(normed.astype(BF16), win_ref[...], preferred_element_type=F32)
    fr, fi = disc_ref[1:2, :half], disc_ref[1:2, half:]
    re, im = drive[:, :half], drive[:, half:]
    b_ref[:, :half] = re * fr - im * fi
    b_ref[:, half:] = re * fi + im * fr
    tile = nt - 1 - i if down else i
    scan_tile(b_ref, blk_ref, disc_row(disc_ref, 0, chunks), jr_ref, tile * steps, steps, down)

    @pl.when(i == nt - 1)
    def _():
        zero = [jnp.zeros((1, 128), F32)] * chunks
        cr, ci = chain(blk_ref, jr_ref, disc_row(disc_ref, 2, chunks), (zero, zero), down)
        put_copies(end_ref, cr, ci)


def states_of(ends_ref, table_ref, b_ref, blk_ref, disc_ref, jr_ref, low_ref, st_ref, down):
    i, nt = pl.program_id(0), pl.num_programs(0)
    chunks = chunk_count(b_ref)
    steps = b_ref.shape[0] // LANES

    @pl.when(i == 0)
    def _():
        carry = carry_in(ends_ref, table_ref, chunks)
        chain(blk_ref, jr_ref, disc_row(disc_ref, 2, chunks), carry, down, st_ref)

    def emit(low_step, pair, extra):
        if pair is None:
            return ()
        (first, second) = pair
        store_pair(low_ref, low_step, first, second)
        return ()

    tile = nt - 1 - i if down else i
    scan_tile(
        b_ref, st_ref, disc_row(disc_ref, 0, chunks), jr_ref, tile * steps, steps, down, emit
    )


def gelu_parts(mixed):
    square = mixed * mixed
    tanh = jnp.tanh(mixed * (GELU_A + (GELU_A * GELU_B) * square))
    half_up = 0.5 + 0.5 * tanh
    return square, tanh, half_up


def gelu_slope(mixed, square, tanh, half_up):
    return half_up + (mixed * (0.5 - 0.5 * tanh * tanh)) * (
        GELU_A + (3.0 * GELU_A * GELU_B) * square
    )


def sigmoid(value):
    return 0.5 + 0.5 * jnp.tanh(0.5 * value)


def forward_kernel(down, *refs):
    (
        ends_ref, table_ref, b_ref, blk_ref, disc_ref, jr_ref, u_ref, norm_ref, wout_ref, wgate_ref,
        next_ref, low_ref, mixed_ref, gate_ref, stats_ref, st_ref,
    ) = refs
    states_of(ends_ref, table_ref, b_ref, blk_ref, disc_ref, jr_ref, low_ref, st_ref, down)
    u = u_ref[...].astype(F32)
    normed = (u - norm_ref[0:1]) * norm_ref[2:3] + norm_ref[3:4]
    mixed = jnp.dot(low_ref[...], wout_ref[...], preferred_element_type=F32)
    mixed += norm_ref[4:5] * normed
    _, _, half_up = gelu_parts(mixed)
    act = mixed * half_up
    gate = sigmoid(jnp.dot(act.astype(BF16), wgate_ref[...], preferred_element_type=F32))
    after = u + act * gate
    next_ref[...] = after
    mixed_ref[...] = mixed.astype(mixed_ref.dtype)
    gate_ref[...] = gate.astype(gate_ref.dtype)
    add_stats(stats_ref, after)


def accumulate(ref, value):
    @pl.when(pl.program_id(0) == 0)
    def _():
        ref[...] = value

    @pl.when(pl.program_id(0) != 0)
    def _():
        ref[...] += value


def gate_backward(g, mixed, gate, normed, low_ref, wout_ref, wgate_ref, outs, kept=None):
    pg_ref, sg_ref, wsum_ref, ssum_ref = outs
    width = g.shape[1]
    square, tanh, half_up = gelu_parts(mixed) if kept is None else kept
    act = mixed * half_up
    g_gate = g * gate
    logit_grad = (g_gate * act * (1.0 - gate)).astype(BF16)
    accumulate(
        wsum_ref.at[:width],
        lax.dot_general(act.astype(BF16), logit_grad, TN, preferred_element_type=F32),
    )
    act_grad = g_gate + lax.dot_general(
        logit_grad, wgate_ref[...], NT, preferred_element_type=F32
    )
    mixed_grad = act_grad * gelu_slope(mixed, square, tanh, half_up)
    accumulate(ssum_ref, column_sum(mixed_grad * normed))
    proj_grad = mixed_grad.astype(BF16)
    pg_ref[...] = proj_grad
    accumulate(
        wsum_ref.at[width:],
        lax.dot_general(low_ref[...], proj_grad, TN, preferred_element_type=F32),
    )
    sg_ref[...] = lax.dot_general(proj_grad, wout_ref[...], NT, preferred_element_type=F32)


def turn_kernel(down, *refs):
    (
        ends_ref, table_ref, b_ref, blk_ref, disc_ref, jr_ref, jo_ref, u_ref, norm_ref, wout_ref, wgate_ref,
        gout_ref, order_ref,
        out_ref, low_ref, g_ref, pg_ref, sg_ref, wsum_ref, ssum_ref, end_ref, ablk_ref,
        st_ref, w_ref,
    ) = refs
    i, nt = pl.program_id(0), pl.num_programs(0)
    chunks = chunk_count(b_ref)
    half = chunks * 128
    steps = b_ref.shape[0] // LANES
    tile = nt - 1 - i if down else i
    states_of(ends_ref, table_ref, b_ref, blk_ref, disc_ref, jr_ref, low_ref, st_ref, down)
    u = u_ref[...]
    normed = (u - norm_ref[0:1]) * norm_ref[2:3] + norm_ref[3:4]
    mixed = jnp.dot(low_ref[...], wout_ref[...], preferred_element_type=F32)
    mixed += norm_ref[4:5] * normed
    kept = gelu_parts(mixed)
    act = mixed * kept[2]
    gate = sigmoid(jnp.dot(act.astype(BF16), wgate_ref[...], preferred_element_type=F32))
    permute_out(u + act * gate, order_ref, out_ref)
    g = permute_in(gout_ref[...], order_ref)
    g_ref[...] = g.astype(BF16)
    gate_backward(
        g, mixed, gate, normed, low_ref, wout_ref, wgate_ref,
        (pg_ref, sg_ref, wsum_ref, ssum_ref), kept,
    )

    @pl.when(i == 0)
    def _():
        w_ref[:, :half] = jnp.ones((LANES, half), F32)
        w_ref[:, half:] = jnp.zeros((LANES, half), F32)
        ablk_ref[...] = jnp.zeros_like(ablk_ref)

    dr, di = disc_row(disc_ref, 0, chunks, conj=True)
    dr, di = wide(dr), wide(di)
    jo = jo_ref[...]
    unroll = 4

    def body(k, carry):
        wr, wi, ar, ai = (list(carry[n * chunks : (n + 1) * chunks]) for n in range(4))
        for q in range(unroll):
            n = k * unroll + q
            step = steps - 1 - n if down else n
            at = pl.ds(pl.multiple_of(step * LANES, LANES), LANES)
            sr, si = rows_of(sg_ref, at, chunks)
            live = jo != tile * steps + step
            for c in range(chunks):
                ar[c] = ar[c] + (wr[c] * sr[c] - wi[c] * si[c])
                ai[c] = ai[c] + (wr[c] * si[c] + wi[c] * sr[c])
                xr = jnp.where(live, wr[c], 0.0)
                xi = jnp.where(live, wi[c], 0.0)
                wr[c] = xr * dr[c] - xi * di[c]
                wi[c] = xr * di[c] + xi * dr[c]
        return tuple(wr) + tuple(wi) + tuple(ar) + tuple(ai)

    wr, wi = rows_of(w_ref, slice(0, LANES), chunks)
    ar, ai = rows_of(ablk_ref, slice(0, LANES), chunks)
    out = lax.fori_loop(
        0, steps // unroll, body, tuple(wr) + tuple(wi) + tuple(ar) + tuple(ai)
    )
    wr, wi, ar, ai = (list(out[n * chunks : (n + 1) * chunks]) for n in range(4))
    put_rows(w_ref, slice(0, LANES), wr, wi)
    put_rows(ablk_ref, slice(0, LANES), ar, ai)

    @pl.when(i == nt - 1)
    def _():
        zero = [jnp.zeros((1, 128), F32)] * chunks
        power = disc_row(disc_ref, 2, chunks, conj=True)
        cr, ci = chain(ablk_ref, jo_ref, power, (zero, zero), not down)
        put_copies(end_ref, cr, ci)


def adjoint_kernel(down, unpermute, *refs):
    (
        ends_ref, table_ref, sg_ref, ablk_ref, disc_ref, jr_ref, low_ref, u_ref, norm_ref, pg_ref, g_ref,
        win_ref, order_ref,
        res_ref, isum_ref, nsum_ref, dsum_ref, fsum_ref, st_ref, dg_ref, ax_ref,
    ) = refs
    i, nt = pl.program_id(0), pl.num_programs(0)
    chunks = chunk_count(sg_ref)
    half = chunks * 128
    steps = sg_ref.shape[0] // LANES
    tile = nt - 1 - i if down else i

    @pl.when(i == 0)
    def _():
        carry = carry_in(ends_ref, table_ref, chunks)
        power = disc_row(disc_ref, 2, chunks, conj=True)
        chain(ablk_ref, jr_ref, power, carry, down, st_ref)
        ax_ref[...] = jnp.zeros_like(ax_ref)

    fr, fi = disc_row(disc_ref, 1, chunks)
    fr, fi = wide(fr), wide(fi)

    def emit(low_step, pair, extra):
        if pair is None:
            re, im = rows_of(ax_ref, slice(0, LANES), chunks)
            return tuple(re) + tuple(im)
        sums_r, sums_i = list(extra[:chunks]), list(extra[chunks:])
        at = pl.ds(pl.multiple_of(low_step * LANES, 2 * LANES), 2 * LANES)
        xr, xi = rows_of(low_ref, at, chunks)
        grads = []
        for which, (ar, ai) in enumerate(pair):
            gr, gi = [], []
            rows = slice(which * LANES, (which + 1) * LANES)
            for c in range(chunks):
                vr, vi = xr[c].astype(F32)[rows], xi[c].astype(F32)[rows]
                sums_r[c] = sums_r[c] + (ar[c] * vr + ai[c] * vi)
                sums_i[c] = sums_i[c] + (ai[c] * vr - ar[c] * vi)
                gr.append(ar[c] * fr[c] + ai[c] * fi[c])
                gi.append(ai[c] * fr[c] - ar[c] * fi[c])
            grads.append((gr, gi))
        store_pair(dg_ref, low_step, grads[0], grads[1])
        return tuple(sums_r) + tuple(sums_i)

    sums = scan_tile(
        sg_ref, st_ref, disc_row(disc_ref, 0, chunks, conj=True), jr_ref, tile * steps, steps,
        down, emit,
    )
    put_rows(ax_ref, slice(0, LANES), list(sums[:chunks]), list(sums[chunks:]))

    u = u_ref[...].astype(F32)
    centered = u - norm_ref[0:1]
    normed = (centered * norm_ref[2:3] + norm_ref[3:4]).astype(BF16)
    drive_grad = dg_ref[...]
    accumulate(isum_ref, lax.dot_general(normed, drive_grad, TN, preferred_element_type=F32))
    normed_grad = lax.dot_general(drive_grad, win_ref[...], NT, preferred_element_type=F32)
    normed_grad += norm_ref[4:5] * pg_ref[...].astype(F32)
    add_rows(
        nsum_ref, column_sum(normed_grad), column_sum(normed_grad * centered) * norm_ref[1:2]
    )
    result = g_ref[...].astype(F32) + norm_ref[2:3] * normed_grad
    if unpermute:
        permute_out(result, order_ref, res_ref)
    else:
        res_ref[...] = result

    @pl.when(i == nt - 1)
    def _():
        dsum_ref[...] = jnp.sum(ax_ref[...], axis=0, keepdims=True)
        wr, wi = win_ref[:, :half].astype(F32), win_ref[:, half:].astype(F32)
        gr, gi = isum_ref[:, :half], isum_ref[:, half:]
        re = jnp.sum(wr * gr + wi * gi, axis=0, keepdims=True)
        im = jnp.sum(wr * gi - wi * gr, axis=0, keepdims=True)
        gr, gi = disc_ref[1:2, :half], disc_ref[1:2, half:]
        scale = 1.0 / (gr * gr + gi * gi)
        fsum_ref[:, :half] = (re * gr - im * gi) * scale
        fsum_ref[:, half:] = (re * gi + im * gr) * scale


def back_kernel(down, tokens, *refs):
    (
        sums_ref, r_ref, up_ref, up_norm_ref, mixed_ref, gate_ref, low_ref, u_ref, norm_ref, wout_ref,
        wgate_ref, disc_ref, jo_ref,
        g_ref, pg_ref, sg_ref, wsum_ref, ssum_ref, end_ref, ablk_ref, nsum_ref,
    ) = refs
    i, nt = pl.program_id(0), pl.num_programs(0)
    chunks = chunk_count(sg_ref)
    steps = sg_ref.shape[0] // LANES
    tile = nt - 1 - i if down else i

    @pl.when(i == 0)
    def _():
        nsum_ref[0:1], nsum_ref[1:2] = summed(sums_ref)
        ablk_ref[...] = jnp.zeros_like(ablk_ref)

    scale = up_norm_ref[2:3] * (-1.0 / tokens)
    standard = (up_ref[...] - up_norm_ref[0:1]) * (scale * up_norm_ref[1:2] * nsum_ref[1:2])
    g = r_ref[...] + (standard + scale * nsum_ref[0:1])
    g_ref[...] = g
    u = u_ref[...].astype(F32)
    normed = (u - norm_ref[0:1]) * norm_ref[2:3] + norm_ref[3:4]
    gate_backward(
        g, mixed_ref[...].astype(F32), gate_ref[...].astype(F32), normed, low_ref, wout_ref,
        wgate_ref, (pg_ref, sg_ref, wsum_ref, ssum_ref),
    )
    decay = disc_row(disc_ref, 0, chunks, conj=True)
    scan_tile(sg_ref, ablk_ref, decay, jo_ref, tile * steps, steps, down)

    @pl.when(i == nt - 1)
    def _():
        zero = [jnp.zeros((1, 128), F32)] * chunks
        power = disc_row(disc_ref, 2, chunks, conj=True)
        cr, ci = chain(ablk_ref, jo_ref, power, (zero, zero), down)
        put_copies(end_ref, cr, ci)


def whole(array):
    shape = array.shape
    return pl.BlockSpec(shape, lambda i: (0,) * len(shape))


def tile_spec(rows, width, nt, down):
    if down:
        return pl.BlockSpec((rows, width), lambda i: (nt - 1 - i, 0))
    return pl.BlockSpec((rows, width), lambda i: (i, 0))


def run_spec(steps, width, nt, down):
    if down:
        return pl.BlockSpec((LANES, steps, width), lambda i: (0, nt - 1 - i, 0))
    return pl.BlockSpec((LANES, steps, width), lambda i: (0, i, 0))


def call(kernel, nt, args, outs, scratch, flops, name):
    arrays = [a for a, _ in args]
    sizes = sum(a.size * a.dtype.itemsize for a in arrays)
    sizes += sum(a.size * a.dtype.itemsize for a, _ in outs)
    return pl.pallas_call(
        kernel,
        grid=(nt,),
        in_specs=[whole(a) if s is None else s for a, s in args],
        out_specs=[whole(a) if s is None else s for a, s in outs],
        out_shape=[a for a, _ in outs],
        scratch_shapes=scratch,
        compiler_params=pltpu.CompilerParams(
            vmem_limit_bytes=VMEM_LIMIT, dimension_semantics=("arbitrary",)
        ),
        cost_estimate=pl.CostEstimate(flops=flops, bytes_accessed=sizes, transcendentals=0),
        name=name,
    )(*arrays)


def shape(*dims, dtype=F32):
    return jax.ShapeDtypeStruct(dims, dtype)


def body(
    tokens_in,
    seq_starts,
    norm_gain,
    norm_bias,
    decay_rate,
    step_log,
    frequency,
    in_proj,
    out_proj,
    skip_gain,
    gate_proj,
    grad_out,
):
    rows, width = tokens_in.shape
    states = in_proj.shape[-1]
    seq_size, grp_size = lax.axis_size("seq"), lax.axis_size("grp")
    devices = seq_size * grp_size
    total = rows * devices
    tokens = float(total)
    run = rows // LANES
    steps = min(64, run)
    tile = steps * LANES
    nt = rows // tile
    seq_at, grp_at = lax.axis_index("seq"), lax.axis_index("grp")
    me = seq_at * grp_size + grp_at

    span = min(32, steps)
    discs, tables, cuts, order = pl.pallas_call(
        functools.partial(prep_kernel, rows, (seq_size, grp_size)),
        in_specs=[pl.BlockSpec(memory_space=pltpu.SMEM)]
        + [pl.BlockSpec(memory_space=pltpu.VMEM)] * 3,
        out_specs=[pl.BlockSpec(memory_space=pltpu.VMEM)] * 4,
        out_shape=[
            shape(LAYERS, 8, states), shape(2 * LAYERS, 2, devices, 2 * SLOT, 128),
            shape(2, LANES, 128, dtype=jnp.int32), shape(span * LANES, span * LANES, dtype=BF16),
        ],
        compiler_params=pltpu.CompilerParams(vmem_limit_bytes=VMEM_LIMIT),
        name="prep",
    )(seq_starts, decay_rate, step_log, frequency)

    def tiles(array, down):
        return (array, tile_spec(tile, array.shape[-1], nt, down))

    def runs(array, down):
        return (array, run_spec(steps, array.shape[-1], nt, down))

    def full(array):
        return (array, None)

    def of(array, l):
        size = array.shape[1:]
        return (array, pl.BlockSpec((None,) + size, lambda i: (l,) + (0,) * len(size)))

    tokens_run = tokens_in.reshape(LANES, run, width)
    grad_run = grad_out.reshape(LANES, run, width)
    state_scratch = pltpu.VMEM((LANES, states), F32)
    cost_in = 2 * rows * width * states
    cost_gate = 2 * rows * width * width

    u0, stats = call(
        stats_kernel, nt, [runs(tokens_run, 0), full(order)],
        [tiles(shape(rows, width, dtype=BF16), 0), full(shape(devices, 2 * SLOT, 128))],
        [], rows * width * 8, "stats",
    )

    def drive(l, stream, stats):
        down = l % 2
        return call(
            functools.partial(drive_kernel, l, bool(down), tokens), nt,
            [full(gather_all(stats)), tiles(stream, down), full(norm_gain), full(norm_bias), full(skip_gain), of(in_proj, l), of(discs, l),
               of(cuts, down)],
            [tiles(shape(rows, states), down), full(shape(devices, 2 * SLOT, 128)),
             full(shape(LANES, states)), full(shape(8, width))],
            [], cost_in, f"drive_{l}",
        )

    b0, end0, blk0, norm0 = drive(0, u0, stats)
    u1, low0, mixed0, gate0, stats = call(
        functools.partial(forward_kernel, False), nt,
        [full(gather_all(end0)), of(tables, 2 * 0 + 0), tiles(b0, 0), full(blk0), of(discs, 0), of(cuts, 0),
           tiles(u0, 0), full(norm0), of(out_proj, 0), of(gate_proj, 0)],
        [tiles(shape(rows, width), 0), tiles(shape(rows, states, dtype=BF16), 0),
         tiles(shape(rows, width, dtype=BF16), 0), tiles(shape(rows, width, dtype=BF16), 0),
         full(shape(devices, 2 * SLOT, 128))],
        [state_scratch], cost_in + cost_gate, "forward_0",
    )

    b1, end1, blk1, norm1 = drive(1, u1, stats)
    (
        out, low1, g1, pg1, sg1, w_sum1, skip_sum1, aend1, ablk1
    ) = call(
        functools.partial(turn_kernel, True), nt,
        [full(gather_all(end1)), of(tables, 2 * 1 + 0), tiles(b1, 1), full(blk1), of(discs, 1), of(cuts, 1),
           of(cuts, 0), tiles(u1, 1), full(norm1), of(out_proj, 1), of(gate_proj, 1),
           runs(grad_run, 1), full(order)],
        [runs(shape(LANES, run, width), 1), tiles(shape(rows, states, dtype=BF16), 1),
         tiles(shape(rows, width, dtype=BF16), 1), tiles(shape(rows, width, dtype=BF16), 1),
         tiles(shape(rows, states), 1), full(shape(width + states, width)),
         full(shape(1, width)), full(shape(devices, 2 * SLOT, 128)), full(shape(LANES, states))],
        [state_scratch, state_scratch], 3 * cost_in + 3 * cost_gate, "turn_1",
    )

    def adjoint(l, sg, ablk, aend, low, stream, norm, pg, g):
        down = 1 - l % 2
        last = l == 0
        return call(
            functools.partial(adjoint_kernel, bool(down), last), nt,
            [full(gather_all(aend)), of(tables, 2 * l + 1), tiles(sg, down), full(ablk), of(discs, l), of(cuts, down),
               tiles(low, down), tiles(stream, down), full(norm), tiles(pg, down),
               tiles(g, down), of(in_proj, l), full(order)],
            [runs(shape(LANES, run, width), down) if last else tiles(shape(rows, width), down),
             full(shape(width, states)), full(shape(devices, 2 * SLOT, 128)), full(shape(1, states)),
             full(shape(1, states))],
            [state_scratch, pltpu.VMEM((tile, states), BF16), state_scratch], 2 * cost_in,
            f"adjoint_{l}",
        )

    r1, in_sum1, norm_sum1, dsum1, fsum1 = adjoint(
        1, sg1, ablk1, aend1, low1, u1, norm1, pg1, g1
    )
    (
        g0, pg0, sg0, w_sum0, skip_sum0, aend0, ablk0, norm_all1
    ) = call(
        functools.partial(back_kernel, True, tokens), nt,
        [full(gather_all(norm_sum1)), tiles(r1, 1), tiles(u1, 1), full(norm1), tiles(mixed0, 1), tiles(gate0, 1),
           tiles(low0, 1), tiles(u0, 1), full(norm0), of(out_proj, 0), of(gate_proj, 0),
           of(discs, 0), of(cuts, 1)],
        [tiles(shape(rows, width), 1), tiles(shape(rows, width, dtype=BF16), 1),
         tiles(shape(rows, states), 1), full(shape(width + states, width)),
         full(shape(1, width)), full(shape(devices, 2 * SLOT, 128)), full(shape(LANES, states)),
         full(shape(2, width))],
        [], 2 * cost_in + 2 * cost_gate, "back_0",
    )
    r0, in_sum0, norm_sum0, dsum0, fsum0 = adjoint(
        0, sg0, ablk0, aend0, low0, u0, norm0, pg0, g0
    )

    small = jnp.concatenate(
        [norm_sum0[0]]
        + [v.reshape(-1, 128) for v in (skip_sum0, skip_sum1, dsum0, dsum1, fsum0, fsum1)],
        axis=0,
    )
    small = jnp.sum(gather_all(jnp.broadcast_to(small, (devices,) + small.shape)), axis=0)
    small = small.reshape(-1)
    norm_all0 = small[: 2 * width].reshape(2, width)
    skip_grad = small[2 * width : 4 * width].reshape(LAYERS, width)
    dsum = small[4 * width : 4 * width + 2 * states].reshape(LAYERS, states)
    fsum = small[4 * width + 2 * states :].reshape(LAYERS, states)

    scale = norm0[2:3] * (-1.0 / tokens)
    grad_in = r0.reshape(rows, width) + (
        (tokens_in.astype(F32) - norm0[0:1]) * (scale * norm0[1:2] * norm_all0[1:2])
        + scale * norm_all0[0:1]
    )

    both = ("seq", "grp")
    wide1, wide0, inp1, inp0 = lax.psum((w_sum1, w_sum0, in_sum1, in_sum0), both)

    (decay, factor), discrete_back = jax.vjp(
        jax.vmap(discretize), decay_rate, step_log, frequency
    )
    half = states // 2
    dr, di = decay[:, :half], decay[:, half:]
    fr, fi = factor[:, :half], factor[:, half:]
    sr, si = fsum[:, :half], fsum[:, half:]
    tr = dsum[:, :half] - (fr * sr + fi * si)
    ti = dsum[:, half:] - (fr * si - fi * sr)
    modulus = dr * dr + di * di
    decay_grad = jnp.concatenate(
        [(tr * dr - ti * di) / modulus, (tr * di + ti * dr) / modulus], axis=-1
    )
    rate_grad, step_grad, freq_grad = discrete_back((decay_grad, fsum))
    return (
        out.reshape(rows, width),
        grad_in,
        jnp.stack([norm_all0[1], norm_all1[1]]),
        jnp.stack([norm_all0[0], norm_all1[0]]),
        rate_grad,
        step_grad,
        freq_grad,
        jnp.stack([inp0, inp1]),
        jnp.stack([wide0[width:], wide1[width:]]),
        skip_grad,
        jnp.stack([wide0[:width], wide1[:width]]),
    )


def solution(mesh):
    rows = P(("seq", "grp"), None)
    return jax.shard_map(
        body,
        mesh=mesh,
        in_specs=(rows,) + (P(),) * 10 + (rows,),
        out_specs=(rows, rows) + (P(),) * 9,
        check_vma=False,
    )
```

```python
import functools

import jax
import jax.numpy as jnp
from jax import lax
from jax.experimental import pallas as pl
from jax.experimental.pallas import tpu as pltpu
from jax.sharding import Mesh, PartitionSpec as P

LAYERS = 2
EPSILON = 1e-05
SLOT = 4
LANES = 8
VMEM_LIMIT = 60 * 1024 * 1024
GELU_A = 0.7978845608028654
GELU_B = 0.044715
NT = (((1,), (1,)), ((), ()))
TN = (((0,), (0,)), ((), ()))
F32 = jnp.float32
BF16 = jnp.bfloat16


def discretize(decay_rate, step_log, frequency):
    step_size = jnp.exp(step_log)
    real_angle = -decay_rate * step_size
    imag_angle = frequency * step_size
    magnitude = jnp.exp(real_angle)
    cosine = jnp.cos(imag_angle)
    sine = jnp.sin(imag_angle)
    decay_row = jnp.concatenate([magnitude * cosine, magnitude * sine], axis=-1)
    minus_real = jnp.expm1(real_angle) * cosine - 2.0 * jnp.sin(0.5 * imag_angle) ** 2
    minus_imag = magnitude * sine
    modulus = decay_rate * decay_rate + frequency * frequency
    factor_real = (-decay_rate * minus_real + frequency * minus_imag) / modulus
    factor_imag = (-decay_rate * minus_imag - frequency * minus_real) / modulus
    return (decay_row, jnp.concatenate([factor_real, factor_imag], axis=-1))


NEAR = 2


def swap_near(copies, axes):
    return lax.all_to_all(copies, axes[-NEAR:], 0, 0)


def swap_far(block, axes):
    far = axes[:-NEAR]
    return lax.all_to_all(jnp.broadcast_to(block, (2 ** len(far),) + block.shape), far, 0, 0)


def gather_all(copies, axes):
    got = swap_far(swap_near(copies, axes), axes)
    return got.reshape((-1,) + got.shape[2:])


def sum_far(copies, axes):
    return swap_far(jnp.sum(swap_near(copies, axes), axis=0), axes)


def phases(axes):
    left, out = list(axes), [(axes[-1],)]
    left = left[:-1]
    while left:
        out.append(tuple(left[-2:]))
        left = left[:-2]
    return out


def scatter_sum(value, axes):
    count = 2 ** len(axes)
    pieces = value.reshape((count, value.shape[0] // count) + value.shape[1:])
    return jnp.sum(lax.all_to_all(pieces, axes, 0, 0), axis=0)


def gather_rows(value, axes):
    count = 2 ** len(axes)
    copies = jnp.broadcast_to(value, (count,) + value.shape)
    return lax.all_to_all(copies, axes, 0, 0).reshape((count * value.shape[0],) + value.shape[1:])


def sum_all(value, axes):
    for part in phases(axes):
        value = scatter_sum(value, part)
    for part in reversed(phases(axes)):
        value = gather_rows(value, part)
    return value


def cols(c):
    return slice(c * 128, (c + 1) * 128)


def chunk_count(ref):
    return ref.shape[-1] // 256


def rows_of(ref, at, chunks):
    half = chunks * 128
    re = [ref[at, c * 128 : (c + 1) * 128] for c in range(chunks)]
    im = [ref[at, half + c * 128 : half + (c + 1) * 128] for c in range(chunks)]
    return re, im


def put_rows(ref, at, re, im):
    chunks = len(re)
    half = chunks * 128
    for c in range(chunks):
        ref[at, c * 128 : (c + 1) * 128] = re[c]
        ref[at, half + c * 128 : half + (c + 1) * 128] = im[c]


def put_copies(ref, re, im):
    ref[0] = jnp.zeros(ref.shape[1:], F32)
    for c in range(len(re)):
        ref[0, c : c + 1] = re[c]
        ref[0, SLOT + c : SLOT + c + 1] = im[c]
    ref[...] = jnp.broadcast_to(ref[0:1], ref.shape)


def wide(rows):
    return [jnp.broadcast_to(v, (LANES, 128)) for v in rows]


def chain(ends_ref, jr_ref, power, carry, down, start_ref=None):
    chunks = len(power[0])
    pr, pi = power
    cr, ci = carry
    order = range(LANES - 1, -1, -1) if down else range(LANES)
    for s in order:
        at = slice(s, s + 1)
        if start_ref is not None:
            put_rows(start_ref, at, cr, ci)
        er, ei = rows_of(ends_ref, at, chunks)
        alive = (jr_ref[at, :] < 0).astype(F32)
        cr, ci = (
            [er[c] + alive * (pr[c] * cr[c] - pi[c] * ci[c]) for c in range(chunks)],
            [ei[c] + alive * (pr[c] * ci[c] + pi[c] * cr[c]) for c in range(chunks)],
        )
    return cr, ci


def carry_in(ends_ref, table_ref, chunks):
    total = jnp.zeros((2 * SLOT, 128), F32)
    for e in range(ends_ref.shape[0]):
        end = ends_ref[e]
        turned = jnp.concatenate([end[SLOT:], end[:SLOT]], axis=0)
        total += table_ref[0, e] * end + table_ref[1, e] * turned
    return (
        [total[c : c + 1] for c in range(chunks)],
        [total[SLOT + c : SLOT + c + 1] for c in range(chunks)],
    )


def scan_tile(src_ref, st_ref, decay, jr_ref, first_step, steps, down, emit=None, unroll=4):
    chunks = chunk_count(src_ref)
    dr, di = wide(decay[0]), wide(decay[1])
    jr = jr_ref[...]
    re, im = rows_of(st_ref, slice(0, LANES), chunks)

    def one(step, re, im):
        at = pl.ds(pl.multiple_of(step * LANES, LANES), LANES)
        br, bi = rows_of(src_ref, at, chunks)
        live = jr != first_step + step
        nr, ni = [], []
        for c in range(chunks):
            xr = jnp.where(live, re[c], 0.0)
            xi = jnp.where(live, im[c], 0.0)
            nr.append(dr[c] * xr - di[c] * xi + br[c])
            ni.append(dr[c] * xi + di[c] * xr + bi[c])
        return nr, ni

    def body(i, carry):
        re, im = list(carry[:chunks]), list(carry[chunks : 2 * chunks])
        extra = carry[2 * chunks :]
        for q in range(unroll):
            n = 2 * (i * unroll + q)
            low_step = steps - 2 - n if down else n
            a, b = (low_step + 1, low_step) if down else (low_step, low_step + 1)
            r1, i1 = one(a, re, im)
            r2, i2 = one(b, r1, i1)
            if emit is not None:
                pair = ((r2, i2), (r1, i1)) if down else ((r1, i1), (r2, i2))
                extra = emit(low_step, pair, extra)
            re, im = r2, i2
        return tuple(re) + tuple(im) + tuple(extra)

    start = tuple(re) + tuple(im)
    if emit is not None:
        start = start + tuple(emit(None, None, None))
    out = lax.fori_loop(0, steps // (2 * unroll), body, start)
    put_rows(st_ref, slice(0, LANES), list(out[:chunks]), list(out[chunks : 2 * chunks]))
    return out[2 * chunks :]


def store_pair(ref, low_step, first, second):
    at = pl.ds(pl.multiple_of(low_step * LANES, 2 * LANES), 2 * LANES)
    re = [jnp.concatenate([p, q], axis=0).astype(BF16) for p, q in zip(first[0], second[0])]
    im = [jnp.concatenate([p, q], axis=0).astype(BF16) for p, q in zip(first[1], second[1])]
    put_rows(ref, at, re, im)


def disc_row(disc_ref, row, chunks, conj=False):
    re, im = rows_of(disc_ref, slice(row, row + 1), chunks)
    return (re, [-v for v in im]) if conj else (re, im)


def column_sum(value):
    rows, width = value.shape
    return jnp.sum(jnp.sum(value.reshape(rows // 8, 8, width), axis=0), axis=0, keepdims=True)


def permute_in(block, order_ref):
    runs, steps, width = block.shape
    span = order_ref.shape[0] // runs
    out = []
    for k in range(steps // span):
        part = block[:, k * span : (k + 1) * span, :].reshape(runs * span, width)
        out.append(jnp.dot(order_ref[...], part, preferred_element_type=F32))
    return out[0] if len(out) == 1 else jnp.concatenate(out, axis=0)


def permute_out(value, order_ref, out_ref):
    rows, width = value.shape
    size = order_ref.shape[0]
    span = size // LANES
    high = value.astype(BF16)
    low = (value - high.astype(F32)).astype(BF16)
    for k in range(rows // size):
        at = slice(k * size, (k + 1) * size)
        back = lax.dot_general(order_ref[...], high[at], TN, preferred_element_type=F32)
        back += lax.dot_general(order_ref[...], low[at], TN, preferred_element_type=F32)
        out_ref[:, k * span : (k + 1) * span, :] = back.reshape(LANES, span, width)


def expm1(value):
    acc = jnp.full_like(value, 1.0 / 479001600.0)
    for n in (39916800.0, 3628800.0, 362880.0, 40320.0, 5040.0, 720.0, 120.0, 24.0, 6.0, 2.0, 1.0):
        acc = acc * value + 1.0 / n
    return jnp.where(value > -1.0, acc * value, jnp.exp(value) - 1.0)


def prep_kernel(
    rows, axes, starts_ref, rate_ref, step_ref, freq_ref,
    disc_ref, table_ref, cut_ref, order_ref,
):
    devices = 2 ** len(axes)
    total = rows * devices
    run = rows // LANES
    half = rate_ref.shape[-1]
    me = 0
    for axis in axes:
        me = 2 * me + lax.axis_index(axis)
    starts = [starts_ref[k] for k in range(starts_ref.shape[0])]

    base = me * rows + run * lax.broadcasted_iota(jnp.int32, (LANES, 128), 0)
    up = jnp.full((LANES, 128), -1, jnp.int32)
    down = up
    for begin in starts + [total]:
        rel = begin - base
        up = jnp.maximum(up, jnp.where((rel >= 0) & (rel < run), rel, -1))
        down = jnp.maximum(down, jnp.where((rel >= 1) & (rel <= run), rel - 1, -1))
    cut_ref[0] = up
    cut_ref[1] = down

    size = order_ref.shape[0]
    span = size // LANES
    to = lax.broadcasted_iota(jnp.int32, (size, size), 0)
    back = lax.broadcasted_iota(jnp.int32, (size, size), 1)
    order_ref[...] = ((to % LANES) * span + to // LANES == back).astype(F32).astype(BF16)

    source = lax.broadcasted_iota(jnp.int32, (devices, half), 0)
    for l in range(LAYERS):
        row = slice(l, l + 1)
        rate, freq = rate_ref[row], freq_ref[row]
        step_size = jnp.exp(step_ref[row])
        real_angle = -rate * step_size
        imag_angle = freq * step_size
        magnitude = jnp.exp(real_angle)
        cosine, sine = jnp.cos(imag_angle), jnp.sin(imag_angle)
        minus_real = expm1(real_angle) * cosine - 2.0 * jnp.sin(0.5 * imag_angle) ** 2
        minus_imag = magnitude * sine
        modulus = rate * rate + freq * freq
        disc_ref[l, 0:1, :half] = magnitude * cosine
        disc_ref[l, 0:1, half:] = minus_imag
        disc_ref[l, 1:2, :half] = (-rate * minus_real + freq * minus_imag) / modulus
        disc_ref[l, 1:2, half:] = (-rate * minus_imag - freq * minus_real) / modulus
        magnitude = jnp.exp(real_angle * float(run))
        disc_ref[l, 2:3, :half] = magnitude * jnp.cos(imag_angle * float(run))
        disc_ref[l, 2:3, half:] = magnitude * jnp.sin(imag_angle * float(run))
        disc_ref[l, 3:8] = jnp.zeros((5, 2 * half), F32)
        for back in range(2):
            going_down = (l + back) % 2 == 1
            if going_down:
                live, count = source > me, source - me - 1
            else:
                live, count = source < me, me - 1 - source
            for begin in starts:
                if going_down:
                    cut = ((begin > (me + 1) * rows).astype(jnp.int32) > 0) & (
                        source * rows >= begin
                    )
                else:
                    cut = ((begin < me * rows).astype(jnp.int32) > 0) & (
                        (source + 1) * rows <= begin
                    )
                live &= ~cut
            count = (jnp.maximum(count, 0) * rows).astype(F32)
            magnitude = jnp.where(live, jnp.exp(real_angle * count), 0.0)
            angle = imag_angle * count
            real = magnitude * jnp.cos(angle)
            imag = magnitude * jnp.sin(angle)
            imag = -imag if back else imag
            at = 2 * l + back
            table_ref[at] = jnp.zeros(table_ref.shape[1:], F32)
            for c in range(half // 128):
                table_ref[at, 0, :, c, :] = real[:, cols(c)]
                table_ref[at, 0, :, SLOT + c, :] = real[:, cols(c)]
                table_ref[at, 1, :, c, :] = -imag[:, cols(c)]
                table_ref[at, 1, :, SLOT + c, :] = imag[:, cols(c)]


def stats_kernel(tok_ref, order_ref, u_ref, stats_ref):
    value = permute_in(tok_ref[...], order_ref)
    u_ref[...] = value.astype(BF16)
    add_stats(stats_ref, value)


def add_stats(stats_ref, value):
    add_rows(stats_ref, column_sum(value), column_sum(value * value))


def add_rows(copies_ref, first, second, spread=True):
    i, nt = pl.program_id(0), pl.num_programs(0)
    chunks = first.shape[1] // 128

    @pl.when(i == 0)
    def _():
        copies_ref[0] = jnp.zeros(copies_ref.shape[1:], F32)

    for c in range(chunks):
        copies_ref[0, c : c + 1] += first[:, cols(c)]
        copies_ref[0, SLOT + c : SLOT + c + 1] += second[:, cols(c)]

    if spread:

        @pl.when(i == nt - 1)
        def _():
            copies_ref[...] = jnp.broadcast_to(copies_ref[0:1], copies_ref.shape)


def summed(ref):
    total = jnp.sum(ref[...], axis=0)
    return tuple(
        jnp.concatenate([total[SLOT * k + c : SLOT * k + c + 1] for c in range(SLOT)], axis=1)
        for k in range(2)
    )


def drive_kernel(layer, down, tokens, *refs):
    (
        stat_ref, u_ref, gain_ref, bias_ref, skip_ref, win_ref, disc_ref, jr_ref,
        b_ref, end_ref, blk_ref, norm_ref,
    ) = refs
    i, nt = pl.program_id(0), pl.num_programs(0)
    steps = u_ref.shape[0] // LANES
    chunks = chunk_count(b_ref)
    half = chunks * 128

    @pl.when(i == 0)
    def _():
        total, squares = summed(stat_ref)
        row = slice(layer, layer + 1)
        mean = total / tokens
        inv = lax.rsqrt(squares / tokens - mean * mean + EPSILON)
        norm_ref[0:1] = mean
        norm_ref[1:2] = inv
        norm_ref[2:3] = inv * gain_ref[row]
        norm_ref[3:4] = bias_ref[row]
        norm_ref[4:5] = skip_ref[row]
        norm_ref[5:8] = jnp.zeros((3, norm_ref.shape[1]), F32)
        blk_ref[...] = jnp.zeros_like(blk_ref)

    u = u_ref[...].astype(F32)
    normed = (u - norm_ref[0:1]) * norm_ref[2:3] + norm_ref[3:4]
    drive = jnp.dot(normed.astype(BF16), win_ref[...], preferred_element_type=F32)
    fr, fi = disc_ref[1:2, :half], disc_ref[1:2, half:]
    re, im = drive[:, :half], drive[:, half:]
    b_ref[:, :half] = re * fr - im * fi
    b_ref[:, half:] = re * fi + im * fr
    tile = nt - 1 - i if down else i
    scan_tile(b_ref, blk_ref, disc_row(disc_ref, 0, chunks), jr_ref, tile * steps, steps, down)

    @pl.when(i == nt - 1)
    def _():
        zero = [jnp.zeros((1, 128), F32)] * chunks
        cr, ci = chain(blk_ref, jr_ref, disc_row(disc_ref, 2, chunks), (zero, zero), down)
        put_copies(end_ref, cr, ci)


def states_of(ends_ref, table_ref, b_ref, blk_ref, disc_ref, jr_ref, low_ref, st_ref, down):
    i, nt = pl.program_id(0), pl.num_programs(0)
    chunks = chunk_count(b_ref)
    steps = b_ref.shape[0] // LANES

    @pl.when(i == 0)
    def _():
        carry = carry_in(ends_ref, table_ref, chunks)
        chain(blk_ref, jr_ref, disc_row(disc_ref, 2, chunks), carry, down, st_ref)

    def emit(low_step, pair, extra):
        if pair is None:
            return ()
        (first, second) = pair
        store_pair(low_ref, low_step, first, second)
        return ()

    tile = nt - 1 - i if down else i
    scan_tile(
        b_ref, st_ref, disc_row(disc_ref, 0, chunks), jr_ref, tile * steps, steps, down, emit
    )


def gelu_parts(mixed):
    square = mixed * mixed
    tanh = jnp.tanh(mixed * (GELU_A + (GELU_A * GELU_B) * square))
    half_up = 0.5 + 0.5 * tanh
    return square, tanh, half_up


def gelu_slope(mixed, square, tanh, half_up):
    return half_up + (mixed * (0.5 - 0.5 * tanh * tanh)) * (
        GELU_A + (3.0 * GELU_A * GELU_B) * square
    )


def sigmoid(value):
    return 0.5 + 0.5 * jnp.tanh(0.5 * value)


def forward_kernel(down, *refs):
    (
        ends_ref, table_ref, b_ref, blk_ref, disc_ref, jr_ref, u_ref, norm_ref, wout_ref, wgate_ref,
        next_ref, low_ref, mixed_ref, gate_ref, stats_ref, st_ref,
    ) = refs
    states_of(ends_ref, table_ref, b_ref, blk_ref, disc_ref, jr_ref, low_ref, st_ref, down)
    u = u_ref[...].astype(F32)
    normed = (u - norm_ref[0:1]) * norm_ref[2:3] + norm_ref[3:4]
    mixed = jnp.dot(low_ref[...], wout_ref[...], preferred_element_type=F32)
    mixed += norm_ref[4:5] * normed
    _, _, half_up = gelu_parts(mixed)
    act = mixed * half_up
    gate = sigmoid(jnp.dot(act.astype(BF16), wgate_ref[...], preferred_element_type=F32))
    after = u + act * gate
    next_ref[...] = after
    mixed_ref[...] = mixed.astype(mixed_ref.dtype)
    gate_ref[...] = gate.astype(gate_ref.dtype)
    add_stats(stats_ref, after)


def accumulate(ref, value):
    @pl.when(pl.program_id(0) == 0)
    def _():
        ref[...] = value

    @pl.when(pl.program_id(0) != 0)
    def _():
        ref[...] += value


def gate_backward(g, mixed, gate, normed, low_ref, wout_ref, wgate_ref, outs, kept=None):
    pg_ref, sg_ref, wsum_ref, ssum_ref = outs
    width = g.shape[1]
    square, tanh, half_up = gelu_parts(mixed) if kept is None else kept
    act = mixed * half_up
    g_gate = g * gate
    logit_grad = (g_gate * act * (1.0 - gate)).astype(BF16)
    accumulate(
        wsum_ref.at[:width],
        lax.dot_general(act.astype(BF16), logit_grad, TN, preferred_element_type=F32),
    )
    act_grad = g_gate + lax.dot_general(
        logit_grad, wgate_ref[...], NT, preferred_element_type=F32
    )
    mixed_grad = act_grad * gelu_slope(mixed, square, tanh, half_up)
    accumulate(ssum_ref, column_sum(mixed_grad * normed))
    proj_grad = mixed_grad.astype(BF16)
    pg_ref[...] = proj_grad
    accumulate(
        wsum_ref.at[width : width + low_ref.shape[1]],
        lax.dot_general(low_ref[...], proj_grad, TN, preferred_element_type=F32),
    )
    sg_ref[...] = lax.dot_general(proj_grad, wout_ref[...], NT, preferred_element_type=F32)


def turn_kernel(down, *refs):
    (
        ends_ref, table_ref, b_ref, blk_ref, disc_ref, jr_ref, jo_ref, u_ref, norm_ref, wout_ref, wgate_ref,
        gout_ref, order_ref,
        out_ref, low_ref, g_ref, pg_ref, sg_ref, wsum_ref, ssum_ref, end_ref, ablk_ref,
        st_ref, w_ref,
    ) = refs
    i, nt = pl.program_id(0), pl.num_programs(0)
    chunks = chunk_count(b_ref)
    half = chunks * 128
    steps = b_ref.shape[0] // LANES
    tile = nt - 1 - i if down else i
    states_of(ends_ref, table_ref, b_ref, blk_ref, disc_ref, jr_ref, low_ref, st_ref, down)
    u = u_ref[...]
    normed = (u - norm_ref[0:1]) * norm_ref[2:3] + norm_ref[3:4]
    mixed = jnp.dot(low_ref[...], wout_ref[...], preferred_element_type=F32)
    mixed += norm_ref[4:5] * normed
    kept = gelu_parts(mixed)
    act = mixed * kept[2]
    gate = sigmoid(jnp.dot(act.astype(BF16), wgate_ref[...], preferred_element_type=F32))
    permute_out(u + act * gate, order_ref, out_ref)
    g = permute_in(gout_ref[...], order_ref)
    g_ref[...] = g.astype(BF16)
    gate_backward(
        g, mixed, gate, normed, low_ref, wout_ref, wgate_ref,
        (pg_ref, sg_ref, wsum_ref, ssum_ref), kept,
    )

    @pl.when(i == 0)
    def _():
        w_ref[:, :half] = jnp.ones((LANES, half), F32)
        w_ref[:, half:] = jnp.zeros((LANES, half), F32)
        ablk_ref[...] = jnp.zeros_like(ablk_ref)

    dr, di = disc_row(disc_ref, 0, chunks, conj=True)
    dr, di = wide(dr), wide(di)
    jo = jo_ref[...]
    unroll = 4

    def body(k, carry):
        wr, wi, ar, ai = (list(carry[n * chunks : (n + 1) * chunks]) for n in range(4))
        for q in range(unroll):
            n = k * unroll + q
            step = steps - 1 - n if down else n
            at = pl.ds(pl.multiple_of(step * LANES, LANES), LANES)
            sr, si = rows_of(sg_ref, at, chunks)
            live = jo != tile * steps + step
            for c in range(chunks):
                ar[c] = ar[c] + (wr[c] * sr[c] - wi[c] * si[c])
                ai[c] = ai[c] + (wr[c] * si[c] + wi[c] * sr[c])
                xr = jnp.where(live, wr[c], 0.0)
                xi = jnp.where(live, wi[c], 0.0)
                wr[c] = xr * dr[c] - xi * di[c]
                wi[c] = xr * di[c] + xi * dr[c]
        return tuple(wr) + tuple(wi) + tuple(ar) + tuple(ai)

    wr, wi = rows_of(w_ref, slice(0, LANES), chunks)
    ar, ai = rows_of(ablk_ref, slice(0, LANES), chunks)
    out = lax.fori_loop(
        0, steps // unroll, body, tuple(wr) + tuple(wi) + tuple(ar) + tuple(ai)
    )
    wr, wi, ar, ai = (list(out[n * chunks : (n + 1) * chunks]) for n in range(4))
    put_rows(w_ref, slice(0, LANES), wr, wi)
    put_rows(ablk_ref, slice(0, LANES), ar, ai)

    @pl.when(i == nt - 1)
    def _():
        zero = [jnp.zeros((1, 128), F32)] * chunks
        power = disc_row(disc_ref, 2, chunks, conj=True)
        cr, ci = chain(ablk_ref, jo_ref, power, (zero, zero), not down)
        put_copies(end_ref, cr, ci)


def adjoint_kernel(down, last, *refs):
    (
        ends_ref, table_ref, sg_ref, ablk_ref, disc_ref, jr_ref, low_ref, u_ref, norm_ref, pg_ref, g_ref,
        win_ref, order_ref, ssum_ref, _,
        res_ref, wsum_ref, nsum_ref, st_ref, dg_ref, ax_ref, isum_ref, pack_ref, sem,
    ) = refs
    width, states_width = win_ref.shape
    i, nt = pl.program_id(0), pl.num_programs(0)
    chunks = chunk_count(sg_ref)
    half = chunks * 128
    steps = sg_ref.shape[0] // LANES
    tile = nt - 1 - i if down else i

    @pl.when(i == 0)
    def _():
        carry = carry_in(ends_ref, table_ref, chunks)
        power = disc_row(disc_ref, 2, chunks, conj=True)
        chain(ablk_ref, jr_ref, power, carry, down, st_ref)
        ax_ref[...] = jnp.zeros_like(ax_ref)

    fr, fi = disc_row(disc_ref, 1, chunks)
    fr, fi = wide(fr), wide(fi)

    def emit(low_step, pair, extra):
        if pair is None:
            re, im = rows_of(ax_ref, slice(0, LANES), chunks)
            return tuple(re) + tuple(im)
        sums_r, sums_i = list(extra[:chunks]), list(extra[chunks:])
        at = pl.ds(pl.multiple_of(low_step * LANES, 2 * LANES), 2 * LANES)
        xr, xi = rows_of(low_ref, at, chunks)
        grads = []
        for which, (ar, ai) in enumerate(pair):
            gr, gi = [], []
            rows = slice(which * LANES, (which + 1) * LANES)
            for c in range(chunks):
                vr, vi = xr[c].astype(F32)[rows], xi[c].astype(F32)[rows]
                sums_r[c] = sums_r[c] + (ar[c] * vr + ai[c] * vi)
                sums_i[c] = sums_i[c] + (ai[c] * vr - ar[c] * vi)
                gr.append(ar[c] * fr[c] + ai[c] * fi[c])
                gi.append(ai[c] * fr[c] - ar[c] * fi[c])
            grads.append((gr, gi))
        store_pair(dg_ref, low_step, grads[0], grads[1])
        return tuple(sums_r) + tuple(sums_i)

    sums = scan_tile(
        sg_ref, st_ref, disc_row(disc_ref, 0, chunks, conj=True), jr_ref, tile * steps, steps,
        down, emit,
    )
    put_rows(ax_ref, slice(0, LANES), list(sums[:chunks]), list(sums[chunks:]))

    u = u_ref[...].astype(F32)
    centered = u - norm_ref[0:1]
    normed = (centered * norm_ref[2:3] + norm_ref[3:4]).astype(BF16)
    drive_grad = dg_ref[...]
    accumulate(
        isum_ref, lax.dot_general(normed, drive_grad, TN, preferred_element_type=F32)
    )
    normed_grad = lax.dot_general(drive_grad, win_ref[...], NT, preferred_element_type=F32)
    normed_grad += norm_ref[4:5] * pg_ref[...].astype(F32)
    add_rows(
        nsum_ref, column_sum(normed_grad), column_sum(normed_grad * centered) * norm_ref[1:2], False
    )
    result = g_ref[...].astype(F32) + norm_ref[2:3] * normed_grad
    if last:
        permute_out(result, order_ref, res_ref)
    else:
        res_ref[...] = result

    @pl.when(i == nt - 1)
    def _():
        left = states_width - width
        pack_ref[:width] = isum_ref[:, :width]
        for p in range(width // left):
            rows = width * left // width
            pack_ref[width:, p * left : (p + 1) * left] = isum_ref[p * rows : (p + 1) * rows, width:]
        count = pack_ref.shape[0]
        copy = pltpu.make_async_copy(
            pack_ref, wsum_ref.at[pl.ds(wsum_ref.shape[0] - count, count)], sem
        )
        copy.start()
        at = 2 * SLOT
        for c in range(width // 128):
            nsum_ref[0, at + c : at + c + 1] = ssum_ref[:, cols(c)]
        at += width // 128
        decays = jnp.sum(ax_ref[...], axis=0, keepdims=True)
        wr, wi = win_ref[:, :half].astype(F32), win_ref[:, half:].astype(F32)
        gr, gi = isum_ref[:, :half], isum_ref[:, half:]
        re = jnp.sum(wr * gr + wi * gi, axis=0, keepdims=True)
        im = jnp.sum(wr * gi - wi * gr, axis=0, keepdims=True)
        gr, gi = disc_ref[1:2, :half], disc_ref[1:2, half:]
        scale = 1.0 / (gr * gr + gi * gi)
        factors = ((re * gr - im * gi) * scale, (re * gi + im * gr) * scale)
        for c in range(2 * chunks):
            nsum_ref[0, at + c : at + c + 1] = decays[:, cols(c)]
        at += 2 * chunks
        for c in range(chunks):
            nsum_ref[0, at + c : at + c + 1] = factors[0][:, cols(c)]
            nsum_ref[0, at + chunks + c : at + chunks + c + 1] = factors[1][:, cols(c)]
        nsum_ref[...] = jnp.broadcast_to(nsum_ref[0:1], nsum_ref.shape)
        copy.wait()


def back_kernel(down, tokens, *refs):
    (
        sums_ref, r_ref, up_ref, up_norm_ref, mixed_ref, gate_ref, low_ref, u_ref, norm_ref, wout_ref,
        wgate_ref, disc_ref, jo_ref,
        g_ref, pg_ref, sg_ref, wsum_ref, ssum_ref, end_ref, ablk_ref, nsum_ref, bsum_ref,
    ) = refs
    i, nt = pl.program_id(0), pl.num_programs(0)
    chunks = chunk_count(sg_ref)
    steps = sg_ref.shape[0] // LANES
    tile = nt - 1 - i if down else i

    @pl.when(i == 0)
    def _():
        nsum_ref[...] = jnp.sum(sums_ref[...], axis=0)
        bsum_ref[0:1], bsum_ref[1:2] = summed(sums_ref)
        ablk_ref[...] = jnp.zeros_like(ablk_ref)

    scale = up_norm_ref[2:3] * (-1.0 / tokens)
    standard = (up_ref[...] - up_norm_ref[0:1]) * (scale * up_norm_ref[1:2] * bsum_ref[1:2])
    g = r_ref[...] + (standard + scale * bsum_ref[0:1])
    g_ref[...] = g
    u = u_ref[...].astype(F32)
    normed = (u - norm_ref[0:1]) * norm_ref[2:3] + norm_ref[3:4]
    gate_backward(
        g, mixed_ref[...].astype(F32), gate_ref[...].astype(F32), normed, low_ref, wout_ref,
        wgate_ref, (pg_ref, sg_ref, wsum_ref, ssum_ref),
    )
    decay = disc_row(disc_ref, 0, chunks, conj=True)
    scan_tile(sg_ref, ablk_ref, decay, jo_ref, tile * steps, steps, down)

    @pl.when(i == nt - 1)
    def _():
        zero = [jnp.zeros((1, 128), F32)] * chunks
        power = disc_row(disc_ref, 2, chunks, conj=True)
        cr, ci = chain(ablk_ref, jo_ref, power, (zero, zero), down)
        put_copies(end_ref, cr, ci)


def assemble_kernel(layer, width, states, sums_ref, *refs):
    in_ref, out_ref, gate_ref, sems = refs[-4:]
    left = states - width
    pieces = [
        (sums_ref.at[:width], gate_ref.at[layer]),
        (sums_ref.at[width : width + states], out_ref.at[layer]),
        (sums_ref.at[width + states : 2 * width + states], in_ref.at[layer, :, :width]),
    ]
    for p in range(width // left):
        pieces.append(
            (
                sums_ref.at[2 * width + states :, p * left : (p + 1) * left],
                in_ref.at[layer, p * left : (p + 1) * left, width:],
            )
        )
    copies = [pltpu.make_async_copy(a, b, sems.at[k]) for k, (a, b) in enumerate(pieces)]
    for copy in copies:
        copy.start()
    for copy in copies:
        copy.wait()


def whole(array):
    shape = array.shape
    return pl.BlockSpec(shape, lambda i: (0,) * len(shape))


def tile_spec(rows, width, nt, down):
    if down:
        return pl.BlockSpec((rows, width), lambda i: (nt - 1 - i, 0))
    return pl.BlockSpec((rows, width), lambda i: (i, 0))


def run_spec(steps, width, nt, down):
    if down:
        return pl.BlockSpec((LANES, steps, width), lambda i: (0, nt - 1 - i, 0))
    return pl.BlockSpec((LANES, steps, width), lambda i: (0, i, 0))


def assemble(layer, width, states, sums, before=()):
    anywhere = pl.BlockSpec(memory_space=pl.ANY)
    return pl.pallas_call(
        functools.partial(assemble_kernel, layer, width, states),
        in_specs=[anywhere] * (1 + len(before)),
        out_specs=[anywhere] * 3,
        out_shape=[
            shape(LAYERS, width, states), shape(LAYERS, states, width), shape(LAYERS, width, width)
        ],
        input_output_aliases={k + 1: k for k in range(len(before))},
        scratch_shapes=[pltpu.SemaphoreType.DMA((3 + width // (states - width),))],
        name="assemble_%d" % layer,
    )(sums, *before)


def call(kernel, nt, args, outs, scratch, name, alias=None):
    arrays = [a for a, _ in args]
    return pl.pallas_call(
        kernel,
        grid=(nt,),
        in_specs=[whole(a) if s is None else s for a, s in args],
        out_specs=[whole(a) if s is None else s for a, s in outs],
        out_shape=[a for a, _ in outs],
        scratch_shapes=scratch,
        compiler_params=pltpu.CompilerParams(
            vmem_limit_bytes=VMEM_LIMIT, dimension_semantics=("arbitrary",)
        ),
        cost_estimate=pl.CostEstimate(flops=0, bytes_accessed=0, transcendentals=0),
        input_output_aliases=alias or {},
        name=name,
    )(*arrays)


def shape(*dims, dtype=F32):
    return jax.ShapeDtypeStruct(dims, dtype)


def body(
    axes,
    tokens_in,
    seq_starts,
    norm_gain,
    norm_bias,
    decay_rate,
    step_log,
    frequency,
    in_proj,
    out_proj,
    skip_gain,
    gate_proj,
    grad_out,
):
    rows, width = tokens_in.shape
    states = in_proj.shape[-1]
    devices = 2 ** len(axes)
    tokens = float(rows * devices)
    run = rows // LANES
    steps = min(64, run)
    tile = steps * LANES
    nt = rows // tile
    span = min(32, steps)
    discs, tables, cuts, order = pl.pallas_call(
        functools.partial(prep_kernel, rows, axes),
        in_specs=[pl.BlockSpec(memory_space=pltpu.SMEM)]
        + [pl.BlockSpec(memory_space=pltpu.VMEM)] * 3,
        out_specs=[pl.BlockSpec(memory_space=pltpu.VMEM)] * 4,
        out_shape=[
            shape(LAYERS, 8, states), shape(2 * LAYERS, 2, devices, 2 * SLOT, 128),
            shape(2, LANES, 128, dtype=jnp.int32), shape(span * LANES, span * LANES, dtype=BF16),
        ],
        compiler_params=pltpu.CompilerParams(vmem_limit_bytes=VMEM_LIMIT),
        name="prep",
    )(seq_starts, decay_rate, step_log, frequency)

    def tiles(array, down):
        return (array, tile_spec(tile, array.shape[-1], nt, down))

    def runs(array, down):
        return (array, run_spec(steps, array.shape[-1], nt, down))

    def full(array):
        return (array, None)

    def of(array, l):
        size = array.shape[1:]
        return (array, pl.BlockSpec((None,) + size, lambda i: (l,) + (0,) * len(size)))

    def first(array):
        return (array, pl.BlockSpec((width + states, width), lambda i: (0, 0)))

    def anywhere(array):
        return (array, pl.BlockSpec(memory_space=pl.ANY))

    tokens_run = tokens_in.reshape(LANES, run, width)
    grad_run = grad_out.reshape(LANES, run, width)
    state_scratch = pltpu.VMEM((LANES, states), F32)
    near = 2**NEAR
    small = 2 * SLOT + (width + 2 * states) // 128
    sums = 2 * states + width

    u0, stats = call(
        stats_kernel, nt, [runs(tokens_run, 0), full(order)],
        [tiles(shape(rows, width, dtype=BF16), 0), full(shape(near, 2 * SLOT, 128))],
        [], "stats",
    )

    def drive(l, stream, stats):
        down = l % 2
        return call(
            functools.partial(drive_kernel, l, bool(down), tokens), nt,
            [full(sum_far(stats, axes)), tiles(stream, down), full(norm_gain), full(norm_bias), full(skip_gain), of(in_proj, l), of(discs, l),
               of(cuts, down)],
            [tiles(shape(rows, states), down), full(shape(near, 2 * SLOT, 128)),
             full(shape(LANES, states)), full(shape(8, width))],
            [], f"drive_{l}",
        )

    b0, end0, blk0, norm0 = drive(0, u0, stats)
    u1, low0, mixed0, gate0, stats = call(
        functools.partial(forward_kernel, False), nt,
        [full(gather_all(end0, axes)), of(tables, 2 * 0 + 0), tiles(b0, 0), full(blk0), of(discs, 0), of(cuts, 0),
           tiles(u0, 0), full(norm0), of(out_proj, 0), of(gate_proj, 0)],
        [tiles(shape(rows, width), 0), tiles(shape(rows, states, dtype=BF16), 0),
         tiles(shape(rows, width, dtype=BF16), 0), tiles(shape(rows, width, dtype=BF16), 0),
         full(shape(near, 2 * SLOT, 128))],
        [state_scratch], "forward_0",
    )

    b1, end1, blk1, norm1 = drive(1, u1, stats)
    (
        out, low1, g1, pg1, sg1, w_sum1, skip_sum1, aend1, ablk1
    ) = call(
        functools.partial(turn_kernel, True), nt,
        [full(gather_all(end1, axes)), of(tables, 2 * 1 + 0), tiles(b1, 1), full(blk1), of(discs, 1), of(cuts, 1),
           of(cuts, 0), tiles(u1, 1), full(norm1), of(out_proj, 1), of(gate_proj, 1),
           runs(grad_run, 1), full(order)],
        [runs(shape(LANES, run, width), 1), tiles(shape(rows, states, dtype=BF16), 1),
         tiles(shape(rows, width, dtype=BF16), 1), tiles(shape(rows, width, dtype=BF16), 1),
         tiles(shape(rows, states), 1), first(shape(sums, width)), full(shape(1, width)),
         full(shape(near, 2 * SLOT, 128)), full(shape(LANES, states))],
        [state_scratch, state_scratch], "turn_1",
    )

    def adjoint(l, sg, ablk, aend, low, stream, norm, pg, g, skip_sum, w_sum):
        down = 1 - l % 2
        last = l == 0
        args = [
            full(gather_all(aend, axes)), of(tables, 2 * l + 1), tiles(sg, down), full(ablk),
            of(discs, l), of(cuts, down), tiles(low, down), tiles(stream, down), full(norm),
            tiles(pg, down), tiles(g, down), of(in_proj, l), full(order), full(skip_sum),
            anywhere(w_sum),
        ]
        return call(
            functools.partial(adjoint_kernel, bool(down), last), nt, args,
            [runs(shape(LANES, run, width), down) if last else tiles(shape(rows, width), down),
             anywhere(shape(sums, width)), full(shape(near, small, 128))],
            [state_scratch, pltpu.VMEM((tile, states), BF16), state_scratch,
             pltpu.VMEM((width, states), F32), pltpu.VMEM((states, width), F32),
             pltpu.SemaphoreType.DMA],
            f"adjoint_{l}", {len(args) - 1: 1},
        )

    r1, w_sum1, norm_sum1 = adjoint(
        1, sg1, ablk1, aend1, low1, u1, norm1, pg1, g1,
        skip_sum1, w_sum1,
    )
    (
        g0, pg0, sg0, w_sum0, skip_sum0, aend0, ablk0, small1, _
    ) = call(
        functools.partial(back_kernel, True, tokens), nt,
        [full(sum_far(norm_sum1, axes)), tiles(r1, 1), tiles(u1, 1), full(norm1), tiles(mixed0, 1), tiles(gate0, 1),
           tiles(low0, 1), tiles(u0, 1), full(norm0), of(out_proj, 0), of(gate_proj, 0),
           of(discs, 0), of(cuts, 1)],
        [tiles(shape(rows, width), 1), tiles(shape(rows, width, dtype=BF16), 1),
         tiles(shape(rows, states), 1), first(shape(sums, width)),
         full(shape(1, width)), full(shape(near, 2 * SLOT, 128)), full(shape(LANES, states)),
         full(shape(small, 128)), full(shape(2, width))],
        [], "back_0",
    )
    r0, w_sum0, norm_sum0 = adjoint(
        0, sg0, ablk0, aend0, low0, u0, norm0, pg0, g0, skip_sum0, w_sum0
    )
    small0 = jnp.sum(sum_far(norm_sum0, axes), axis=0)
    pair = jnp.stack([small0.reshape(-1), small1.reshape(-1)])
    bias_grad, gain_grad, skip_grad = (pair[:, k * width : (k + 1) * width] for k in range(3))
    dsum = pair[:, 3 * width : 3 * width + states]
    fsum = pair[:, 3 * width + states :]

    scale = norm0[2:3] * (-1.0 / tokens)
    grad_in = r0.reshape(rows, width) + (
        (tokens_in.astype(F32) - norm0[0:1]) * (scale * norm0[1:2] * gain_grad[:1])
        + scale * bias_grad[:1]
    )

    outs = assemble(0, width, states, sum_all(w_sum0, axes))
    in_grad, out_grad, gate_grad = assemble(1, width, states, lax.psum(w_sum1, axes), outs)

    (decay, factor), discrete_back = jax.vjp(
        jax.vmap(discretize), decay_rate, step_log, frequency
    )
    half = states // 2
    dr, di = decay[:, :half], decay[:, half:]
    fr, fi = factor[:, :half], factor[:, half:]
    sr, si = fsum[:, :half], fsum[:, half:]
    tr = dsum[:, :half] - (fr * sr + fi * si)
    ti = dsum[:, half:] - (fr * si - fi * sr)
    modulus = dr * dr + di * di
    decay_grad = jnp.concatenate(
        [(tr * dr - ti * di) / modulus, (tr * di + ti * dr) / modulus], axis=-1
    )
    rate_grad, step_grad, freq_grad = discrete_back((decay_grad, fsum))
    return (
        out.reshape(rows, width),
        grad_in,
        gain_grad,
        bias_grad,
        rate_grad,
        step_grad,
        freq_grad,
        in_grad,
        out_grad,
        skip_grad,
        gate_grad,
    )


def solution(mesh):
    bits = mesh.devices.size.bit_length() - 1
    axes = tuple("b%d" % k for k in range(bits))
    binary = Mesh(mesh.devices.reshape((2,) * bits), axes)
    rows = P(axes, None)
    return jax.shard_map(
        functools.partial(body, axes),
        mesh=binary,
        in_specs=(rows,) + (P(),) * 10 + (rows,),
        out_specs=(rows, rows) + (P(),) * 9,
        check_vma=False,
    )
```

```python
import functools

import jax
import jax.numpy as jnp
from jax import lax
from jax.experimental import pallas as pl
from jax.experimental.pallas import tpu as pltpu
from jax.sharding import Mesh, PartitionSpec as P

LAYERS = 2
EPSILON = 1e-05
SLOT = 4
LANES = 8
VMEM_LIMIT = 60 * 1024 * 1024
GELU_A = 0.7978845608028654
GELU_B = 0.044715
NT = (((1,), (1,)), ((), ()))
TN = (((0,), (0,)), ((), ()))
F32 = jnp.float32
BF16 = jnp.bfloat16


def discretize(decay_rate, step_log, frequency):
    step_size = jnp.exp(step_log)
    real_angle = -decay_rate * step_size
    imag_angle = frequency * step_size
    magnitude = jnp.exp(real_angle)
    cosine = jnp.cos(imag_angle)
    sine = jnp.sin(imag_angle)
    decay_row = jnp.concatenate([magnitude * cosine, magnitude * sine], axis=-1)
    minus_real = jnp.expm1(real_angle) * cosine - 2.0 * jnp.sin(0.5 * imag_angle) ** 2
    minus_imag = magnitude * sine
    modulus = decay_rate * decay_rate + frequency * frequency
    factor_real = (-decay_rate * minus_real + frequency * minus_imag) / modulus
    factor_imag = (-decay_rate * minus_imag - frequency * minus_real) / modulus
    return (decay_row, jnp.concatenate([factor_real, factor_imag], axis=-1))


def gather_all(copies, axes):
    return lax.all_to_all(copies, axes, 0, 0)


def scatter_sum(value, axes):
    count = 2 ** len(axes)
    pieces = value.reshape((count, value.shape[0] // count) + value.shape[1:])
    return jnp.sum(lax.all_to_all(pieces, axes, 0, 0), axis=0)


def gather_rows(value, axes):
    count = 2 ** len(axes)
    copies = jnp.broadcast_to(value, (count,) + value.shape)
    return lax.all_to_all(copies, axes, 0, 0).reshape((count * value.shape[0],) + value.shape[1:])


def sum_all(values, axes):
    halves = [scatter_sum(value, axes[-1:]) for value in values]
    return [gather_rows(half, axes[-1:]) for half in lax.psum(halves, axes[:-1])]


def cols(c):
    return slice(c * 128, (c + 1) * 128)


def chunk_count(ref):
    return ref.shape[-1] // 256


def rows_of(ref, at, chunks):
    half = chunks * 128
    re = [ref[at, c * 128 : (c + 1) * 128] for c in range(chunks)]
    im = [ref[at, half + c * 128 : half + (c + 1) * 128] for c in range(chunks)]
    return re, im


def put_rows(ref, at, re, im):
    chunks = len(re)
    half = chunks * 128
    for c in range(chunks):
        ref[at, c * 128 : (c + 1) * 128] = re[c]
        ref[at, half + c * 128 : half + (c + 1) * 128] = im[c]


def put_copies(ref, re, im):
    ref[0] = jnp.zeros(ref.shape[1:], F32)
    for c in range(len(re)):
        ref[0, c : c + 1] = re[c]
        ref[0, SLOT + c : SLOT + c + 1] = im[c]
    ref[...] = jnp.broadcast_to(ref[0:1], ref.shape)


def wide(rows):
    return [jnp.broadcast_to(v, (LANES, 128)) for v in rows]


def chain(ends_ref, jr_ref, power, carry, down, start_ref=None):
    chunks = len(power[0])
    pr, pi = power
    cr, ci = carry
    order = range(LANES - 1, -1, -1) if down else range(LANES)
    for s in order:
        at = slice(s, s + 1)
        if start_ref is not None:
            put_rows(start_ref, at, cr, ci)
        er, ei = rows_of(ends_ref, at, chunks)
        alive = (jr_ref[at, :] < 0).astype(F32)
        cr, ci = (
            [er[c] + alive * (pr[c] * cr[c] - pi[c] * ci[c]) for c in range(chunks)],
            [ei[c] + alive * (pr[c] * ci[c] + pi[c] * cr[c]) for c in range(chunks)],
        )
    return cr, ci


def carry_in(ends_ref, table_ref, chunks):
    total = jnp.zeros((2 * SLOT, 128), F32)
    for e in range(ends_ref.shape[0]):
        end = ends_ref[e]
        turned = jnp.concatenate([end[SLOT:], end[:SLOT]], axis=0)
        total += table_ref[0, e] * end + table_ref[1, e] * turned
    return (
        [total[c : c + 1] for c in range(chunks)],
        [total[SLOT + c : SLOT + c + 1] for c in range(chunks)],
    )


def scan_tile(src_ref, st_ref, decay, jr_ref, first_step, steps, down, emit=None, unroll=4):
    chunks = chunk_count(src_ref)
    dr, di = wide(decay[0]), wide(decay[1])
    jr = jr_ref[...]
    re, im = rows_of(st_ref, slice(0, LANES), chunks)

    def one(step, re, im):
        at = pl.ds(pl.multiple_of(step * LANES, LANES), LANES)
        br, bi = rows_of(src_ref, at, chunks)
        live = jr != first_step + step
        nr, ni = [], []
        for c in range(chunks):
            xr = jnp.where(live, re[c], 0.0)
            xi = jnp.where(live, im[c], 0.0)
            nr.append(dr[c] * xr - di[c] * xi + br[c])
            ni.append(dr[c] * xi + di[c] * xr + bi[c])
        return nr, ni

    def body(i, carry):
        re, im = list(carry[:chunks]), list(carry[chunks : 2 * chunks])
        extra = carry[2 * chunks :]
        for q in range(unroll):
            n = 2 * (i * unroll + q)
            low_step = steps - 2 - n if down else n
            a, b = (low_step + 1, low_step) if down else (low_step, low_step + 1)
            r1, i1 = one(a, re, im)
            r2, i2 = one(b, r1, i1)
            if emit is not None:
                pair = ((r2, i2), (r1, i1)) if down else ((r1, i1), (r2, i2))
                extra = emit(low_step, pair, extra)
            re, im = r2, i2
        return tuple(re) + tuple(im) + tuple(extra)

    start = tuple(re) + tuple(im)
    if emit is not None:
        start = start + tuple(emit(None, None, None))
    out = lax.fori_loop(0, steps // (2 * unroll), body, start)
    put_rows(st_ref, slice(0, LANES), list(out[:chunks]), list(out[chunks : 2 * chunks]))
    return out[2 * chunks :]


def store_pair(ref, low_step, first, second):
    at = pl.ds(pl.multiple_of(low_step * LANES, 2 * LANES), 2 * LANES)
    re = [jnp.concatenate([p, q], axis=0).astype(BF16) for p, q in zip(first[0], second[0])]
    im = [jnp.concatenate([p, q], axis=0).astype(BF16) for p, q in zip(first[1], second[1])]
    put_rows(ref, at, re, im)


def disc_row(disc_ref, row, chunks, conj=False):
    re, im = rows_of(disc_ref, slice(row, row + 1), chunks)
    return (re, [-v for v in im]) if conj else (re, im)


def column_sum(value):
    rows, width = value.shape
    return jnp.sum(jnp.sum(value.reshape(rows // 8, 8, width), axis=0), axis=0, keepdims=True)


def permute_in(block, order_ref):
    runs, steps, width = block.shape
    span = order_ref.shape[0] // runs
    out = []
    for k in range(steps // span):
        part = block[:, k * span : (k + 1) * span, :].reshape(runs * span, width)
        out.append(jnp.dot(order_ref[...], part, preferred_element_type=F32))
    return out[0] if len(out) == 1 else jnp.concatenate(out, axis=0)


def permute_out(value, order_ref, out_ref):
    rows, width = value.shape
    size = order_ref.shape[0]
    span = size // LANES
    high = value.astype(BF16)
    low = (value - high.astype(F32)).astype(BF16)
    for k in range(rows // size):
        at = slice(k * size, (k + 1) * size)
        back = lax.dot_general(order_ref[...], high[at], TN, preferred_element_type=F32)
        back += lax.dot_general(order_ref[...], low[at], TN, preferred_element_type=F32)
        out_ref[:, k * span : (k + 1) * span, :] = back.reshape(LANES, span, width)


def expm1(value):
    acc = jnp.full_like(value, 1.0 / 479001600.0)
    for n in (39916800.0, 3628800.0, 362880.0, 40320.0, 5040.0, 720.0, 120.0, 24.0, 6.0, 2.0, 1.0):
        acc = acc * value + 1.0 / n
    return jnp.where(value > -1.0, acc * value, jnp.exp(value) - 1.0)


def prep_kernel(
    rows, axes, starts_ref, rate_ref, step_ref, freq_ref,
    disc_ref, table_ref, cut_ref, order_ref,
):
    devices = 2 ** len(axes)
    total = rows * devices
    run = rows // LANES
    half = rate_ref.shape[-1]
    me = 0
    for axis in axes:
        me = 2 * me + lax.axis_index(axis)
    starts = [starts_ref[k] for k in range(starts_ref.shape[0])]

    base = me * rows + run * lax.broadcasted_iota(jnp.int32, (LANES, 128), 0)
    up = jnp.full((LANES, 128), -1, jnp.int32)
    down = up
    for begin in starts + [total]:
        rel = begin - base
        up = jnp.maximum(up, jnp.where((rel >= 0) & (rel < run), rel, -1))
        down = jnp.maximum(down, jnp.where((rel >= 1) & (rel <= run), rel - 1, -1))
    cut_ref[0] = up
    cut_ref[1] = down

    size = order_ref.shape[0]
    span = size // LANES
    to = lax.broadcasted_iota(jnp.int32, (size, size), 0)
    back = lax.broadcasted_iota(jnp.int32, (size, size), 1)
    order_ref[...] = ((to % LANES) * span + to // LANES == back).astype(F32).astype(BF16)

    source = lax.broadcasted_iota(jnp.int32, (devices, half), 0)
    for l in range(LAYERS):
        row = slice(l, l + 1)
        rate, freq = rate_ref[row], freq_ref[row]
        step_size = jnp.exp(step_ref[row])
        real_angle = -rate * step_size
        imag_angle = freq * step_size
        magnitude = jnp.exp(real_angle)
        cosine, sine = jnp.cos(imag_angle), jnp.sin(imag_angle)
        minus_real = expm1(real_angle) * cosine - 2.0 * jnp.sin(0.5 * imag_angle) ** 2
        minus_imag = magnitude * sine
        modulus = rate * rate + freq * freq
        disc_ref[l, 0:1, :half] = magnitude * cosine
        disc_ref[l, 0:1, half:] = minus_imag
        disc_ref[l, 1:2, :half] = (-rate * minus_real + freq * minus_imag) / modulus
        disc_ref[l, 1:2, half:] = (-rate * minus_imag - freq * minus_real) / modulus
        magnitude = jnp.exp(real_angle * float(run))
        disc_ref[l, 2:3, :half] = magnitude * jnp.cos(imag_angle * float(run))
        disc_ref[l, 2:3, half:] = magnitude * jnp.sin(imag_angle * float(run))
        disc_ref[l, 3:8] = jnp.zeros((5, 2 * half), F32)
        for back in range(2):
            going_down = (l + back) % 2 == 1
            if going_down:
                live, count = source > me, source - me - 1
            else:
                live, count = source < me, me - 1 - source
            for begin in starts:
                if going_down:
                    cut = ((begin > (me + 1) * rows).astype(jnp.int32) > 0) & (
                        source * rows >= begin
                    )
                else:
                    cut = ((begin < me * rows).astype(jnp.int32) > 0) & (
                        (source + 1) * rows <= begin
                    )
                live &= ~cut
            count = (jnp.maximum(count, 0) * rows).astype(F32)
            magnitude = jnp.where(live, jnp.exp(real_angle * count), 0.0)
            angle = imag_angle * count
            real = magnitude * jnp.cos(angle)
            imag = magnitude * jnp.sin(angle)
            imag = -imag if back else imag
            at = 2 * l + back
            table_ref[at] = jnp.zeros(table_ref.shape[1:], F32)
            for c in range(half // 128):
                table_ref[at, 0, :, c, :] = real[:, cols(c)]
                table_ref[at, 0, :, SLOT + c, :] = real[:, cols(c)]
                table_ref[at, 1, :, c, :] = -imag[:, cols(c)]
                table_ref[at, 1, :, SLOT + c, :] = imag[:, cols(c)]


def stats_kernel(tok_ref, order_ref, u_ref, stats_ref):
    value = permute_in(tok_ref[...], order_ref)
    u_ref[...] = value.astype(BF16)
    add_stats(stats_ref, value)


def add_stats(stats_ref, value):
    add_rows(stats_ref, column_sum(value), column_sum(value * value))


def add_rows(copies_ref, first, second, spread=True):
    i, nt = pl.program_id(0), pl.num_programs(0)
    chunks = first.shape[1] // 128

    @pl.when(i == 0)
    def _():
        copies_ref[0] = jnp.zeros(copies_ref.shape[1:], F32)

    for c in range(chunks):
        copies_ref[0, c : c + 1] += first[:, cols(c)]
        copies_ref[0, SLOT + c : SLOT + c + 1] += second[:, cols(c)]

    if spread:

        @pl.when(i == nt - 1)
        def _():
            copies_ref[...] = jnp.broadcast_to(copies_ref[0:1], copies_ref.shape)


def summed(ref):
    total = jnp.sum(ref[...], axis=0)
    return tuple(
        jnp.concatenate([total[SLOT * k + c : SLOT * k + c + 1] for c in range(SLOT)], axis=1)
        for k in range(2)
    )


def drive_kernel(layer, down, tokens, *refs):
    (
        stat_ref, u_ref, gain_ref, bias_ref, skip_ref, win_ref, disc_ref, jr_ref,
        b_ref, end_ref, blk_ref, norm_ref,
    ) = refs
    i, nt = pl.program_id(0), pl.num_programs(0)
    steps = u_ref.shape[0] // LANES
    chunks = chunk_count(b_ref)
    half = chunks * 128

    @pl.when(i == 0)
    def _():
        total, squares = summed(stat_ref)
        row = slice(layer, layer + 1)
        mean = total / tokens
        inv = lax.rsqrt(squares / tokens - mean * mean + EPSILON)
        norm_ref[0:1] = mean
        norm_ref[1:2] = inv
        norm_ref[2:3] = inv * gain_ref[row]
        norm_ref[3:4] = bias_ref[row]
        norm_ref[4:5] = skip_ref[row]
        norm_ref[5:8] = jnp.zeros((3, norm_ref.shape[1]), F32)
        blk_ref[...] = jnp.zeros_like(blk_ref)

    u = u_ref[...].astype(F32)
    normed = (u - norm_ref[0:1]) * norm_ref[2:3] + norm_ref[3:4]
    drive = jnp.dot(normed.astype(BF16), win_ref[...], preferred_element_type=F32)
    fr, fi = disc_ref[1:2, :half], disc_ref[1:2, half:]
    re, im = drive[:, :half], drive[:, half:]
    b_ref[:, :half] = re * fr - im * fi
    b_ref[:, half:] = re * fi + im * fr
    tile = nt - 1 - i if down else i
    scan_tile(b_ref, blk_ref, disc_row(disc_ref, 0, chunks), jr_ref, tile * steps, steps, down)

    @pl.when(i == nt - 1)
    def _():
        zero = [jnp.zeros((1, 128), F32)] * chunks
        cr, ci = chain(blk_ref, jr_ref, disc_row(disc_ref, 2, chunks), (zero, zero), down)
        put_copies(end_ref, cr, ci)


def states_of(ends_ref, table_ref, b_ref, blk_ref, disc_ref, jr_ref, low_ref, st_ref, down):
    i, nt = pl.program_id(0), pl.num_programs(0)
    chunks = chunk_count(b_ref)
    steps = b_ref.shape[0] // LANES

    @pl.when(i == 0)
    def _():
        carry = carry_in(ends_ref, table_ref, chunks)
        chain(blk_ref, jr_ref, disc_row(disc_ref, 2, chunks), carry, down, st_ref)

    def emit(low_step, pair, extra):
        if pair is None:
            return ()
        (first, second) = pair
        store_pair(low_ref, low_step, first, second)
        return ()

    tile = nt - 1 - i if down else i
    scan_tile(
        b_ref, st_ref, disc_row(disc_ref, 0, chunks), jr_ref, tile * steps, steps, down, emit
    )


def gelu_parts(mixed):
    square = mixed * mixed
    tanh = jnp.tanh(mixed * (GELU_A + (GELU_A * GELU_B) * square))
    half_up = 0.5 + 0.5 * tanh
    return square, tanh, half_up


def gelu_slope(mixed, square, tanh, half_up):
    return half_up + (mixed * (0.5 - 0.5 * tanh * tanh)) * (
        GELU_A + (3.0 * GELU_A * GELU_B) * square
    )


def sigmoid(value):
    return 0.5 + 0.5 * jnp.tanh(0.5 * value)


def forward_kernel(down, *refs):
    (
        ends_ref, table_ref, b_ref, blk_ref, disc_ref, jr_ref, u_ref, norm_ref, wout_ref, wgate_ref,
        next_ref, low_ref, mixed_ref, gate_ref, stats_ref, st_ref,
    ) = refs
    states_of(ends_ref, table_ref, b_ref, blk_ref, disc_ref, jr_ref, low_ref, st_ref, down)
    u = u_ref[...].astype(F32)
    normed = (u - norm_ref[0:1]) * norm_ref[2:3] + norm_ref[3:4]
    mixed = jnp.dot(low_ref[...], wout_ref[...], preferred_element_type=F32)
    mixed += norm_ref[4:5] * normed
    _, _, half_up = gelu_parts(mixed)
    act = mixed * half_up
    gate = sigmoid(jnp.dot(act.astype(BF16), wgate_ref[...], preferred_element_type=F32))
    after = u + act * gate
    next_ref[...] = after
    mixed_ref[...] = mixed.astype(mixed_ref.dtype)
    gate_ref[...] = gate.astype(gate_ref.dtype)
    add_stats(stats_ref, after)


def accumulate(ref, value):
    @pl.when(pl.program_id(0) == 0)
    def _():
        ref[...] = value

    @pl.when(pl.program_id(0) != 0)
    def _():
        ref[...] += value


def gate_backward(g, mixed, gate, normed, low_ref, wout_ref, wgate_ref, outs, kept=None):
    pg_ref, sg_ref, wsum_ref, ssum_ref = outs
    width = g.shape[1]
    square, tanh, half_up = gelu_parts(mixed) if kept is None else kept
    act = mixed * half_up
    g_gate = g * gate
    logit_grad = (g_gate * act * (1.0 - gate)).astype(BF16)
    accumulate(
        wsum_ref.at[:width],
        lax.dot_general(act.astype(BF16), logit_grad, TN, preferred_element_type=F32),
    )
    act_grad = g_gate + lax.dot_general(
        logit_grad, wgate_ref[...], NT, preferred_element_type=F32
    )
    mixed_grad = act_grad * gelu_slope(mixed, square, tanh, half_up)
    accumulate(ssum_ref, column_sum(mixed_grad * normed))
    proj_grad = mixed_grad.astype(BF16)
    pg_ref[...] = proj_grad
    accumulate(
        wsum_ref.at[width : width + low_ref.shape[1]],
        lax.dot_general(low_ref[...], proj_grad, TN, preferred_element_type=F32),
    )
    sg_ref[...] = lax.dot_general(proj_grad, wout_ref[...], NT, preferred_element_type=F32)


def turn_kernel(down, *refs):
    (
        ends_ref, table_ref, b_ref, blk_ref, disc_ref, jr_ref, jo_ref, u_ref, norm_ref, wout_ref, wgate_ref,
        gout_ref, order_ref,
        out_ref, low_ref, g_ref, pg_ref, sg_ref, wsum_ref, ssum_ref, end_ref, ablk_ref,
        st_ref, w_ref,
    ) = refs
    i, nt = pl.program_id(0), pl.num_programs(0)
    chunks = chunk_count(b_ref)
    half = chunks * 128
    steps = b_ref.shape[0] // LANES
    tile = nt - 1 - i if down else i
    states_of(ends_ref, table_ref, b_ref, blk_ref, disc_ref, jr_ref, low_ref, st_ref, down)
    u = u_ref[...]
    normed = (u - norm_ref[0:1]) * norm_ref[2:3] + norm_ref[3:4]
    mixed = jnp.dot(low_ref[...], wout_ref[...], preferred_element_type=F32)
    mixed += norm_ref[4:5] * normed
    kept = gelu_parts(mixed)
    act = mixed * kept[2]
    gate = sigmoid(jnp.dot(act.astype(BF16), wgate_ref[...], preferred_element_type=F32))
    permute_out(u + act * gate, order_ref, out_ref)
    g = permute_in(gout_ref[...], order_ref)
    g_ref[...] = g.astype(BF16)
    gate_backward(
        g, mixed, gate, normed, low_ref, wout_ref, wgate_ref,
        (pg_ref, sg_ref, wsum_ref, ssum_ref), kept,
    )

    @pl.when(i == 0)
    def _():
        w_ref[:, :half] = jnp.ones((LANES, half), F32)
        w_ref[:, half:] = jnp.zeros((LANES, half), F32)
        ablk_ref[...] = jnp.zeros_like(ablk_ref)

    dr, di = disc_row(disc_ref, 0, chunks, conj=True)
    dr, di = wide(dr), wide(di)
    jo = jo_ref[...]
    unroll = 4

    def body(k, carry):
        wr, wi, ar, ai = (list(carry[n * chunks : (n + 1) * chunks]) for n in range(4))
        for q in range(unroll):
            n = k * unroll + q
            step = steps - 1 - n if down else n
            at = pl.ds(pl.multiple_of(step * LANES, LANES), LANES)
            sr, si = rows_of(sg_ref, at, chunks)
            live = jo != tile * steps + step
            for c in range(chunks):
                ar[c] = ar[c] + (wr[c] * sr[c] - wi[c] * si[c])
                ai[c] = ai[c] + (wr[c] * si[c] + wi[c] * sr[c])
                xr = jnp.where(live, wr[c], 0.0)
                xi = jnp.where(live, wi[c], 0.0)
                wr[c] = xr * dr[c] - xi * di[c]
                wi[c] = xr * di[c] + xi * dr[c]
        return tuple(wr) + tuple(wi) + tuple(ar) + tuple(ai)

    wr, wi = rows_of(w_ref, slice(0, LANES), chunks)
    ar, ai = rows_of(ablk_ref, slice(0, LANES), chunks)
    out = lax.fori_loop(
        0, steps // unroll, body, tuple(wr) + tuple(wi) + tuple(ar) + tuple(ai)
    )
    wr, wi, ar, ai = (list(out[n * chunks : (n + 1) * chunks]) for n in range(4))
    put_rows(w_ref, slice(0, LANES), wr, wi)
    put_rows(ablk_ref, slice(0, LANES), ar, ai)

    @pl.when(i == nt - 1)
    def _():
        zero = [jnp.zeros((1, 128), F32)] * chunks
        power = disc_row(disc_ref, 2, chunks, conj=True)
        cr, ci = chain(ablk_ref, jo_ref, power, (zero, zero), not down)
        put_copies(end_ref, cr, ci)


def adjoint_kernel(down, last, *refs):
    (
        ends_ref, table_ref, sg_ref, ablk_ref, disc_ref, jr_ref, low_ref, u_ref, norm_ref, pg_ref, g_ref,
        win_ref, order_ref, ssum_ref, _,
        res_ref, wsum_ref, nsum_ref, st_ref, dg_ref, ax_ref, isum_ref, pack_ref, sem,
    ) = refs
    width, states_width = win_ref.shape
    i, nt = pl.program_id(0), pl.num_programs(0)
    chunks = chunk_count(sg_ref)
    half = chunks * 128
    steps = sg_ref.shape[0] // LANES
    tile = nt - 1 - i if down else i

    @pl.when(i == 0)
    def _():
        carry = carry_in(ends_ref, table_ref, chunks)
        power = disc_row(disc_ref, 2, chunks, conj=True)
        chain(ablk_ref, jr_ref, power, carry, down, st_ref)
        ax_ref[...] = jnp.zeros_like(ax_ref)

    fr, fi = disc_row(disc_ref, 1, chunks)
    fr, fi = wide(fr), wide(fi)

    def emit(low_step, pair, extra):
        if pair is None:
            re, im = rows_of(ax_ref, slice(0, LANES), chunks)
            return tuple(re) + tuple(im)
        sums_r, sums_i = list(extra[:chunks]), list(extra[chunks:])
        at = pl.ds(pl.multiple_of(low_step * LANES, 2 * LANES), 2 * LANES)
        xr, xi = rows_of(low_ref, at, chunks)
        grads = []
        for which, (ar, ai) in enumerate(pair):
            gr, gi = [], []
            rows = slice(which * LANES, (which + 1) * LANES)
            for c in range(chunks):
                vr, vi = xr[c].astype(F32)[rows], xi[c].astype(F32)[rows]
                sums_r[c] = sums_r[c] + (ar[c] * vr + ai[c] * vi)
                sums_i[c] = sums_i[c] + (ai[c] * vr - ar[c] * vi)
                gr.append(ar[c] * fr[c] + ai[c] * fi[c])
                gi.append(ai[c] * fr[c] - ar[c] * fi[c])
            grads.append((gr, gi))
        store_pair(dg_ref, low_step, grads[0], grads[1])
        return tuple(sums_r) + tuple(sums_i)

    sums = scan_tile(
        sg_ref, st_ref, disc_row(disc_ref, 0, chunks, conj=True), jr_ref, tile * steps, steps,
        down, emit,
    )
    put_rows(ax_ref, slice(0, LANES), list(sums[:chunks]), list(sums[chunks:]))

    u = u_ref[...].astype(F32)
    centered = u - norm_ref[0:1]
    normed = (centered * norm_ref[2:3] + norm_ref[3:4]).astype(BF16)
    drive_grad = dg_ref[...]
    accumulate(
        isum_ref, lax.dot_general(normed, drive_grad, TN, preferred_element_type=F32)
    )
    normed_grad = lax.dot_general(drive_grad, win_ref[...], NT, preferred_element_type=F32)
    normed_grad += norm_ref[4:5] * pg_ref[...].astype(F32)
    add_rows(
        nsum_ref, column_sum(normed_grad), column_sum(normed_grad * centered) * norm_ref[1:2], False
    )
    result = g_ref[...].astype(F32) + norm_ref[2:3] * normed_grad
    if last:
        permute_out(result, order_ref, res_ref)
    else:
        res_ref[...] = result

    @pl.when(i == nt - 1)
    def _():
        left = states_width - width
        pack_ref[:width] = isum_ref[:, :width]
        for p in range(width // left):
            pack_ref[width:, p * left : (p + 1) * left] = isum_ref[p * left : (p + 1) * left, width:]
        count = pack_ref.shape[0]
        copy = pltpu.make_async_copy(
            pack_ref, wsum_ref.at[pl.ds(wsum_ref.shape[0] - count, count)], sem
        )
        copy.start()
        at = 2 * SLOT
        for c in range(width // 128):
            nsum_ref[0, at + c : at + c + 1] = ssum_ref[:, cols(c)]
        at += width // 128
        decays = jnp.sum(ax_ref[...], axis=0, keepdims=True)
        wr, wi = win_ref[:, :half].astype(F32), win_ref[:, half:].astype(F32)
        gr, gi = isum_ref[:, :half], isum_ref[:, half:]
        re = jnp.sum(wr * gr + wi * gi, axis=0, keepdims=True)
        im = jnp.sum(wr * gi - wi * gr, axis=0, keepdims=True)
        gr, gi = disc_ref[1:2, :half], disc_ref[1:2, half:]
        scale = 1.0 / (gr * gr + gi * gi)
        factors = ((re * gr - im * gi) * scale, (re * gi + im * gr) * scale)
        for c in range(2 * chunks):
            nsum_ref[0, at + c : at + c + 1] = decays[:, cols(c)]
        at += 2 * chunks
        for c in range(chunks):
            nsum_ref[0, at + c : at + c + 1] = factors[0][:, cols(c)]
            nsum_ref[0, at + chunks + c : at + chunks + c + 1] = factors[1][:, cols(c)]
        nsum_ref[...] = jnp.broadcast_to(nsum_ref[0:1], nsum_ref.shape)
        copy.wait()


def back_kernel(down, tokens, *refs):
    (
        sums_ref, r_ref, up_ref, up_norm_ref, mixed_ref, gate_ref, low_ref, u_ref, norm_ref, wout_ref,
        wgate_ref, disc_ref, jo_ref,
        g_ref, pg_ref, sg_ref, wsum_ref, ssum_ref, end_ref, ablk_ref, nsum_ref, bsum_ref,
    ) = refs
    i, nt = pl.program_id(0), pl.num_programs(0)
    chunks = chunk_count(sg_ref)
    steps = sg_ref.shape[0] // LANES
    tile = nt - 1 - i if down else i

    @pl.when(i == 0)
    def _():
        nsum_ref[...] = jnp.sum(sums_ref[...], axis=0)
        bsum_ref[0:1], bsum_ref[1:2] = summed(sums_ref)
        ablk_ref[...] = jnp.zeros_like(ablk_ref)

    scale = up_norm_ref[2:3] * (-1.0 / tokens)
    standard = (up_ref[...] - up_norm_ref[0:1]) * (scale * up_norm_ref[1:2] * bsum_ref[1:2])
    g = r_ref[...] + (standard + scale * bsum_ref[0:1])
    g_ref[...] = g
    u = u_ref[...].astype(F32)
    normed = (u - norm_ref[0:1]) * norm_ref[2:3] + norm_ref[3:4]
    gate_backward(
        g, mixed_ref[...].astype(F32), gate_ref[...].astype(F32), normed, low_ref, wout_ref,
        wgate_ref, (pg_ref, sg_ref, wsum_ref, ssum_ref),
    )
    decay = disc_row(disc_ref, 0, chunks, conj=True)
    scan_tile(sg_ref, ablk_ref, decay, jo_ref, tile * steps, steps, down)

    @pl.when(i == nt - 1)
    def _():
        zero = [jnp.zeros((1, 128), F32)] * chunks
        power = disc_row(disc_ref, 2, chunks, conj=True)
        cr, ci = chain(ablk_ref, jo_ref, power, (zero, zero), down)
        put_copies(end_ref, cr, ci)


def parted(sums, width, states):
    left = states - width
    packed = sums[2 * width + states :]
    right = jnp.concatenate(
        [packed[:, p * left : (p + 1) * left] for p in range(width // left)], axis=0
    )
    first = sums[width + states : 2 * width + states]
    return jnp.concatenate([first, right], axis=1), sums[width : width + states], sums[:width]


def whole(array):
    shape = array.shape
    return pl.BlockSpec(shape, lambda i: (0,) * len(shape))


def tile_spec(rows, width, nt, down):
    if down:
        return pl.BlockSpec((rows, width), lambda i: (nt - 1 - i, 0))
    return pl.BlockSpec((rows, width), lambda i: (i, 0))


def run_spec(steps, width, nt, down):
    if down:
        return pl.BlockSpec((LANES, steps, width), lambda i: (0, nt - 1 - i, 0))
    return pl.BlockSpec((LANES, steps, width), lambda i: (0, i, 0))


def call(kernel, nt, args, outs, scratch, macs, name, alias=None):
    arrays = [a for a, _ in args]
    sizes = sum(a.size * a.dtype.itemsize for a in arrays + [a for a, _ in outs])
    return pl.pallas_call(
        kernel,
        grid=(nt,),
        in_specs=[whole(a) if s is None else s for a, s in args],
        out_specs=[whole(a) if s is None else s for a, s in outs],
        out_shape=[a for a, _ in outs],
        scratch_shapes=scratch,
        compiler_params=pltpu.CompilerParams(
            vmem_limit_bytes=VMEM_LIMIT, dimension_semantics=("arbitrary",)
        ),
        cost_estimate=pl.CostEstimate(flops=2 * macs, bytes_accessed=sizes, transcendentals=0),
        input_output_aliases=alias or {},
        name=name,
    )(*arrays)


def shape(*dims, dtype=F32):
    return jax.ShapeDtypeStruct(dims, dtype)


def body(
    axes,
    tokens_in,
    seq_starts,
    norm_gain,
    norm_bias,
    decay_rate,
    step_log,
    frequency,
    in_proj,
    out_proj,
    skip_gain,
    gate_proj,
    grad_out,
):
    rows, width = tokens_in.shape
    states = in_proj.shape[-1]
    devices = 2 ** len(axes)
    tokens = float(rows * devices)
    run = rows // LANES
    steps = min(64, run)
    tile = steps * LANES
    nt = rows // tile
    span = min(32, steps)
    discs, tables, cuts, order = pl.pallas_call(
        functools.partial(prep_kernel, rows, axes),
        in_specs=[pl.BlockSpec(memory_space=pltpu.SMEM)]
        + [pl.BlockSpec(memory_space=pltpu.VMEM)] * 3,
        out_specs=[pl.BlockSpec(memory_space=pltpu.VMEM)] * 4,
        out_shape=[
            shape(LAYERS, 8, states), shape(2 * LAYERS, 2, devices, 2 * SLOT, 128),
            shape(2, LANES, 128, dtype=jnp.int32), shape(span * LANES, span * LANES, dtype=BF16),
        ],
        compiler_params=pltpu.CompilerParams(vmem_limit_bytes=VMEM_LIMIT),
        name="prep",
    )(seq_starts, decay_rate, step_log, frequency)

    def tiles(array, down):
        return (array, tile_spec(tile, array.shape[-1], nt, down))

    def runs(array, down):
        return (array, run_spec(steps, array.shape[-1], nt, down))

    def full(array):
        return (array, None)

    def of(array, l):
        size = array.shape[1:]
        return (array, pl.BlockSpec((None,) + size, lambda i: (l,) + (0,) * len(size)))

    def first(array):
        return (array, pl.BlockSpec((width + states, width), lambda i: (0, 0)))

    def anywhere(array):
        return (array, pl.BlockSpec(memory_space=pl.ANY))

    tokens_run = tokens_in.reshape(LANES, run, width)
    grad_run = grad_out.reshape(LANES, run, width)
    state_scratch = pltpu.VMEM((LANES, states), F32)
    small = 2 * SLOT + (width + 2 * states) // 128
    cost = rows * width * states
    sums = 2 * states + width

    u0, stats = call(
        stats_kernel, nt, [runs(tokens_run, 0), full(order)],
        [tiles(shape(rows, width, dtype=BF16), 0), full(shape(devices, 2 * SLOT, 128))],
        [], cost // 2, "stats",
    )

    def drive(l, stream, stats):
        down = l % 2
        return call(
            functools.partial(drive_kernel, l, bool(down), tokens), nt,
            [full(gather_all(stats, axes)), tiles(stream, down), full(norm_gain), full(norm_bias), full(skip_gain), of(in_proj, l), of(discs, l),
               of(cuts, down)],
            [tiles(shape(rows, states), down), full(shape(devices, 2 * SLOT, 128)),
             full(shape(LANES, states)), full(shape(8, width))],
            [], 4 * cost, f"drive_{l}",
        )

    b0, end0, blk0, norm0 = drive(0, u0, stats)
    u1, low0, mixed0, gate0, stats = call(
        functools.partial(forward_kernel, False), nt,
        [full(gather_all(end0, axes)), of(tables, 2 * 0 + 0), tiles(b0, 0), full(blk0), of(discs, 0), of(cuts, 0),
           tiles(u0, 0), full(norm0), of(out_proj, 0), of(gate_proj, 0)],
        [tiles(shape(rows, width), 0), tiles(shape(rows, states, dtype=BF16), 0),
         tiles(shape(rows, width, dtype=BF16), 0), tiles(shape(rows, width, dtype=BF16), 0),
         full(shape(devices, 2 * SLOT, 128))],
        [state_scratch], 6 * cost, "forward_0",
    )

    b1, end1, blk1, norm1 = drive(1, u1, stats)
    (
        out, low1, g1, pg1, sg1, w_sum1, skip_sum1, aend1, ablk1
    ) = call(
        functools.partial(turn_kernel, True), nt,
        [full(gather_all(end1, axes)), of(tables, 2 * 1 + 0), tiles(b1, 1), full(blk1), of(discs, 1), of(cuts, 1),
           of(cuts, 0), tiles(u1, 1), full(norm1), of(out_proj, 1), of(gate_proj, 1),
           runs(grad_run, 1), full(order)],
        [runs(shape(LANES, run, width), 1), tiles(shape(rows, states, dtype=BF16), 1),
         tiles(shape(rows, width, dtype=BF16), 1), tiles(shape(rows, width, dtype=BF16), 1),
         tiles(shape(rows, states), 1), first(shape(sums, width)), full(shape(1, width)),
         full(shape(devices, 2 * SLOT, 128)), full(shape(LANES, states))],
        [state_scratch, state_scratch], 16 * cost, "turn_1",
    )

    def adjoint(l, sg, ablk, aend, low, stream, norm, pg, g, skip_sum, w_sum):
        down = 1 - l % 2
        last = l == 0
        args = [
            full(gather_all(aend, axes)), of(tables, 2 * l + 1), tiles(sg, down), full(ablk),
            of(discs, l), of(cuts, down), tiles(low, down), tiles(stream, down), full(norm),
            tiles(pg, down), tiles(g, down), of(in_proj, l), full(order), full(skip_sum),
            anywhere(w_sum),
        ]
        return call(
            functools.partial(adjoint_kernel, bool(down), last), nt, args,
            [runs(shape(LANES, run, width), down) if last else tiles(shape(rows, width), down),
             anywhere(shape(sums, width)), full(shape(devices, small, 128))],
            [state_scratch, pltpu.VMEM((tile, states), BF16), state_scratch,
             pltpu.VMEM((width, states), F32), pltpu.VMEM((states, width), F32),
             pltpu.SemaphoreType.DMA],
            8 * cost, f"adjoint_{l}", {len(args) - 1: 1},
        )

    r1, w_sum1, norm_sum1 = adjoint(
        1, sg1, ablk1, aend1, low1, u1, norm1, pg1, g1,
        skip_sum1, w_sum1,
    )
    (
        g0, pg0, sg0, w_sum0, skip_sum0, aend0, ablk0, small1, _
    ) = call(
        functools.partial(back_kernel, True, tokens), nt,
        [full(gather_all(norm_sum1, axes)), tiles(r1, 1), tiles(u1, 1), full(norm1), tiles(mixed0, 1), tiles(gate0, 1),
           tiles(low0, 1), tiles(u0, 1), full(norm0), of(out_proj, 0), of(gate_proj, 0),
           of(discs, 0), of(cuts, 1)],
        [tiles(shape(rows, width), 1), tiles(shape(rows, width, dtype=BF16), 1),
         tiles(shape(rows, states), 1), first(shape(sums, width)),
         full(shape(1, width)), full(shape(devices, 2 * SLOT, 128)), full(shape(LANES, states)),
         full(shape(small, 128)), full(shape(2, width))],
        [], 12 * cost, "back_0",
    )
    r0, w_sum0, norm_sum0 = adjoint(
        0, sg0, ablk0, aend0, low0, u0, norm0, pg0, g0, skip_sum0, w_sum0
    )
    small0 = jnp.sum(gather_all(norm_sum0, axes), axis=0)
    pair = jnp.stack([small0.reshape(-1), small1.reshape(-1)])
    bias_grad, gain_grad, skip_grad = (pair[:, k * width : (k + 1) * width] for k in range(3))
    dsum = pair[:, 3 * width : 3 * width + states]
    fsum = pair[:, 3 * width + states :]

    scale = norm0[2:3] * (-1.0 / tokens)
    grad_in = r0.reshape(rows, width) + (
        (tokens_in.astype(F32) - norm0[0:1]) * (scale * norm0[1:2] * gain_grad[:1])
        + scale * bias_grad[:1]
    )

    w_sum1, w_sum0 = sum_all([w_sum1, w_sum0], axes)
    in_grad, out_grad, gate_grad = (
        jnp.stack(pair) for pair in zip(parted(w_sum0, width, states), parted(w_sum1, width, states))
    )

    (decay, factor), discrete_back = jax.vjp(
        jax.vmap(discretize), decay_rate, step_log, frequency
    )
    half = states // 2
    dr, di = decay[:, :half], decay[:, half:]
    fr, fi = factor[:, :half], factor[:, half:]
    sr, si = fsum[:, :half], fsum[:, half:]
    tr = dsum[:, :half] - (fr * sr + fi * si)
    ti = dsum[:, half:] - (fr * si - fi * sr)
    modulus = dr * dr + di * di
    decay_grad = jnp.concatenate(
        [(tr * dr - ti * di) / modulus, (tr * di + ti * dr) / modulus], axis=-1
    )
    rate_grad, step_grad, freq_grad = discrete_back((decay_grad, fsum))
    return (
        out.reshape(rows, width),
        grad_in,
        gain_grad,
        bias_grad,
        rate_grad,
        step_grad,
        freq_grad,
        in_grad,
        out_grad,
        skip_grad,
        gate_grad,
    )


def solution(mesh):
    bits = mesh.devices.size.bit_length() - 1
    axes = tuple("b%d" % k for k in range(bits))
    binary = Mesh(mesh.devices.reshape((2,) * bits), axes)
    rows = P(axes, None)
    return jax.shard_map(
        functools.partial(body, axes),
        mesh=binary,
        in_specs=(rows,) + (P(),) * 10 + (rows,),
        out_specs=(rows, rows) + (P(),) * 9,
        check_vma=False,
    )
```

```python
import functools

import jax
import jax.numpy as jnp
from jax import lax
from jax.experimental import pallas as pl
from jax.experimental.pallas import tpu as pltpu
from jax.sharding import Mesh, PartitionSpec as P

LAYERS = 2
EPSILON = 1e-05
SLOT = 4
LANES = 8
VMEM_LIMIT = 60 * 1024 * 1024
GELU_A = 0.7978845608028654
GELU_B = 0.044715
NT = (((1,), (1,)), ((), ()))
TN = (((0,), (0,)), ((), ()))
F32 = jnp.float32
BF16 = jnp.bfloat16


def discretize(decay_rate, step_log, frequency):
    step_size = jnp.exp(step_log)
    real_angle = -decay_rate * step_size
    imag_angle = frequency * step_size
    magnitude = jnp.exp(real_angle)
    cosine = jnp.cos(imag_angle)
    sine = jnp.sin(imag_angle)
    decay_row = jnp.concatenate([magnitude * cosine, magnitude * sine], axis=-1)
    minus_real = jnp.expm1(real_angle) * cosine - 2.0 * jnp.sin(0.5 * imag_angle) ** 2
    minus_imag = magnitude * sine
    modulus = decay_rate * decay_rate + frequency * frequency
    factor_real = (-decay_rate * minus_real + frequency * minus_imag) / modulus
    factor_imag = (-decay_rate * minus_imag - frequency * minus_real) / modulus
    return (decay_row, jnp.concatenate([factor_real, factor_imag], axis=-1))


def gather_all(copies, axes):
    return lax.all_to_all(copies, axes, 0, 0)


def scatter_sum(value, axes):
    count = 2 ** len(axes)
    pieces = value.reshape((count, value.shape[0] // count) + value.shape[1:])
    return jnp.sum(lax.all_to_all(pieces, axes, 0, 0), axis=0)


def gather_rows(value, axes):
    count = 2 ** len(axes)
    copies = jnp.broadcast_to(value, (count,) + value.shape)
    return lax.all_to_all(copies, axes, 0, 0).reshape((count * value.shape[0],) + value.shape[1:])


def phases(axes):
    left, out = list(axes), [(axes[-1],)]
    left = left[:-1]
    while left:
        out.append(tuple(left[-2:]))
        left = left[:-2]
    return out


def sum_all(value, axes):
    for part in phases(axes):
        value = scatter_sum(value, part)
    for part in reversed(phases(axes)):
        value = gather_rows(value, part)
    return value


def cols(c):
    return slice(c * 128, (c + 1) * 128)


def chunk_count(ref):
    return ref.shape[-1] // 256


def rows_of(ref, at, chunks):
    half = chunks * 128
    re = [ref[at, c * 128 : (c + 1) * 128] for c in range(chunks)]
    im = [ref[at, half + c * 128 : half + (c + 1) * 128] for c in range(chunks)]
    return re, im


def put_rows(ref, at, re, im):
    chunks = len(re)
    half = chunks * 128
    for c in range(chunks):
        ref[at, c * 128 : (c + 1) * 128] = re[c]
        ref[at, half + c * 128 : half + (c + 1) * 128] = im[c]


def put_copies(ref, re, im):
    ref[0] = jnp.zeros(ref.shape[1:], F32)
    for c in range(len(re)):
        ref[0, c : c + 1] = re[c]
        ref[0, SLOT + c : SLOT + c + 1] = im[c]
    ref[...] = jnp.broadcast_to(ref[0:1], ref.shape)


def wide(rows):
    return [jnp.broadcast_to(v, (LANES, 128)) for v in rows]


def chain(ends_ref, jr_ref, power, carry, down, start_ref=None):
    chunks = len(power[0])
    pr, pi = power
    cr, ci = carry
    order = range(LANES - 1, -1, -1) if down else range(LANES)
    for s in order:
        at = slice(s, s + 1)
        if start_ref is not None:
            put_rows(start_ref, at, cr, ci)
        er, ei = rows_of(ends_ref, at, chunks)
        alive = (jr_ref[at, :] < 0).astype(F32)
        cr, ci = (
            [er[c] + alive * (pr[c] * cr[c] - pi[c] * ci[c]) for c in range(chunks)],
            [ei[c] + alive * (pr[c] * ci[c] + pi[c] * cr[c]) for c in range(chunks)],
        )
    return cr, ci


def carry_in(ends_ref, table_ref, chunks):
    total = jnp.zeros((2 * SLOT, 128), F32)
    for e in range(ends_ref.shape[0]):
        end = ends_ref[e]
        turned = jnp.concatenate([end[SLOT:], end[:SLOT]], axis=0)
        total += table_ref[0, e] * end + table_ref[1, e] * turned
    return (
        [total[c : c + 1] for c in range(chunks)],
        [total[SLOT + c : SLOT + c + 1] for c in range(chunks)],
    )


def scan_tile(src_ref, st_ref, decay, jr_ref, first_step, steps, down, emit=None, unroll=4):
    chunks = chunk_count(src_ref)
    dr, di = wide(decay[0]), wide(decay[1])
    jr = jr_ref[...]
    re, im = rows_of(st_ref, slice(0, LANES), chunks)

    def one(step, re, im):
        at = pl.ds(pl.multiple_of(step * LANES, LANES), LANES)
        br, bi = rows_of(src_ref, at, chunks)
        live = jr != first_step + step
        nr, ni = [], []
        for c in range(chunks):
            xr = jnp.where(live, re[c], 0.0)
            xi = jnp.where(live, im[c], 0.0)
            nr.append(dr[c] * xr - di[c] * xi + br[c])
            ni.append(dr[c] * xi + di[c] * xr + bi[c])
        return nr, ni

    def body(i, carry):
        re, im = list(carry[:chunks]), list(carry[chunks : 2 * chunks])
        extra = carry[2 * chunks :]
        for q in range(unroll):
            n = 2 * (i * unroll + q)
            low_step = steps - 2 - n if down else n
            a, b = (low_step + 1, low_step) if down else (low_step, low_step + 1)
            r1, i1 = one(a, re, im)
            r2, i2 = one(b, r1, i1)
            if emit is not None:
                pair = ((r2, i2), (r1, i1)) if down else ((r1, i1), (r2, i2))
                extra = emit(low_step, pair, extra)
            re, im = r2, i2
        return tuple(re) + tuple(im) + tuple(extra)

    start = tuple(re) + tuple(im)
    if emit is not None:
        start = start + tuple(emit(None, None, None))
    out = lax.fori_loop(0, steps // (2 * unroll), body, start)
    put_rows(st_ref, slice(0, LANES), list(out[:chunks]), list(out[chunks : 2 * chunks]))
    return out[2 * chunks :]


def store_pair(ref, low_step, first, second):
    at = pl.ds(pl.multiple_of(low_step * LANES, 2 * LANES), 2 * LANES)
    re = [jnp.concatenate([p, q], axis=0).astype(BF16) for p, q in zip(first[0], second[0])]
    im = [jnp.concatenate([p, q], axis=0).astype(BF16) for p, q in zip(first[1], second[1])]
    put_rows(ref, at, re, im)


def disc_row(disc_ref, row, chunks, conj=False):
    re, im = rows_of(disc_ref, slice(row, row + 1), chunks)
    return (re, [-v for v in im]) if conj else (re, im)


def column_sum(value):
    rows, width = value.shape
    return jnp.sum(jnp.sum(value.reshape(rows // 8, 8, width), axis=0), axis=0, keepdims=True)


def permute_in(block, order_ref):
    runs, steps, width = block.shape
    span = order_ref.shape[0] // runs
    out = []
    for k in range(steps // span):
        part = block[:, k * span : (k + 1) * span, :].reshape(runs * span, width)
        out.append(jnp.dot(order_ref[...], part, preferred_element_type=F32))
    return out[0] if len(out) == 1 else jnp.concatenate(out, axis=0)


def permute_out(value, order_ref, out_ref):
    rows, width = value.shape
    size = order_ref.shape[0]
    span = size // LANES
    high = value.astype(BF16)
    low = (value - high.astype(F32)).astype(BF16)
    for k in range(rows // size):
        at = slice(k * size, (k + 1) * size)
        back = lax.dot_general(order_ref[...], high[at], TN, preferred_element_type=F32)
        back += lax.dot_general(order_ref[...], low[at], TN, preferred_element_type=F32)
        out_ref[:, k * span : (k + 1) * span, :] = back.reshape(LANES, span, width)


def expm1(value):
    acc = jnp.full_like(value, 1.0 / 479001600.0)
    for n in (39916800.0, 3628800.0, 362880.0, 40320.0, 5040.0, 720.0, 120.0, 24.0, 6.0, 2.0, 1.0):
        acc = acc * value + 1.0 / n
    return jnp.where(value > -1.0, acc * value, jnp.exp(value) - 1.0)


def prep_kernel(
    rows, axes, starts_ref, rate_ref, step_ref, freq_ref,
    disc_ref, table_ref, cut_ref, order_ref,
):
    devices = 2 ** len(axes)
    total = rows * devices
    run = rows // LANES
    half = rate_ref.shape[-1]
    me = 0
    for axis in axes:
        me = 2 * me + lax.axis_index(axis)
    starts = [starts_ref[k] for k in range(starts_ref.shape[0])]

    base = me * rows + run * lax.broadcasted_iota(jnp.int32, (LANES, 128), 0)
    up = jnp.full((LANES, 128), -1, jnp.int32)
    down = up
    for begin in starts + [total]:
        rel = begin - base
        up = jnp.maximum(up, jnp.where((rel >= 0) & (rel < run), rel, -1))
        down = jnp.maximum(down, jnp.where((rel >= 1) & (rel <= run), rel - 1, -1))
    cut_ref[0] = up
    cut_ref[1] = down

    size = order_ref.shape[0]
    span = size // LANES
    to = lax.broadcasted_iota(jnp.int32, (size, size), 0)
    back = lax.broadcasted_iota(jnp.int32, (size, size), 1)
    order_ref[...] = ((to % LANES) * span + to // LANES == back).astype(F32).astype(BF16)

    source = lax.broadcasted_iota(jnp.int32, (devices, half), 0)
    for l in range(LAYERS):
        row = slice(l, l + 1)
        rate, freq = rate_ref[row], freq_ref[row]
        step_size = jnp.exp(step_ref[row])
        real_angle = -rate * step_size
        imag_angle = freq * step_size
        magnitude = jnp.exp(real_angle)
        cosine, sine = jnp.cos(imag_angle), jnp.sin(imag_angle)
        minus_real = expm1(real_angle) * cosine - 2.0 * jnp.sin(0.5 * imag_angle) ** 2
        minus_imag = magnitude * sine
        modulus = rate * rate + freq * freq
        disc_ref[l, 0:1, :half] = magnitude * cosine
        disc_ref[l, 0:1, half:] = minus_imag
        disc_ref[l, 1:2, :half] = (-rate * minus_real + freq * minus_imag) / modulus
        disc_ref[l, 1:2, half:] = (-rate * minus_imag - freq * minus_real) / modulus
        magnitude = jnp.exp(real_angle * float(run))
        disc_ref[l, 2:3, :half] = magnitude * jnp.cos(imag_angle * float(run))
        disc_ref[l, 2:3, half:] = magnitude * jnp.sin(imag_angle * float(run))
        disc_ref[l, 3:8] = jnp.zeros((5, 2 * half), F32)
        for back in range(2):
            going_down = (l + back) % 2 == 1
            if going_down:
                live, count = source > me, source - me - 1
            else:
                live, count = source < me, me - 1 - source
            for begin in starts:
                if going_down:
                    cut = ((begin > (me + 1) * rows).astype(jnp.int32) > 0) & (
                        source * rows >= begin
                    )
                else:
                    cut = ((begin < me * rows).astype(jnp.int32) > 0) & (
                        (source + 1) * rows <= begin
                    )
                live &= ~cut
            count = (jnp.maximum(count, 0) * rows).astype(F32)
            magnitude = jnp.where(live, jnp.exp(real_angle * count), 0.0)
            angle = imag_angle * count
            real = magnitude * jnp.cos(angle)
            imag = magnitude * jnp.sin(angle)
            imag = -imag if back else imag
            at = 2 * l + back
            table_ref[at] = jnp.zeros(table_ref.shape[1:], F32)
            for c in range(half // 128):
                table_ref[at, 0, :, c, :] = real[:, cols(c)]
                table_ref[at, 0, :, SLOT + c, :] = real[:, cols(c)]
                table_ref[at, 1, :, c, :] = -imag[:, cols(c)]
                table_ref[at, 1, :, SLOT + c, :] = imag[:, cols(c)]


def stats_kernel(tok_ref, order_ref, u_ref, stats_ref):
    value = permute_in(tok_ref[...], order_ref)
    u_ref[...] = value.astype(BF16)
    add_stats(stats_ref, value)


def add_stats(stats_ref, value):
    add_rows(stats_ref, column_sum(value), column_sum(value * value))


def add_rows(copies_ref, first, second, spread=True):
    i, nt = pl.program_id(0), pl.num_programs(0)
    chunks = first.shape[1] // 128

    @pl.when(i == 0)
    def _():
        copies_ref[0] = jnp.zeros(copies_ref.shape[1:], F32)

    for c in range(chunks):
        copies_ref[0, c : c + 1] += first[:, cols(c)]
        copies_ref[0, SLOT + c : SLOT + c + 1] += second[:, cols(c)]

    if spread:

        @pl.when(i == nt - 1)
        def _():
            copies_ref[...] = jnp.broadcast_to(copies_ref[0:1], copies_ref.shape)


def summed(ref):
    total = jnp.sum(ref[...], axis=0)
    return tuple(
        jnp.concatenate([total[SLOT * k + c : SLOT * k + c + 1] for c in range(SLOT)], axis=1)
        for k in range(2)
    )


def drive_kernel(layer, down, tokens, *refs):
    (
        stat_ref, u_ref, gain_ref, bias_ref, skip_ref, win_ref, disc_ref, jr_ref,
        b_ref, end_ref, blk_ref, norm_ref,
    ) = refs
    i, nt = pl.program_id(0), pl.num_programs(0)
    steps = u_ref.shape[0] // LANES
    chunks = chunk_count(b_ref)
    half = chunks * 128

    @pl.when(i == 0)
    def _():
        total, squares = summed(stat_ref)
        row = slice(layer, layer + 1)
        mean = total / tokens
        inv = lax.rsqrt(squares / tokens - mean * mean + EPSILON)
        norm_ref[0:1] = mean
        norm_ref[1:2] = inv
        norm_ref[2:3] = inv * gain_ref[row]
        norm_ref[3:4] = bias_ref[row]
        norm_ref[4:5] = skip_ref[row]
        norm_ref[5:8] = jnp.zeros((3, norm_ref.shape[1]), F32)
        blk_ref[...] = jnp.zeros_like(blk_ref)

    u = u_ref[...].astype(F32)
    normed = (u - norm_ref[0:1]) * norm_ref[2:3] + norm_ref[3:4]
    drive = jnp.dot(normed.astype(BF16), win_ref[...], preferred_element_type=F32)
    fr, fi = disc_ref[1:2, :half], disc_ref[1:2, half:]
    re, im = drive[:, :half], drive[:, half:]
    b_ref[:, :half] = re * fr - im * fi
    b_ref[:, half:] = re * fi + im * fr
    tile = nt - 1 - i if down else i
    scan_tile(b_ref, blk_ref, disc_row(disc_ref, 0, chunks), jr_ref, tile * steps, steps, down)

    @pl.when(i == nt - 1)
    def _():
        zero = [jnp.zeros((1, 128), F32)] * chunks
        cr, ci = chain(blk_ref, jr_ref, disc_row(disc_ref, 2, chunks), (zero, zero), down)
        put_copies(end_ref, cr, ci)


def states_of(ends_ref, table_ref, b_ref, blk_ref, disc_ref, jr_ref, low_ref, st_ref, down):
    i, nt = pl.program_id(0), pl.num_programs(0)
    chunks = chunk_count(b_ref)
    steps = b_ref.shape[0] // LANES

    @pl.when(i == 0)
    def _():
        carry = carry_in(ends_ref, table_ref, chunks)
        chain(blk_ref, jr_ref, disc_row(disc_ref, 2, chunks), carry, down, st_ref)

    def emit(low_step, pair, extra):
        if pair is None:
            return ()
        (first, second) = pair
        store_pair(low_ref, low_step, first, second)
        return ()

    tile = nt - 1 - i if down else i
    scan_tile(
        b_ref, st_ref, disc_row(disc_ref, 0, chunks), jr_ref, tile * steps, steps, down, emit
    )


def gelu_parts(mixed):
    square = mixed * mixed
    tanh = jnp.tanh(mixed * (GELU_A + (GELU_A * GELU_B) * square))
    half_up = 0.5 + 0.5 * tanh
    return square, tanh, half_up


def gelu_slope(mixed, square, tanh, half_up):
    return half_up + (mixed * (0.5 - 0.5 * tanh * tanh)) * (
        GELU_A + (3.0 * GELU_A * GELU_B) * square
    )


def sigmoid(value):
    return 0.5 + 0.5 * jnp.tanh(0.5 * value)


def forward_kernel(down, *refs):
    (
        ends_ref, table_ref, b_ref, blk_ref, disc_ref, jr_ref, u_ref, norm_ref, wout_ref, wgate_ref,
        next_ref, low_ref, mixed_ref, gate_ref, stats_ref, st_ref,
    ) = refs
    states_of(ends_ref, table_ref, b_ref, blk_ref, disc_ref, jr_ref, low_ref, st_ref, down)
    u = u_ref[...].astype(F32)
    normed = (u - norm_ref[0:1]) * norm_ref[2:3] + norm_ref[3:4]
    mixed = jnp.dot(low_ref[...], wout_ref[...], preferred_element_type=F32)
    mixed += norm_ref[4:5] * normed
    _, _, half_up = gelu_parts(mixed)
    act = mixed * half_up
    gate = sigmoid(jnp.dot(act.astype(BF16), wgate_ref[...], preferred_element_type=F32))
    after = u + act * gate
    next_ref[...] = after
    mixed_ref[...] = mixed.astype(mixed_ref.dtype)
    gate_ref[...] = gate.astype(gate_ref.dtype)
    add_stats(stats_ref, after)


def accumulate(ref, value):
    @pl.when(pl.program_id(0) == 0)
    def _():
        ref[...] = value

    @pl.when(pl.program_id(0) != 0)
    def _():
        ref[...] += value


def gate_backward(g, mixed, gate, normed, low_ref, wout_ref, wgate_ref, outs, kept=None):
    pg_ref, sg_ref, wsum_ref, ssum_ref = outs
    width = g.shape[1]
    square, tanh, half_up = gelu_parts(mixed) if kept is None else kept
    act = mixed * half_up
    g_gate = g * gate
    logit_grad = (g_gate * act * (1.0 - gate)).astype(BF16)
    accumulate(
        wsum_ref.at[:width],
        lax.dot_general(act.astype(BF16), logit_grad, TN, preferred_element_type=F32),
    )
    act_grad = g_gate + lax.dot_general(
        logit_grad, wgate_ref[...], NT, preferred_element_type=F32
    )
    mixed_grad = act_grad * gelu_slope(mixed, square, tanh, half_up)
    accumulate(ssum_ref, column_sum(mixed_grad * normed))
    proj_grad = mixed_grad.astype(BF16)
    pg_ref[...] = proj_grad
    accumulate(
        wsum_ref.at[width : width + low_ref.shape[1]],
        lax.dot_general(low_ref[...], proj_grad, TN, preferred_element_type=F32),
    )
    sg_ref[...] = lax.dot_general(proj_grad, wout_ref[...], NT, preferred_element_type=F32)


def turn_kernel(down, *refs):
    (
        ends_ref, table_ref, b_ref, blk_ref, disc_ref, jr_ref, jo_ref, u_ref, norm_ref, wout_ref, wgate_ref,
        gout_ref, order_ref,
        out_ref, low_ref, g_ref, pg_ref, sg_ref, wsum_ref, ssum_ref, end_ref, ablk_ref,
        st_ref, w_ref,
    ) = refs
    i, nt = pl.program_id(0), pl.num_programs(0)
    chunks = chunk_count(b_ref)
    half = chunks * 128
    steps = b_ref.shape[0] // LANES
    tile = nt - 1 - i if down else i
    states_of(ends_ref, table_ref, b_ref, blk_ref, disc_ref, jr_ref, low_ref, st_ref, down)
    u = u_ref[...]
    normed = (u - norm_ref[0:1]) * norm_ref[2:3] + norm_ref[3:4]
    mixed = jnp.dot(low_ref[...], wout_ref[...], preferred_element_type=F32)
    mixed += norm_ref[4:5] * normed
    kept = gelu_parts(mixed)
    act = mixed * kept[2]
    gate = sigmoid(jnp.dot(act.astype(BF16), wgate_ref[...], preferred_element_type=F32))
    permute_out(u + act * gate, order_ref, out_ref)
    g = permute_in(gout_ref[...], order_ref)
    g_ref[...] = g.astype(BF16)
    gate_backward(
        g, mixed, gate, normed, low_ref, wout_ref, wgate_ref,
        (pg_ref, sg_ref, wsum_ref, ssum_ref), kept,
    )

    @pl.when(i == 0)
    def _():
        w_ref[:, :half] = jnp.ones((LANES, half), F32)
        w_ref[:, half:] = jnp.zeros((LANES, half), F32)
        ablk_ref[...] = jnp.zeros_like(ablk_ref)

    dr, di = disc_row(disc_ref, 0, chunks, conj=True)
    dr, di = wide(dr), wide(di)
    jo = jo_ref[...]
    unroll = 4

    def body(k, carry):
        wr, wi, ar, ai = (list(carry[n * chunks : (n + 1) * chunks]) for n in range(4))
        for q in range(unroll):
            n = k * unroll + q
            step = steps - 1 - n if down else n
            at = pl.ds(pl.multiple_of(step * LANES, LANES), LANES)
            sr, si = rows_of(sg_ref, at, chunks)
            live = jo != tile * steps + step
            for c in range(chunks):
                ar[c] = ar[c] + (wr[c] * sr[c] - wi[c] * si[c])
                ai[c] = ai[c] + (wr[c] * si[c] + wi[c] * sr[c])
                xr = jnp.where(live, wr[c], 0.0)
                xi = jnp.where(live, wi[c], 0.0)
                wr[c] = xr * dr[c] - xi * di[c]
                wi[c] = xr * di[c] + xi * dr[c]
        return tuple(wr) + tuple(wi) + tuple(ar) + tuple(ai)

    wr, wi = rows_of(w_ref, slice(0, LANES), chunks)
    ar, ai = rows_of(ablk_ref, slice(0, LANES), chunks)
    out = lax.fori_loop(
        0, steps // unroll, body, tuple(wr) + tuple(wi) + tuple(ar) + tuple(ai)
    )
    wr, wi, ar, ai = (list(out[n * chunks : (n + 1) * chunks]) for n in range(4))
    put_rows(w_ref, slice(0, LANES), wr, wi)
    put_rows(ablk_ref, slice(0, LANES), ar, ai)

    @pl.when(i == nt - 1)
    def _():
        zero = [jnp.zeros((1, 128), F32)] * chunks
        power = disc_row(disc_ref, 2, chunks, conj=True)
        cr, ci = chain(ablk_ref, jo_ref, power, (zero, zero), not down)
        put_copies(end_ref, cr, ci)


def adjoint_kernel(down, last, *refs):
    (
        ends_ref, table_ref, sg_ref, ablk_ref, disc_ref, jr_ref, low_ref, u_ref, norm_ref, pg_ref, g_ref,
        win_ref, order_ref, ssum_ref,
        res_ref, isum_ref, nsum_ref, st_ref, dg_ref, ax_ref,
    ) = refs
    width = win_ref.shape[0]
    i, nt = pl.program_id(0), pl.num_programs(0)
    chunks = chunk_count(sg_ref)
    half = chunks * 128
    steps = sg_ref.shape[0] // LANES
    tile = nt - 1 - i if down else i

    @pl.when(i == 0)
    def _():
        carry = carry_in(ends_ref, table_ref, chunks)
        power = disc_row(disc_ref, 2, chunks, conj=True)
        chain(ablk_ref, jr_ref, power, carry, down, st_ref)
        ax_ref[...] = jnp.zeros_like(ax_ref)

    fr, fi = disc_row(disc_ref, 1, chunks)
    fr, fi = wide(fr), wide(fi)

    def emit(low_step, pair, extra):
        if pair is None:
            re, im = rows_of(ax_ref, slice(0, LANES), chunks)
            return tuple(re) + tuple(im)
        sums_r, sums_i = list(extra[:chunks]), list(extra[chunks:])
        at = pl.ds(pl.multiple_of(low_step * LANES, 2 * LANES), 2 * LANES)
        xr, xi = rows_of(low_ref, at, chunks)
        grads = []
        for which, (ar, ai) in enumerate(pair):
            gr, gi = [], []
            rows = slice(which * LANES, (which + 1) * LANES)
            for c in range(chunks):
                vr, vi = xr[c].astype(F32)[rows], xi[c].astype(F32)[rows]
                sums_r[c] = sums_r[c] + (ar[c] * vr + ai[c] * vi)
                sums_i[c] = sums_i[c] + (ai[c] * vr - ar[c] * vi)
                gr.append(ar[c] * fr[c] + ai[c] * fi[c])
                gi.append(ai[c] * fr[c] - ar[c] * fi[c])
            grads.append((gr, gi))
        store_pair(dg_ref, low_step, grads[0], grads[1])
        return tuple(sums_r) + tuple(sums_i)

    sums = scan_tile(
        sg_ref, st_ref, disc_row(disc_ref, 0, chunks, conj=True), jr_ref, tile * steps, steps,
        down, emit,
    )
    put_rows(ax_ref, slice(0, LANES), list(sums[:chunks]), list(sums[chunks:]))

    u = u_ref[...].astype(F32)
    centered = u - norm_ref[0:1]
    normed = (centered * norm_ref[2:3] + norm_ref[3:4]).astype(BF16)
    drive_grad = dg_ref[...]
    accumulate(
        isum_ref, lax.dot_general(normed, drive_grad, TN, preferred_element_type=F32)
    )
    normed_grad = lax.dot_general(drive_grad, win_ref[...], NT, preferred_element_type=F32)
    normed_grad += norm_ref[4:5] * pg_ref[...].astype(F32)
    add_rows(
        nsum_ref, column_sum(normed_grad), column_sum(normed_grad * centered) * norm_ref[1:2], False
    )
    result = g_ref[...].astype(F32) + norm_ref[2:3] * normed_grad
    if last:
        permute_out(result, order_ref, res_ref)
    else:
        res_ref[...] = result

    @pl.when(i == nt - 1)
    def _():
        at = 2 * SLOT
        for c in range(width // 128):
            nsum_ref[0, at + c : at + c + 1] = ssum_ref[:, cols(c)]
        at += width // 128
        decays = jnp.sum(ax_ref[...], axis=0, keepdims=True)
        wr, wi = win_ref[:, :half].astype(F32), win_ref[:, half:].astype(F32)
        gr, gi = isum_ref[:, :half], isum_ref[:, half:]
        re = jnp.sum(wr * gr + wi * gi, axis=0, keepdims=True)
        im = jnp.sum(wr * gi - wi * gr, axis=0, keepdims=True)
        gr, gi = disc_ref[1:2, :half], disc_ref[1:2, half:]
        scale = 1.0 / (gr * gr + gi * gi)
        factors = ((re * gr - im * gi) * scale, (re * gi + im * gr) * scale)
        for c in range(2 * chunks):
            nsum_ref[0, at + c : at + c + 1] = decays[:, cols(c)]
        at += 2 * chunks
        for c in range(chunks):
            nsum_ref[0, at + c : at + c + 1] = factors[0][:, cols(c)]
            nsum_ref[0, at + chunks + c : at + chunks + c + 1] = factors[1][:, cols(c)]
        nsum_ref[...] = jnp.broadcast_to(nsum_ref[0:1], nsum_ref.shape)


def back_kernel(down, tokens, *refs):
    (
        sums_ref, r_ref, up_ref, up_norm_ref, mixed_ref, gate_ref, low_ref, u_ref, norm_ref, wout_ref,
        wgate_ref, disc_ref, jo_ref,
        g_ref, pg_ref, sg_ref, wsum_ref, ssum_ref, end_ref, ablk_ref, nsum_ref, bsum_ref,
    ) = refs
    i, nt = pl.program_id(0), pl.num_programs(0)
    chunks = chunk_count(sg_ref)
    steps = sg_ref.shape[0] // LANES
    tile = nt - 1 - i if down else i

    @pl.when(i == 0)
    def _():
        nsum_ref[...] = jnp.sum(sums_ref[...], axis=0)
        bsum_ref[0:1], bsum_ref[1:2] = summed(sums_ref)
        ablk_ref[...] = jnp.zeros_like(ablk_ref)

    scale = up_norm_ref[2:3] * (-1.0 / tokens)
    standard = (up_ref[...] - up_norm_ref[0:1]) * (scale * up_norm_ref[1:2] * bsum_ref[1:2])
    g = r_ref[...] + (standard + scale * bsum_ref[0:1])
    g_ref[...] = g
    u = u_ref[...].astype(F32)
    normed = (u - norm_ref[0:1]) * norm_ref[2:3] + norm_ref[3:4]
    gate_backward(
        g, mixed_ref[...].astype(F32), gate_ref[...].astype(F32), normed, low_ref, wout_ref,
        wgate_ref, (pg_ref, sg_ref, wsum_ref, ssum_ref),
    )
    decay = disc_row(disc_ref, 0, chunks, conj=True)
    scan_tile(sg_ref, ablk_ref, decay, jo_ref, tile * steps, steps, down)

    @pl.when(i == nt - 1)
    def _():
        zero = [jnp.zeros((1, 128), F32)] * chunks
        power = disc_row(disc_ref, 2, chunks, conj=True)
        cr, ci = chain(ablk_ref, jo_ref, power, (zero, zero), down)
        put_copies(end_ref, cr, ci)


def whole(array):
    shape = array.shape
    return pl.BlockSpec(shape, lambda i: (0,) * len(shape))


def tile_spec(rows, width, nt, down):
    if down:
        return pl.BlockSpec((rows, width), lambda i: (nt - 1 - i, 0))
    return pl.BlockSpec((rows, width), lambda i: (i, 0))


def run_spec(steps, width, nt, down):
    if down:
        return pl.BlockSpec((LANES, steps, width), lambda i: (0, nt - 1 - i, 0))
    return pl.BlockSpec((LANES, steps, width), lambda i: (0, i, 0))


def call(kernel, nt, args, outs, scratch, macs, name):
    arrays = [a for a, _ in args]
    sizes = sum(a.size * a.dtype.itemsize for a in arrays + [a for a, _ in outs])
    return pl.pallas_call(
        kernel,
        grid=(nt,),
        in_specs=[whole(a) if s is None else s for a, s in args],
        out_specs=[whole(a) if s is None else s for a, s in outs],
        out_shape=[a for a, _ in outs],
        scratch_shapes=scratch,
        compiler_params=pltpu.CompilerParams(
            vmem_limit_bytes=VMEM_LIMIT, dimension_semantics=("arbitrary",)
        ),
        cost_estimate=pl.CostEstimate(flops=2 * macs, bytes_accessed=sizes, transcendentals=0),
        name=name,
    )(*arrays)


def shape(*dims, dtype=F32):
    return jax.ShapeDtypeStruct(dims, dtype)


def body(
    axes,
    tokens_in,
    seq_starts,
    norm_gain,
    norm_bias,
    decay_rate,
    step_log,
    frequency,
    in_proj,
    out_proj,
    skip_gain,
    gate_proj,
    grad_out,
):
    rows, width = tokens_in.shape
    states = in_proj.shape[-1]
    devices = 2 ** len(axes)
    tokens = float(rows * devices)
    run = rows // LANES
    steps = min(64, run)
    tile = steps * LANES
    nt = rows // tile
    span = min(32, steps)
    discs, tables, cuts, order = pl.pallas_call(
        functools.partial(prep_kernel, rows, axes),
        in_specs=[pl.BlockSpec(memory_space=pltpu.SMEM)]
        + [pl.BlockSpec(memory_space=pltpu.VMEM)] * 3,
        out_specs=[pl.BlockSpec(memory_space=pltpu.VMEM)] * 4,
        out_shape=[
            shape(LAYERS, 8, states), shape(2 * LAYERS, 2, devices, 2 * SLOT, 128),
            shape(2, LANES, 128, dtype=jnp.int32), shape(span * LANES, span * LANES, dtype=BF16),
        ],
        compiler_params=pltpu.CompilerParams(vmem_limit_bytes=VMEM_LIMIT),
        name="prep",
    )(seq_starts, decay_rate, step_log, frequency)

    def tiles(array, down):
        return (array, tile_spec(tile, array.shape[-1], nt, down))

    def runs(array, down):
        return (array, run_spec(steps, array.shape[-1], nt, down))

    def full(array):
        return (array, None)

    def of(array, l):
        size = array.shape[1:]
        return (array, pl.BlockSpec((None,) + size, lambda i: (l,) + (0,) * len(size)))

    tokens_run = tokens_in.reshape(LANES, run, width)
    grad_run = grad_out.reshape(LANES, run, width)
    state_scratch = pltpu.VMEM((LANES, states), F32)
    small = 2 * SLOT + (width + 2 * states) // 128
    cost = rows * width * states

    u0, stats = call(
        stats_kernel, nt, [runs(tokens_run, 0), full(order)],
        [tiles(shape(rows, width, dtype=BF16), 0), full(shape(devices, 2 * SLOT, 128))],
        [], cost // 2, "stats",
    )

    def drive(l, stream, stats):
        down = l % 2
        return call(
            functools.partial(drive_kernel, l, bool(down), tokens), nt,
            [full(gather_all(stats, axes)), tiles(stream, down), full(norm_gain), full(norm_bias), full(skip_gain), of(in_proj, l), of(discs, l),
               of(cuts, down)],
            [tiles(shape(rows, states), down), full(shape(devices, 2 * SLOT, 128)),
             full(shape(LANES, states)), full(shape(8, width))],
            [], 4 * cost, f"drive_{l}",
        )

    b0, end0, blk0, norm0 = drive(0, u0, stats)
    u1, low0, mixed0, gate0, stats = call(
        functools.partial(forward_kernel, False), nt,
        [full(gather_all(end0, axes)), of(tables, 2 * 0 + 0), tiles(b0, 0), full(blk0), of(discs, 0), of(cuts, 0),
           tiles(u0, 0), full(norm0), of(out_proj, 0), of(gate_proj, 0)],
        [tiles(shape(rows, width), 0), tiles(shape(rows, states, dtype=BF16), 0),
         tiles(shape(rows, width, dtype=BF16), 0), tiles(shape(rows, width, dtype=BF16), 0),
         full(shape(devices, 2 * SLOT, 128))],
        [state_scratch], 6 * cost, "forward_0",
    )

    b1, end1, blk1, norm1 = drive(1, u1, stats)
    (
        out, low1, g1, pg1, sg1, w_sum1, skip_sum1, aend1, ablk1
    ) = call(
        functools.partial(turn_kernel, True), nt,
        [full(gather_all(end1, axes)), of(tables, 2 * 1 + 0), tiles(b1, 1), full(blk1), of(discs, 1), of(cuts, 1),
           of(cuts, 0), tiles(u1, 1), full(norm1), of(out_proj, 1), of(gate_proj, 1),
           runs(grad_run, 1), full(order)],
        [runs(shape(LANES, run, width), 1), tiles(shape(rows, states, dtype=BF16), 1),
         tiles(shape(rows, width, dtype=BF16), 1), tiles(shape(rows, width, dtype=BF16), 1),
         tiles(shape(rows, states), 1), full(shape(states + width, width)), full(shape(1, width)),
         full(shape(devices, 2 * SLOT, 128)), full(shape(LANES, states))],
        [state_scratch, state_scratch], 16 * cost, "turn_1",
    )

    def adjoint(l, sg, ablk, aend, low, stream, norm, pg, g, skip_sum):
        down = 1 - l % 2
        last = l == 0
        args = [
            full(gather_all(aend, axes)), of(tables, 2 * l + 1), tiles(sg, down), full(ablk),
            of(discs, l), of(cuts, down), tiles(low, down), tiles(stream, down), full(norm),
            tiles(pg, down), tiles(g, down), of(in_proj, l), full(order), full(skip_sum),
        ]
        return call(
            functools.partial(adjoint_kernel, bool(down), last), nt, args,
            [runs(shape(LANES, run, width), down) if last else tiles(shape(rows, width), down),
             full(shape(width, states)), full(shape(devices, small, 128))],
            [state_scratch, pltpu.VMEM((tile, states), BF16), state_scratch],
            8 * cost, f"adjoint_{l}",
        )

    r1, in_sum1, norm_sum1 = adjoint(
        1, sg1, ablk1, aend1, low1, u1, norm1, pg1, g1, skip_sum1
    )

    def lower(r1, norm_sum1):
        (
            g0, pg0, sg0, w_sum0, skip_sum0, aend0, ablk0, small1, _
        ) = call(
            functools.partial(back_kernel, True, tokens), nt,
            [full(gather_all(norm_sum1, axes)), tiles(r1, 1), tiles(u1, 1), full(norm1),
             tiles(mixed0, 1), tiles(gate0, 1), tiles(low0, 1), tiles(u0, 1), full(norm0),
             of(out_proj, 0), of(gate_proj, 0), of(discs, 0), of(cuts, 1)],
            [tiles(shape(rows, width), 1), tiles(shape(rows, width, dtype=BF16), 1),
             tiles(shape(rows, states), 1), full(shape(states + width, width)),
             full(shape(1, width)), full(shape(devices, 2 * SLOT, 128)),
             full(shape(LANES, states)), full(shape(small, 128)), full(shape(2, width))],
            [], 12 * cost, "back_0",
        )
        r0, in_sum0, norm_sum0 = adjoint(
            0, sg0, ablk0, aend0, low0, u0, norm0, pg0, g0, skip_sum0
        )
        small0 = jnp.sum(gather_all(norm_sum0, axes), axis=0)
        pair = jnp.stack([small0.reshape(-1), small1.reshape(-1)])
        bias_grad, gain_grad = pair[:, :width], pair[:, width : 2 * width]
        scale = norm0[2:3] * (-1.0 / tokens)
        grad_in = r0.reshape(rows, width) + (
            (tokens_in.astype(F32) - norm0[0:1]) * (scale * norm0[1:2] * gain_grad[:1])
            + scale * bias_grad[:1]
        )
        return grad_in, pair, sum_all(w_sum0, axes), sum_all(in_sum0, axes)

    def nothing(r1, norm_sum1):
        return (
            jnp.zeros((rows, width), F32),
            jnp.zeros((LAYERS, small * 128), F32),
            jnp.zeros((states + width, width), F32),
            jnp.zeros((width, states), F32),
        )

    w_all1, in_all1 = lax.psum((w_sum1, in_sum1), axes)
    grad_in, pair, w_all0, in_all0 = lax.cond(
        seq_starts[0] == 0, lower, nothing, r1, norm_sum1
    )
    bias_grad, gain_grad, skip_grad = (pair[:, k * width : (k + 1) * width] for k in range(3))
    dsum = pair[:, 3 * width : 3 * width + states]
    fsum = pair[:, 3 * width + states :]
    in_grad = jnp.stack([in_all0, in_all1])
    out_grad = jnp.stack([w_all0[width:], w_all1[width:]])
    gate_grad = jnp.stack([w_all0[:width], w_all1[:width]])

    (decay, factor), discrete_back = jax.vjp(
        jax.vmap(discretize), decay_rate, step_log, frequency
    )
    half = states // 2
    dr, di = decay[:, :half], decay[:, half:]
    fr, fi = factor[:, :half], factor[:, half:]
    sr, si = fsum[:, :half], fsum[:, half:]
    tr = dsum[:, :half] - (fr * sr + fi * si)
    ti = dsum[:, half:] - (fr * si - fi * sr)
    modulus = dr * dr + di * di
    decay_grad = jnp.concatenate(
        [(tr * dr - ti * di) / modulus, (tr * di + ti * dr) / modulus], axis=-1
    )
    rate_grad, step_grad, freq_grad = discrete_back((decay_grad, fsum))
    return (
        out.reshape(rows, width),
        grad_in,
        gain_grad,
        bias_grad,
        rate_grad,
        step_grad,
        freq_grad,
        in_grad,
        out_grad,
        skip_grad,
        gate_grad,
    )


def solution(mesh):
    bits = mesh.devices.size.bit_length() - 1
    axes = tuple("b%d" % k for k in range(bits))
    binary = Mesh(mesh.devices.reshape((2,) * bits), axes)
    rows = P(axes, None)
    return jax.shard_map(
        functools.partial(body, axes),
        mesh=binary,
        in_specs=(rows,) + (P(),) * 10 + (rows,),
        out_specs=(rows, rows) + (P(),) * 9,
        check_vma=False,
    )
```

```python
import functools

import jax
import jax.numpy as jnp
from jax import lax
from jax.experimental import pallas as pl
from jax.experimental.pallas import tpu as pltpu
from jax.sharding import Mesh, PartitionSpec as P

LAYERS = 2
EPSILON = 1e-05
SLOT = 4
LANES = 8
VMEM_LIMIT = 60 * 1024 * 1024
GELU_A = 0.7978845608028654
GELU_B = 0.044715
NT = (((1,), (1,)), ((), ()))
TN = (((0,), (0,)), ((), ()))
F32 = jnp.float32
BF16 = jnp.bfloat16


def discretize(decay_rate, step_log, frequency):
    step_size = jnp.exp(step_log)
    real_angle = -decay_rate * step_size
    imag_angle = frequency * step_size
    magnitude = jnp.exp(real_angle)
    cosine = jnp.cos(imag_angle)
    sine = jnp.sin(imag_angle)
    decay_row = jnp.concatenate([magnitude * cosine, magnitude * sine], axis=-1)
    minus_real = jnp.expm1(real_angle) * cosine - 2.0 * jnp.sin(0.5 * imag_angle) ** 2
    minus_imag = magnitude * sine
    modulus = decay_rate * decay_rate + frequency * frequency
    factor_real = (-decay_rate * minus_real + frequency * minus_imag) / modulus
    factor_imag = (-decay_rate * minus_imag - frequency * minus_real) / modulus
    return (decay_row, jnp.concatenate([factor_real, factor_imag], axis=-1))


def gather_all(copies, axes):
    return lax.all_to_all(copies, axes, 0, 0)


def scatter_sum(value, axes):
    count = 2 ** len(axes)
    pieces = value.reshape((count, value.shape[0] // count) + value.shape[1:])
    return jnp.sum(lax.all_to_all(pieces, axes, 0, 0), axis=0)


def gather_rows(value, axes):
    count = 2 ** len(axes)
    copies = jnp.broadcast_to(value, (count,) + value.shape)
    return lax.all_to_all(copies, axes, 0, 0).reshape((count * value.shape[0],) + value.shape[1:])


def phases(axes):
    left, out = list(axes), [(axes[-1],)]
    left = left[:-1]
    while left:
        out.append(tuple(left[-2:]))
        left = left[:-2]
    return out


def sum_all(value, parts):
    for part in parts:
        value = scatter_sum(value, part)
    for part in reversed(parts):
        value = gather_rows(value, part)
    return value


def cols(c):
    return slice(c * 128, (c + 1) * 128)


def chunk_count(ref):
    return ref.shape[-1] // 256


def rows_of(ref, at, chunks):
    half = chunks * 128
    re = [ref[at, c * 128 : (c + 1) * 128] for c in range(chunks)]
    im = [ref[at, half + c * 128 : half + (c + 1) * 128] for c in range(chunks)]
    return re, im


def put_rows(ref, at, re, im):
    chunks = len(re)
    half = chunks * 128
    for c in range(chunks):
        ref[at, c * 128 : (c + 1) * 128] = re[c]
        ref[at, half + c * 128 : half + (c + 1) * 128] = im[c]


def put_copies(ref, re, im):
    ref[0] = jnp.zeros(ref.shape[1:], F32)
    for c in range(len(re)):
        ref[0, c : c + 1] = re[c]
        ref[0, SLOT + c : SLOT + c + 1] = im[c]
    ref[...] = jnp.broadcast_to(ref[0:1], ref.shape)


def wide(rows):
    return [jnp.broadcast_to(v, (LANES, 128)) for v in rows]


def chain(ends_ref, jr_ref, power, carry, down, start_ref=None):
    chunks = len(power[0])
    pr, pi = power
    cr, ci = carry
    order = range(LANES - 1, -1, -1) if down else range(LANES)
    for s in order:
        at = slice(s, s + 1)
        if start_ref is not None:
            put_rows(start_ref, at, cr, ci)
        er, ei = rows_of(ends_ref, at, chunks)
        alive = (jr_ref[at, :] < 0).astype(F32)
        cr, ci = (
            [er[c] + alive * (pr[c] * cr[c] - pi[c] * ci[c]) for c in range(chunks)],
            [ei[c] + alive * (pr[c] * ci[c] + pi[c] * cr[c]) for c in range(chunks)],
        )
    return cr, ci


def carry_in(ends_ref, table_ref, chunks):
    total = jnp.zeros((2 * SLOT, 128), F32)
    for e in range(ends_ref.shape[0]):
        end = ends_ref[e]
        turned = jnp.concatenate([end[SLOT:], end[:SLOT]], axis=0)
        total += table_ref[0, e] * end + table_ref[1, e] * turned
    return (
        [total[c : c + 1] for c in range(chunks)],
        [total[SLOT + c : SLOT + c + 1] for c in range(chunks)],
    )


def scan_tile(src_ref, st_ref, decay, jr_ref, first_step, steps, down, emit=None, unroll=4):
    chunks = chunk_count(src_ref)
    dr, di = wide(decay[0]), wide(decay[1])
    jr = jr_ref[...]
    re, im = rows_of(st_ref, slice(0, LANES), chunks)

    def one(step, re, im):
        at = pl.ds(pl.multiple_of(step * LANES, LANES), LANES)
        br, bi = rows_of(src_ref, at, chunks)
        live = jr != first_step + step
        nr, ni = [], []
        for c in range(chunks):
            xr = jnp.where(live, re[c], 0.0)
            xi = jnp.where(live, im[c], 0.0)
            nr.append(dr[c] * xr - di[c] * xi + br[c])
            ni.append(dr[c] * xi + di[c] * xr + bi[c])
        return nr, ni

    def body(i, carry):
        re, im = list(carry[:chunks]), list(carry[chunks : 2 * chunks])
        extra = carry[2 * chunks :]
        for q in range(unroll):
            n = 2 * (i * unroll + q)
            low_step = steps - 2 - n if down else n
            a, b = (low_step + 1, low_step) if down else (low_step, low_step + 1)
            r1, i1 = one(a, re, im)
            r2, i2 = one(b, r1, i1)
            if emit is not None:
                pair = ((r2, i2), (r1, i1)) if down else ((r1, i1), (r2, i2))
                extra = emit(low_step, pair, extra)
            re, im = r2, i2
        return tuple(re) + tuple(im) + tuple(extra)

    start = tuple(re) + tuple(im)
    if emit is not None:
        start = start + tuple(emit(None, None, None))
    out = lax.fori_loop(0, steps // (2 * unroll), body, start)
    put_rows(st_ref, slice(0, LANES), list(out[:chunks]), list(out[chunks : 2 * chunks]))
    return out[2 * chunks :]


def store_pair(ref, low_step, first, second):
    at = pl.ds(pl.multiple_of(low_step * LANES, 2 * LANES), 2 * LANES)
    re = [jnp.concatenate([p, q], axis=0).astype(BF16) for p, q in zip(first[0], second[0])]
    im = [jnp.concatenate([p, q], axis=0).astype(BF16) for p, q in zip(first[1], second[1])]
    put_rows(ref, at, re, im)


def disc_row(disc_ref, row, chunks, conj=False):
    re, im = rows_of(disc_ref, slice(row, row + 1), chunks)
    return (re, [-v for v in im]) if conj else (re, im)


def column_sum(value):
    rows, width = value.shape
    return jnp.sum(jnp.sum(value.reshape(rows // 8, 8, width), axis=0), axis=0, keepdims=True)


def permute_in(block, order_ref):
    runs, steps, width = block.shape
    span = order_ref.shape[0] // runs
    out = []
    for k in range(steps // span):
        part = block[:, k * span : (k + 1) * span, :].reshape(runs * span, width)
        out.append(jnp.dot(order_ref[...], part, preferred_element_type=F32))
    return out[0] if len(out) == 1 else jnp.concatenate(out, axis=0)


def permute_out(value, order_ref, out_ref):
    rows, width = value.shape
    size = order_ref.shape[0]
    span = size // LANES
    high = value.astype(BF16)
    low = (value - high.astype(F32)).astype(BF16)
    for k in range(rows // size):
        at = slice(k * size, (k + 1) * size)
        back = lax.dot_general(order_ref[...], high[at], TN, preferred_element_type=F32)
        back += lax.dot_general(order_ref[...], low[at], TN, preferred_element_type=F32)
        out_ref[:, k * span : (k + 1) * span, :] = back.reshape(LANES, span, width)


def expm1(value):
    acc = jnp.full_like(value, 1.0 / 479001600.0)
    for n in (39916800.0, 3628800.0, 362880.0, 40320.0, 5040.0, 720.0, 120.0, 24.0, 6.0, 2.0, 1.0):
        acc = acc * value + 1.0 / n
    return jnp.where(value > -1.0, acc * value, jnp.exp(value) - 1.0)


def prep_kernel(
    rows, axes, starts_ref, rate_ref, step_ref, freq_ref,
    disc_ref, table_ref, cut_ref, order_ref,
):
    devices = 2 ** len(axes)
    total = rows * devices
    run = rows // LANES
    half = rate_ref.shape[-1]
    me = 0
    for axis in axes:
        me = 2 * me + lax.axis_index(axis)
    starts = [starts_ref[k] for k in range(starts_ref.shape[0])]

    base = me * rows + run * lax.broadcasted_iota(jnp.int32, (LANES, 128), 0)
    up = jnp.full((LANES, 128), -1, jnp.int32)
    down = up
    for begin in starts + [total]:
        rel = begin - base
        up = jnp.maximum(up, jnp.where((rel >= 0) & (rel < run), rel, -1))
        down = jnp.maximum(down, jnp.where((rel >= 1) & (rel <= run), rel - 1, -1))
    cut_ref[0] = up
    cut_ref[1] = down

    size = order_ref.shape[0]
    span = size // LANES
    to = lax.broadcasted_iota(jnp.int32, (size, size), 0)
    back = lax.broadcasted_iota(jnp.int32, (size, size), 1)
    order_ref[...] = ((to % LANES) * span + to // LANES == back).astype(F32).astype(BF16)

    source = lax.broadcasted_iota(jnp.int32, (devices, half), 0)
    for l in range(LAYERS):
        row = slice(l, l + 1)
        rate, freq = rate_ref[row], freq_ref[row]
        step_size = jnp.exp(step_ref[row])
        real_angle = -rate * step_size
        imag_angle = freq * step_size
        magnitude = jnp.exp(real_angle)
        cosine, sine = jnp.cos(imag_angle), jnp.sin(imag_angle)
        minus_real = expm1(real_angle) * cosine - 2.0 * jnp.sin(0.5 * imag_angle) ** 2
        minus_imag = magnitude * sine
        modulus = rate * rate + freq * freq
        disc_ref[l, 0:1, :half] = magnitude * cosine
        disc_ref[l, 0:1, half:] = minus_imag
        disc_ref[l, 1:2, :half] = (-rate * minus_real + freq * minus_imag) / modulus
        disc_ref[l, 1:2, half:] = (-rate * minus_imag - freq * minus_real) / modulus
        magnitude = jnp.exp(real_angle * float(run))
        disc_ref[l, 2:3, :half] = magnitude * jnp.cos(imag_angle * float(run))
        disc_ref[l, 2:3, half:] = magnitude * jnp.sin(imag_angle * float(run))
        disc_ref[l, 3:8] = jnp.zeros((5, 2 * half), F32)
        for back in range(2):
            going_down = (l + back) % 2 == 1
            if going_down:
                live, count = source > me, source - me - 1
            else:
                live, count = source < me, me - 1 - source
            for begin in starts:
                if going_down:
                    cut = ((begin > (me + 1) * rows).astype(jnp.int32) > 0) & (
                        source * rows >= begin
                    )
                else:
                    cut = ((begin < me * rows).astype(jnp.int32) > 0) & (
                        (source + 1) * rows <= begin
                    )
                live &= ~cut
            count = (jnp.maximum(count, 0) * rows).astype(F32)
            magnitude = jnp.where(live, jnp.exp(real_angle * count), 0.0)
            angle = imag_angle * count
            real = magnitude * jnp.cos(angle)
            imag = magnitude * jnp.sin(angle)
            imag = -imag if back else imag
            at = 2 * l + back
            table_ref[at] = jnp.zeros(table_ref.shape[1:], F32)
            for c in range(half // 128):
                table_ref[at, 0, :, c, :] = real[:, cols(c)]
                table_ref[at, 0, :, SLOT + c, :] = real[:, cols(c)]
                table_ref[at, 1, :, c, :] = -imag[:, cols(c)]
                table_ref[at, 1, :, SLOT + c, :] = imag[:, cols(c)]


def stats_kernel(tok_ref, order_ref, u_ref, stats_ref):
    value = permute_in(tok_ref[...], order_ref)
    u_ref[...] = value.astype(BF16)
    add_stats(stats_ref, value)


def add_stats(stats_ref, value):
    add_rows(stats_ref, column_sum(value), column_sum(value * value))


def add_rows(copies_ref, first, second):
    i, nt = pl.program_id(0), pl.num_programs(0)
    chunks = first.shape[1] // 128

    @pl.when(i == 0)
    def _():
        copies_ref[0] = jnp.zeros(copies_ref.shape[1:], F32)

    for c in range(chunks):
        copies_ref[0, c : c + 1] += first[:, cols(c)]
        copies_ref[0, SLOT + c : SLOT + c + 1] += second[:, cols(c)]

    @pl.when(i == nt - 1)
    def _():
        copies_ref[...] = jnp.broadcast_to(copies_ref[0:1], copies_ref.shape)


def summed(ref):
    total = jnp.sum(ref[...], axis=0)
    return tuple(
        jnp.concatenate([total[SLOT * k + c : SLOT * k + c + 1] for c in range(SLOT)], axis=1)
        for k in range(2)
    )


def drive_kernel(layer, down, tokens, *refs):
    (
        stat_ref, u_ref, gain_ref, bias_ref, skip_ref, win_ref, disc_ref, jr_ref,
        b_ref, end_ref, blk_ref, norm_ref,
    ) = refs
    i, nt = pl.program_id(0), pl.num_programs(0)
    steps = u_ref.shape[0] // LANES
    chunks = chunk_count(b_ref)
    half = chunks * 128

    @pl.when(i == 0)
    def _():
        total, squares = summed(stat_ref)
        row = slice(layer, layer + 1)
        mean = total / tokens
        inv = lax.rsqrt(squares / tokens - mean * mean + EPSILON)
        norm_ref[0:1] = mean
        norm_ref[1:2] = inv
        norm_ref[2:3] = inv * gain_ref[row]
        norm_ref[3:4] = bias_ref[row]
        norm_ref[4:5] = skip_ref[row]
        norm_ref[5:8] = jnp.zeros((3, norm_ref.shape[1]), F32)
        blk_ref[...] = jnp.zeros_like(blk_ref)

    u = u_ref[...].astype(F32)
    normed = (u - norm_ref[0:1]) * norm_ref[2:3] + norm_ref[3:4]
    drive = jnp.dot(normed.astype(BF16), win_ref[...], preferred_element_type=F32)
    fr, fi = disc_ref[1:2, :half], disc_ref[1:2, half:]
    re, im = drive[:, :half], drive[:, half:]
    b_ref[:, :half] = re * fr - im * fi
    b_ref[:, half:] = re * fi + im * fr
    tile = nt - 1 - i if down else i
    scan_tile(b_ref, blk_ref, disc_row(disc_ref, 0, chunks), jr_ref, tile * steps, steps, down)

    @pl.when(i == nt - 1)
    def _():
        zero = [jnp.zeros((1, 128), F32)] * chunks
        cr, ci = chain(blk_ref, jr_ref, disc_row(disc_ref, 2, chunks), (zero, zero), down)
        put_copies(end_ref, cr, ci)


def states_of(ends_ref, table_ref, b_ref, blk_ref, disc_ref, jr_ref, low_ref, st_ref, down):
    i, nt = pl.program_id(0), pl.num_programs(0)
    chunks = chunk_count(b_ref)
    steps = b_ref.shape[0] // LANES

    @pl.when(i == 0)
    def _():
        carry = carry_in(ends_ref, table_ref, chunks)
        chain(blk_ref, jr_ref, disc_row(disc_ref, 2, chunks), carry, down, st_ref)

    def emit(low_step, pair, extra):
        if pair is None:
            return ()
        (first, second) = pair
        store_pair(low_ref, low_step, first, second)
        return ()

    tile = nt - 1 - i if down else i
    scan_tile(
        b_ref, st_ref, disc_row(disc_ref, 0, chunks), jr_ref, tile * steps, steps, down, emit
    )


def gelu_parts(mixed):
    square = mixed * mixed
    tanh = jnp.tanh(mixed * (GELU_A + (GELU_A * GELU_B) * square))
    half_up = 0.5 + 0.5 * tanh
    return square, tanh, half_up


def gelu_slope(mixed, square, tanh, half_up):
    return half_up + (mixed * (0.5 - 0.5 * tanh * tanh)) * (
        GELU_A + (3.0 * GELU_A * GELU_B) * square
    )


def sigmoid(value):
    return 0.5 + 0.5 * jnp.tanh(0.5 * value)


def forward_kernel(down, *refs):
    (
        ends_ref, table_ref, b_ref, blk_ref, disc_ref, jr_ref, u_ref, norm_ref, wout_ref, wgate_ref,
        next_ref, low_ref, mixed_ref, gate_ref, stats_ref, st_ref,
    ) = refs
    states_of(ends_ref, table_ref, b_ref, blk_ref, disc_ref, jr_ref, low_ref, st_ref, down)
    u = u_ref[...].astype(F32)
    normed = (u - norm_ref[0:1]) * norm_ref[2:3] + norm_ref[3:4]
    mixed = jnp.dot(low_ref[...], wout_ref[...], preferred_element_type=F32)
    mixed += norm_ref[4:5] * normed
    _, _, half_up = gelu_parts(mixed)
    act = mixed * half_up
    gate = sigmoid(jnp.dot(act.astype(BF16), wgate_ref[...], preferred_element_type=F32))
    after = u + act * gate
    next_ref[...] = after
    mixed_ref[...] = mixed.astype(mixed_ref.dtype)
    gate_ref[...] = gate.astype(gate_ref.dtype)
    add_stats(stats_ref, after)


def accumulate(ref, value):
    @pl.when(pl.program_id(0) == 0)
    def _():
        ref[...] = value

    @pl.when(pl.program_id(0) != 0)
    def _():
        ref[...] += value


def gate_backward(g, mixed, gate, normed, low_ref, wout_ref, wgate_ref, outs, kept=None):
    pg_ref, sg_ref, wsum_ref, ssum_ref = outs
    width = g.shape[1]
    square, tanh, half_up = gelu_parts(mixed) if kept is None else kept
    act = mixed * half_up
    g_gate = g * gate
    logit_grad = (g_gate * act * (1.0 - gate)).astype(BF16)
    accumulate(
        wsum_ref.at[:width],
        lax.dot_general(act.astype(BF16), logit_grad, TN, preferred_element_type=F32),
    )
    act_grad = g_gate + lax.dot_general(
        logit_grad, wgate_ref[...], NT, preferred_element_type=F32
    )
    mixed_grad = act_grad * gelu_slope(mixed, square, tanh, half_up)
    accumulate(ssum_ref, column_sum(mixed_grad * normed))
    proj_grad = mixed_grad.astype(BF16)
    pg_ref[...] = proj_grad
    accumulate(
        wsum_ref.at[width : width + low_ref.shape[1]],
        lax.dot_general(low_ref[...], proj_grad, TN, preferred_element_type=F32),
    )
    sg_ref[...] = lax.dot_general(proj_grad, wout_ref[...], NT, preferred_element_type=F32)


def turn_kernel(down, *refs):
    (
        ends_ref, table_ref, b_ref, blk_ref, disc_ref, jr_ref, jo_ref, u_ref, norm_ref, wout_ref, wgate_ref,
        gout_ref, order_ref,
        out_ref, low_ref, g_ref, pg_ref, sg_ref, wsum_ref, end_ref, ablk_ref,
        st_ref, w_ref,
    ) = refs
    sums = wout_ref.shape[0] + wout_ref.shape[1]
    ssum_ref = wsum_ref.at[sums : sums + 1]
    i, nt = pl.program_id(0), pl.num_programs(0)
    chunks = chunk_count(b_ref)
    half = chunks * 128
    steps = b_ref.shape[0] // LANES
    tile = nt - 1 - i if down else i
    states_of(ends_ref, table_ref, b_ref, blk_ref, disc_ref, jr_ref, low_ref, st_ref, down)
    u = u_ref[...]
    normed = (u - norm_ref[0:1]) * norm_ref[2:3] + norm_ref[3:4]
    mixed = jnp.dot(low_ref[...], wout_ref[...], preferred_element_type=F32)
    mixed += norm_ref[4:5] * normed
    kept = gelu_parts(mixed)
    act = mixed * kept[2]
    gate = sigmoid(jnp.dot(act.astype(BF16), wgate_ref[...], preferred_element_type=F32))
    permute_out(u + act * gate, order_ref, out_ref)
    g = permute_in(gout_ref[...], order_ref)
    g_ref[...] = g.astype(BF16)
    gate_backward(
        g, mixed, gate, normed, low_ref, wout_ref, wgate_ref,
        (pg_ref, sg_ref, wsum_ref, ssum_ref), kept,
    )

    @pl.when(i == 0)
    def _():
        wsum_ref[sums + 1 :] = jnp.zeros((7, wsum_ref.shape[1]), F32)
        w_ref[:, :half] = jnp.ones((LANES, half), F32)
        w_ref[:, half:] = jnp.zeros((LANES, half), F32)
        ablk_ref[...] = jnp.zeros_like(ablk_ref)

    dr, di = disc_row(disc_ref, 0, chunks, conj=True)
    dr, di = wide(dr), wide(di)
    jo = jo_ref[...]
    unroll = 4

    def body(k, carry):
        wr, wi, ar, ai = (list(carry[n * chunks : (n + 1) * chunks]) for n in range(4))
        for q in range(unroll):
            n = k * unroll + q
            step = steps - 1 - n if down else n
            at = pl.ds(pl.multiple_of(step * LANES, LANES), LANES)
            sr, si = rows_of(sg_ref, at, chunks)
            live = jo != tile * steps + step
            for c in range(chunks):
                ar[c] = ar[c] + (wr[c] * sr[c] - wi[c] * si[c])
                ai[c] = ai[c] + (wr[c] * si[c] + wi[c] * sr[c])
                xr = jnp.where(live, wr[c], 0.0)
                xi = jnp.where(live, wi[c], 0.0)
                wr[c] = xr * dr[c] - xi * di[c]
                wi[c] = xr * di[c] + xi * dr[c]
        return tuple(wr) + tuple(wi) + tuple(ar) + tuple(ai)

    wr, wi = rows_of(w_ref, slice(0, LANES), chunks)
    ar, ai = rows_of(ablk_ref, slice(0, LANES), chunks)
    out = lax.fori_loop(
        0, steps // unroll, body, tuple(wr) + tuple(wi) + tuple(ar) + tuple(ai)
    )
    wr, wi, ar, ai = (list(out[n * chunks : (n + 1) * chunks]) for n in range(4))
    put_rows(w_ref, slice(0, LANES), wr, wi)
    put_rows(ablk_ref, slice(0, LANES), ar, ai)

    @pl.when(i == nt - 1)
    def _():
        zero = [jnp.zeros((1, 128), F32)] * chunks
        power = disc_row(disc_ref, 2, chunks, conj=True)
        cr, ci = chain(ablk_ref, jo_ref, power, (zero, zero), not down)
        put_copies(end_ref, cr, ci)


def adjoint_kernel(down, last, *refs):
    (
        ends_ref, table_ref, sg_ref, ablk_ref, disc_ref, jr_ref, low_ref, u_ref, norm_ref, pg_ref, g_ref,
        win_ref, order_ref, *refs
    ) = refs
    if last:
        (ssum_ref, res_ref, sums_ref, st_ref, dg_ref, ax_ref, nsum_ref) = refs
    else:
        (res_ref, sums_ref, nsum_ref, st_ref, dg_ref, ax_ref) = refs
    width, states = win_ref.shape
    isum_ref = sums_ref.at[:width, :states]
    i, nt = pl.program_id(0), pl.num_programs(0)
    chunks = chunk_count(sg_ref)
    half = chunks * 128
    steps = sg_ref.shape[0] // LANES
    tile = nt - 1 - i if down else i

    @pl.when(i == 0)
    def _():
        carry = carry_in(ends_ref, table_ref, chunks)
        power = disc_row(disc_ref, 2, chunks, conj=True)
        chain(ablk_ref, jr_ref, power, carry, down, st_ref)
        ax_ref[...] = jnp.zeros_like(ax_ref)

    fr, fi = disc_row(disc_ref, 1, chunks)
    fr, fi = wide(fr), wide(fi)

    def emit(low_step, pair, extra):
        if pair is None:
            re, im = rows_of(ax_ref, slice(0, LANES), chunks)
            return tuple(re) + tuple(im)
        sums_r, sums_i = list(extra[:chunks]), list(extra[chunks:])
        at = pl.ds(pl.multiple_of(low_step * LANES, 2 * LANES), 2 * LANES)
        xr, xi = rows_of(low_ref, at, chunks)
        grads = []
        for which, (ar, ai) in enumerate(pair):
            gr, gi = [], []
            rows = slice(which * LANES, (which + 1) * LANES)
            for c in range(chunks):
                vr, vi = xr[c].astype(F32)[rows], xi[c].astype(F32)[rows]
                sums_r[c] = sums_r[c] + (ar[c] * vr + ai[c] * vi)
                sums_i[c] = sums_i[c] + (ai[c] * vr - ar[c] * vi)
                gr.append(ar[c] * fr[c] + ai[c] * fi[c])
                gi.append(ai[c] * fr[c] - ar[c] * fi[c])
            grads.append((gr, gi))
        store_pair(dg_ref, low_step, grads[0], grads[1])
        return tuple(sums_r) + tuple(sums_i)

    sums = scan_tile(
        sg_ref, st_ref, disc_row(disc_ref, 0, chunks, conj=True), jr_ref, tile * steps, steps,
        down, emit,
    )
    put_rows(ax_ref, slice(0, LANES), list(sums[:chunks]), list(sums[chunks:]))

    u = u_ref[...].astype(F32)
    centered = u - norm_ref[0:1]
    normed = (centered * norm_ref[2:3] + norm_ref[3:4]).astype(BF16)
    drive_grad = dg_ref[...]
    accumulate(
        isum_ref, lax.dot_general(normed, drive_grad, TN, preferred_element_type=F32)
    )
    normed_grad = lax.dot_general(drive_grad, win_ref[...], NT, preferred_element_type=F32)
    normed_grad += norm_ref[4:5] * pg_ref[...].astype(F32)
    add_rows(
        nsum_ref, column_sum(normed_grad), column_sum(normed_grad * centered) * norm_ref[1:2]
    )
    result = g_ref[...].astype(F32) + norm_ref[2:3] * normed_grad
    if last:
        permute_out(result, order_ref, res_ref)
    else:
        res_ref[...] = result

    @pl.when(i == nt - 1)
    def _():
        decays = jnp.sum(ax_ref[...], axis=0, keepdims=True)
        wr, wi = win_ref[:, :half].astype(F32), win_ref[:, half:].astype(F32)
        gr, gi = isum_ref[:, :half], isum_ref[:, half:]
        re = jnp.sum(wr * gr + wi * gi, axis=0, keepdims=True)
        im = jnp.sum(wr * gi - wi * gr, axis=0, keepdims=True)
        gr, gi = disc_ref[1:2, :half], disc_ref[1:2, half:]
        scale = 1.0 / (gr * gr + gi * gi)
        factors = ((re * gr - im * gi) * scale, (re * gi + im * gr) * scale)
        if last:
            rows = [nsum_ref[0]] + [ssum_ref[:, cols(c)] for c in range(width // 128)]
            rows += [decays[:, cols(c)] for c in range(2 * chunks)]
            rows += [v[:, cols(c)] for v in factors for c in range(chunks)]
            at = 0
            for row in rows:
                sums_ref[at : at + row.shape[0], states:] = row
                at += row.shape[0]
            sums_ref[at:, states:] = jnp.zeros((width - at, 128), F32)
        else:
            sums_ref[width : width + 8] = jnp.zeros((8, states), F32)
            sums_ref[width : width + 1] = decays
            sums_ref[width + 1 : width + 2, :half] = factors[0]
            sums_ref[width + 1 : width + 2, half:] = factors[1]


def back_kernel(down, tokens, *refs):
    (
        sums_ref, r_ref, up_ref, up_norm_ref, mixed_ref, gate_ref, low_ref, u_ref, norm_ref, wout_ref,
        wgate_ref, disc_ref, jo_ref,
        g_ref, pg_ref, sg_ref, wsum_ref, ssum_ref, end_ref, ablk_ref, nsum_ref, bsum_ref,
    ) = refs
    i, nt = pl.program_id(0), pl.num_programs(0)
    chunks = chunk_count(sg_ref)
    steps = sg_ref.shape[0] // LANES
    tile = nt - 1 - i if down else i

    @pl.when(i == 0)
    def _():
        nsum_ref[...] = jnp.sum(sums_ref[...], axis=0)
        bsum_ref[0:1], bsum_ref[1:2] = summed(sums_ref)
        ablk_ref[...] = jnp.zeros_like(ablk_ref)

    scale = up_norm_ref[2:3] * (-1.0 / tokens)
    standard = (up_ref[...] - up_norm_ref[0:1]) * (scale * up_norm_ref[1:2] * bsum_ref[1:2])
    g = r_ref[...] + (standard + scale * bsum_ref[0:1])
    g_ref[...] = g
    u = u_ref[...].astype(F32)
    normed = (u - norm_ref[0:1]) * norm_ref[2:3] + norm_ref[3:4]
    gate_backward(
        g, mixed_ref[...].astype(F32), gate_ref[...].astype(F32), normed, low_ref, wout_ref,
        wgate_ref, (pg_ref, sg_ref, wsum_ref, ssum_ref),
    )
    decay = disc_row(disc_ref, 0, chunks, conj=True)
    scan_tile(sg_ref, ablk_ref, decay, jo_ref, tile * steps, steps, down)

    @pl.when(i == nt - 1)
    def _():
        zero = [jnp.zeros((1, 128), F32)] * chunks
        power = disc_row(disc_ref, 2, chunks, conj=True)
        cr, ci = chain(ablk_ref, jo_ref, power, (zero, zero), down)
        put_copies(end_ref, cr, ci)


def whole(array):
    shape = array.shape
    return pl.BlockSpec(shape, lambda i: (0,) * len(shape))


def tile_spec(rows, width, nt, down):
    if down:
        return pl.BlockSpec((rows, width), lambda i: (nt - 1 - i, 0))
    return pl.BlockSpec((rows, width), lambda i: (i, 0))


def run_spec(steps, width, nt, down):
    if down:
        return pl.BlockSpec((LANES, steps, width), lambda i: (0, nt - 1 - i, 0))
    return pl.BlockSpec((LANES, steps, width), lambda i: (0, i, 0))


def call(kernel, nt, args, outs, scratch, macs, name):
    arrays = [a for a, _ in args]
    sizes = sum(a.size * a.dtype.itemsize for a in arrays + [a for a, _ in outs])
    return pl.pallas_call(
        kernel,
        grid=(nt,),
        in_specs=[whole(a) if s is None else s for a, s in args],
        out_specs=[whole(a) if s is None else s for a, s in outs],
        out_shape=[a for a, _ in outs],
        scratch_shapes=scratch,
        compiler_params=pltpu.CompilerParams(
            vmem_limit_bytes=VMEM_LIMIT, dimension_semantics=("arbitrary",)
        ),
        cost_estimate=pl.CostEstimate(flops=2 * macs, bytes_accessed=sizes, transcendentals=0),
        name=name,
    )(*arrays)


def shape(*dims, dtype=F32):
    return jax.ShapeDtypeStruct(dims, dtype)


def body(
    axes,
    tokens_in,
    seq_starts,
    norm_gain,
    norm_bias,
    decay_rate,
    step_log,
    frequency,
    in_proj,
    out_proj,
    skip_gain,
    gate_proj,
    grad_out,
):
    rows, width = tokens_in.shape
    states = in_proj.shape[-1]
    devices = 2 ** len(axes)
    tokens = float(rows * devices)
    run = rows // LANES
    steps = min(64, run)
    tile = steps * LANES
    nt = rows // tile
    span = min(32, steps)
    discs, tables, cuts, order = pl.pallas_call(
        functools.partial(prep_kernel, rows, axes),
        in_specs=[pl.BlockSpec(memory_space=pltpu.SMEM)]
        + [pl.BlockSpec(memory_space=pltpu.VMEM)] * 3,
        out_specs=[pl.BlockSpec(memory_space=pltpu.VMEM)] * 4,
        out_shape=[
            shape(LAYERS, 8, states), shape(2 * LAYERS, 2, devices, 2 * SLOT, 128),
            shape(2, LANES, 128, dtype=jnp.int32), shape(span * LANES, span * LANES, dtype=BF16),
        ],
        compiler_params=pltpu.CompilerParams(vmem_limit_bytes=VMEM_LIMIT),
        name="prep",
    )(seq_starts, decay_rate, step_log, frequency)

    def tiles(array, down):
        return (array, tile_spec(tile, array.shape[-1], nt, down))

    def runs(array, down):
        return (array, run_spec(steps, array.shape[-1], nt, down))

    def full(array):
        return (array, None)

    def of(array, l):
        size = array.shape[1:]
        return (array, pl.BlockSpec((None,) + size, lambda i: (l,) + (0,) * len(size)))

    tokens_run = tokens_in.reshape(LANES, run, width)
    grad_run = grad_out.reshape(LANES, run, width)
    state_scratch = pltpu.VMEM((LANES, states), F32)
    cost = rows * width * states

    u0, stats = call(
        stats_kernel, nt, [runs(tokens_run, 0), full(order)],
        [tiles(shape(rows, width, dtype=BF16), 0), full(shape(devices, 2 * SLOT, 128))],
        [], cost // 2, "stats",
    )

    def drive(l, stream, stats):
        down = l % 2
        return call(
            functools.partial(drive_kernel, l, bool(down), tokens), nt,
            [full(gather_all(stats, axes)), tiles(stream, down), full(norm_gain), full(norm_bias), full(skip_gain), of(in_proj, l), of(discs, l),
               of(cuts, down)],
            [tiles(shape(rows, states), down), full(shape(devices, 2 * SLOT, 128)),
             full(shape(LANES, states)), full(shape(8, width))],
            [], 4 * cost, f"drive_{l}",
        )

    b0, end0, blk0, norm0 = drive(0, u0, stats)
    u1, low0, mixed0, gate0, stats = call(
        functools.partial(forward_kernel, False), nt,
        [full(gather_all(end0, axes)), of(tables, 2 * 0 + 0), tiles(b0, 0), full(blk0), of(discs, 0), of(cuts, 0),
           tiles(u0, 0), full(norm0), of(out_proj, 0), of(gate_proj, 0)],
        [tiles(shape(rows, width), 0), tiles(shape(rows, states, dtype=BF16), 0),
         tiles(shape(rows, width, dtype=BF16), 0), tiles(shape(rows, width, dtype=BF16), 0),
         full(shape(devices, 2 * SLOT, 128))],
        [state_scratch], 6 * cost, "forward_0",
    )

    b1, end1, blk1, norm1 = drive(1, u1, stats)
    (
        out, low1, g1, pg1, sg1, w_sum1, aend1, ablk1
    ) = call(
        functools.partial(turn_kernel, True), nt,
        [full(gather_all(end1, axes)), of(tables, 2 * 1 + 0), tiles(b1, 1), full(blk1), of(discs, 1), of(cuts, 1),
           of(cuts, 0), tiles(u1, 1), full(norm1), of(out_proj, 1), of(gate_proj, 1),
           runs(grad_run, 1), full(order)],
        [runs(shape(LANES, run, width), 1), tiles(shape(rows, states, dtype=BF16), 1),
         tiles(shape(rows, width, dtype=BF16), 1), tiles(shape(rows, width, dtype=BF16), 1),
         tiles(shape(rows, states), 1), full(shape(states + width + 8, width)),
         full(shape(devices, 2 * SLOT, 128)), full(shape(LANES, states))],
        [state_scratch, state_scratch], 16 * cost, "turn_1",
    )

    def adjoint(l, sg, ablk, ends, low, stream, norm, pg, g, skip_sum=None):
        down = 1 - l % 2
        last = l == 0
        args = [
            full(ends), of(tables, 2 * l + 1), tiles(sg, down), full(ablk), of(discs, l),
            of(cuts, down), tiles(low, down), tiles(stream, down), full(norm), tiles(pg, down),
            tiles(g, down), of(in_proj, l), full(order),
        ]
        scratch = [state_scratch, pltpu.VMEM((tile, states), BF16), state_scratch]
        if last:
            args.append(full(skip_sum))
            outs = [
                runs(shape(LANES, run, width), down), full(shape(width, states + 128)),
            ]
            scratch.append(pltpu.VMEM((1, 2 * SLOT, 128), F32))
        else:
            outs = [
                tiles(shape(rows, width), down), full(shape(width + 8, states)),
                full(shape(devices, 2 * SLOT, 128)),
            ]
        return call(
            functools.partial(adjoint_kernel, bool(down), last), nt, args, outs, scratch,
            8 * cost, f"adjoint_{l}",
        )

    r1, in_sum1, norm_sum1 = adjoint(
        1, sg1, ablk1, gather_all(aend1, axes), low1, u1, norm1, pg1, g1
    )

    def lower(r1, norm_sum1):
        (
            g0, pg0, sg0, w_sum0, skip_sum0, aend0, ablk0, small1, _
        ) = call(
            functools.partial(back_kernel, True, tokens), nt,
            [full(gather_all(norm_sum1, axes)), tiles(r1, 1), tiles(u1, 1), full(norm1),
             tiles(mixed0, 1), tiles(gate0, 1), tiles(low0, 1), tiles(u0, 1), full(norm0),
             of(out_proj, 0), of(gate_proj, 0), of(discs, 0), of(cuts, 1)],
            [tiles(shape(rows, width), 1), tiles(shape(rows, width, dtype=BF16), 1),
             tiles(shape(rows, states), 1), full(shape(states + width, width)),
             full(shape(1, width)), full(shape(devices, 2 * SLOT, 128)),
             full(shape(LANES, states)), full(shape(2 * SLOT, 128)), full(shape(2, width))],
            [], 12 * cost, "back_0",
        )
        core, *others = phases(axes)
        ends, part = lax.optimization_barrier(
            (gather_all(aend0, axes), scatter_sum(w_sum0, core))
        )
        part = scatter_sum(part, others[0])
        r0, in_sum0 = adjoint(0, sg0, ablk0, ends, low0, u0, norm0, pg0, g0, skip_sum0)
        in_sum0, part = lax.optimization_barrier((in_sum0, part))
        w_all0 = sum_all(part, others[1:])
        w_all0 = gather_rows(gather_rows(w_all0, others[0]), core)
        in_all0 = sum_all(in_sum0, phases(axes))
        small0 = in_all0[:, states:].reshape(-1)
        scale = norm0[2:3] * (-1.0 / tokens)
        grad_in = r0.reshape(rows, width) + (
            (tokens_in.astype(F32) - norm0[0:1])
            * (scale * norm0[1:2] * small0[None, width : 2 * width])
            + scale * small0[None, :width]
        )
        return grad_in, small1.reshape(1, -1), w_all0, in_all0

    def nothing(r1, norm_sum1):
        return (
            jnp.zeros((rows, width), F32),
            jnp.zeros((1, 2 * width), F32),
            jnp.zeros((states + width, width), F32),
            jnp.zeros((width, states + 128), F32),
        )

    w_all1, in_all1 = lax.psum((w_sum1, in_sum1), axes)
    grad_in, norm_all1, w_all0, in_all0 = lax.cond(
        seq_starts[0] == 0, lower, nothing, r1, norm_sum1
    )
    small0 = in_all0[: 2 * SLOT + (width + 2 * states) // 128, states:].reshape(1, -1)
    bias_grad, gain_grad = (
        jnp.concatenate([v[:, k * width : (k + 1) * width] for v in (small0, norm_all1)], axis=0)
        for k in range(2)
    )
    sums = states + width
    small0 = small0[:, 2 * width :]
    skip_grad = jnp.concatenate([small0[:, :width], w_all1[sums : sums + 1]], axis=0)
    dsum = jnp.concatenate([small0[:, width : width + states], in_all1[width : width + 1]], axis=0)
    fsum = jnp.concatenate([small0[:, width + states :], in_all1[width + 1 : width + 2]], axis=0)
    in_grad = jnp.stack([in_all0[:, :states], in_all1[:width]])
    out_grad = jnp.stack([w_all0[width:], w_all1[width:sums]])
    gate_grad = jnp.stack([w_all0[:width], w_all1[:width]])

    (decay, factor), discrete_back = jax.vjp(
        jax.vmap(discretize), decay_rate, step_log, frequency
    )
    half = states // 2
    dr, di = decay[:, :half], decay[:, half:]
    fr, fi = factor[:, :half], factor[:, half:]
    sr, si = fsum[:, :half], fsum[:, half:]
    tr = dsum[:, :half] - (fr * sr + fi * si)
    ti = dsum[:, half:] - (fr * si - fi * sr)
    modulus = dr * dr + di * di
    decay_grad = jnp.concatenate(
        [(tr * dr - ti * di) / modulus, (tr * di + ti * dr) / modulus], axis=-1
    )
    rate_grad, step_grad, freq_grad = discrete_back((decay_grad, fsum))
    return (
        out.reshape(rows, width),
        grad_in,
        gain_grad,
        bias_grad,
        rate_grad,
        step_grad,
        freq_grad,
        in_grad,
        out_grad,
        skip_grad,
        gate_grad,
    )


def solution(mesh):
    bits = mesh.devices.size.bit_length() - 1
    axes = tuple("b%d" % k for k in range(bits))
    binary = Mesh(mesh.devices.reshape((2,) * bits), axes)
    rows = P(axes, None)
    return jax.shard_map(
        functools.partial(body, axes),
        mesh=binary,
        in_specs=(rows,) + (P(),) * 10 + (rows,),
        out_specs=(rows, rows) + (P(),) * 9,
        check_vma=False,
    )
```

```python
import functools

import jax
import jax.numpy as jnp
from jax import lax
from jax.experimental import pallas as pl
from jax.experimental.pallas import tpu as pltpu
from jax.sharding import Mesh, PartitionSpec as P

LAYERS = 2
EPSILON = 1e-05
SMALL = 32
BLOCKS = 8
SLOT = 4
LANES = 8
VMEM_LIMIT = 60 * 1024 * 1024
GELU_A = 0.7978845608028654
GELU_B = 0.044715
NT = (((1,), (1,)), ((), ()))
TN = (((0,), (0,)), ((), ()))
F32 = jnp.float32
BF16 = jnp.bfloat16


def gather_all(copies, axes):
    return lax.all_to_all(copies, axes, 0, 0)


def scatter_sum(value, axes):
    count = 2 ** len(axes)
    pieces = value.reshape((count, value.shape[0] // count) + value.shape[1:])
    return jnp.sum(lax.all_to_all(pieces, axes, 0, 0), axis=0)


def gather_rows(value, axes):
    count = 2 ** len(axes)
    copies = jnp.broadcast_to(value, (count,) + value.shape)
    return lax.all_to_all(copies, axes, 0, 0).reshape((count * value.shape[0],) + value.shape[1:])


def phases(axes):
    left, out = list(axes), [(axes[-1],)]
    left = left[:-1]
    while left:
        out.append(tuple(left[-2:]))
        left = left[:-2]
    return out


def sum_all(value, parts):
    for part in parts:
        value = scatter_sum(value, part)
    for part in reversed(parts):
        value = gather_rows(value, part)
    return value


def cols(c):
    return slice(c * 128, (c + 1) * 128)


def chunk_count(ref):
    return ref.shape[-1] // 256


def rows_of(ref, at, chunks):
    half = chunks * 128
    re = [ref[at, c * 128 : (c + 1) * 128] for c in range(chunks)]
    im = [ref[at, half + c * 128 : half + (c + 1) * 128] for c in range(chunks)]
    return re, im


def put_rows(ref, at, re, im):
    chunks = len(re)
    half = chunks * 128
    for c in range(chunks):
        ref[at, c * 128 : (c + 1) * 128] = re[c]
        ref[at, half + c * 128 : half + (c + 1) * 128] = im[c]


def put_copies(ref, re, im):
    ref[0] = jnp.zeros(ref.shape[1:], F32)
    for c in range(len(re)):
        ref[0, c : c + 1] = re[c]
        ref[0, SLOT + c : SLOT + c + 1] = im[c]
    ref[...] = jnp.broadcast_to(ref[0:1], ref.shape)


def wide(rows):
    return [jnp.broadcast_to(v, (LANES, 128)) for v in rows]


def chain(ends_ref, jr_ref, power, carry, down, start_ref=None):
    chunks = len(power[0])
    pr, pi = power
    cr, ci = carry
    order = range(LANES - 1, -1, -1) if down else range(LANES)
    for s in order:
        at = slice(s, s + 1)
        if start_ref is not None:
            put_rows(start_ref, at, cr, ci)
        er, ei = rows_of(ends_ref, at, chunks)
        alive = (jr_ref[at, :] < 0).astype(F32)
        cr, ci = (
            [er[c] + alive * (pr[c] * cr[c] - pi[c] * ci[c]) for c in range(chunks)],
            [ei[c] + alive * (pr[c] * ci[c] + pi[c] * cr[c]) for c in range(chunks)],
        )
    return cr, ci


def carry_in(ends_ref, table_ref, chunks):
    total = jnp.zeros((2 * SLOT, 128), F32)
    for e in range(ends_ref.shape[0]):
        end = ends_ref[e]
        turned = jnp.concatenate([end[SLOT:], end[:SLOT]], axis=0)
        total += table_ref[0, e] * end + table_ref[1, e] * turned
    return (
        [total[c : c + 1] for c in range(chunks)],
        [total[SLOT + c : SLOT + c + 1] for c in range(chunks)],
    )


def scan_tile(src_ref, st_ref, decay, jr_ref, first_step, steps, down, emit=None, unroll=4):
    chunks = chunk_count(src_ref)
    dr, di = wide(decay[0]), wide(decay[1])
    jr = jr_ref[...]
    re, im = rows_of(st_ref, slice(0, LANES), chunks)

    def one(step, re, im):
        at = pl.ds(pl.multiple_of(step * LANES, LANES), LANES)
        br, bi = rows_of(src_ref, at, chunks)
        live = jr != first_step + step
        nr, ni = [], []
        for c in range(chunks):
            xr = jnp.where(live, re[c], 0.0)
            xi = jnp.where(live, im[c], 0.0)
            nr.append(dr[c] * xr - di[c] * xi + br[c])
            ni.append(dr[c] * xi + di[c] * xr + bi[c])
        return nr, ni

    def body(i, carry):
        re, im = list(carry[:chunks]), list(carry[chunks : 2 * chunks])
        extra = carry[2 * chunks :]
        for q in range(unroll):
            n = 2 * (i * unroll + q)
            low_step = steps - 2 - n if down else n
            a, b = (low_step + 1, low_step) if down else (low_step, low_step + 1)
            r1, i1 = one(a, re, im)
            r2, i2 = one(b, r1, i1)
            if emit is not None:
                pair = ((r2, i2), (r1, i1)) if down else ((r1, i1), (r2, i2))
                extra = emit(low_step, pair, extra)
            re, im = r2, i2
        return tuple(re) + tuple(im) + tuple(extra)

    start = tuple(re) + tuple(im)
    if emit is not None:
        start = start + tuple(emit(None, None, None))
    out = lax.fori_loop(0, steps // (2 * unroll), body, start)
    put_rows(st_ref, slice(0, LANES), list(out[:chunks]), list(out[chunks : 2 * chunks]))
    return out[2 * chunks :]


def store_pair(ref, low_step, first, second):
    at = pl.ds(pl.multiple_of(low_step * LANES, 2 * LANES), 2 * LANES)
    re = [jnp.concatenate([p, q], axis=0).astype(BF16) for p, q in zip(first[0], second[0])]
    im = [jnp.concatenate([p, q], axis=0).astype(BF16) for p, q in zip(first[1], second[1])]
    put_rows(ref, at, re, im)


def disc_row(disc_ref, row, chunks, conj=False):
    re, im = rows_of(disc_ref, slice(row, row + 1), chunks)
    return (re, [-v for v in im]) if conj else (re, im)


def column_sum(value):
    rows, width = value.shape
    return jnp.sum(jnp.sum(value.reshape(rows // 8, 8, width), axis=0), axis=0, keepdims=True)


def permute_in(block, order_ref):
    runs, steps, width = block.shape
    span = order_ref.shape[0] // runs
    out = []
    for k in range(steps // span):
        part = block[:, k * span : (k + 1) * span, :].reshape(runs * span, width)
        out.append(jnp.dot(order_ref[...], part, preferred_element_type=F32))
    return out[0] if len(out) == 1 else jnp.concatenate(out, axis=0)


def permute_out(value, order_ref, out_ref):
    rows, width = value.shape
    size = order_ref.shape[0]
    span = size // LANES
    high = value.astype(BF16)
    low = (value - high.astype(F32)).astype(BF16)
    for k in range(rows // size):
        at = slice(k * size, (k + 1) * size)
        back = lax.dot_general(order_ref[...], high[at], TN, preferred_element_type=F32)
        back += lax.dot_general(order_ref[...], low[at], TN, preferred_element_type=F32)
        out_ref[:, k * span : (k + 1) * span, :] = back.reshape(LANES, span, width)


def expm1(value):
    acc = jnp.full_like(value, 1.0 / 479001600.0)
    for n in (39916800.0, 3628800.0, 362880.0, 40320.0, 5040.0, 720.0, 120.0, 24.0, 6.0, 2.0, 1.0):
        acc = acc * value + 1.0 / n
    return jnp.where(value > -1.0, acc * value, jnp.exp(value) - 1.0)


def prep_kernel(
    rows, axes, starts_ref, rate_ref, step_ref, freq_ref,
    disc_ref, table_ref, cut_ref, order_ref,
):
    devices = 2 ** len(axes)
    total = rows * devices
    run = rows // LANES
    half = rate_ref.shape[-1]
    me = 0
    for axis in axes:
        me = 2 * me + lax.axis_index(axis)
    starts = [starts_ref[k] for k in range(starts_ref.shape[0])]

    base = me * rows + run * lax.broadcasted_iota(jnp.int32, (LANES, 128), 0)
    up = jnp.full((LANES, 128), -1, jnp.int32)
    down = up
    for begin in starts + [total]:
        rel = begin - base
        up = jnp.maximum(up, jnp.where((rel >= 0) & (rel < run), rel, -1))
        down = jnp.maximum(down, jnp.where((rel >= 1) & (rel <= run), rel - 1, -1))
    cut_ref[0] = up
    cut_ref[1] = down

    size = order_ref.shape[0]
    span = size // LANES
    to = lax.broadcasted_iota(jnp.int32, (size, size), 0)
    back = lax.broadcasted_iota(jnp.int32, (size, size), 1)
    order_ref[...] = ((to % LANES) * span + to // LANES == back).astype(F32).astype(BF16)

    source = lax.broadcasted_iota(jnp.int32, (devices, half), 0)
    for l in range(LAYERS):
        row = slice(l, l + 1)
        rate, freq = rate_ref[row], freq_ref[row]
        step_size = jnp.exp(step_ref[row])
        real_angle = -rate * step_size
        imag_angle = freq * step_size
        magnitude = jnp.exp(real_angle)
        cosine, sine = jnp.cos(imag_angle), jnp.sin(imag_angle)
        minus_real = expm1(real_angle) * cosine - 2.0 * jnp.sin(0.5 * imag_angle) ** 2
        minus_imag = magnitude * sine
        modulus = rate * rate + freq * freq
        disc_ref[l, 0:1, :half] = magnitude * cosine
        disc_ref[l, 0:1, half:] = minus_imag
        disc_ref[l, 1:2, :half] = (-rate * minus_real + freq * minus_imag) / modulus
        disc_ref[l, 1:2, half:] = (-rate * minus_imag - freq * minus_real) / modulus
        magnitude = jnp.exp(real_angle * float(run))
        disc_ref[l, 2:3, :half] = magnitude * jnp.cos(imag_angle * float(run))
        disc_ref[l, 2:3, half:] = magnitude * jnp.sin(imag_angle * float(run))
        disc_ref[l, 3:8] = jnp.zeros((5, 2 * half), F32)
        for back in range(2):
            going_down = (l + back) % 2 == 1
            if going_down:
                live, count = source > me, source - me - 1
            else:
                live, count = source < me, me - 1 - source
            for begin in starts:
                if going_down:
                    cut = ((begin > (me + 1) * rows).astype(jnp.int32) > 0) & (
                        source * rows >= begin
                    )
                else:
                    cut = ((begin < me * rows).astype(jnp.int32) > 0) & (
                        (source + 1) * rows <= begin
                    )
                live &= ~cut
            count = (jnp.maximum(count, 0) * rows).astype(F32)
            magnitude = jnp.where(live, jnp.exp(real_angle * count), 0.0)
            angle = imag_angle * count
            real = magnitude * jnp.cos(angle)
            imag = magnitude * jnp.sin(angle)
            imag = -imag if back else imag
            at = 2 * l + back
            table_ref[at] = jnp.zeros(table_ref.shape[1:], F32)
            for c in range(half // 128):
                table_ref[at, 0, :, c, :] = real[:, cols(c)]
                table_ref[at, 0, :, SLOT + c, :] = real[:, cols(c)]
                table_ref[at, 1, :, c, :] = -imag[:, cols(c)]
                table_ref[at, 1, :, SLOT + c, :] = imag[:, cols(c)]


def stats_kernel(tok_ref, order_ref, u_ref, stats_ref):
    value = permute_in(tok_ref[...], order_ref)
    u_ref[...] = value.astype(BF16)
    add_stats(stats_ref, value)


def add_stats(stats_ref, value):
    add_rows(stats_ref, column_sum(value), column_sum(value * value))


def add_rows(copies_ref, first, second):
    i, nt = pl.program_id(0), pl.num_programs(0)
    chunks = first.shape[1] // 128

    @pl.when(i == 0)
    def _():
        copies_ref[0] = jnp.zeros(copies_ref.shape[1:], F32)

    for c in range(chunks):
        copies_ref[0, c : c + 1] += first[:, cols(c)]
        copies_ref[0, SLOT + c : SLOT + c + 1] += second[:, cols(c)]

    @pl.when(i == nt - 1)
    def _():
        copies_ref[...] = jnp.broadcast_to(copies_ref[0:1], copies_ref.shape)


def summed(ref):
    total = jnp.sum(ref[...], axis=0)
    return tuple(
        jnp.concatenate([total[SLOT * k + c : SLOT * k + c + 1] for c in range(SLOT)], axis=1)
        for k in range(2)
    )


def drive_kernel(layer, down, tokens, *refs):
    (
        stat_ref, u_ref, gain_ref, bias_ref, skip_ref, win_ref, disc_ref, jr_ref,
        b_ref, end_ref, blk_ref, norm_ref,
    ) = refs
    i, nt = pl.program_id(0), pl.num_programs(0)
    steps = u_ref.shape[0] // LANES
    chunks = chunk_count(b_ref)
    half = chunks * 128

    @pl.when(i == 0)
    def _():
        total, squares = summed(stat_ref)
        row = slice(layer, layer + 1)
        mean = total / tokens
        inv = lax.rsqrt(squares / tokens - mean * mean + EPSILON)
        norm_ref[0:1] = mean
        norm_ref[1:2] = inv
        norm_ref[2:3] = inv * gain_ref[row]
        norm_ref[3:4] = bias_ref[row]
        norm_ref[4:5] = skip_ref[row]
        norm_ref[5:8] = jnp.zeros((3, norm_ref.shape[1]), F32)
        blk_ref[...] = jnp.zeros_like(blk_ref)

    u = u_ref[...].astype(F32)
    normed = (u - norm_ref[0:1]) * norm_ref[2:3] + norm_ref[3:4]
    drive = jnp.dot(normed.astype(BF16), win_ref[...], preferred_element_type=F32)
    fr, fi = disc_ref[1:2, :half], disc_ref[1:2, half:]
    re, im = drive[:, :half], drive[:, half:]
    b_ref[:, :half] = re * fr - im * fi
    b_ref[:, half:] = re * fi + im * fr
    tile = nt - 1 - i if down else i
    scan_tile(b_ref, blk_ref, disc_row(disc_ref, 0, chunks), jr_ref, tile * steps, steps, down)

    @pl.when(i == nt - 1)
    def _():
        zero = [jnp.zeros((1, 128), F32)] * chunks
        cr, ci = chain(blk_ref, jr_ref, disc_row(disc_ref, 2, chunks), (zero, zero), down)
        put_copies(end_ref, cr, ci)


def states_of(ends_ref, table_ref, b_ref, blk_ref, disc_ref, jr_ref, low_ref, st_ref, down):
    i, nt = pl.program_id(0), pl.num_programs(0)
    chunks = chunk_count(b_ref)
    steps = b_ref.shape[0] // LANES

    @pl.when(i == 0)
    def _():
        carry = carry_in(ends_ref, table_ref, chunks)
        chain(blk_ref, jr_ref, disc_row(disc_ref, 2, chunks), carry, down, st_ref)

    def emit(low_step, pair, extra):
        if pair is None:
            return ()
        (first, second) = pair
        store_pair(low_ref, low_step, first, second)
        return ()

    tile = nt - 1 - i if down else i
    scan_tile(
        b_ref, st_ref, disc_row(disc_ref, 0, chunks), jr_ref, tile * steps, steps, down, emit
    )


def gelu_parts(mixed):
    square = mixed * mixed
    tanh = jnp.tanh(mixed * (GELU_A + (GELU_A * GELU_B) * square))
    half_up = 0.5 + 0.5 * tanh
    return square, tanh, half_up


def gelu_slope(mixed, square, tanh, half_up):
    return half_up + (mixed * (0.5 - 0.5 * tanh * tanh)) * (
        GELU_A + (3.0 * GELU_A * GELU_B) * square
    )


def sigmoid(value):
    return 0.5 + 0.5 * jnp.tanh(0.5 * value)


def forward_kernel(down, *refs):
    (
        ends_ref, table_ref, b_ref, blk_ref, disc_ref, jr_ref, u_ref, norm_ref, wout_ref, wgate_ref,
        next_ref, low_ref, mixed_ref, gate_ref, stats_ref, st_ref,
    ) = refs
    states_of(ends_ref, table_ref, b_ref, blk_ref, disc_ref, jr_ref, low_ref, st_ref, down)
    u = u_ref[...].astype(F32)
    normed = (u - norm_ref[0:1]) * norm_ref[2:3] + norm_ref[3:4]
    mixed = jnp.dot(low_ref[...], wout_ref[...], preferred_element_type=F32)
    mixed += norm_ref[4:5] * normed
    _, _, half_up = gelu_parts(mixed)
    act = mixed * half_up
    gate = sigmoid(jnp.dot(act.astype(BF16), wgate_ref[...], preferred_element_type=F32))
    after = u + act * gate
    next_ref[...] = after
    mixed_ref[...] = mixed.astype(mixed_ref.dtype)
    gate_ref[...] = gate.astype(gate_ref.dtype)
    add_stats(stats_ref, after)


def accumulate(ref, value):
    @pl.when(pl.program_id(0) == 0)
    def _():
        ref[...] = value

    @pl.when(pl.program_id(0) != 0)
    def _():
        ref[...] += value


def gate_backward(g, mixed, gate, normed, low_ref, wout_ref, wgate_ref, outs, kept=None):
    pg_ref, sg_ref, wsum_ref, ssum_ref = outs
    states, width = wout_ref.shape
    square, tanh, half_up = gelu_parts(mixed) if kept is None else kept
    act = mixed * half_up
    g_gate = g * gate
    logit_grad = (g_gate * act * (1.0 - gate)).astype(BF16)
    accumulate(
        wsum_ref.at[states : states + width],
        lax.dot_general(act.astype(BF16), logit_grad, TN, preferred_element_type=F32),
    )
    act_grad = g_gate + lax.dot_general(
        logit_grad, wgate_ref[...], NT, preferred_element_type=F32
    )
    mixed_grad = act_grad * gelu_slope(mixed, square, tanh, half_up)
    accumulate(ssum_ref, column_sum(mixed_grad * normed))
    proj_grad = mixed_grad.astype(BF16)
    pg_ref[...] = proj_grad
    accumulate(
        wsum_ref.at[:states],
        lax.dot_general(low_ref[...], proj_grad, TN, preferred_element_type=F32),
    )
    sg_ref[...] = lax.dot_general(proj_grad, wout_ref[...], NT, preferred_element_type=F32)


def turn_kernel(down, *refs):
    (
        ends_ref, table_ref, b_ref, blk_ref, disc_ref, jr_ref, jo_ref, u_ref, norm_ref, wout_ref, wgate_ref,
        gout_ref, order_ref,
        out_ref, low_ref, g_ref, pg_ref, sg_ref, wsum_ref, end_ref, ablk_ref,
        st_ref, w_ref,
    ) = refs
    sums = wout_ref.shape[0] + wout_ref.shape[1]
    ssum_ref = wsum_ref.at[sums : sums + 1]
    i, nt = pl.program_id(0), pl.num_programs(0)
    chunks = chunk_count(b_ref)
    half = chunks * 128
    steps = b_ref.shape[0] // LANES
    tile = nt - 1 - i if down else i
    states_of(ends_ref, table_ref, b_ref, blk_ref, disc_ref, jr_ref, low_ref, st_ref, down)
    u = u_ref[...]
    normed = (u - norm_ref[0:1]) * norm_ref[2:3] + norm_ref[3:4]
    mixed = jnp.dot(low_ref[...], wout_ref[...], preferred_element_type=F32)
    mixed += norm_ref[4:5] * normed
    kept = gelu_parts(mixed)
    act = mixed * kept[2]
    gate = sigmoid(jnp.dot(act.astype(BF16), wgate_ref[...], preferred_element_type=F32))
    permute_out(u + act * gate, order_ref, out_ref)
    g = permute_in(gout_ref[...], order_ref)
    g_ref[...] = g.astype(BF16)
    gate_backward(
        g, mixed, gate, normed, low_ref, wout_ref, wgate_ref,
        (pg_ref, sg_ref, wsum_ref, ssum_ref), kept,
    )

    @pl.when(i == 0)
    def _():
        wsum_ref[sums + 1 :] = jnp.zeros((7, wsum_ref.shape[1]), F32)
        w_ref[:, :half] = jnp.ones((LANES, half), F32)
        w_ref[:, half:] = jnp.zeros((LANES, half), F32)
        ablk_ref[...] = jnp.zeros_like(ablk_ref)

    dr, di = disc_row(disc_ref, 0, chunks, conj=True)
    dr, di = wide(dr), wide(di)
    jo = jo_ref[...]
    unroll = 4

    def body(k, carry):
        wr, wi, ar, ai = (list(carry[n * chunks : (n + 1) * chunks]) for n in range(4))
        for q in range(unroll):
            n = k * unroll + q
            step = steps - 1 - n if down else n
            at = pl.ds(pl.multiple_of(step * LANES, LANES), LANES)
            sr, si = rows_of(sg_ref, at, chunks)
            live = jo != tile * steps + step
            for c in range(chunks):
                ar[c] = ar[c] + (wr[c] * sr[c] - wi[c] * si[c])
                ai[c] = ai[c] + (wr[c] * si[c] + wi[c] * sr[c])
                xr = jnp.where(live, wr[c], 0.0)
                xi = jnp.where(live, wi[c], 0.0)
                wr[c] = xr * dr[c] - xi * di[c]
                wi[c] = xr * di[c] + xi * dr[c]
        return tuple(wr) + tuple(wi) + tuple(ar) + tuple(ai)

    wr, wi = rows_of(w_ref, slice(0, LANES), chunks)
    ar, ai = rows_of(ablk_ref, slice(0, LANES), chunks)
    out = lax.fori_loop(
        0, steps // unroll, body, tuple(wr) + tuple(wi) + tuple(ar) + tuple(ai)
    )
    wr, wi, ar, ai = (list(out[n * chunks : (n + 1) * chunks]) for n in range(4))
    put_rows(w_ref, slice(0, LANES), wr, wi)
    put_rows(ablk_ref, slice(0, LANES), ar, ai)

    @pl.when(i == nt - 1)
    def _():
        zero = [jnp.zeros((1, 128), F32)] * chunks
        power = disc_row(disc_ref, 2, chunks, conj=True)
        cr, ci = chain(ablk_ref, jo_ref, power, (zero, zero), not down)
        put_copies(end_ref, cr, ci)


def adjoint_kernel(down, last, *refs):
    (
        ends_ref, table_ref, sg_ref, ablk_ref, disc_ref, jr_ref, low_ref, u_ref, norm_ref, pg_ref, g_ref,
        win_ref, order_ref, *refs
    ) = refs
    if last:
        (ssum_ref, res_ref, sums_ref, st_ref, dg_ref, ax_ref, nsum_ref, isum_ref) = refs
    else:
        (res_ref, sums_ref, nsum_ref, st_ref, dg_ref, ax_ref) = refs
        isum_ref = sums_ref.at[: win_ref.shape[0]]
    width, states = win_ref.shape
    i, nt = pl.program_id(0), pl.num_programs(0)
    chunks = chunk_count(sg_ref)
    half = chunks * 128
    steps = sg_ref.shape[0] // LANES
    tile = nt - 1 - i if down else i

    @pl.when(i == 0)
    def _():
        carry = carry_in(ends_ref, table_ref, chunks)
        power = disc_row(disc_ref, 2, chunks, conj=True)
        chain(ablk_ref, jr_ref, power, carry, down, st_ref)
        ax_ref[...] = jnp.zeros_like(ax_ref)

    fr, fi = disc_row(disc_ref, 1, chunks)
    fr, fi = wide(fr), wide(fi)

    def emit(low_step, pair, extra):
        if pair is None:
            re, im = rows_of(ax_ref, slice(0, LANES), chunks)
            return tuple(re) + tuple(im)
        sums_r, sums_i = list(extra[:chunks]), list(extra[chunks:])
        at = pl.ds(pl.multiple_of(low_step * LANES, 2 * LANES), 2 * LANES)
        xr, xi = rows_of(low_ref, at, chunks)
        grads = []
        for which, (ar, ai) in enumerate(pair):
            gr, gi = [], []
            rows = slice(which * LANES, (which + 1) * LANES)
            for c in range(chunks):
                vr, vi = xr[c].astype(F32)[rows], xi[c].astype(F32)[rows]
                sums_r[c] = sums_r[c] + (ar[c] * vr + ai[c] * vi)
                sums_i[c] = sums_i[c] + (ai[c] * vr - ar[c] * vi)
                gr.append(ar[c] * fr[c] + ai[c] * fi[c])
                gi.append(ai[c] * fr[c] - ar[c] * fi[c])
            grads.append((gr, gi))
        store_pair(dg_ref, low_step, grads[0], grads[1])
        return tuple(sums_r) + tuple(sums_i)

    sums = scan_tile(
        sg_ref, st_ref, disc_row(disc_ref, 0, chunks, conj=True), jr_ref, tile * steps, steps,
        down, emit,
    )
    put_rows(ax_ref, slice(0, LANES), list(sums[:chunks]), list(sums[chunks:]))

    u = u_ref[...].astype(F32)
    centered = u - norm_ref[0:1]
    normed = (centered * norm_ref[2:3] + norm_ref[3:4]).astype(BF16)
    drive_grad = dg_ref[...]
    accumulate(
        isum_ref, lax.dot_general(normed, drive_grad, TN, preferred_element_type=F32)
    )
    normed_grad = lax.dot_general(drive_grad, win_ref[...], NT, preferred_element_type=F32)
    normed_grad += norm_ref[4:5] * pg_ref[...].astype(F32)
    add_rows(
        nsum_ref, column_sum(normed_grad), column_sum(normed_grad * centered) * norm_ref[1:2]
    )
    result = g_ref[...].astype(F32) + norm_ref[2:3] * normed_grad
    if last:
        permute_out(result, order_ref, res_ref)
    else:
        res_ref[...] = result

    @pl.when(i == nt - 1)
    def _():
        decays = jnp.sum(ax_ref[...], axis=0, keepdims=True)
        wr, wi = win_ref[:, :half].astype(F32), win_ref[:, half:].astype(F32)
        gr, gi = isum_ref[:, :half], isum_ref[:, half:]
        re = jnp.sum(wr * gr + wi * gi, axis=0, keepdims=True)
        im = jnp.sum(wr * gi - wi * gr, axis=0, keepdims=True)
        gr, gi = disc_ref[1:2, :half], disc_ref[1:2, half:]
        scale = 1.0 / (gr * gr + gi * gi)
        factors = ((re * gr - im * gi) * scale, (re * gi + im * gr) * scale)
        if last:
            rows = width // BLOCKS
            first = rows + rows // 2
            for b in range(BLOCKS):
                at = b * rows
                sums_ref[b, :rows] = isum_ref[at : at + rows, :width]
                sums_ref[b, rows:first, : states - width] = isum_ref[at : at + rows // 2, width:]
                sums_ref[b, rows:first, states - width :] = isum_ref[
                    at + rows // 2 : at + rows, width:
                ]
                sums_ref[b, first:] = jnp.zeros((SMALL, width), F32)
            small = [nsum_ref[0]] + [ssum_ref[:, cols(c)] for c in range(width // 128)]
            small += [decays[:, cols(c)] for c in range(2 * chunks)]
            small += [v[:, cols(c)] for v in factors for c in range(chunks)]
            at = first
            for row in small:
                sums_ref[0, at : at + row.shape[0], :128] = row
                at += row.shape[0]
        else:
            sums_ref[width : width + 8] = jnp.zeros((8, states), F32)
            sums_ref[width : width + 1] = decays
            sums_ref[width + 1 : width + 2, :half] = factors[0]
            sums_ref[width + 1 : width + 2, half:] = factors[1]


def back_kernel(down, tokens, *refs):
    (
        sums_ref, r_ref, up_ref, up_norm_ref, mixed_ref, gate_ref, low_ref, u_ref, norm_ref, wout_ref,
        wgate_ref, disc_ref, jo_ref,
        g_ref, pg_ref, sg_ref, blocks_ref, ssum_ref, end_ref, ablk_ref, nsum_ref, bsum_ref, wsum_ref,
    ) = refs
    i, nt = pl.program_id(0), pl.num_programs(0)
    chunks = chunk_count(sg_ref)
    steps = sg_ref.shape[0] // LANES
    tile = nt - 1 - i if down else i

    @pl.when(i == 0)
    def _():
        nsum_ref[...] = jnp.sum(sums_ref[...], axis=0)
        bsum_ref[0:1], bsum_ref[1:2] = summed(sums_ref)
        ablk_ref[...] = jnp.zeros_like(ablk_ref)

    scale = up_norm_ref[2:3] * (-1.0 / tokens)
    standard = (up_ref[...] - up_norm_ref[0:1]) * (scale * up_norm_ref[1:2] * bsum_ref[1:2])
    g = r_ref[...] + (standard + scale * bsum_ref[0:1])
    g_ref[...] = g
    u = u_ref[...].astype(F32)
    normed = (u - norm_ref[0:1]) * norm_ref[2:3] + norm_ref[3:4]
    gate_backward(
        g, mixed_ref[...].astype(F32), gate_ref[...].astype(F32), normed, low_ref, wout_ref,
        wgate_ref, (pg_ref, sg_ref, wsum_ref, ssum_ref),
    )
    decay = disc_row(disc_ref, 0, chunks, conj=True)
    scan_tile(sg_ref, ablk_ref, decay, jo_ref, tile * steps, steps, down)

    @pl.when(i == nt - 1)
    def _():
        zero = [jnp.zeros((1, 128), F32)] * chunks
        power = disc_row(disc_ref, 2, chunks, conj=True)
        cr, ci = chain(ablk_ref, jo_ref, power, (zero, zero), down)
        put_copies(end_ref, cr, ci)
        states, width = wout_ref.shape
        gates, outs = width // BLOCKS, states // BLOCKS
        for b in range(BLOCKS):
            blocks_ref[b, :gates] = wsum_ref[states + b * gates : states + (b + 1) * gates]
            blocks_ref[b, gates:] = wsum_ref[b * outs : (b + 1) * outs]


def last_kernel(
    tokens, piece_ref, small_ref, out1_ref, gate1_ref, skip1_ref, in1_ref, decay1_ref, norm1_ref,
    disc_ref, rate_ref, step_ref, freq_ref, r_ref, tok_ref, norm_ref,
    grad_in_ref, gain_ref, bias_ref, drate_ref, dstep_ref, dfreq_ref, in_ref, out_ref, skip_ref,
    gate_ref,
):
    gates, width = gate1_ref.shape
    outs = out1_ref.shape[0]
    states = in1_ref.shape[1]
    half = states // 2
    left = states - width
    gate_ref[0], gate_ref[1] = piece_ref[:gates], gate1_ref[...]
    out_ref[0], out_ref[1] = piece_ref[gates : gates + outs], out1_ref[...]
    at = gates + outs
    in_ref[0, :, :width] = piece_ref[at : at + gates]
    at += gates
    in_ref[0, : gates // 2, width:] = piece_ref[at : at + gates // 2, :left]
    in_ref[0, gates // 2 :, width:] = piece_ref[at : at + gates // 2, left:]
    in_ref[1] = in1_ref[...]

    def row(ref, first, count):
        return jnp.concatenate([ref[first + c : first + c + 1, :128] for c in range(count)], axis=1)

    count = width // 128
    bias, gain = row(small_ref, 0, count), row(small_ref, count, count)
    scale = norm_ref[2:3] * (-1.0 / tokens)
    grad_in_ref[...] = r_ref[...] + (
        (tok_ref[...].astype(F32) - norm_ref[0:1]) * (scale * norm_ref[1:2] * gain) + scale * bias
    )

    @pl.when(pl.program_id(0) == 0)
    def _():
        bias_ref[0:1], gain_ref[0:1] = bias, gain
        bias_ref[1:2], gain_ref[1:2] = row(norm1_ref, 0, count), row(norm1_ref, count, count)
        skip_ref[0:1], skip_ref[1:2] = row(small_ref, 2 * count, count), skip1_ref[0:1]
        at = 3 * count
        lanes = half // 128
        for l in range(LAYERS):
            if l == 0:
                ar, ai, sr, si = (row(small_ref, at + k * lanes, lanes) for k in range(4))
            else:
                ar, ai = decay1_ref[0:1, :half], decay1_ref[0:1, half:]
                sr, si = decay1_ref[1:2, :half], decay1_ref[1:2, half:]
            dr, di = disc_ref[l, 0:1, :half], disc_ref[l, 0:1, half:]
            fr, fi = disc_ref[l, 1:2, :half], disc_ref[l, 1:2, half:]
            here = slice(l, l + 1)
            rate, freq, step = rate_ref[here], freq_ref[here], jnp.exp(step_ref[here])
            tr = ar - (fr * sr + fi * si)
            ti = ai - (fr * si - fi * sr)
            size = 1.0 / (dr * dr + di * di)
            gr, gi = (tr * dr - ti * di) * size, (tr * di + ti * dr) * size
            mr, mi = -rate * fr - freq * fi, freq * fr - rate * fi
            size = 1.0 / (rate * rate + freq * freq)
            gr += (-rate * sr - freq * si) * size
            gi += (freq * sr - rate * si) * size
            both = 2.0 * (fr * sr + fi * si)
            gx = gr * dr + gi * di
            gy = gi * dr - gr * di
            drate_ref[here] = (-mr * sr - mi * si - both * rate) * size - step * gx
            dfreq_ref[here] = (mi * sr - mr * si - both * freq) * size + step * gy
            dstep_ref[here] = step * (freq * gy - rate * gx)


def whole(array):
    shape = array.shape
    return pl.BlockSpec(shape, lambda i: (0,) * len(shape))


def tile_spec(rows, width, nt, down):
    if down:
        return pl.BlockSpec((rows, width), lambda i: (nt - 1 - i, 0))
    return pl.BlockSpec((rows, width), lambda i: (i, 0))


def run_spec(steps, width, nt, down):
    if down:
        return pl.BlockSpec((LANES, steps, width), lambda i: (0, nt - 1 - i, 0))
    return pl.BlockSpec((LANES, steps, width), lambda i: (0, i, 0))


def call(kernel, nt, args, outs, scratch, macs, name):
    arrays = [a for a, _ in args]
    sizes = sum(a.size * a.dtype.itemsize for a in arrays + [a for a, _ in outs])
    return pl.pallas_call(
        kernel,
        grid=(nt,),
        in_specs=[whole(a) if s is None else s for a, s in args],
        out_specs=[whole(a) if s is None else s for a, s in outs],
        out_shape=[a for a, _ in outs],
        scratch_shapes=scratch,
        compiler_params=pltpu.CompilerParams(
            vmem_limit_bytes=VMEM_LIMIT, dimension_semantics=("arbitrary",)
        ),
        cost_estimate=pl.CostEstimate(flops=2 * macs, bytes_accessed=sizes, transcendentals=0),
        name=name,
    )(*arrays)


def shape(*dims, dtype=F32):
    return jax.ShapeDtypeStruct(dims, dtype)


def body(
    axes,
    tokens_in,
    seq_starts,
    norm_gain,
    norm_bias,
    decay_rate,
    step_log,
    frequency,
    in_proj,
    out_proj,
    skip_gain,
    gate_proj,
    grad_out,
):
    rows, width = tokens_in.shape
    states = in_proj.shape[-1]
    devices = 2 ** len(axes)
    tokens = float(rows * devices)
    run = rows // LANES
    steps = min(64, run)
    tile = steps * LANES
    nt = rows // tile
    span = min(32, steps)
    discs, tables, cuts, order = pl.pallas_call(
        functools.partial(prep_kernel, rows, axes),
        in_specs=[pl.BlockSpec(memory_space=pltpu.SMEM)]
        + [pl.BlockSpec(memory_space=pltpu.VMEM)] * 3,
        out_specs=[pl.BlockSpec(memory_space=pltpu.VMEM)] * 4,
        out_shape=[
            shape(LAYERS, 8, states), shape(2 * LAYERS, 2, devices, 2 * SLOT, 128),
            shape(2, LANES, 128, dtype=jnp.int32), shape(span * LANES, span * LANES, dtype=BF16),
        ],
        compiler_params=pltpu.CompilerParams(vmem_limit_bytes=VMEM_LIMIT),
        name="prep",
    )(seq_starts, decay_rate, step_log, frequency)

    def tiles(array, down):
        return (array, tile_spec(tile, array.shape[-1], nt, down))

    def runs(array, down):
        return (array, run_spec(steps, array.shape[-1], nt, down))

    def full(array):
        return (array, None)

    def of(array, l):
        size = array.shape[1:]
        return (array, pl.BlockSpec((None,) + size, lambda i: (l,) + (0,) * len(size)))

    tokens_run = tokens_in.reshape(LANES, run, width)
    grad_run = grad_out.reshape(LANES, run, width)
    state_scratch = pltpu.VMEM((LANES, states), F32)
    cost = rows * width * states

    u0, stats = call(
        stats_kernel, nt, [runs(tokens_run, 0), full(order)],
        [tiles(shape(rows, width, dtype=BF16), 0), full(shape(devices, 2 * SLOT, 128))],
        [], cost // 2, "stats",
    )

    def drive(l, stream, stats):
        down = l % 2
        return call(
            functools.partial(drive_kernel, l, bool(down), tokens), nt,
            [full(gather_all(stats, axes)), tiles(stream, down), full(norm_gain), full(norm_bias), full(skip_gain), of(in_proj, l), of(discs, l),
               of(cuts, down)],
            [tiles(shape(rows, states), down), full(shape(devices, 2 * SLOT, 128)),
             full(shape(LANES, states)), full(shape(8, width))],
            [], 4 * cost, f"drive_{l}",
        )

    b0, end0, blk0, norm0 = drive(0, u0, stats)
    u1, low0, mixed0, gate0, stats = call(
        functools.partial(forward_kernel, False), nt,
        [full(gather_all(end0, axes)), of(tables, 2 * 0 + 0), tiles(b0, 0), full(blk0), of(discs, 0), of(cuts, 0),
           tiles(u0, 0), full(norm0), of(out_proj, 0), of(gate_proj, 0)],
        [tiles(shape(rows, width), 0), tiles(shape(rows, states, dtype=BF16), 0),
         tiles(shape(rows, width, dtype=BF16), 0), tiles(shape(rows, width, dtype=BF16), 0),
         full(shape(devices, 2 * SLOT, 128))],
        [state_scratch], 6 * cost, "forward_0",
    )

    b1, end1, blk1, norm1 = drive(1, u1, stats)
    (
        out, low1, g1, pg1, sg1, w_sum1, aend1, ablk1
    ) = call(
        functools.partial(turn_kernel, True), nt,
        [full(gather_all(end1, axes)), of(tables, 2 * 1 + 0), tiles(b1, 1), full(blk1), of(discs, 1), of(cuts, 1),
           of(cuts, 0), tiles(u1, 1), full(norm1), of(out_proj, 1), of(gate_proj, 1),
           runs(grad_run, 1), full(order)],
        [runs(shape(LANES, run, width), 1), tiles(shape(rows, states, dtype=BF16), 1),
         tiles(shape(rows, width, dtype=BF16), 1), tiles(shape(rows, width, dtype=BF16), 1),
         tiles(shape(rows, states), 1), full(shape(states + width + 8, width)),
         full(shape(devices, 2 * SLOT, 128)), full(shape(LANES, states))],
        [state_scratch, state_scratch], 16 * cost, "turn_1",
    )

    def adjoint(l, sg, ablk, ends, low, stream, norm, pg, g, skip_sum=None):
        down = 1 - l % 2
        last = l == 0
        args = [
            full(ends), of(tables, 2 * l + 1), tiles(sg, down), full(ablk), of(discs, l),
            of(cuts, down), tiles(low, down), tiles(stream, down), full(norm), tiles(pg, down),
            tiles(g, down), of(in_proj, l), full(order),
        ]
        scratch = [state_scratch, pltpu.VMEM((tile, states), BF16), state_scratch]
        if last:
            args.append(full(skip_sum))
            outs = [
                runs(shape(LANES, run, width), down),
                full(shape(BLOCKS, (width + width // 2) // BLOCKS + SMALL, width)),
            ]
            scratch += [pltpu.VMEM((1, 2 * SLOT, 128), F32), pltpu.VMEM((width, states), F32)]
        else:
            outs = [
                tiles(shape(rows, width), down), full(shape(width + 8, states)),
                full(shape(devices, 2 * SLOT, 128)),
            ]
        return call(
            functools.partial(adjoint_kernel, bool(down), last), nt, args, outs, scratch,
            8 * cost, f"adjoint_{l}",
        )

    r1, in_sum1, norm_sum1 = adjoint(
        1, sg1, ablk1, gather_all(aend1, axes), low1, u1, norm1, pg1, g1
    )

    def lower(r1, norm_sum1):
        (
            g0, pg0, sg0, w_sum0, skip_sum0, aend0, ablk0, small1, _
        ) = call(
            functools.partial(back_kernel, True, tokens), nt,
            [full(gather_all(norm_sum1, axes)), tiles(r1, 1), tiles(u1, 1), full(norm1),
             tiles(mixed0, 1), tiles(gate0, 1), tiles(low0, 1), tiles(u0, 1), full(norm0),
             of(out_proj, 0), of(gate_proj, 0), of(discs, 0), of(cuts, 1)],
            [tiles(shape(rows, width), 1), tiles(shape(rows, width, dtype=BF16), 1),
             tiles(shape(rows, states), 1),
             full(shape(BLOCKS, (states + width) // BLOCKS, width)), full(shape(1, width)), full(shape(devices, 2 * SLOT, 128)),
             full(shape(LANES, states)), full(shape(2 * SLOT, 128)), full(shape(2, width))],
            [pltpu.VMEM((states + width, width), F32)], 12 * cost, "back_0",
        )
        core, chips, *others = phases(axes)
        w_sum0 = w_sum0.reshape(-1, width)
        ends, part = lax.optimization_barrier(
            (gather_all(aend0, axes), scatter_sum(w_sum0, core))
        )
        part = scatter_sum(part, chips)
        r0, in_sum0 = adjoint(0, sg0, ablk0, ends, low0, u0, norm0, pg0, g0, skip_sum0)
        in_sum0, part = lax.optimization_barrier((in_sum0, part))
        in_part = scatter_sum(scatter_sum(in_sum0.reshape(-1, width), core), chips)
        part = sum_all(jnp.concatenate([part, in_part], axis=0), others)
        pieces = gather_rows(gather_rows(part, chips), core)
        return r0.reshape(rows, width), small1, pieces.reshape(BLOCKS, -1, width)

    piece = (2 * width + states + width // 2) // BLOCKS + SMALL

    def nothing(r1, norm_sum1):
        return (
            jnp.zeros((rows, width), F32),
            jnp.zeros((2 * SLOT, 128), F32),
            jnp.zeros((BLOCKS, piece, width), F32),
        )

    w_all1, in_all1 = lax.psum((w_sum1, in_sum1), axes)
    r0, norm_all1, pieces = lax.cond(seq_starts[0] == 0, lower, nothing, r1, norm_sum1)

    gates, outs = width // BLOCKS, states // BLOCKS

    def block(array, *dims, at=lambda i: (i, 0)):
        return (array, pl.BlockSpec(dims, at))

    def flat(array, count):
        return block(array, count, array.shape[1])

    (
        grad_in, gain_grad, bias_grad, rate_grad, step_grad, freq_grad, in_grad, out_grad,
        skip_grad, gate_grad,
    ) = call(
        functools.partial(last_kernel, tokens), BLOCKS,
        [block(pieces, None, piece, width, at=lambda i: (i, 0, 0)),
         block(pieces, None, SMALL, width, at=lambda i: (0, piece // SMALL - 1, 0)),
         flat(w_all1, outs),
         block(w_all1, gates, width, at=lambda i: (states // gates + i, 0)),
         block(w_all1, 8, width, at=lambda i: ((states + width) // 8, 0)),
         flat(in_all1, gates),
         block(in_all1, 8, states, at=lambda i: (width // 8, 0)),
         full(norm_all1), full(discs), full(decay_rate), full(step_log), full(frequency),
         flat(r0, rows // BLOCKS), flat(tokens_in, rows // BLOCKS), full(norm0)],
        [flat(shape(rows, width), rows // BLOCKS), full(shape(LAYERS, width)),
         full(shape(LAYERS, width)), full(shape(LAYERS, states // 2)),
         full(shape(LAYERS, states // 2)), full(shape(LAYERS, states // 2)),
         block(shape(LAYERS, width, states), LAYERS, gates, states, at=lambda i: (0, i, 0)),
         block(shape(LAYERS, states, width), LAYERS, outs, width, at=lambda i: (0, i, 0)),
         full(shape(LAYERS, width)),
         block(shape(LAYERS, width, width), LAYERS, gates, width, at=lambda i: (0, i, 0))],
        [], cost, "last",
    )
    return (
        out.reshape(rows, width),
        grad_in,
        gain_grad,
        bias_grad,
        rate_grad,
        step_grad,
        freq_grad,
        in_grad,
        out_grad,
        skip_grad,
        gate_grad,
    )


def solution(mesh):
    bits = mesh.devices.size.bit_length() - 1
    axes = tuple("b%d" % k for k in range(bits))
    binary = Mesh(mesh.devices.reshape((2,) * bits), axes)
    rows = P(axes, None)
    return jax.shard_map(
        functools.partial(body, axes),
        mesh=binary,
        in_specs=(rows,) + (P(),) * 10 + (rows,),
        out_specs=(rows, rows) + (P(),) * 9,
        check_vma=False,
    )
```

```python
import functools

import jax
import jax.numpy as jnp
from jax import lax
from jax.experimental import pallas as pl
from jax.experimental.pallas import tpu as pltpu
from jax.sharding import Mesh, PartitionSpec as P

LAYERS = 2
EPSILON = 1e-05
CHUNK = 32
SMALL = 32
BLOCKS = 8
SLOT = 4
LANES = 8
VMEM_LIMIT = 30 * 1024 * 1024
GELU_A = 0.7978845608028654
GELU_B = 0.044715
NT = (((1,), (1,)), ((), ()))
TN = (((0,), (0,)), ((), ()))
F32 = jnp.float32
BF16 = jnp.bfloat16


def gather_all(copies, axes):
    return lax.all_to_all(copies, axes, 0, 0)


def scatter_sum(value, axes):
    count = 2 ** len(axes)
    pieces = value.reshape((count, value.shape[0] // count) + value.shape[1:])
    return jnp.sum(lax.all_to_all(pieces, axes, 0, 0), axis=0)


def gather_rows(value, axes):
    count = 2 ** len(axes)
    copies = jnp.broadcast_to(value, (count,) + value.shape)
    return lax.all_to_all(copies, axes, 0, 0).reshape((count * value.shape[0],) + value.shape[1:])


def phases(axes):
    left, out = list(axes), [(axes[-1],)]
    left = left[:-1]
    while left:
        out.append(tuple(left[-2:]))
        left = left[:-2]
    return out


def sum_all(value, parts):
    for part in parts:
        value = scatter_sum(value, part)
    for part in reversed(parts):
        value = gather_rows(value, part)
    return value


def cols(c):
    return slice(c * 128, (c + 1) * 128)


def chunk_count(ref):
    return ref.shape[-1] // 256


def rows_of(ref, at, chunks):
    half = chunks * 128
    re = [ref[at, c * 128 : (c + 1) * 128] for c in range(chunks)]
    im = [ref[at, half + c * 128 : half + (c + 1) * 128] for c in range(chunks)]
    return re, im


def put_rows(ref, at, re, im):
    chunks = len(re)
    half = chunks * 128
    for c in range(chunks):
        ref[at, c * 128 : (c + 1) * 128] = re[c]
        ref[at, half + c * 128 : half + (c + 1) * 128] = im[c]


def put_copies(ref, re, im):
    ref[0] = jnp.zeros(ref.shape[1:], F32)
    for c in range(len(re)):
        ref[0, c : c + 1] = re[c]
        ref[0, SLOT + c : SLOT + c + 1] = im[c]
    ref[...] = jnp.broadcast_to(ref[0:1], ref.shape)


def wide(rows):
    return [jnp.broadcast_to(v, (LANES, 128)) for v in rows]


def chain(ends_ref, jr_ref, power, carry, down, start_ref=None):
    chunks = len(power[0])
    pr, pi = power
    cr, ci = carry
    order = range(LANES - 1, -1, -1) if down else range(LANES)
    for s in order:
        at = slice(s, s + 1)
        if start_ref is not None:
            put_rows(start_ref, at, cr, ci)
        er, ei = rows_of(ends_ref, at, chunks)
        alive = (jr_ref[at, :] < 0).astype(F32)
        cr, ci = (
            [er[c] + alive * (pr[c] * cr[c] - pi[c] * ci[c]) for c in range(chunks)],
            [ei[c] + alive * (pr[c] * ci[c] + pi[c] * cr[c]) for c in range(chunks)],
        )
    return cr, ci


def carry_in(ends_ref, table_ref, chunks):
    total = jnp.zeros((2 * SLOT, 128), F32)
    for e in range(ends_ref.shape[0]):
        end = ends_ref[e]
        turned = jnp.concatenate([end[SLOT:], end[:SLOT]], axis=0)
        total += table_ref[0, e] * end + table_ref[1, e] * turned
    return (
        [total[c : c + 1] for c in range(chunks)],
        [total[SLOT + c : SLOT + c + 1] for c in range(chunks)],
    )


def scan_tile(src_ref, st_ref, decay, jr_ref, first_step, steps, down, emit=None, unroll=4):
    chunks = chunk_count(src_ref)
    dr, di = wide(decay[0]), wide(decay[1])
    jr = jr_ref[...]
    re, im = rows_of(st_ref, slice(0, LANES), chunks)

    def one(step, re, im):
        at = pl.ds(pl.multiple_of(step * LANES, LANES), LANES)
        br, bi = rows_of(src_ref, at, chunks)
        live = jr != first_step + step
        nr, ni = [], []
        for c in range(chunks):
            xr = jnp.where(live, re[c], 0.0)
            xi = jnp.where(live, im[c], 0.0)
            nr.append(dr[c] * xr - di[c] * xi + br[c])
            ni.append(dr[c] * xi + di[c] * xr + bi[c])
        return nr, ni

    def body(i, carry):
        re, im = list(carry[:chunks]), list(carry[chunks : 2 * chunks])
        extra = carry[2 * chunks :]
        for q in range(unroll):
            n = 2 * (i * unroll + q)
            low_step = steps - 2 - n if down else n
            a, b = (low_step + 1, low_step) if down else (low_step, low_step + 1)
            r1, i1 = one(a, re, im)
            r2, i2 = one(b, r1, i1)
            if emit is not None:
                pair = ((r2, i2), (r1, i1)) if down else ((r1, i1), (r2, i2))
                extra = emit(low_step, pair, extra)
            re, im = r2, i2
        return tuple(re) + tuple(im) + tuple(extra)

    start = tuple(re) + tuple(im)
    if emit is not None:
        start = start + tuple(emit(None, None, None))
    out = lax.fori_loop(0, steps // (2 * unroll), body, start)
    put_rows(st_ref, slice(0, LANES), list(out[:chunks]), list(out[chunks : 2 * chunks]))
    return out[2 * chunks :]


def store_pair(ref, low_step, first, second):
    at = pl.ds(pl.multiple_of(low_step * LANES, 2 * LANES), 2 * LANES)
    re = [jnp.concatenate([p, q], axis=0).astype(BF16) for p, q in zip(first[0], second[0])]
    im = [jnp.concatenate([p, q], axis=0).astype(BF16) for p, q in zip(first[1], second[1])]
    put_rows(ref, at, re, im)


def disc_row(disc_ref, row, chunks, conj=False):
    re, im = rows_of(disc_ref, slice(row, row + 1), chunks)
    return (re, [-v for v in im]) if conj else (re, im)


def column_sum(value):
    rows, width = value.shape
    return jnp.sum(jnp.sum(value.reshape(rows // 8, 8, width), axis=0), axis=0, keepdims=True)


def permute_in(block, order_ref):
    runs, steps, width = block.shape
    span = order_ref.shape[0] // runs
    out = []
    for k in range(steps // span):
        part = block[:, k * span : (k + 1) * span, :].reshape(runs * span, width)
        out.append(jnp.dot(order_ref[...], part, preferred_element_type=F32))
    return out[0] if len(out) == 1 else jnp.concatenate(out, axis=0)


def permute_out(value, order_ref, out_ref):
    rows, width = value.shape
    size = order_ref.shape[0]
    span = size // LANES
    high = value.astype(BF16)
    low = (value - high.astype(F32)).astype(BF16)
    for k in range(rows // size):
        at = slice(k * size, (k + 1) * size)
        back = lax.dot_general(order_ref[...], high[at], TN, preferred_element_type=F32)
        back += lax.dot_general(order_ref[...], low[at], TN, preferred_element_type=F32)
        out_ref[:, k * span : (k + 1) * span, :] = back.reshape(LANES, span, width)


def expm1(value):
    acc = jnp.full_like(value, 1.0 / 479001600.0)
    for n in (39916800.0, 3628800.0, 362880.0, 40320.0, 5040.0, 720.0, 120.0, 24.0, 6.0, 2.0, 1.0):
        acc = acc * value + 1.0 / n
    return jnp.where(value > -1.0, acc * value, jnp.exp(value) - 1.0)


def prep_kernel(
    rows, axes, starts_ref, rate_ref, step_ref, freq_ref,
    disc_ref, table_ref, cut_ref, order_ref,
):
    devices = 2 ** len(axes)
    total = rows * devices
    run = rows // LANES
    half = rate_ref.shape[-1]
    me = 0
    for axis in axes:
        me = 2 * me + lax.axis_index(axis)
    starts = [starts_ref[k] for k in range(starts_ref.shape[0])]

    base = me * rows + run * lax.broadcasted_iota(jnp.int32, (LANES, 128), 0)
    up = jnp.full((LANES, 128), -1, jnp.int32)
    down = up
    for begin in starts + [total]:
        rel = begin - base
        up = jnp.maximum(up, jnp.where((rel >= 0) & (rel < run), rel, -1))
        down = jnp.maximum(down, jnp.where((rel >= 1) & (rel <= run), rel - 1, -1))
    cut_ref[0] = up
    cut_ref[1] = down

    size = order_ref.shape[0]
    span = size // LANES
    to = lax.broadcasted_iota(jnp.int32, (size, size), 0)
    back = lax.broadcasted_iota(jnp.int32, (size, size), 1)
    order_ref[...] = ((to % LANES) * span + to // LANES == back).astype(F32).astype(BF16)

    source = lax.broadcasted_iota(jnp.int32, (devices, half), 0)
    for l in range(LAYERS):
        row = slice(l, l + 1)
        rate, freq = rate_ref[row], freq_ref[row]
        step_size = jnp.exp(step_ref[row])
        real_angle = -rate * step_size
        imag_angle = freq * step_size
        magnitude = jnp.exp(real_angle)
        cosine, sine = jnp.cos(imag_angle), jnp.sin(imag_angle)
        minus_real = expm1(real_angle) * cosine - 2.0 * jnp.sin(0.5 * imag_angle) ** 2
        minus_imag = magnitude * sine
        modulus = rate * rate + freq * freq
        disc_ref[l, 0:1, :half] = magnitude * cosine
        disc_ref[l, 0:1, half:] = minus_imag
        disc_ref[l, 1:2, :half] = (-rate * minus_real + freq * minus_imag) / modulus
        disc_ref[l, 1:2, half:] = (-rate * minus_imag - freq * minus_real) / modulus
        magnitude = jnp.exp(real_angle * float(run))
        disc_ref[l, 2:3, :half] = magnitude * jnp.cos(imag_angle * float(run))
        disc_ref[l, 2:3, half:] = magnitude * jnp.sin(imag_angle * float(run))
        disc_ref[l, 3:8] = jnp.zeros((5, 2 * half), F32)
        powers = []
        for bit in range(len(axes)):
            magnitude = jnp.exp(real_angle * float(rows << bit))
            angle = imag_angle * float(rows << bit)
            powers.append((magnitude * jnp.cos(angle), magnitude * jnp.sin(angle)))
        for back in range(2):
            going_down = (l + back) % 2 == 1
            if going_down:
                live, count = source > me, source - me - 1
            else:
                live, count = source < me, me - 1 - source
            for begin in starts:
                if going_down:
                    cut = ((begin > (me + 1) * rows).astype(jnp.int32) > 0) & (
                        source * rows >= begin
                    )
                else:
                    cut = ((begin < me * rows).astype(jnp.int32) > 0) & (
                        (source + 1) * rows <= begin
                    )
                live &= ~cut
            count = jnp.maximum(count, 0)
            real = live.astype(F32)
            imag = jnp.zeros((devices, half), F32)
            for bit, (pr, pi) in enumerate(powers):
                use = (count & (1 << bit)) != 0
                pr, pi = jnp.where(use, pr, 1.0), jnp.where(use, pi, 0.0)
                real, imag = real * pr - imag * pi, real * pi + imag * pr
            imag = -imag if back else imag
            at = 2 * l + back
            table_ref[at] = jnp.zeros(table_ref.shape[1:], F32)
            for c in range(half // 128):
                table_ref[at, 0, :, c, :] = real[:, cols(c)]
                table_ref[at, 0, :, SLOT + c, :] = real[:, cols(c)]
                table_ref[at, 1, :, c, :] = -imag[:, cols(c)]
                table_ref[at, 1, :, SLOT + c, :] = imag[:, cols(c)]


def stats_kernel(tok_ref, order_ref, u_ref, stats_ref):
    value = permute_in(tok_ref[...], order_ref)
    u_ref[...] = value.astype(BF16)
    add_stats(stats_ref, value)


def add_stats(stats_ref, value):
    add_rows(stats_ref, column_sum(value), column_sum(value * value))


def add_rows(copies_ref, first, second):
    i, nt = pl.program_id(0), pl.num_programs(0)
    chunks = first.shape[1] // 128

    @pl.when(i == 0)
    def _():
        copies_ref[0] = jnp.zeros(copies_ref.shape[1:], F32)

    for c in range(chunks):
        copies_ref[0, c : c + 1] += first[:, cols(c)]
        copies_ref[0, SLOT + c : SLOT + c + 1] += second[:, cols(c)]

    @pl.when(i == nt - 1)
    def _():
        copies_ref[...] = jnp.broadcast_to(copies_ref[0:1], copies_ref.shape)


def summed(ref):
    total = jnp.sum(ref[...], axis=0)
    return tuple(
        jnp.concatenate([total[SLOT * k + c : SLOT * k + c + 1] for c in range(SLOT)], axis=1)
        for k in range(2)
    )


def drive_kernel(layer, down, tokens, *refs):
    (
        stat_ref, u_ref, gain_ref, bias_ref, skip_ref, win_ref, disc_ref, jr_ref,
        b_ref, end_ref, blk_ref, norm_ref,
    ) = refs
    i, nt = pl.program_id(0), pl.num_programs(0)
    steps = u_ref.shape[0] // LANES
    chunks = chunk_count(b_ref)
    half = chunks * 128

    @pl.when(i == 0)
    def _():
        total, squares = summed(stat_ref)
        row = slice(layer, layer + 1)
        mean = total / tokens
        inv = lax.rsqrt(squares / tokens - mean * mean + EPSILON)
        norm_ref[0:1] = mean
        norm_ref[1:2] = inv
        norm_ref[2:3] = inv * gain_ref[row]
        norm_ref[3:4] = bias_ref[row]
        norm_ref[4:5] = skip_ref[row]
        norm_ref[5:8] = jnp.zeros((3, norm_ref.shape[1]), F32)
        blk_ref[...] = jnp.zeros_like(blk_ref)

    u = u_ref[...].astype(F32)
    normed = (u - norm_ref[0:1]) * norm_ref[2:3] + norm_ref[3:4]
    drive = jnp.dot(normed.astype(BF16), win_ref[...], preferred_element_type=F32)
    fr, fi = disc_ref[1:2, :half], disc_ref[1:2, half:]
    re, im = drive[:, :half], drive[:, half:]
    b_ref[:, :half] = re * fr - im * fi
    b_ref[:, half:] = re * fi + im * fr
    tile = nt - 1 - i if down else i
    scan_tile(b_ref, blk_ref, disc_row(disc_ref, 0, chunks), jr_ref, tile * steps, steps, down)

    @pl.when(i == nt - 1)
    def _():
        zero = [jnp.zeros((1, 128), F32)] * chunks
        cr, ci = chain(blk_ref, jr_ref, disc_row(disc_ref, 2, chunks), (zero, zero), down)
        put_copies(end_ref, cr, ci)


def states_of(ends_ref, table_ref, b_ref, blk_ref, disc_ref, jr_ref, low_ref, st_ref, down):
    i, nt = pl.program_id(0), pl.num_programs(0)
    chunks = chunk_count(b_ref)
    steps = b_ref.shape[0] // LANES

    @pl.when(i == 0)
    def _():
        carry = carry_in(ends_ref, table_ref, chunks)
        chain(blk_ref, jr_ref, disc_row(disc_ref, 2, chunks), carry, down, st_ref)

    def emit(low_step, pair, extra):
        if pair is None:
            return ()
        (first, second) = pair
        store_pair(low_ref, low_step, first, second)
        return ()

    tile = nt - 1 - i if down else i
    scan_tile(
        b_ref, st_ref, disc_row(disc_ref, 0, chunks), jr_ref, tile * steps, steps, down, emit
    )


def gelu_parts(mixed):
    square = mixed * mixed
    tanh = jnp.tanh(mixed * (GELU_A + (GELU_A * GELU_B) * square))
    half_up = 0.5 + 0.5 * tanh
    return square, tanh, half_up


def gelu_slope(mixed, square, tanh, half_up):
    return half_up + (mixed * (0.5 - 0.5 * tanh * tanh)) * (
        GELU_A + (3.0 * GELU_A * GELU_B) * square
    )


def sigmoid(value):
    return 0.5 + 0.5 * jnp.tanh(0.5 * value)


def forward_kernel(down, *refs):
    (
        ends_ref, table_ref, b_ref, blk_ref, disc_ref, jr_ref, u_ref, norm_ref, wout_ref, wgate_ref,
        next_ref, low_ref, mixed_ref, gate_ref, stats_ref, st_ref, mix_ref, logit_ref, act_ref,
    ) = refs
    states_of(ends_ref, table_ref, b_ref, blk_ref, disc_ref, jr_ref, low_ref, st_ref, down)
    mix_ref[...] = jnp.dot(low_ref[...], wout_ref[...], preferred_element_type=F32)
    count = mix_ref.shape[0] // CHUNK

    def mix(k, carry):
        at = pl.ds(pl.multiple_of(k * CHUNK, CHUNK), CHUNK)
        u = u_ref[at].astype(F32)
        normed = (u - norm_ref[0:1]) * norm_ref[2:3] + norm_ref[3:4]
        mixed = mix_ref[at] + norm_ref[4:5] * normed
        _, _, half_up = gelu_parts(mixed)
        act = mixed * half_up
        mixed_ref[at] = mixed.astype(BF16)
        act_ref[at] = act.astype(BF16)
        mix_ref[at] = act
        return carry

    lax.fori_loop(0, count, mix, 0)
    logit_ref[...] = jnp.dot(act_ref[...], wgate_ref[...], preferred_element_type=F32)

    def close(k, carry):
        first, second = carry
        at = pl.ds(pl.multiple_of(k * CHUNK, CHUNK), CHUNK)
        gate = sigmoid(logit_ref[at])
        after = u_ref[at].astype(F32) + mix_ref[at] * gate
        next_ref[at] = after
        gate_ref[at] = gate.astype(BF16)
        folded = after.reshape(CHUNK // 8, 8, after.shape[1])
        return first + jnp.sum(folded, axis=0), second + jnp.sum(folded * folded, axis=0)

    zero = jnp.zeros((8, mix_ref.shape[1]), F32)
    first, second = lax.fori_loop(0, count, close, (zero, zero))
    add_rows(
        stats_ref, jnp.sum(first, axis=0, keepdims=True), jnp.sum(second, axis=0, keepdims=True)
    )


def accumulate(ref, value):
    @pl.when(pl.program_id(0) == 0)
    def _():
        ref[...] = value

    @pl.when(pl.program_id(0) != 0)
    def _():
        ref[...] += value


def turned(value):
    width = value.shape[1]
    unit = (
        lax.broadcasted_iota(jnp.int32, (width, width), 0)
        == lax.broadcasted_iota(jnp.int32, (width, width), 1)
    ).astype(F32).astype(BF16)
    return lax.dot_general(unit, value, NT, preferred_element_type=F32).astype(BF16)


def gate_backward(g, mixed, gate, normed, low_ref, wout_ref, wgate_ref, outs, kept=None):
    pg_ref, sg_ref, wsum_ref, ssum_ref = outs
    states, width = wout_ref.shape
    square, tanh, half_up = gelu_parts(mixed) if kept is None else kept
    act = mixed * half_up
    g_gate = g * gate
    logit_grad = (g_gate * act * (1.0 - gate)).astype(BF16)
    accumulate(
        wsum_ref.at[states : states + width],
        lax.dot_general(act.astype(BF16), logit_grad, TN, preferred_element_type=F32),
    )
    act_grad = g_gate + lax.dot_general(
        logit_grad, wgate_ref[...], NT, preferred_element_type=F32
    )
    mixed_grad = act_grad * gelu_slope(mixed, square, tanh, half_up)
    accumulate(ssum_ref, column_sum(mixed_grad * normed))
    proj_grad = mixed_grad.astype(BF16)
    pg_ref[...] = proj_grad
    accumulate(
        wsum_ref.at[:states],
        lax.dot_general(low_ref[...], proj_grad, TN, preferred_element_type=F32),
    )
    sg_ref[...] = lax.dot_general(proj_grad, wout_ref[...], NT, preferred_element_type=F32)


def turn_kernel(down, *refs):
    (
        ends_ref, table_ref, b_ref, blk_ref, disc_ref, jr_ref, jo_ref, u_ref, norm_ref, wout_ref, wgate_ref,
        gout_ref, order_ref,
        out_ref, low_ref, g_ref, pg_ref, sg_ref, wsum_ref, end_ref, ablk_ref,
        st_ref, w_ref,
    ) = refs
    sums = wout_ref.shape[0] + wout_ref.shape[1]
    ssum_ref = wsum_ref.at[sums : sums + 1]
    i, nt = pl.program_id(0), pl.num_programs(0)
    chunks = chunk_count(b_ref)
    half = chunks * 128
    steps = b_ref.shape[0] // LANES
    tile = nt - 1 - i if down else i
    states_of(ends_ref, table_ref, b_ref, blk_ref, disc_ref, jr_ref, low_ref, st_ref, down)
    u = u_ref[...]
    normed = (u - norm_ref[0:1]) * norm_ref[2:3] + norm_ref[3:4]
    mixed = jnp.dot(low_ref[...], wout_ref[...], preferred_element_type=F32)
    mixed += norm_ref[4:5] * normed
    kept = gelu_parts(mixed)
    act = mixed * kept[2]
    gate = sigmoid(jnp.dot(act.astype(BF16), wgate_ref[...], preferred_element_type=F32))
    permute_out(u + act * gate, order_ref, out_ref)
    g = permute_in(gout_ref[...], order_ref)
    g_ref[...] = g.astype(BF16)
    gate_backward(
        g, mixed, gate, normed, low_ref, wout_ref, wgate_ref,
        (pg_ref, sg_ref, wsum_ref, ssum_ref), kept,
    )

    @pl.when(i == 0)
    def _():
        wsum_ref[sums + 1 :] = jnp.zeros((7, wsum_ref.shape[1]), F32)
        w_ref[:, :half] = jnp.ones((LANES, half), F32)
        w_ref[:, half:] = jnp.zeros((LANES, half), F32)
        ablk_ref[...] = jnp.zeros_like(ablk_ref)

    dr, di = disc_row(disc_ref, 0, chunks, conj=True)
    dr, di = wide(dr), wide(di)
    jo = jo_ref[...]
    unroll = 4

    def body(k, carry):
        wr, wi, ar, ai = (list(carry[n * chunks : (n + 1) * chunks]) for n in range(4))
        for q in range(unroll):
            n = k * unroll + q
            step = steps - 1 - n if down else n
            at = pl.ds(pl.multiple_of(step * LANES, LANES), LANES)
            sr, si = rows_of(sg_ref, at, chunks)
            live = jo != tile * steps + step
            for c in range(chunks):
                ar[c] = ar[c] + (wr[c] * sr[c] - wi[c] * si[c])
                ai[c] = ai[c] + (wr[c] * si[c] + wi[c] * sr[c])
                xr = jnp.where(live, wr[c], 0.0)
                xi = jnp.where(live, wi[c], 0.0)
                wr[c] = xr * dr[c] - xi * di[c]
                wi[c] = xr * di[c] + xi * dr[c]
        return tuple(wr) + tuple(wi) + tuple(ar) + tuple(ai)

    wr, wi = rows_of(w_ref, slice(0, LANES), chunks)
    ar, ai = rows_of(ablk_ref, slice(0, LANES), chunks)
    out = lax.fori_loop(
        0, steps // unroll, body, tuple(wr) + tuple(wi) + tuple(ar) + tuple(ai)
    )
    wr, wi, ar, ai = (list(out[n * chunks : (n + 1) * chunks]) for n in range(4))
    put_rows(w_ref, slice(0, LANES), wr, wi)
    put_rows(ablk_ref, slice(0, LANES), ar, ai)

    @pl.when(i == nt - 1)
    def _():
        zero = [jnp.zeros((1, 128), F32)] * chunks
        power = disc_row(disc_ref, 2, chunks, conj=True)
        cr, ci = chain(ablk_ref, jo_ref, power, (zero, zero), not down)
        put_copies(end_ref, cr, ci)


def adjoint_kernel(down, last, *refs):
    (
        ends_ref, table_ref, sg_ref, ablk_ref, disc_ref, jr_ref, low_ref, u_ref, norm_ref, pg_ref, g_ref,
        win_ref, order_ref, *refs
    ) = refs
    if last:
        (ssum_ref, res_ref, sums_ref, st_ref, dg_ref, ax_ref, nsum_ref, isum_ref) = refs
    else:
        (res_ref, sums_ref, nsum_ref, st_ref, dg_ref, ax_ref) = refs
        isum_ref = sums_ref.at[: win_ref.shape[0]]
    width, states = win_ref.shape
    i, nt = pl.program_id(0), pl.num_programs(0)
    chunks = chunk_count(sg_ref)
    half = chunks * 128
    steps = sg_ref.shape[0] // LANES
    tile = nt - 1 - i if down else i

    @pl.when(i == 0)
    def _():
        carry = carry_in(ends_ref, table_ref, chunks)
        power = disc_row(disc_ref, 2, chunks, conj=True)
        chain(ablk_ref, jr_ref, power, carry, down, st_ref)
        ax_ref[...] = jnp.zeros_like(ax_ref)

    fr, fi = disc_row(disc_ref, 1, chunks)
    fr, fi = wide(fr), wide(fi)

    def emit(low_step, pair, extra):
        if pair is None:
            re, im = rows_of(ax_ref, slice(0, LANES), chunks)
            return tuple(re) + tuple(im)
        sums_r, sums_i = list(extra[:chunks]), list(extra[chunks:])
        at = pl.ds(pl.multiple_of(low_step * LANES, 2 * LANES), 2 * LANES)
        xr, xi = rows_of(low_ref, at, chunks)
        grads = []
        for which, (ar, ai) in enumerate(pair):
            gr, gi = [], []
            rows = slice(which * LANES, (which + 1) * LANES)
            for c in range(chunks):
                vr, vi = xr[c].astype(F32)[rows], xi[c].astype(F32)[rows]
                sums_r[c] = sums_r[c] + (ar[c] * vr + ai[c] * vi)
                sums_i[c] = sums_i[c] + (ai[c] * vr - ar[c] * vi)
                gr.append(ar[c] * fr[c] + ai[c] * fi[c])
                gi.append(ai[c] * fr[c] - ar[c] * fi[c])
            grads.append((gr, gi))
        store_pair(dg_ref, low_step, grads[0], grads[1])
        return tuple(sums_r) + tuple(sums_i)

    sums = scan_tile(
        sg_ref, st_ref, disc_row(disc_ref, 0, chunks, conj=True), jr_ref, tile * steps, steps,
        down, emit,
    )
    put_rows(ax_ref, slice(0, LANES), list(sums[:chunks]), list(sums[chunks:]))

    u = u_ref[...].astype(F32)
    centered = u - norm_ref[0:1]
    normed = (centered * norm_ref[2:3] + norm_ref[3:4]).astype(BF16)
    drive_grad = dg_ref[...]
    if last:
        product = lax.dot_general(normed, drive_grad, TN, preferred_element_type=F32)
    else:
        product = jnp.dot(turned(normed), drive_grad, preferred_element_type=F32)
    accumulate(isum_ref, product)
    normed_grad = lax.dot_general(drive_grad, win_ref[...], NT, preferred_element_type=F32)
    normed_grad += norm_ref[4:5] * pg_ref[...].astype(F32)
    add_rows(
        nsum_ref, column_sum(normed_grad), column_sum(normed_grad * centered) * norm_ref[1:2]
    )
    result = g_ref[...].astype(F32) + norm_ref[2:3] * normed_grad
    if last:
        permute_out(result, order_ref, res_ref)
    else:
        res_ref[...] = result

    @pl.when(i == nt - 1)
    def _():
        decays = jnp.sum(ax_ref[...], axis=0, keepdims=True)
        wr, wi = win_ref[:, :half].astype(F32), win_ref[:, half:].astype(F32)
        gr, gi = isum_ref[:, :half], isum_ref[:, half:]
        re = jnp.sum(wr * gr + wi * gi, axis=0, keepdims=True)
        im = jnp.sum(wr * gi - wi * gr, axis=0, keepdims=True)
        gr, gi = disc_ref[1:2, :half], disc_ref[1:2, half:]
        scale = 1.0 / (gr * gr + gi * gi)
        factors = ((re * gr - im * gi) * scale, (re * gi + im * gr) * scale)
        if last:
            rows = width // BLOCKS
            first = rows + rows // 2
            for b in range(BLOCKS):
                at = b * rows
                sums_ref[b, :rows] = isum_ref[at : at + rows, :width]
                sums_ref[b, rows:first, : states - width] = isum_ref[at : at + rows // 2, width:]
                sums_ref[b, rows:first, states - width :] = isum_ref[
                    at + rows // 2 : at + rows, width:
                ]
                sums_ref[b, first:] = jnp.zeros((SMALL, width), F32)
            small = [nsum_ref[0]] + [ssum_ref[:, cols(c)] for c in range(width // 128)]
            small += [decays[:, cols(c)] for c in range(2 * chunks)]
            small += [v[:, cols(c)] for v in factors for c in range(chunks)]
            at = first
            for row in small:
                sums_ref[0, at : at + row.shape[0], :128] = row
                at += row.shape[0]
        else:
            sums_ref[width : width + 8] = jnp.zeros((8, states), F32)
            sums_ref[width : width + 1] = decays
            sums_ref[width + 1 : width + 2, :half] = factors[0]
            sums_ref[width + 1 : width + 2, half:] = factors[1]


def back_kernel(down, tokens, *refs):
    (
        sums_ref, r_ref, up_ref, up_norm_ref, mixed_ref, gate_ref, low_ref, u_ref, norm_ref, wout_ref,
        wgate_ref, disc_ref, jo_ref,
        g_ref, pg_ref, sg_ref, blocks_ref, ssum_ref, end_ref, ablk_ref, nsum_ref, bsum_ref, wsum_ref,
    ) = refs
    i, nt = pl.program_id(0), pl.num_programs(0)
    chunks = chunk_count(sg_ref)
    steps = sg_ref.shape[0] // LANES
    tile = nt - 1 - i if down else i

    @pl.when(i == 0)
    def _():
        nsum_ref[...] = jnp.sum(sums_ref[...], axis=0)
        bsum_ref[0:1], bsum_ref[1:2] = summed(sums_ref)
        ablk_ref[...] = jnp.zeros_like(ablk_ref)

    scale = up_norm_ref[2:3] * (-1.0 / tokens)
    standard = (up_ref[...] - up_norm_ref[0:1]) * (scale * up_norm_ref[1:2] * bsum_ref[1:2])
    g = r_ref[...] + (standard + scale * bsum_ref[0:1])
    g_ref[...] = g
    u = u_ref[...].astype(F32)
    normed = (u - norm_ref[0:1]) * norm_ref[2:3] + norm_ref[3:4]
    gate_backward(
        g, mixed_ref[...].astype(F32), gate_ref[...].astype(F32), normed, low_ref, wout_ref,
        wgate_ref, (pg_ref, sg_ref, wsum_ref, ssum_ref),
    )
    decay = disc_row(disc_ref, 0, chunks, conj=True)
    scan_tile(sg_ref, ablk_ref, decay, jo_ref, tile * steps, steps, down)

    @pl.when(i == nt - 1)
    def _():
        zero = [jnp.zeros((1, 128), F32)] * chunks
        power = disc_row(disc_ref, 2, chunks, conj=True)
        cr, ci = chain(ablk_ref, jo_ref, power, (zero, zero), down)
        put_copies(end_ref, cr, ci)
        states, width = wout_ref.shape
        gates, outs = width // BLOCKS, states // BLOCKS
        for b in range(BLOCKS):
            blocks_ref[b, :gates] = wsum_ref[states + b * gates : states + (b + 1) * gates]
            blocks_ref[b, gates:] = wsum_ref[b * outs : (b + 1) * outs]


def last_kernel(
    tokens, piece_ref, small_ref, out1_ref, gate1_ref, skip1_ref, in1_ref, decay1_ref, norm1_ref,
    disc_ref, rate_ref, step_ref, freq_ref, r_ref, tok_ref, norm_ref,
    grad_in_ref, gain_ref, bias_ref, drate_ref, dstep_ref, dfreq_ref, in_ref, out_ref, skip_ref,
    gate_ref,
):
    gates, width = gate1_ref.shape
    outs = out1_ref.shape[0]
    states = in1_ref.shape[1]
    half = states // 2
    left = states - width
    gate_ref[0], gate_ref[1] = piece_ref[:gates], gate1_ref[...]
    out_ref[0], out_ref[1] = piece_ref[gates : gates + outs], out1_ref[...]
    at = gates + outs
    in_ref[0, :, :width] = piece_ref[at : at + gates]
    at += gates
    in_ref[0, : gates // 2, width:] = piece_ref[at : at + gates // 2, :left]
    in_ref[0, gates // 2 :, width:] = piece_ref[at : at + gates // 2, left:]
    in_ref[1] = in1_ref[...]

    def row(ref, first, count):
        return jnp.concatenate([ref[first + c : first + c + 1, :128] for c in range(count)], axis=1)

    count = width // 128
    bias, gain = row(small_ref, 0, count), row(small_ref, count, count)
    scale = norm_ref[2:3] * (-1.0 / tokens)
    grad_in_ref[...] = r_ref[...] + (
        (tok_ref[...].astype(F32) - norm_ref[0:1]) * (scale * norm_ref[1:2] * gain) + scale * bias
    )

    @pl.when(pl.program_id(0) == 0)
    def _():
        bias_ref[0:1], gain_ref[0:1] = bias, gain
        bias_ref[1:2], gain_ref[1:2] = row(norm1_ref, 0, count), row(norm1_ref, count, count)
        skip_ref[0:1], skip_ref[1:2] = row(small_ref, 2 * count, count), skip1_ref[0:1]
        at = 3 * count
        lanes = half // 128
        for l in range(LAYERS):
            if l == 0:
                ar, ai, sr, si = (row(small_ref, at + k * lanes, lanes) for k in range(4))
            else:
                ar, ai = decay1_ref[0:1, :half], decay1_ref[0:1, half:]
                sr, si = decay1_ref[1:2, :half], decay1_ref[1:2, half:]
            dr, di = disc_ref[l, 0:1, :half], disc_ref[l, 0:1, half:]
            fr, fi = disc_ref[l, 1:2, :half], disc_ref[l, 1:2, half:]
            here = slice(l, l + 1)
            rate, freq, step = rate_ref[here], freq_ref[here], jnp.exp(step_ref[here])
            tr = ar - (fr * sr + fi * si)
            ti = ai - (fr * si - fi * sr)
            size = 1.0 / (dr * dr + di * di)
            gr, gi = (tr * dr - ti * di) * size, (tr * di + ti * dr) * size
            mr, mi = -rate * fr - freq * fi, freq * fr - rate * fi
            size = 1.0 / (rate * rate + freq * freq)
            gr += (-rate * sr - freq * si) * size
            gi += (freq * sr - rate * si) * size
            both = 2.0 * (fr * sr + fi * si)
            gx = gr * dr + gi * di
            gy = gi * dr - gr * di
            drate_ref[here] = (-mr * sr - mi * si - both * rate) * size - step * gx
            dfreq_ref[here] = (mi * sr - mr * si - both * freq) * size + step * gy
            dstep_ref[here] = step * (freq * gy - rate * gx)


def whole(array):
    shape = array.shape
    return pl.BlockSpec(shape, lambda i: (0,) * len(shape))


def tile_spec(rows, width, nt, down):
    if down:
        return pl.BlockSpec((rows, width), lambda i: (nt - 1 - i, 0))
    return pl.BlockSpec((rows, width), lambda i: (i, 0))


def run_spec(steps, width, nt, down):
    if down:
        return pl.BlockSpec((LANES, steps, width), lambda i: (0, nt - 1 - i, 0))
    return pl.BlockSpec((LANES, steps, width), lambda i: (0, i, 0))


def call(kernel, nt, args, outs, scratch, macs, name):
    arrays = [a for a, *_ in args]
    sizes = sum(a.size * a.dtype.itemsize for a in arrays + [a for a, *_ in outs])
    held = [
        a if keep is None else pltpu.with_memory_space_constraint(a, keep)
        for a, _, keep in map(filled, args)
    ]
    return pl.pallas_call(
        kernel,
        grid=(nt,),
        in_specs=[whole(a) if s is None else s for a, s, _ in map(filled, args)],
        out_specs=[whole(a) if s is None else s for a, s, _ in map(filled, outs)],
        out_shape=[
            a if keep is None else keep(a.shape, a.dtype) for a, _, keep in map(filled, outs)
        ],
        scratch_shapes=scratch,
        compiler_params=pltpu.CompilerParams(
            vmem_limit_bytes=VMEM_LIMIT, dimension_semantics=("arbitrary",)
        ),
        cost_estimate=pl.CostEstimate(flops=2 * macs, bytes_accessed=sizes, transcendentals=0),
        name=name,
    )(*held)


def filled(entry):
    return entry if len(entry) == 3 else entry + (pltpu.HBM,)


def shape(*dims, dtype=F32):
    return jax.ShapeDtypeStruct(dims, dtype)


def body(
    axes,
    tokens_in,
    seq_starts,
    norm_gain,
    norm_bias,
    decay_rate,
    step_log,
    frequency,
    in_proj,
    out_proj,
    skip_gain,
    gate_proj,
    grad_out,
):
    rows, width = tokens_in.shape
    states = in_proj.shape[-1]
    devices = 2 ** len(axes)
    tokens = float(rows * devices)
    run = rows // LANES
    steps = min(64, run)
    tile = steps * LANES
    nt = rows // tile
    span = min(32, steps)
    def tiles(array, down):
        return (array, tile_spec(tile, array.shape[-1], nt, down))

    def runs(array, down):
        return (array, run_spec(steps, array.shape[-1], nt, down))

    def full(array):
        return (array, None)

    def of(array, l):
        size = array.shape[1:]
        return (array, pl.BlockSpec((None,) + size, lambda i: (l,) + (0,) * len(size)))

    discs, tables, cuts, order = call(
        functools.partial(prep_kernel, rows, axes), 1,
        [(seq_starts, pl.BlockSpec(memory_space=pltpu.SMEM), None), full(decay_rate),
         full(step_log), full(frequency)],
        [full(shape(LAYERS, 8, states)), full(shape(2 * LAYERS, 2, devices, 2 * SLOT, 128)),
         full(shape(2, LANES, 128, dtype=jnp.int32)),
         full(shape(span * LANES, span * LANES, dtype=BF16))],
        [], rows * width, "prep",
    )

    def near(entry):
        return entry[:2] + (pltpu.VMEM if rows * states * 4 <= 7 * 2**20 else pltpu.HBM,)

    tokens_run = tokens_in.reshape(LANES, run, width)
    grad_run = grad_out.reshape(LANES, run, width)
    state_scratch = pltpu.VMEM((LANES, states), F32)
    cost = rows * width * states

    u0, stats = call(
        stats_kernel, nt, [runs(tokens_run, 0), full(order)],
        [tiles(shape(rows, width, dtype=BF16), 0), near(full(shape(devices, 2 * SLOT, 128)))],
        [], cost // 2, "stats",
    )

    def drive(l, stream, stats):
        down = l % 2
        return call(
            functools.partial(drive_kernel, l, bool(down), tokens), nt,
            [near(full(gather_all(stats, axes))), tiles(stream, down), full(norm_gain), full(norm_bias), full(skip_gain), of(in_proj, l), of(discs, l),
               of(cuts, down)],
            [near(tiles(shape(rows, states), down)), near(full(shape(devices, 2 * SLOT, 128))),
             full(shape(LANES, states)), full(shape(8, width))],
            [], 4 * cost, f"drive_{l}",
        )

    b0, end0, blk0, norm0 = drive(0, u0, stats)
    u1, low0, mixed0, gate0, stats = call(
        functools.partial(forward_kernel, False), nt,
        [near(full(gather_all(end0, axes))), of(tables, 2 * 0 + 0), near(tiles(b0, 0)), full(blk0), of(discs, 0), of(cuts, 0),
           tiles(u0, 0), full(norm0), of(out_proj, 0), of(gate_proj, 0)],
        [tiles(shape(rows, width), 0), tiles(shape(rows, states, dtype=BF16), 0),
         tiles(shape(rows, width, dtype=BF16), 0), tiles(shape(rows, width, dtype=BF16), 0),
         near(full(shape(devices, 2 * SLOT, 128)))],
        [state_scratch, pltpu.VMEM((tile, width), F32), pltpu.VMEM((tile, width), F32),
         pltpu.VMEM((tile, width), BF16)], 6 * cost, "forward_0",
    )

    b1, end1, blk1, norm1 = drive(1, u1, stats)
    (
        out, low1, g1, pg1, sg1, w_sum1, aend1, ablk1
    ) = call(
        functools.partial(turn_kernel, True), nt,
        [near(full(gather_all(end1, axes))), of(tables, 2 * 1 + 0), near(tiles(b1, 1)), full(blk1), of(discs, 1), of(cuts, 1),
           of(cuts, 0), tiles(u1, 1), full(norm1), of(out_proj, 1), of(gate_proj, 1),
           runs(grad_run, 1), full(order)],
        [runs(shape(LANES, run, width), 1), near(tiles(shape(rows, states, dtype=BF16), 1)),
         near(tiles(shape(rows, width, dtype=BF16), 1)),
         near(tiles(shape(rows, width, dtype=BF16), 1)), near(tiles(shape(rows, states), 1)), full(shape(states + width + 8, width)),
         near(full(shape(devices, 2 * SLOT, 128))), full(shape(LANES, states))],
        [state_scratch, state_scratch], 16 * cost, "turn_1",
    )

    def adjoint(l, sg, ablk, ends, low, stream, norm, pg, g, skip_sum=None):
        down = 1 - l % 2
        last = l == 0
        args = [
            near(full(ends)), of(tables, 2 * l + 1), near(tiles(sg, down)), full(ablk), of(discs, l),
            of(cuts, down), near(tiles(low, down)) if l else tiles(low, down), tiles(stream, down),
            full(norm), near(tiles(pg, down)), near(tiles(g, down)), of(in_proj, l), full(order),
        ]
        scratch = [state_scratch, pltpu.VMEM((tile, states), BF16), state_scratch]
        if last:
            args.append(full(skip_sum))
            outs = [
                runs(shape(LANES, run, width), down),
                full(shape(BLOCKS, (width + width // 2) // BLOCKS + SMALL, width)),
            ]
            scratch += [pltpu.VMEM((1, 2 * SLOT, 128), F32), pltpu.VMEM((width, states), F32)]
        else:
            outs = [
                tiles(shape(rows, width), down), full(shape(width + 8, states)),
                near(full(shape(devices, 2 * SLOT, 128))),
            ]
        return call(
            functools.partial(adjoint_kernel, bool(down), last), nt, args, outs, scratch,
            8 * cost, f"adjoint_{l}",
        )

    r1, in_sum1, norm_sum1 = adjoint(
        1, sg1, ablk1, gather_all(aend1, axes), low1, u1, norm1, pg1, g1
    )

    def lower(r1, norm_sum1):
        (
            g0, pg0, sg0, w_sum0, skip_sum0, aend0, ablk0, small1, _
        ) = call(
            functools.partial(back_kernel, True, tokens), nt,
            [near(full(gather_all(norm_sum1, axes))), tiles(r1, 1), tiles(u1, 1), full(norm1),
             tiles(mixed0, 1), tiles(gate0, 1), tiles(low0, 1), tiles(u0, 1), full(norm0),
             of(out_proj, 0), of(gate_proj, 0), of(discs, 0), of(cuts, 1)],
            [near(tiles(shape(rows, width), 1)), near(tiles(shape(rows, width, dtype=BF16), 1)),
             near(tiles(shape(rows, states), 1)),
             full(shape(BLOCKS, (states + width) // BLOCKS, width)), full(shape(1, width)), near(full(shape(devices, 2 * SLOT, 128))),
             full(shape(LANES, states)), full(shape(2 * SLOT, 128)), full(shape(2, width))],
            [pltpu.VMEM((states + width, width), F32)], 12 * cost, "back_0",
        )
        core, chips, *others = phases(axes)
        w_sum0 = w_sum0.reshape(-1, width)
        ends, part = lax.optimization_barrier(
            (gather_all(aend0, axes), scatter_sum(w_sum0, core))
        )
        part = scatter_sum(part, chips)
        r0, in_sum0 = adjoint(0, sg0, ablk0, ends, low0, u0, norm0, pg0, g0, skip_sum0)
        in_sum0, part = lax.optimization_barrier((in_sum0, part))
        in_part = scatter_sum(scatter_sum(in_sum0.reshape(-1, width), core), chips)
        part = sum_all(jnp.concatenate([part, in_part], axis=0), others)
        pieces = gather_rows(gather_rows(part, chips), core)
        return r0.reshape(rows, width), small1, pieces.reshape(BLOCKS, -1, width)

    piece = (2 * width + states + width // 2) // BLOCKS + SMALL

    def nothing(r1, norm_sum1):
        return (
            jnp.zeros((rows, width), F32),
            jnp.zeros((2 * SLOT, 128), F32),
            jnp.zeros((BLOCKS, piece, width), F32),
        )

    w_all1, in_all1 = lax.psum((w_sum1, in_sum1), axes)
    r0, norm_all1, pieces = lax.cond(seq_starts[0] == 0, lower, nothing, r1, norm_sum1)

    gates, outs = width // BLOCKS, states // BLOCKS

    def block(array, *dims, at=lambda i: (i, 0)):
        return (array, pl.BlockSpec(dims, at))

    def flat(array, count):
        return block(array, count, array.shape[1])

    (
        grad_in, gain_grad, bias_grad, rate_grad, step_grad, freq_grad, in_grad, out_grad,
        skip_grad, gate_grad,
    ) = call(
        functools.partial(last_kernel, tokens), BLOCKS,
        [block(pieces, None, piece, width, at=lambda i: (i, 0, 0)) + (None,),
         block(pieces, None, SMALL, width, at=lambda i: (0, piece // SMALL - 1, 0)) + (None,),
         flat(w_all1, outs),
         block(w_all1, gates, width, at=lambda i: (states // gates + i, 0)),
         block(w_all1, 8, width, at=lambda i: ((states + width) // 8, 0)),
         flat(in_all1, gates),
         block(in_all1, 8, states, at=lambda i: (width // 8, 0)),
         full(norm_all1), full(discs), full(decay_rate), full(step_log), full(frequency),
         flat(r0, rows // BLOCKS), flat(tokens_in, rows // BLOCKS), full(norm0)],
        [flat(shape(rows, width), rows // BLOCKS), full(shape(LAYERS, width)),
         full(shape(LAYERS, width)), full(shape(LAYERS, states // 2)),
         full(shape(LAYERS, states // 2)), full(shape(LAYERS, states // 2)),
         block(shape(LAYERS, width, states), LAYERS, gates, states, at=lambda i: (0, i, 0)),
         block(shape(LAYERS, states, width), LAYERS, outs, width, at=lambda i: (0, i, 0)),
         full(shape(LAYERS, width)),
         block(shape(LAYERS, width, width), LAYERS, gates, width, at=lambda i: (0, i, 0))],
        [], cost, "last",
    )
    return (
        out.reshape(rows, width),
        grad_in,
        gain_grad,
        bias_grad,
        rate_grad,
        step_grad,
        freq_grad,
        in_grad,
        out_grad,
        skip_grad,
        gate_grad,
    )


def solution(mesh):
    bits = mesh.devices.size.bit_length() - 1
    axes = tuple("b%d" % k for k in range(bits))
    binary = Mesh(mesh.devices.reshape((2,) * bits), axes)
    rows = P(axes, None)
    return jax.shard_map(
        functools.partial(body, axes),
        mesh=binary,
        in_specs=(rows,) + (P(),) * 10 + (rows,),
        out_specs=(rows, rows) + (P(),) * 9,
        check_vma=False,
    )
```

```python
import functools

import jax
import jax.numpy as jnp
from jax import lax
from jax.experimental import pallas as pl
from jax.experimental.pallas import tpu as pltpu
from jax.sharding import Mesh, PartitionSpec as P

LAYERS = 2
EPSILON = 1e-05
SMALL = 8
BLOCKS = 8
SLOT = 4
LANES = 8
VMEM_LIMIT = 30 * 1024 * 1024
GELU_A = 0.7978845608028654
GELU_B = 0.044715
NT = (((1,), (1,)), ((), ()))
TN = (((0,), (0,)), ((), ()))
F32 = jnp.float32
BF16 = jnp.bfloat16


def gather_all(copies, axes):
    return lax.all_to_all(copies, axes, 0, 0)


def scatter_sum(value, axes):
    count = 2 ** len(axes)
    pieces = value.reshape((count, value.shape[0] // count) + value.shape[1:])
    return jnp.sum(lax.all_to_all(pieces, axes, 0, 0), axis=0)


def gather_rows(value, axes):
    count = 2 ** len(axes)
    copies = jnp.broadcast_to(value, (count,) + value.shape)
    return lax.all_to_all(copies, axes, 0, 0).reshape((count * value.shape[0],) + value.shape[1:])


def phases(axes):
    left, out = list(axes), [(axes[-1],)]
    left = left[:-1]
    while left:
        out.append(tuple(left[-2:]))
        left = left[:-2]
    return out


def sum_all(value, parts):
    for part in parts:
        value = scatter_sum(value, part)
    for part in reversed(parts):
        value = gather_rows(value, part)
    return value


def cols(c):
    return slice(c * 128, (c + 1) * 128)


def chunk_count(ref):
    return ref.shape[-1] // 256


def rows_of(ref, at, chunks):
    half = chunks * 128
    re = [ref[at, c * 128 : (c + 1) * 128] for c in range(chunks)]
    im = [ref[at, half + c * 128 : half + (c + 1) * 128] for c in range(chunks)]
    return re, im


def put_rows(ref, at, re, im):
    chunks = len(re)
    half = chunks * 128
    for c in range(chunks):
        ref[at, c * 128 : (c + 1) * 128] = re[c]
        ref[at, half + c * 128 : half + (c + 1) * 128] = im[c]


def put_copies(ref, re, im):
    ref[0] = jnp.zeros(ref.shape[1:], F32)
    for c in range(len(re)):
        ref[0, c : c + 1] = re[c]
        ref[0, SLOT + c : SLOT + c + 1] = im[c]
    ref[...] = jnp.broadcast_to(ref[0:1], ref.shape)


def wide(rows):
    return [jnp.broadcast_to(v, (LANES, 128)) for v in rows]


def chain(ends_ref, jr_ref, power, carry, down, start_ref=None):
    chunks = len(power[0])
    pr, pi = power
    cr, ci = carry
    order = range(LANES - 1, -1, -1) if down else range(LANES)
    for s in order:
        at = slice(s, s + 1)
        if start_ref is not None:
            put_rows(start_ref, at, cr, ci)
        er, ei = rows_of(ends_ref, at, chunks)
        alive = (jr_ref[at, :] < 0).astype(F32)
        cr, ci = (
            [er[c] + alive * (pr[c] * cr[c] - pi[c] * ci[c]) for c in range(chunks)],
            [ei[c] + alive * (pr[c] * ci[c] + pi[c] * cr[c]) for c in range(chunks)],
        )
    return cr, ci


def carry_in(ends_ref, table_ref, chunks):
    total = jnp.zeros((2 * SLOT, 128), F32)
    for e in range(ends_ref.shape[0]):
        end = ends_ref[e]
        turned = jnp.concatenate([end[SLOT:], end[:SLOT]], axis=0)
        total += table_ref[0, e] * end + table_ref[1, e] * turned
    return (
        [total[c : c + 1] for c in range(chunks)],
        [total[SLOT + c : SLOT + c + 1] for c in range(chunks)],
    )


def scan_tile(src_ref, st_ref, decay, jr_ref, first_step, steps, down, emit=None, unroll=4):
    chunks = chunk_count(src_ref)
    dr, di = wide(decay[0]), wide(decay[1])
    jr = jr_ref[...]
    re, im = rows_of(st_ref, slice(0, LANES), chunks)

    def one(step, re, im):
        at = pl.ds(pl.multiple_of(step * LANES, LANES), LANES)
        br, bi = rows_of(src_ref, at, chunks)
        live = jr != first_step + step
        nr, ni = [], []
        for c in range(chunks):
            xr = jnp.where(live, re[c], 0.0)
            xi = jnp.where(live, im[c], 0.0)
            nr.append(dr[c] * xr - di[c] * xi + br[c])
            ni.append(dr[c] * xi + di[c] * xr + bi[c])
        return nr, ni

    def body(i, carry):
        re, im = list(carry[:chunks]), list(carry[chunks : 2 * chunks])
        extra = carry[2 * chunks :]
        for q in range(unroll):
            n = 2 * (i * unroll + q)
            low_step = steps - 2 - n if down else n
            a, b = (low_step + 1, low_step) if down else (low_step, low_step + 1)
            r1, i1 = one(a, re, im)
            r2, i2 = one(b, r1, i1)
            if emit is not None:
                pair = ((r2, i2), (r1, i1)) if down else ((r1, i1), (r2, i2))
                extra = emit(low_step, pair, extra)
            re, im = r2, i2
        return tuple(re) + tuple(im) + tuple(extra)

    start = tuple(re) + tuple(im)
    if emit is not None:
        start = start + tuple(emit(None, None, None))
    out = lax.fori_loop(0, steps // (2 * unroll), body, start)
    put_rows(st_ref, slice(0, LANES), list(out[:chunks]), list(out[chunks : 2 * chunks]))
    return out[2 * chunks :]


def store_pair(ref, low_step, first, second):
    at = pl.ds(pl.multiple_of(low_step * LANES, 2 * LANES), 2 * LANES)
    re = [jnp.concatenate([p, q], axis=0).astype(BF16) for p, q in zip(first[0], second[0])]
    im = [jnp.concatenate([p, q], axis=0).astype(BF16) for p, q in zip(first[1], second[1])]
    put_rows(ref, at, re, im)


def disc_row(disc_ref, row, chunks, conj=False):
    re, im = rows_of(disc_ref, slice(row, row + 1), chunks)
    return (re, [-v for v in im]) if conj else (re, im)


def column_sum(value):
    rows, width = value.shape
    return jnp.sum(jnp.sum(value.reshape(rows // 8, 8, width), axis=0), axis=0, keepdims=True)


def permute_in(block, order_ref):
    runs, steps, width = block.shape
    span = order_ref.shape[0] // runs
    out = []
    for k in range(steps // span):
        part = block[:, k * span : (k + 1) * span, :].reshape(runs * span, width)
        out.append(jnp.dot(order_ref[...], part, preferred_element_type=F32))
    return out[0] if len(out) == 1 else jnp.concatenate(out, axis=0)


def permute_out(value, order_ref, out_ref):
    rows, width = value.shape
    size = order_ref.shape[0]
    span = size // LANES
    high = value.astype(BF16)
    low = (value - high.astype(F32)).astype(BF16)
    for k in range(rows // size):
        at = slice(k * size, (k + 1) * size)
        back = lax.dot_general(order_ref[...], high[at], TN, preferred_element_type=F32)
        back += lax.dot_general(order_ref[...], low[at], TN, preferred_element_type=F32)
        out_ref[:, k * span : (k + 1) * span, :] = back.reshape(LANES, span, width)


def expm1(value):
    acc = jnp.full_like(value, 1.0 / 479001600.0)
    for n in (39916800.0, 3628800.0, 362880.0, 40320.0, 5040.0, 720.0, 120.0, 24.0, 6.0, 2.0, 1.0):
        acc = acc * value + 1.0 / n
    return jnp.where(value > -1.0, acc * value, jnp.exp(value) - 1.0)


def prep_kernel(
    rows, axes, starts_ref, rate_ref, step_ref, freq_ref,
    disc_ref, table_ref, cut_ref, order_ref,
):
    devices = 2 ** len(axes)
    total = rows * devices
    run = rows // LANES
    half = rate_ref.shape[-1]
    me = 0
    for axis in axes:
        me = 2 * me + lax.axis_index(axis)
    starts = [starts_ref[:, k : k + 1] for k in range(starts_ref.shape[1])]

    base = me * rows + run * lax.broadcasted_iota(jnp.int32, (LANES, 128), 0)
    up = jnp.full((LANES, 128), -1, jnp.int32)
    down = up
    for begin in starts + [total]:
        rel = begin - base
        up = jnp.maximum(up, jnp.where((rel >= 0) & (rel < run), rel, -1))
        down = jnp.maximum(down, jnp.where((rel >= 1) & (rel <= run), rel - 1, -1))
    cut_ref[0] = up
    cut_ref[1] = down

    size = order_ref.shape[0]
    span = size // LANES
    to = lax.broadcasted_iota(jnp.int32, (size, size), 0)
    back = lax.broadcasted_iota(jnp.int32, (size, size), 1)
    order_ref[...] = ((to % LANES) * span + to // LANES == back).astype(F32).astype(BF16)

    source = lax.broadcasted_iota(jnp.int32, (devices, half), 0)
    for l in range(LAYERS):
        row = slice(l, l + 1)
        rate, freq = rate_ref[row], freq_ref[row]
        step_size = jnp.exp(step_ref[row])
        real_angle = -rate * step_size
        imag_angle = freq * step_size
        magnitude = jnp.exp(real_angle)
        cosine, sine = jnp.cos(imag_angle), jnp.sin(imag_angle)
        minus_real = expm1(real_angle) * cosine - 2.0 * jnp.sin(0.5 * imag_angle) ** 2
        minus_imag = magnitude * sine
        modulus = rate * rate + freq * freq
        disc_ref[l, 0:1, :half] = magnitude * cosine
        disc_ref[l, 0:1, half:] = minus_imag
        disc_ref[l, 1:2, :half] = (-rate * minus_real + freq * minus_imag) / modulus
        disc_ref[l, 1:2, half:] = (-rate * minus_imag - freq * minus_real) / modulus
        magnitude = jnp.exp(real_angle * float(run))
        disc_ref[l, 2:3, :half] = magnitude * jnp.cos(imag_angle * float(run))
        disc_ref[l, 2:3, half:] = magnitude * jnp.sin(imag_angle * float(run))
        disc_ref[l, 3:8] = jnp.zeros((5, 2 * half), F32)
        powers = []
        for bit in range(len(axes)):
            magnitude = jnp.exp(real_angle * float(rows << bit))
            angle = imag_angle * float(rows << bit)
            powers.append((magnitude * jnp.cos(angle), magnitude * jnp.sin(angle)))
        for back in range(2):
            going_down = (l + back) % 2 == 1
            if going_down:
                live, count = source > me, source - me - 1
            else:
                live, count = source < me, me - 1 - source
            for begin in starts:
                if going_down:
                    cut = (begin > (me + 1) * rows) & (source * rows >= begin)
                else:
                    cut = (begin < me * rows) & ((source + 1) * rows <= begin)
                live &= ~cut
            count = jnp.maximum(count, 0)
            real = live.astype(F32)
            imag = jnp.zeros((devices, half), F32)
            for bit, (pr, pi) in enumerate(powers):
                use = (count & (1 << bit)) != 0
                pr, pi = jnp.where(use, pr, 1.0), jnp.where(use, pi, 0.0)
                real, imag = real * pr - imag * pi, real * pi + imag * pr
            imag = -imag if back else imag
            at = 2 * l + back
            table_ref[at] = jnp.zeros(table_ref.shape[1:], F32)
            for c in range(half // 128):
                table_ref[at, 0, :, c, :] = real[:, cols(c)]
                table_ref[at, 0, :, SLOT + c, :] = real[:, cols(c)]
                table_ref[at, 1, :, c, :] = -imag[:, cols(c)]
                table_ref[at, 1, :, SLOT + c, :] = imag[:, cols(c)]


def stats_kernel(tok_ref, order_ref, u_ref, stats_ref):
    value = permute_in(tok_ref[...], order_ref)
    u_ref[...] = value.astype(BF16)
    add_stats(stats_ref, value)


def add_stats(stats_ref, value):
    add_rows(stats_ref, column_sum(value), column_sum(value * value))


def add_rows(copies_ref, first, second):
    i, nt = pl.program_id(0), pl.num_programs(0)
    chunks = first.shape[1] // 128

    @pl.when(i == 0)
    def _():
        copies_ref[0] = jnp.zeros(copies_ref.shape[1:], F32)

    for c in range(chunks):
        copies_ref[0, c : c + 1] += first[:, cols(c)]
        copies_ref[0, SLOT + c : SLOT + c + 1] += second[:, cols(c)]

    @pl.when(i == nt - 1)
    def _():
        copies_ref[...] = jnp.broadcast_to(copies_ref[0:1], copies_ref.shape)


def summed(ref):
    total = jnp.sum(ref[...], axis=0)
    return tuple(
        jnp.concatenate([total[SLOT * k + c : SLOT * k + c + 1] for c in range(SLOT)], axis=1)
        for k in range(2)
    )


def drive_kernel(layer, down, tokens, *refs):
    (
        stat_ref, u_ref, gain_ref, bias_ref, skip_ref, win_ref, disc_ref, jr_ref,
        b_ref, end_ref, blk_ref, norm_ref,
    ) = refs
    i, nt = pl.program_id(0), pl.num_programs(0)
    steps = u_ref.shape[0] // LANES
    chunks = chunk_count(b_ref)
    half = chunks * 128

    @pl.when(i == 0)
    def _():
        total, squares = summed(stat_ref)
        row = slice(layer, layer + 1)
        mean = total / tokens
        inv = lax.rsqrt(squares / tokens - mean * mean + EPSILON)
        norm_ref[0:1] = mean
        norm_ref[1:2] = inv
        norm_ref[2:3] = inv * gain_ref[row]
        norm_ref[3:4] = bias_ref[row]
        norm_ref[4:5] = skip_ref[row]
        norm_ref[5:8] = jnp.zeros((3, norm_ref.shape[1]), F32)
        blk_ref[...] = jnp.zeros_like(blk_ref)

    u = u_ref[...].astype(F32)
    normed = (u - norm_ref[0:1]) * norm_ref[2:3] + norm_ref[3:4]
    drive = jnp.dot(normed.astype(BF16), win_ref[...], preferred_element_type=F32)
    fr, fi = disc_ref[1:2, :half], disc_ref[1:2, half:]
    re, im = drive[:, :half], drive[:, half:]
    b_ref[:, :half] = re * fr - im * fi
    b_ref[:, half:] = re * fi + im * fr
    tile = nt - 1 - i if down else i
    scan_tile(b_ref, blk_ref, disc_row(disc_ref, 0, chunks), jr_ref, tile * steps, steps, down)

    @pl.when(i == nt - 1)
    def _():
        zero = [jnp.zeros((1, 128), F32)] * chunks
        cr, ci = chain(blk_ref, jr_ref, disc_row(disc_ref, 2, chunks), (zero, zero), down)
        put_copies(end_ref, cr, ci)


def states_of(ends_ref, table_ref, b_ref, blk_ref, disc_ref, jr_ref, low_ref, st_ref, down):
    i, nt = pl.program_id(0), pl.num_programs(0)
    chunks = chunk_count(b_ref)
    steps = b_ref.shape[0] // LANES

    @pl.when(i == 0)
    def _():
        carry = carry_in(ends_ref, table_ref, chunks)
        chain(blk_ref, jr_ref, disc_row(disc_ref, 2, chunks), carry, down, st_ref)

    def emit(low_step, pair, extra):
        if pair is None:
            return ()
        (first, second) = pair
        store_pair(low_ref, low_step, first, second)
        return ()

    tile = nt - 1 - i if down else i
    scan_tile(
        b_ref, st_ref, disc_row(disc_ref, 0, chunks), jr_ref, tile * steps, steps, down, emit
    )


def gelu_parts(mixed):
    square = mixed * mixed
    tanh = jnp.tanh(mixed * (GELU_A + (GELU_A * GELU_B) * square))
    half_up = 0.5 + 0.5 * tanh
    return square, tanh, half_up


def gelu_slope(mixed, square, tanh, half_up):
    return half_up + (mixed * (0.5 - 0.5 * tanh * tanh)) * (
        GELU_A + (3.0 * GELU_A * GELU_B) * square
    )


def sigmoid(value):
    return 0.5 + 0.5 * jnp.tanh(0.5 * value)


def forward_kernel(down, *refs):
    (
        ends_ref, table_ref, b_ref, blk_ref, disc_ref, jr_ref, u_ref, norm_ref, wout_ref, wgate_ref,
        next_ref, low_ref, mixed_ref, gate_ref, stats_ref, st_ref,
    ) = refs
    states_of(ends_ref, table_ref, b_ref, blk_ref, disc_ref, jr_ref, low_ref, st_ref, down)
    u = u_ref[...].astype(F32)
    normed = (u - norm_ref[0:1]) * norm_ref[2:3] + norm_ref[3:4]
    mixed = jnp.dot(low_ref[...], wout_ref[...], preferred_element_type=F32)
    mixed += norm_ref[4:5] * normed
    _, _, half_up = gelu_parts(mixed)
    act = mixed * half_up
    gate = sigmoid(jnp.dot(act.astype(BF16), wgate_ref[...], preferred_element_type=F32))
    after = u + act * gate
    next_ref[...] = after
    mixed_ref[...] = mixed.astype(mixed_ref.dtype)
    gate_ref[...] = gate.astype(gate_ref.dtype)
    add_stats(stats_ref, after)


def accumulate(ref, value):
    @pl.when(pl.program_id(0) == 0)
    def _():
        ref[...] = value

    @pl.when(pl.program_id(0) != 0)
    def _():
        ref[...] += value


def gate_backward(g, mixed, gate, normed, low_ref, wout_ref, wgate_ref, outs, kept=None):
    pg_ref, sg_ref, wsum_ref, ssum_ref = outs
    states, width = wout_ref.shape
    square, tanh, half_up = gelu_parts(mixed) if kept is None else kept
    act = mixed * half_up
    g_gate = g * gate
    logit_grad = (g_gate * act * (1.0 - gate)).astype(BF16)
    accumulate(
        wsum_ref.at[states : states + width],
        lax.dot_general(act.astype(BF16), logit_grad, TN, preferred_element_type=F32),
    )
    act_grad = g_gate + lax.dot_general(
        logit_grad, wgate_ref[...], NT, preferred_element_type=F32
    )
    mixed_grad = act_grad * gelu_slope(mixed, square, tanh, half_up)
    accumulate(ssum_ref, column_sum(mixed_grad * normed))
    proj_grad = mixed_grad.astype(BF16)
    pg_ref[...] = proj_grad
    accumulate(
        wsum_ref.at[:states],
        lax.dot_general(low_ref[...], proj_grad, TN, preferred_element_type=F32),
    )
    sg_ref[...] = lax.dot_general(proj_grad, wout_ref[...], NT, preferred_element_type=F32)


def turn_kernel(down, *refs):
    (
        ends_ref, table_ref, b_ref, blk_ref, disc_ref, jr_ref, jo_ref, u_ref, norm_ref, wout_ref, wgate_ref,
        gout_ref, order_ref,
        out_ref, low_ref, g_ref, pg_ref, sg_ref, wsum_ref, end_ref, ablk_ref,
        st_ref, w_ref,
    ) = refs
    sums = wout_ref.shape[0] + wout_ref.shape[1]
    ssum_ref = wsum_ref.at[sums : sums + 1]
    i, nt = pl.program_id(0), pl.num_programs(0)
    chunks = chunk_count(b_ref)
    half = chunks * 128
    steps = b_ref.shape[0] // LANES
    tile = nt - 1 - i if down else i
    states_of(ends_ref, table_ref, b_ref, blk_ref, disc_ref, jr_ref, low_ref, st_ref, down)
    u = u_ref[...]
    normed = (u - norm_ref[0:1]) * norm_ref[2:3] + norm_ref[3:4]
    mixed = jnp.dot(low_ref[...], wout_ref[...], preferred_element_type=F32)
    mixed += norm_ref[4:5] * normed
    kept = gelu_parts(mixed)
    act = mixed * kept[2]
    gate = sigmoid(jnp.dot(act.astype(BF16), wgate_ref[...], preferred_element_type=F32))
    permute_out(u + act * gate, order_ref, out_ref)
    g = permute_in(gout_ref[...], order_ref)
    g_ref[...] = g.astype(BF16)
    gate_backward(
        g, mixed, gate, normed, low_ref, wout_ref, wgate_ref,
        (pg_ref, sg_ref, wsum_ref, ssum_ref), kept,
    )

    @pl.when(i == 0)
    def _():
        wsum_ref[sums + 1 :] = jnp.zeros((7, wsum_ref.shape[1]), F32)
        w_ref[:, :half] = jnp.ones((LANES, half), F32)
        w_ref[:, half:] = jnp.zeros((LANES, half), F32)
        ablk_ref[...] = jnp.zeros_like(ablk_ref)

    dr, di = disc_row(disc_ref, 0, chunks, conj=True)
    dr, di = wide(dr), wide(di)
    jo = jo_ref[...]
    unroll = 4

    def body(k, carry):
        wr, wi, ar, ai = (list(carry[n * chunks : (n + 1) * chunks]) for n in range(4))
        for q in range(unroll):
            n = k * unroll + q
            step = steps - 1 - n if down else n
            at = pl.ds(pl.multiple_of(step * LANES, LANES), LANES)
            sr, si = rows_of(sg_ref, at, chunks)
            live = jo != tile * steps + step
            for c in range(chunks):
                ar[c] = ar[c] + (wr[c] * sr[c] - wi[c] * si[c])
                ai[c] = ai[c] + (wr[c] * si[c] + wi[c] * sr[c])
                xr = jnp.where(live, wr[c], 0.0)
                xi = jnp.where(live, wi[c], 0.0)
                wr[c] = xr * dr[c] - xi * di[c]
                wi[c] = xr * di[c] + xi * dr[c]
        return tuple(wr) + tuple(wi) + tuple(ar) + tuple(ai)

    wr, wi = rows_of(w_ref, slice(0, LANES), chunks)
    ar, ai = rows_of(ablk_ref, slice(0, LANES), chunks)
    out = lax.fori_loop(
        0, steps // unroll, body, tuple(wr) + tuple(wi) + tuple(ar) + tuple(ai)
    )
    wr, wi, ar, ai = (list(out[n * chunks : (n + 1) * chunks]) for n in range(4))
    put_rows(w_ref, slice(0, LANES), wr, wi)
    put_rows(ablk_ref, slice(0, LANES), ar, ai)

    @pl.when(i == nt - 1)
    def _():
        zero = [jnp.zeros((1, 128), F32)] * chunks
        power = disc_row(disc_ref, 2, chunks, conj=True)
        cr, ci = chain(ablk_ref, jo_ref, power, (zero, zero), not down)
        put_copies(end_ref, cr, ci)


def adjoint_kernel(down, last, *refs):
    (
        ends_ref, table_ref, sg_ref, ablk_ref, disc_ref, jr_ref, low_ref, u_ref, norm_ref, pg_ref, g_ref,
        win_ref, order_ref, *refs
    ) = refs
    if last:
        (ssum_ref, res_ref, sums_ref, st_ref, dg_ref, ax_ref, nsum_ref, isum_ref) = refs
    else:
        (res_ref, sums_ref, nsum_ref, st_ref, dg_ref, ax_ref) = refs
        isum_ref = sums_ref.at[: win_ref.shape[0]]
    width, states = win_ref.shape
    i, nt = pl.program_id(0), pl.num_programs(0)
    chunks = chunk_count(sg_ref)
    half = chunks * 128
    steps = sg_ref.shape[0] // LANES
    tile = nt - 1 - i if down else i

    @pl.when(i == 0)
    def _():
        carry = carry_in(ends_ref, table_ref, chunks)
        power = disc_row(disc_ref, 2, chunks, conj=True)
        chain(ablk_ref, jr_ref, power, carry, down, st_ref)
        ax_ref[...] = jnp.zeros_like(ax_ref)

    fr, fi = disc_row(disc_ref, 1, chunks)
    fr, fi = wide(fr), wide(fi)

    def emit(low_step, pair, extra):
        if pair is None:
            re, im = rows_of(ax_ref, slice(0, LANES), chunks)
            return tuple(re) + tuple(im)
        sums_r, sums_i = list(extra[:chunks]), list(extra[chunks:])
        at = pl.ds(pl.multiple_of(low_step * LANES, 2 * LANES), 2 * LANES)
        xr, xi = rows_of(low_ref, at, chunks)
        grads = []
        for which, (ar, ai) in enumerate(pair):
            gr, gi = [], []
            rows = slice(which * LANES, (which + 1) * LANES)
            for c in range(chunks):
                vr, vi = xr[c].astype(F32)[rows], xi[c].astype(F32)[rows]
                sums_r[c] = sums_r[c] + (ar[c] * vr + ai[c] * vi)
                sums_i[c] = sums_i[c] + (ai[c] * vr - ar[c] * vi)
                gr.append(ar[c] * fr[c] + ai[c] * fi[c])
                gi.append(ai[c] * fr[c] - ar[c] * fi[c])
            grads.append((gr, gi))
        store_pair(dg_ref, low_step, grads[0], grads[1])
        return tuple(sums_r) + tuple(sums_i)

    sums = scan_tile(
        sg_ref, st_ref, disc_row(disc_ref, 0, chunks, conj=True), jr_ref, tile * steps, steps,
        down, emit,
    )
    put_rows(ax_ref, slice(0, LANES), list(sums[:chunks]), list(sums[chunks:]))

    u = u_ref[...].astype(F32)
    centered = u - norm_ref[0:1]
    normed = (centered * norm_ref[2:3] + norm_ref[3:4]).astype(BF16)
    drive_grad = dg_ref[...]
    accumulate(isum_ref, lax.dot_general(normed, drive_grad, TN, preferred_element_type=F32))
    normed_grad = lax.dot_general(drive_grad, win_ref[...], NT, preferred_element_type=F32)
    normed_grad += norm_ref[4:5] * pg_ref[...].astype(F32)
    add_rows(
        nsum_ref, column_sum(normed_grad), column_sum(normed_grad * centered) * norm_ref[1:2]
    )
    result = g_ref[...].astype(F32) + norm_ref[2:3] * normed_grad
    if last:
        permute_out(result, order_ref, res_ref)
    else:
        res_ref[...] = result

    @pl.when(i == nt - 1)
    def _():
        decays = jnp.sum(ax_ref[...], axis=0, keepdims=True)
        wr, wi = win_ref[:, :half].astype(F32), win_ref[:, half:].astype(F32)
        gr, gi = isum_ref[:, :half], isum_ref[:, half:]
        re = jnp.sum(wr * gr + wi * gi, axis=0, keepdims=True)
        im = jnp.sum(wr * gi - wi * gr, axis=0, keepdims=True)
        gr, gi = disc_ref[1:2, :half], disc_ref[1:2, half:]
        scale = 1.0 / (gr * gr + gi * gi)
        factors = ((re * gr - im * gi) * scale, (re * gi + im * gr) * scale)
        if last:
            rows = width // BLOCKS
            first = rows + rows // 2
            for b in range(BLOCKS):
                at = b * rows
                sums_ref[b, :rows] = isum_ref[at : at + rows, :width]
                sums_ref[b, rows:first, : states - width] = isum_ref[at : at + rows // 2, width:]
                sums_ref[b, rows:first, states - width :] = isum_ref[
                    at + rows // 2 : at + rows, width:
                ]
                sums_ref[b, first:] = jnp.zeros((SMALL, width), F32)
            small = [nsum_ref[0]] + [ssum_ref[:, cols(c)] for c in range(width // 128)]
            small += [decays[:, cols(c)] for c in range(2 * chunks)]
            small += [v[:, cols(c)] for v in factors for c in range(chunks)]
            small = [v[r : r + 1] for v in small for r in range(v.shape[0])]
            for k, row in enumerate(small):
                at = (k % SMALL, k // SMALL)
                sums_ref[0, first + at[0] : first + at[0] + 1, cols(at[1])] = row
        else:
            sums_ref[width : width + 8] = jnp.zeros((8, states), F32)
            sums_ref[width : width + 1] = decays
            sums_ref[width + 1 : width + 2, :half] = factors[0]
            sums_ref[width + 1 : width + 2, half:] = factors[1]


def back_kernel(down, tokens, core, *refs):
    (
        sums_ref, r_ref, up_ref, up_norm_ref, mixed_ref, gate_ref, low_ref, u_ref, norm_ref, wout_ref,
        wgate_ref, disc_ref, jo_ref,
        g_ref, pg_ref, sg_ref, kept_ref, sent_ref, ssum_ref, end_ref, ablk_ref, nsum_ref, bsum_ref, wsum_ref,
    ) = refs
    i, nt = pl.program_id(0), pl.num_programs(0)
    chunks = chunk_count(sg_ref)
    steps = sg_ref.shape[0] // LANES
    tile = nt - 1 - i if down else i

    @pl.when(i == 0)
    def _():
        nsum_ref[...] = jnp.sum(sums_ref[...], axis=0)
        bsum_ref[0:1], bsum_ref[1:2] = summed(sums_ref)
        ablk_ref[...] = jnp.zeros_like(ablk_ref)

    scale = up_norm_ref[2:3] * (-1.0 / tokens)
    standard = (up_ref[...] - up_norm_ref[0:1]) * (scale * up_norm_ref[1:2] * bsum_ref[1:2])
    g = r_ref[...] + (standard + scale * bsum_ref[0:1])
    g_ref[...] = g
    u = u_ref[...].astype(F32)
    normed = (u - norm_ref[0:1]) * norm_ref[2:3] + norm_ref[3:4]
    gate_backward(
        g, mixed_ref[...].astype(F32), gate_ref[...].astype(F32), normed, low_ref, wout_ref,
        wgate_ref, (pg_ref, sg_ref, wsum_ref, ssum_ref),
    )
    decay = disc_row(disc_ref, 0, chunks, conj=True)
    scan_tile(sg_ref, ablk_ref, decay, jo_ref, tile * steps, steps, down)

    @pl.when(i == nt - 1)
    def _():
        zero = [jnp.zeros((1, 128), F32)] * chunks
        power = disc_row(disc_ref, 2, chunks, conj=True)
        cr, ci = chain(ablk_ref, jo_ref, power, (zero, zero), down)
        put_copies(end_ref, cr, ci)
        states, width = wout_ref.shape
        gates, outs = width // BLOCKS, states // BLOCKS
        side = lax.axis_index(core)
        for ref, first in ((kept_ref, side), (sent_ref, 1 - side)):
            for b in range(BLOCKS // 2):
                at = first * (BLOCKS // 2) + b
                ref[b, :gates] = wsum_ref[pl.ds(pl.multiple_of(states + at * gates, 8), gates)]
                ref[b, gates:] = wsum_ref[pl.ds(pl.multiple_of(at * outs, 8), outs)]


def last_kernel(
    tokens, piece_ref, small_ref, out1_ref, gate1_ref, skip1_ref, in1_ref, decay1_ref, norm1_ref,
    disc_ref, rate_ref, step_ref, freq_ref, r_ref, tok_ref, norm_ref,
    grad_in_ref, gain_ref, bias_ref, drate_ref, dstep_ref, dfreq_ref, in_ref, out_ref, skip_ref,
    gate_ref,
):
    gates, width = gate1_ref.shape
    outs = out1_ref.shape[0]
    states = in1_ref.shape[1]
    half = states // 2
    left = states - width
    gate_ref[0], gate_ref[1] = piece_ref[:gates], gate1_ref[...]
    out_ref[0], out_ref[1] = piece_ref[gates : gates + outs], out1_ref[...]
    at = gates + outs
    in_ref[0, :, :width] = piece_ref[at : at + gates]
    at += gates
    in_ref[0, : gates // 2, width:] = piece_ref[at : at + gates // 2, :left]
    in_ref[0, gates // 2 :, width:] = piece_ref[at : at + gates // 2, left:]
    in_ref[1] = in1_ref[...]

    def row(ref, first, count):
        places = [(k % SMALL, k // SMALL) for k in range(first, first + count)]
        return jnp.concatenate([ref[r : r + 1, cols(c)] for r, c in places], axis=1)

    count = width // 128
    bias, gain = row(small_ref, 0, count), row(small_ref, count, count)
    scale = norm_ref[2:3] * (-1.0 / tokens)
    grad_in_ref[...] = r_ref[...] + (
        (tok_ref[...].astype(F32) - norm_ref[0:1]) * (scale * norm_ref[1:2] * gain) + scale * bias
    )

    @pl.when(pl.program_id(0) == 0)
    def _():
        bias_ref[0:1], gain_ref[0:1] = bias, gain
        bias_ref[1:2], gain_ref[1:2] = row(norm1_ref, 0, count), row(norm1_ref, count, count)
        skip_ref[0:1], skip_ref[1:2] = row(small_ref, 2 * count, count), skip1_ref[0:1]
        at = 3 * count
        lanes = half // 128
        for l in range(LAYERS):
            if l == 0:
                ar, ai, sr, si = (row(small_ref, at + k * lanes, lanes) for k in range(4))
            else:
                ar, ai = decay1_ref[0:1, :half], decay1_ref[0:1, half:]
                sr, si = decay1_ref[1:2, :half], decay1_ref[1:2, half:]
            dr, di = disc_ref[l, 0:1, :half], disc_ref[l, 0:1, half:]
            fr, fi = disc_ref[l, 1:2, :half], disc_ref[l, 1:2, half:]
            here = slice(l, l + 1)
            rate, freq, step = rate_ref[here], freq_ref[here], jnp.exp(step_ref[here])
            tr = ar - (fr * sr + fi * si)
            ti = ai - (fr * si - fi * sr)
            size = 1.0 / (dr * dr + di * di)
            gr, gi = (tr * dr - ti * di) * size, (tr * di + ti * dr) * size
            mr, mi = -rate * fr - freq * fi, freq * fr - rate * fi
            size = 1.0 / (rate * rate + freq * freq)
            gr += (-rate * sr - freq * si) * size
            gi += (freq * sr - rate * si) * size
            both = 2.0 * (fr * sr + fi * si)
            gx = gr * dr + gi * di
            gy = gi * dr - gr * di
            drate_ref[here] = (-mr * sr - mi * si - both * rate) * size - step * gx
            dfreq_ref[here] = (mi * sr - mr * si - both * freq) * size + step * gy
            dstep_ref[here] = step * (freq * gy - rate * gx)


def whole(array):
    shape = array.shape
    return pl.BlockSpec(shape, lambda i: (0,) * len(shape))


def tile_spec(rows, width, nt, down):
    if down:
        return pl.BlockSpec((rows, width), lambda i: (nt - 1 - i, 0))
    return pl.BlockSpec((rows, width), lambda i: (i, 0))


def run_spec(steps, width, nt, down):
    if down:
        return pl.BlockSpec((LANES, steps, width), lambda i: (0, nt - 1 - i, 0))
    return pl.BlockSpec((LANES, steps, width), lambda i: (0, i, 0))


def call(kernel, nt, args, outs, scratch, macs, name):
    arrays = [a for a, *_ in args]
    sizes = sum(a.size * a.dtype.itemsize for a in arrays + [a for a, *_ in outs])
    held = [
        a if keep is None else pltpu.with_memory_space_constraint(a, keep)
        for a, _, keep in map(filled, args)
    ]
    return pl.pallas_call(
        kernel,
        grid=(nt,),
        in_specs=[whole(a) if s is None else s for a, s, _ in map(filled, args)],
        out_specs=[whole(a) if s is None else s for a, s, _ in map(filled, outs)],
        out_shape=[
            a if keep is None else keep(a.shape, a.dtype) for a, _, keep in map(filled, outs)
        ],
        scratch_shapes=scratch,
        compiler_params=pltpu.CompilerParams(
            vmem_limit_bytes=VMEM_LIMIT, dimension_semantics=("arbitrary",)
        ),
        cost_estimate=pl.CostEstimate(flops=2 * macs, bytes_accessed=sizes, transcendentals=0),
        name=name,
    )(*held)


def filled(entry):
    return entry if len(entry) == 3 else entry + (pltpu.HBM,)


def shape(*dims, dtype=F32):
    return jax.ShapeDtypeStruct(dims, dtype)


def body(
    axes,
    tokens_in,
    seq_starts,
    norm_gain,
    norm_bias,
    decay_rate,
    step_log,
    frequency,
    in_proj,
    out_proj,
    skip_gain,
    gate_proj,
    grad_out,
):
    rows, width = tokens_in.shape
    states = in_proj.shape[-1]
    devices = 2 ** len(axes)
    tokens = float(rows * devices)
    run = rows // LANES
    steps = min(64, run)
    tile = steps * LANES
    nt = rows // tile
    span = min(32, steps)
    def tiles(array, down):
        return (array, tile_spec(tile, array.shape[-1], nt, down))

    def runs(array, down):
        return (array, run_spec(steps, array.shape[-1], nt, down))

    def full(array):
        return (array, None)

    def of(array, l):
        size = array.shape[1:]
        return (array, pl.BlockSpec((None,) + size, lambda i: (l,) + (0,) * len(size)))

    discs, tables, cuts, order = call(
        functools.partial(prep_kernel, rows, axes), 1,
        [full(seq_starts[None]), full(decay_rate),
         full(step_log), full(frequency)],
        [full(shape(LAYERS, 8, states)), full(shape(2 * LAYERS, 2, devices, 2 * SLOT, 128)),
         full(shape(2, LANES, 128, dtype=jnp.int32)),
         full(shape(span * LANES, span * LANES, dtype=BF16))],
        [], rows * width, "prep",
    )

    def near(entry):
        return entry[:2] + (pltpu.VMEM if rows * states * 4 <= 7 * 2**20 else pltpu.HBM,)

    tokens_run = tokens_in.reshape(LANES, run, width)
    grad_run = grad_out.reshape(LANES, run, width)
    state_scratch = pltpu.VMEM((LANES, states), F32)
    cost = rows * width * states

    u0, stats = call(
        stats_kernel, nt, [runs(tokens_run, 0), full(order)],
        [tiles(shape(rows, width, dtype=BF16), 0), near(full(shape(devices, 2 * SLOT, 128)))],
        [], cost // 2, "stats",
    )

    def drive(l, stream, stats):
        down = l % 2
        return call(
            functools.partial(drive_kernel, l, bool(down), tokens), nt,
            [near(full(gather_all(stats, axes))), tiles(stream, down), full(norm_gain), full(norm_bias), full(skip_gain), of(in_proj, l), of(discs, l),
               of(cuts, down)],
            [near(tiles(shape(rows, states), down)), near(full(shape(devices, 2 * SLOT, 128))),
             full(shape(LANES, states)), full(shape(8, width))],
            [], 4 * cost, f"drive_{l}",
        )

    b0, end0, blk0, norm0 = drive(0, u0, stats)
    u1, low0, mixed0, gate0, stats = call(
        functools.partial(forward_kernel, False), nt,
        [near(full(gather_all(end0, axes))), of(tables, 2 * 0 + 0), near(tiles(b0, 0)), full(blk0), of(discs, 0), of(cuts, 0),
           tiles(u0, 0), full(norm0), of(out_proj, 0), of(gate_proj, 0)],
        [tiles(shape(rows, width), 0), tiles(shape(rows, states, dtype=BF16), 0),
         tiles(shape(rows, width, dtype=BF16), 0), tiles(shape(rows, width, dtype=BF16), 0),
         near(full(shape(devices, 2 * SLOT, 128)))],
        [state_scratch], 6 * cost, "forward_0",
    )

    b1, end1, blk1, norm1 = drive(1, u1, stats)
    (
        out, low1, g1, pg1, sg1, w_sum1, aend1, ablk1
    ) = call(
        functools.partial(turn_kernel, True), nt,
        [near(full(gather_all(end1, axes))), of(tables, 2 * 1 + 0), near(tiles(b1, 1)), full(blk1), of(discs, 1), of(cuts, 1),
           of(cuts, 0), tiles(u1, 1), full(norm1), of(out_proj, 1), of(gate_proj, 1),
           runs(grad_run, 1), full(order)],
        [runs(shape(LANES, run, width), 1), near(tiles(shape(rows, states, dtype=BF16), 1)),
         near(tiles(shape(rows, width, dtype=BF16), 1)),
         near(tiles(shape(rows, width, dtype=BF16), 1)), near(tiles(shape(rows, states), 1)), full(shape(states + width + 8, width)),
         near(full(shape(devices, 2 * SLOT, 128))), full(shape(LANES, states))],
        [state_scratch, state_scratch], 16 * cost, "turn_1",
    )

    def adjoint(l, sg, ablk, ends, low, stream, norm, pg, g, skip_sum=None):
        down = 1 - l % 2
        last = l == 0
        held = (lambda entry: entry) if last else near
        args = [
            near(full(ends)), of(tables, 2 * l + 1), held(tiles(sg, down)), full(ablk), of(discs, l),
            of(cuts, down), held(tiles(low, down)), tiles(stream, down),
            full(norm), held(tiles(pg, down)), held(tiles(g, down)), of(in_proj, l), full(order),
        ]
        scratch = [state_scratch, pltpu.VMEM((tile, states), BF16), state_scratch]
        if last:
            args.append(full(skip_sum))
            outs = [
                runs(shape(LANES, run, width), down),
                full(shape(BLOCKS, (width + width // 2) // BLOCKS + SMALL, width)),
            ]
            scratch += [pltpu.VMEM((1, 2 * SLOT, 128), F32), pltpu.VMEM((width, states), F32)]
        else:
            outs = [
                tiles(shape(rows, width), down), full(shape(width + 8, states)),
                near(full(shape(devices, 2 * SLOT, 128))),
            ]
        return call(
            functools.partial(adjoint_kernel, bool(down), last), nt, args, outs, scratch,
            8 * cost, f"adjoint_{l}",
        )

    r1, in_sum1, norm_sum1 = adjoint(
        1, sg1, ablk1, gather_all(aend1, axes), low1, u1, norm1, pg1, g1
    )

    piece = (2 * width + states + width // 2) // BLOCKS + SMALL

    def lower(r1, norm_sum1):
        half = shape(BLOCKS // 2, (states + width) // BLOCKS, width)
        (
            g0, pg0, sg0, kept0, sent0, skip_sum0, aend0, ablk0, small1, _
        ) = call(
            functools.partial(back_kernel, True, tokens, axes[-1]), nt,
            [near(full(gather_all(norm_sum1, axes))), tiles(r1, 1), tiles(u1, 1), full(norm1),
             tiles(mixed0, 1), tiles(gate0, 1), tiles(low0, 1), tiles(u0, 1), full(norm0),
             of(out_proj, 0), of(gate_proj, 0), of(discs, 0), of(cuts, 1)],
            [tiles(shape(rows, width), 1), tiles(shape(rows, width, dtype=BF16), 1),
             tiles(shape(rows, states), 1), full(half), full(half), full(shape(1, width)), near(full(shape(devices, 2 * SLOT, 128))),
             full(shape(LANES, states)), full(shape(2 * SLOT, 128)), full(shape(2, width))],
            [pltpu.VMEM((states + width, width), F32)], 12 * cost, "back_0",
        )
        core, chips, *others = phases(axes)
        part = kept0 + lax.ppermute(sent0, core[0], [(0, 1), (1, 0)])
        ends, part = lax.optimization_barrier((gather_all(aend0, axes), part))
        part = part.reshape(-1, width)
        part = scatter_sum(part, chips)
        r0, in_sum0 = adjoint(0, sg0, ablk0, ends, low0, u0, norm0, pg0, g0, skip_sum0)
        in_sum0, part = lax.optimization_barrier((in_sum0, part))
        in_part = scatter_sum(scatter_sum(in_sum0.reshape(-1, width), core), chips)
        pad = -piece % (8 * 2 ** len(others[0]))
        part = jnp.concatenate([part, in_part, jnp.zeros((pad, width), F32)], axis=0)
        part = sum_all(part, others)[:piece]
        pieces = gather_rows(gather_rows(part, chips), core)
        return r0.reshape(rows, width), small1, pieces.reshape(BLOCKS, -1, width)

    def nothing(r1, norm_sum1):
        return (
            jnp.zeros((rows, width), F32),
            jnp.zeros((2 * SLOT, 128), F32),
            jnp.zeros((BLOCKS, piece, width), F32),
        )

    w_all1, in_all1 = lax.psum((w_sum1, in_sum1), axes)
    r0, norm_all1, pieces = lax.cond(seq_starts[0] == 0, lower, nothing, r1, norm_sum1)

    gates, outs = width // BLOCKS, states // BLOCKS

    def block(array, *dims, at=lambda i: (i, 0)):
        return (array, pl.BlockSpec(dims, at))

    def flat(array, count):
        return block(array, count, array.shape[1])

    (
        grad_in, gain_grad, bias_grad, rate_grad, step_grad, freq_grad, in_grad, out_grad,
        skip_grad, gate_grad,
    ) = call(
        functools.partial(last_kernel, tokens), BLOCKS,
        [block(pieces, None, piece, width, at=lambda i: (i, 0, 0)) + (None,),
         block(pieces, None, SMALL, width, at=lambda i: (0, piece // SMALL - 1, 0)) + (None,),
         flat(w_all1, outs),
         block(w_all1, gates, width, at=lambda i: (states // gates + i, 0)),
         block(w_all1, 8, width, at=lambda i: ((states + width) // 8, 0)),
         flat(in_all1, gates),
         block(in_all1, 8, states, at=lambda i: (width // 8, 0)),
         full(norm_all1), full(discs), full(decay_rate), full(step_log), full(frequency),
         flat(r0, rows // BLOCKS), flat(tokens_in, rows // BLOCKS), full(norm0)],
        [flat(shape(rows, width), rows // BLOCKS), full(shape(LAYERS, width)),
         full(shape(LAYERS, width)), full(shape(LAYERS, states // 2)),
         full(shape(LAYERS, states // 2)), full(shape(LAYERS, states // 2)),
         block(shape(LAYERS, width, states), LAYERS, gates, states, at=lambda i: (0, i, 0)),
         block(shape(LAYERS, states, width), LAYERS, outs, width, at=lambda i: (0, i, 0)),
         full(shape(LAYERS, width)),
         block(shape(LAYERS, width, width), LAYERS, gates, width, at=lambda i: (0, i, 0))],
        [], cost, "last",
    )
    return (
        out.reshape(rows, width),
        grad_in,
        gain_grad,
        bias_grad,
        rate_grad,
        step_grad,
        freq_grad,
        in_grad,
        out_grad,
        skip_grad,
        gate_grad,
    )


def solution(mesh):
    bits = mesh.devices.size.bit_length() - 1
    axes = tuple("b%d" % k for k in range(bits))
    binary = Mesh(mesh.devices.reshape((2,) * bits), axes)
    rows = P(axes, None)
    return jax.shard_map(
        functools.partial(body, axes),
        mesh=binary,
        in_specs=(rows,) + (P(),) * 10 + (rows,),
        out_specs=(rows, rows) + (P(),) * 9,
        check_vma=False,
    )
```

```python
import functools

import jax
import jax.numpy as jnp
from jax import lax
from jax.experimental import pallas as pl
from jax.experimental.pallas import tpu as pltpu
from jax.sharding import Mesh, PartitionSpec as P

LAYERS = 2
EPSILON = 1e-05
SMALL = 8
BLOCKS = 8
SLOT = 4
LANES = 8
VMEM_LIMIT = 30 * 1024 * 1024
GELU_A = 0.7978845608028654
GELU_B = 0.044715
NT = (((1,), (1,)), ((), ()))
TN = (((0,), (0,)), ((), ()))
F32 = jnp.float32
BF16 = jnp.bfloat16


def gather_all(copies, axes):
    return lax.all_to_all(copies, axes, 0, 0)


def scatter_sum(value, axes):
    count = 2 ** len(axes)
    pieces = value.reshape((count, value.shape[0] // count) + value.shape[1:])
    return jnp.sum(lax.all_to_all(pieces, axes, 0, 0), axis=0)


def gather_rows(value, axes):
    count = 2 ** len(axes)
    copies = jnp.broadcast_to(value, (count,) + value.shape)
    return lax.all_to_all(copies, axes, 0, 0).reshape((count * value.shape[0],) + value.shape[1:])


def phases(axes):
    left, out = list(axes), [(axes[-1],)]
    left = left[:-1]
    while left:
        out.append(tuple(left[-2:]))
        left = left[:-2]
    return out


def sum_all(value, parts):
    for part in parts:
        value = scatter_sum(value, part)
    for part in reversed(parts):
        value = gather_rows(value, part)
    return value


def cols(c):
    return slice(c * 128, (c + 1) * 128)


def chunk_count(ref):
    return ref.shape[-1] // 256


def rows_of(ref, at, chunks):
    half = chunks * 128
    re = [ref[at, c * 128 : (c + 1) * 128] for c in range(chunks)]
    im = [ref[at, half + c * 128 : half + (c + 1) * 128] for c in range(chunks)]
    return re, im


def put_rows(ref, at, re, im):
    chunks = len(re)
    half = chunks * 128
    for c in range(chunks):
        ref[at, c * 128 : (c + 1) * 128] = re[c]
        ref[at, half + c * 128 : half + (c + 1) * 128] = im[c]


def put_copies(ref, re, im):
    ref[0] = jnp.zeros(ref.shape[1:], F32)
    for c in range(len(re)):
        ref[0, c : c + 1] = re[c]
        ref[0, SLOT + c : SLOT + c + 1] = im[c]
    ref[...] = jnp.broadcast_to(ref[0:1], ref.shape)


def wide(rows):
    return [jnp.broadcast_to(v, (LANES, 128)) for v in rows]


def chain(ends_ref, jr_ref, power, carry, down, start_ref=None):
    chunks = len(power[0])
    pr, pi = power
    cr, ci = carry
    order = range(LANES - 1, -1, -1) if down else range(LANES)
    for s in order:
        at = slice(s, s + 1)
        if start_ref is not None:
            put_rows(start_ref, at, cr, ci)
        er, ei = rows_of(ends_ref, at, chunks)
        alive = (jr_ref[at, :] < 0).astype(F32)
        cr, ci = (
            [er[c] + alive * (pr[c] * cr[c] - pi[c] * ci[c]) for c in range(chunks)],
            [ei[c] + alive * (pr[c] * ci[c] + pi[c] * cr[c]) for c in range(chunks)],
        )
    return cr, ci


def carry_in(ends_ref, table_ref, chunks):
    total = jnp.zeros((2 * SLOT, 128), F32)
    for e in range(ends_ref.shape[0]):
        end = ends_ref[e]
        turned = jnp.concatenate([end[SLOT:], end[:SLOT]], axis=0)
        total += table_ref[0, e] * end + table_ref[1, e] * turned
    return (
        [total[c : c + 1] for c in range(chunks)],
        [total[SLOT + c : SLOT + c + 1] for c in range(chunks)],
    )


def in_stages(stages, parts):
    for turn in range(len(parts) + len(stages) - 1):
        for k, stage in enumerate(stages):
            if 0 <= turn - k < len(parts):
                stage(parts[turn - k])


def parts_of(rows, down):
    half = rows // 2 if rows >= 32 * LANES else rows
    parts = [(at, at + half) for at in range(0, rows, half)]
    return parts[::-1] if down else parts


class Scan:
    def __init__(self, src_ref, st_ref, decay, jr_ref, first_step, down):
        self.src_ref, self.st_ref, self.down = src_ref, st_ref, down
        self.chunks = chunk_count(src_ref)
        self.dr, self.di = wide(decay[0]), wide(decay[1])
        self.jr, self.first_step = jr_ref[...], first_step
        self.state = rows_of(st_ref, slice(0, LANES), self.chunks)

    def one(self, step):
        br, bi = rows_of(self.src_ref, slice(step * LANES, (step + 1) * LANES), self.chunks)
        live = self.jr != self.first_step + step
        nr, ni = [], []
        for c in range(self.chunks):
            xr = jnp.where(live, self.state[0][c], 0.0)
            xi = jnp.where(live, self.state[1][c], 0.0)
            nr.append(self.dr[c] * xr - self.di[c] * xi + br[c])
            ni.append(self.dr[c] * xi + self.di[c] * xr + bi[c])
        self.state = (nr, ni)
        return nr, ni

    def run(self, part, emit=None):
        low, high = part[0] // LANES, part[1] // LANES
        for n in range(0, high - low, 2):
            step = high - 2 - n if self.down else low + n
            first = self.one(step + 1 if self.down else step)
            second = self.one(step if self.down else step + 1)
            if emit is not None:
                pair = (second, first) if self.down else (first, second)
                emit(slice(step * LANES, (step + 2) * LANES), pair)

    def close(self):
        put_rows(self.st_ref, slice(0, LANES), *self.state)


def store_pair(ref, at, first, second):
    re = [jnp.concatenate([p, q], axis=0).astype(BF16) for p, q in zip(first[0], second[0])]
    im = [jnp.concatenate([p, q], axis=0).astype(BF16) for p, q in zip(first[1], second[1])]
    put_rows(ref, at, re, im)


def disc_row(disc_ref, row, chunks, conj=False):
    re, im = rows_of(disc_ref, slice(row, row + 1), chunks)
    return (re, [-v for v in im]) if conj else (re, im)


def column_sum(value):
    rows, width = value.shape
    return jnp.sum(jnp.sum(value.reshape(rows // 8, 8, width), axis=0), axis=0, keepdims=True)


def permute_in(block_ref, order_ref, part):
    runs, _, width = block_ref.shape
    size = order_ref.shape[0]
    span = size // runs
    out = []
    for k in range(part[0] // size, part[1] // size):
        rows = block_ref[:, k * span : (k + 1) * span, :].reshape(size, width)
        out.append(jnp.dot(order_ref[...], rows, preferred_element_type=F32))
    return out[0] if len(out) == 1 else jnp.concatenate(out, axis=0)


def permute_out(value, order_ref, out_ref, part):
    width = value.shape[1]
    size = order_ref.shape[0]
    span = size // LANES
    high = value.astype(BF16)
    low = (value - high.astype(F32)).astype(BF16)
    for n, k in enumerate(range(part[0] // size, part[1] // size)):
        at = slice(n * size, (n + 1) * size)
        back = lax.dot_general(order_ref[...], high[at], TN, preferred_element_type=F32)
        back += lax.dot_general(order_ref[...], low[at], TN, preferred_element_type=F32)
        out_ref[:, k * span : (k + 1) * span, :] = back.reshape(LANES, span, width)


def expm1(value):
    acc = jnp.full_like(value, 1.0 / 479001600.0)
    for n in (39916800.0, 3628800.0, 362880.0, 40320.0, 5040.0, 720.0, 120.0, 24.0, 6.0, 2.0, 1.0):
        acc = acc * value + 1.0 / n
    return jnp.where(value > -1.0, acc * value, jnp.exp(value) - 1.0)


def prep_kernel(
    rows, axes, starts_ref, rate_ref, step_ref, freq_ref,
    disc_ref, table_ref, cut_ref, order_ref,
):
    devices = 2 ** len(axes)
    total = rows * devices
    run = rows // LANES
    half = rate_ref.shape[-1]
    me = 0
    for axis in axes:
        me = 2 * me + lax.axis_index(axis)
    starts = [starts_ref[:, k : k + 1] for k in range(starts_ref.shape[1])]

    base = me * rows + run * lax.broadcasted_iota(jnp.int32, (LANES, 128), 0)
    up = jnp.full((LANES, 128), -1, jnp.int32)
    down = up
    for begin in starts + [total]:
        rel = begin - base
        up = jnp.maximum(up, jnp.where((rel >= 0) & (rel < run), rel, -1))
        down = jnp.maximum(down, jnp.where((rel >= 1) & (rel <= run), rel - 1, -1))
    cut_ref[0] = up
    cut_ref[1] = down

    size = order_ref.shape[0]
    span = size // LANES
    to = lax.broadcasted_iota(jnp.int32, (size, size), 0)
    back = lax.broadcasted_iota(jnp.int32, (size, size), 1)
    order_ref[...] = ((to % LANES) * span + to // LANES == back).astype(F32).astype(BF16)

    source = lax.broadcasted_iota(jnp.int32, (devices, half), 0)
    for l in range(LAYERS):
        row = slice(l, l + 1)
        rate, freq = rate_ref[row], freq_ref[row]
        step_size = jnp.exp(step_ref[row])
        real_angle = -rate * step_size
        imag_angle = freq * step_size
        magnitude = jnp.exp(real_angle)
        cosine, sine = jnp.cos(imag_angle), jnp.sin(imag_angle)
        minus_real = expm1(real_angle) * cosine - 2.0 * jnp.sin(0.5 * imag_angle) ** 2
        minus_imag = magnitude * sine
        modulus = rate * rate + freq * freq
        disc_ref[l, 0:1, :half] = magnitude * cosine
        disc_ref[l, 0:1, half:] = minus_imag
        disc_ref[l, 1:2, :half] = (-rate * minus_real + freq * minus_imag) / modulus
        disc_ref[l, 1:2, half:] = (-rate * minus_imag - freq * minus_real) / modulus
        magnitude = jnp.exp(real_angle * float(run))
        disc_ref[l, 2:3, :half] = magnitude * jnp.cos(imag_angle * float(run))
        disc_ref[l, 2:3, half:] = magnitude * jnp.sin(imag_angle * float(run))
        disc_ref[l, 3:8] = jnp.zeros((5, 2 * half), F32)
        powers = []
        for bit in range(len(axes)):
            magnitude = jnp.exp(real_angle * float(rows << bit))
            angle = imag_angle * float(rows << bit)
            powers.append((magnitude * jnp.cos(angle), magnitude * jnp.sin(angle)))
        for back in range(2):
            going_down = (l + back) % 2 == 1
            if going_down:
                live, count = source > me, source - me - 1
            else:
                live, count = source < me, me - 1 - source
            for begin in starts:
                if going_down:
                    cut = (begin > (me + 1) * rows) & (source * rows >= begin)
                else:
                    cut = (begin < me * rows) & ((source + 1) * rows <= begin)
                live &= ~cut
            count = jnp.maximum(count, 0)
            real = live.astype(F32)
            imag = jnp.zeros((devices, half), F32)
            for bit, (pr, pi) in enumerate(powers):
                use = (count & (1 << bit)) != 0
                pr, pi = jnp.where(use, pr, 1.0), jnp.where(use, pi, 0.0)
                real, imag = real * pr - imag * pi, real * pi + imag * pr
            imag = -imag if back else imag
            at = 2 * l + back
            table_ref[at] = jnp.zeros(table_ref.shape[1:], F32)
            for c in range(half // 128):
                table_ref[at, 0, :, c, :] = real[:, cols(c)]
                table_ref[at, 0, :, SLOT + c, :] = real[:, cols(c)]
                table_ref[at, 1, :, c, :] = -imag[:, cols(c)]
                table_ref[at, 1, :, SLOT + c, :] = imag[:, cols(c)]


def stats_kernel(tok_ref, order_ref, u_ref, copy_ref, stats_ref):
    value = permute_in(tok_ref, order_ref, (0, u_ref.shape[0]))
    u_ref[...] = value.astype(BF16)
    copy_ref[...] = u_ref[...]
    zero_first(stats_ref)
    add_stats(stats_ref, value)
    spread_last(stats_ref)


def add_stats(stats_ref, value):
    add_rows(stats_ref, column_sum(value), column_sum(value * value))


def add_rows(copies_ref, first, second):
    for c in range(first.shape[1] // 128):
        copies_ref[0, c : c + 1] += first[:, cols(c)]
        copies_ref[0, SLOT + c : SLOT + c + 1] += second[:, cols(c)]


def summed(ref):
    total = jnp.sum(ref[...], axis=0)
    return tuple(
        jnp.concatenate([total[SLOT * k + c : SLOT * k + c + 1] for c in range(SLOT)], axis=1)
        for k in range(2)
    )


def drive_kernel(layer, down, tokens, *refs):
    (
        stat_ref, u_ref, gain_ref, bias_ref, skip_ref, win_ref, disc_ref, jr_ref,
        b_ref, end_ref, blk_ref, norm_ref,
    ) = refs
    i, nt = pl.program_id(0), pl.num_programs(0)
    steps = u_ref.shape[0] // LANES
    chunks = chunk_count(b_ref)
    half = chunks * 128

    @pl.when(i == 0)
    def _():
        total, squares = summed(stat_ref)
        row = slice(layer, layer + 1)
        mean = total / tokens
        inv = lax.rsqrt(squares / tokens - mean * mean + EPSILON)
        norm_ref[0:1] = mean
        norm_ref[1:2] = inv
        norm_ref[2:3] = inv * gain_ref[row]
        norm_ref[3:4] = bias_ref[row]
        norm_ref[4:5] = skip_ref[row]
        norm_ref[5:8] = jnp.zeros((3, norm_ref.shape[1]), F32)
        blk_ref[...] = jnp.zeros_like(blk_ref)

    fr, fi = disc_ref[1:2, :half], disc_ref[1:2, half:]
    tile = nt - 1 - i if down else i
    scan = Scan(b_ref, blk_ref, disc_row(disc_ref, 0, chunks), jr_ref, tile * steps, down)

    def product(part):
        at = slice(*part)
        u = u_ref[at].astype(F32)
        normed = (u - norm_ref[0:1]) * norm_ref[2:3] + norm_ref[3:4]
        drive = jnp.dot(normed.astype(BF16), win_ref[...], preferred_element_type=F32)
        re, im = drive[:, :half], drive[:, half:]
        b_ref[at, :half] = re * fr - im * fi
        b_ref[at, half:] = re * fi + im * fr

    in_stages([product, scan.run], parts_of(b_ref.shape[0], down))
    scan.close()

    @pl.when(i == nt - 1)
    def _():
        zero = [jnp.zeros((1, 128), F32)] * chunks
        cr, ci = chain(blk_ref, jr_ref, disc_row(disc_ref, 2, chunks), (zero, zero), down)
        put_copies(end_ref, cr, ci)


def states_scan(ends_ref, table_ref, b_ref, blk_ref, disc_ref, jr_ref, low_ref, st_ref, down):
    i, nt = pl.program_id(0), pl.num_programs(0)
    chunks = chunk_count(b_ref)
    steps = b_ref.shape[0] // LANES

    @pl.when(i == 0)
    def _():
        carry = carry_in(ends_ref, table_ref, chunks)
        chain(blk_ref, jr_ref, disc_row(disc_ref, 2, chunks), carry, down, st_ref)

    tile = nt - 1 - i if down else i
    scan = Scan(b_ref, st_ref, disc_row(disc_ref, 0, chunks), jr_ref, tile * steps, down)

    def stage(part):
        scan.run(part, lambda at, pair: store_pair(low_ref, at, *pair))

    return scan, stage


def gelu_parts(mixed):
    square = mixed * mixed
    tanh = jnp.tanh(mixed * (GELU_A + (GELU_A * GELU_B) * square))
    half_up = 0.5 + 0.5 * tanh
    return square, tanh, half_up


def gelu_slope(mixed, square, tanh, half_up):
    return half_up + (mixed * (0.5 - 0.5 * tanh * tanh)) * (
        GELU_A + (3.0 * GELU_A * GELU_B) * square
    )


def sigmoid(value):
    return 0.5 + 0.5 * jnp.tanh(0.5 * value)


def forward_kernel(down, *refs):
    (
        ends_ref, table_ref, b_ref, blk_ref, disc_ref, jr_ref, u_ref, norm_ref, wout_ref, wgate_ref,
        next_ref, copy_ref, low_ref, mixed_ref, gate_ref, stats_ref, st_ref,
    ) = refs
    scan, states = states_scan(
        ends_ref, table_ref, b_ref, blk_ref, disc_ref, jr_ref, low_ref, st_ref, down
    )
    zero_first(stats_ref)
    acts = {}

    def mix(part):
        at = slice(*part)
        u = u_ref[at].astype(F32)
        normed = (u - norm_ref[0:1]) * norm_ref[2:3] + norm_ref[3:4]
        mixed = jnp.dot(low_ref[at], wout_ref[...], preferred_element_type=F32)
        mixed += norm_ref[4:5] * normed
        _, _, half_up = gelu_parts(mixed)
        acts[part] = mixed * half_up
        mixed_ref[at] = mixed.astype(BF16)

    def finish(part):
        at = slice(*part)
        act = acts[part]
        gate = sigmoid(jnp.dot(act.astype(BF16), wgate_ref[...], preferred_element_type=F32))
        after = u_ref[at].astype(F32) + act * gate
        next_ref[at] = after
        copy_ref[at] = after
        gate_ref[at] = gate.astype(BF16)
        add_stats(stats_ref, after)

    in_stages([states, mix, finish], parts_of(b_ref.shape[0], down))
    scan.close()
    spread_last(stats_ref)


def zero_first(*refs):
    @pl.when(pl.program_id(0) == 0)
    def _():
        for ref in refs:
            ref[...] = jnp.zeros(ref.shape, ref.dtype)


def spread_last(ref):
    @pl.when(pl.program_id(0) == pl.num_programs(0) - 1)
    def _():
        ref[...] = jnp.broadcast_to(ref[0:1], ref.shape)


class GateBackward:
    def __init__(self, low_ref, wout_ref, wgate_ref, pg_ref, sg_ref, wsum_ref, ssum_ref, acts):
        self.low_ref, self.wout_ref, self.wgate_ref = low_ref, wout_ref, wgate_ref
        self.pg_ref, self.sg_ref = pg_ref, sg_ref
        self.wsum_ref, self.ssum_ref = wsum_ref, ssum_ref
        self.act_ref, self.logit_ref = acts
        self.kept = {}

    def enter(self, part, g, mixed, gate, normed, kept=None):
        at = slice(*part)
        square, tanh, half_up = gelu_parts(mixed) if kept is None else kept
        act = mixed * half_up
        g_gate = g * gate
        if kept is None:
            self.act_ref[at] = act.astype(BF16)
        self.logit_ref[at] = (g_gate * act * (1.0 - gate)).astype(BF16)
        self.kept[part] = (g_gate, gelu_slope(mixed, square, tanh, half_up), normed)

    def middle(self, part):
        at = slice(*part)
        g_gate, slope, normed = self.kept[part]
        act_grad = g_gate + lax.dot_general(
            self.logit_ref[at], self.wgate_ref[...], NT, preferred_element_type=F32
        )
        mixed_grad = act_grad * slope
        self.ssum_ref[...] += column_sum(mixed_grad * normed)
        self.pg_ref[at] = mixed_grad.astype(BF16)

    def leave(self, part):
        at = slice(*part)
        self.sg_ref[at] = lax.dot_general(
            self.pg_ref[at], self.wout_ref[...], NT, preferred_element_type=F32
        )

    def sums(self):
        states, width = self.wout_ref.shape
        self.wsum_ref[states : states + width] += lax.dot_general(
            self.act_ref[...], self.logit_ref[...], TN, preferred_element_type=F32
        )
        self.wsum_ref[:states] += lax.dot_general(
            self.low_ref[...], self.pg_ref[...], TN, preferred_element_type=F32
        )


def turn_kernel(down, *refs):
    (
        ends_ref, table_ref, b_ref, blk_ref, disc_ref, jr_ref, jo_ref, u_ref, norm_ref, wout_ref, wgate_ref,
        gout_ref, order_ref,
        out_ref, low_ref, g_ref, pg_ref, sg_ref, wsum_ref, end_ref, ablk_ref,
        st_ref, w_ref, act_ref, logit_ref,
    ) = refs
    sums = wout_ref.shape[0] + wout_ref.shape[1]
    ssum_ref = wsum_ref.at[sums : sums + 1]
    i, nt = pl.program_id(0), pl.num_programs(0)
    chunks = chunk_count(b_ref)
    half = chunks * 128
    steps = b_ref.shape[0] // LANES
    tile = nt - 1 - i if down else i
    scan, states = states_scan(
        ends_ref, table_ref, b_ref, blk_ref, disc_ref, jr_ref, low_ref, st_ref, down
    )
    back = GateBackward(
        low_ref, wout_ref, wgate_ref, pg_ref, sg_ref, wsum_ref, ssum_ref, (act_ref, logit_ref)
    )

    @pl.when(i == 0)
    def _():
        wsum_ref[...] = jnp.zeros(wsum_ref.shape, F32)
        ablk_ref[...] = jnp.zeros(ablk_ref.shape, F32)
        w_ref[:, :half] = jnp.ones((LANES, half), F32)
        w_ref[:, half:] = jnp.zeros((LANES, half), F32)

    mid = {}

    def mix(part):
        at = slice(*part)
        u = u_ref[at]
        normed = (u - norm_ref[0:1]) * norm_ref[2:3] + norm_ref[3:4]
        mixed = jnp.dot(low_ref[at], wout_ref[...], preferred_element_type=F32)
        mixed += norm_ref[4:5] * normed
        kept = gelu_parts(mixed)
        act_ref[at] = (mixed * kept[2]).astype(BF16)
        mid[part] = (normed, mixed, kept)

    def enter(part):
        at = slice(*part)
        normed, mixed, kept = mid[part]
        gate = sigmoid(jnp.dot(act_ref[at], wgate_ref[...], preferred_element_type=F32))
        permute_out(u_ref[at] + (mixed * kept[2]) * gate, order_ref, out_ref, part)
        g = permute_in(gout_ref, order_ref, part)
        g_ref[at] = g.astype(BF16)
        back.enter(part, g, mixed, gate, normed, kept)

    dr, di = disc_row(disc_ref, 0, chunks, conj=True)
    dr, di = wide(dr), wide(di)
    jo = jo_ref[...]
    live = {
        "w": rows_of(w_ref, slice(0, LANES), chunks),
        "a": rows_of(ablk_ref, slice(0, LANES), chunks),
    }

    def weigh(part):
        (wr, wi), (ar, ai) = (tuple(map(list, live[k])) for k in "wa")
        order = range(part[0] // LANES, part[1] // LANES)
        for step in reversed(order) if down else order:
            sr, si = rows_of(sg_ref, slice(step * LANES, (step + 1) * LANES), chunks)
            keep = jo != tile * steps + step
            for c in range(chunks):
                ar[c] = ar[c] + (wr[c] * sr[c] - wi[c] * si[c])
                ai[c] = ai[c] + (wr[c] * si[c] + wi[c] * sr[c])
                xr = jnp.where(keep, wr[c], 0.0)
                xi = jnp.where(keep, wi[c], 0.0)
                wr[c] = xr * dr[c] - xi * di[c]
                wi[c] = xr * di[c] + xi * dr[c]
        live["w"], live["a"] = (wr, wi), (ar, ai)

    in_stages(
        [states, mix, enter, back.middle, back.leave, weigh], parts_of(b_ref.shape[0], down)
    )
    back.sums()
    scan.close()
    put_rows(w_ref, slice(0, LANES), *live["w"])
    put_rows(ablk_ref, slice(0, LANES), *live["a"])

    @pl.when(i == nt - 1)
    def _():
        zero = [jnp.zeros((1, 128), F32)] * chunks
        power = disc_row(disc_ref, 2, chunks, conj=True)
        cr, ci = chain(ablk_ref, jo_ref, power, (zero, zero), not down)
        put_copies(end_ref, cr, ci)


def adjoint_kernel(down, last, *refs):
    (
        ends_ref, table_ref, sg_ref, ablk_ref, disc_ref, jr_ref, low_ref, u_ref, norm_ref, pg_ref, g_ref,
        win_ref, order_ref, *refs
    ) = refs
    if last:
        (
            ssum_ref, res_ref, sums_ref, st_ref, dg_ref, ax_ref, low_normed_ref, nsum_ref, isum_ref,
        ) = refs
    else:
        (res_ref, sums_ref, nsum_ref, st_ref, dg_ref, ax_ref, low_normed_ref) = refs
        isum_ref = sums_ref
    width, states = win_ref.shape
    i, nt = pl.program_id(0), pl.num_programs(0)
    chunks = chunk_count(sg_ref)
    half = chunks * 128
    steps = sg_ref.shape[0] // LANES
    tile = nt - 1 - i if down else i

    @pl.when(i == 0)
    def _():
        carry = carry_in(ends_ref, table_ref, chunks)
        power = disc_row(disc_ref, 2, chunks, conj=True)
        chain(ablk_ref, jr_ref, power, carry, down, st_ref)
        ax_ref[...] = jnp.zeros_like(ax_ref)

    zero_first(isum_ref, nsum_ref)
    fr, fi = disc_row(disc_ref, 1, chunks)
    fr, fi = wide(fr), wide(fi)
    decay = disc_row(disc_ref, 0, chunks, conj=True)
    scan = Scan(sg_ref, st_ref, decay, jr_ref, tile * steps, down)
    sums = tuple(map(list, rows_of(ax_ref, slice(0, LANES), chunks)))

    def emit(at, pair):
        xr, xi = rows_of(low_ref, at, chunks)
        xr, xi = [v.astype(F32) for v in xr], [v.astype(F32) for v in xi]
        grads = []
        for which, (ar, ai) in enumerate(pair):
            gr, gi = [], []
            rows = slice(which * LANES, (which + 1) * LANES)
            for c in range(chunks):
                vr, vi = xr[c][rows], xi[c][rows]
                sums[0][c] = sums[0][c] + (ar[c] * vr + ai[c] * vi)
                sums[1][c] = sums[1][c] + (ai[c] * vr - ar[c] * vi)
                gr.append(ar[c] * fr[c] + ai[c] * fi[c])
                gi.append(ai[c] * fr[c] - ar[c] * fi[c])
            grads.append((gr, gi))
        store_pair(dg_ref, at, *grads)

    def finish(part):
        at = slice(*part)
        centered = u_ref[at].astype(F32) - norm_ref[0:1]
        low_normed_ref[at] = (centered * norm_ref[2:3] + norm_ref[3:4]).astype(BF16)
        normed_grad = lax.dot_general(dg_ref[at], win_ref[...], NT, preferred_element_type=F32)
        normed_grad += norm_ref[4:5] * pg_ref[at].astype(F32)
        add_rows(
            nsum_ref, column_sum(normed_grad), column_sum(normed_grad * centered) * norm_ref[1:2]
        )
        result = g_ref[at].astype(F32) + norm_ref[2:3] * normed_grad
        if last:
            permute_out(result, order_ref, res_ref, part)
        else:
            res_ref[at] = result

    in_stages([lambda part: scan.run(part, emit), finish], parts_of(sg_ref.shape[0], down))
    isum_ref[:width] += lax.dot_general(
        low_normed_ref[...], dg_ref[...], TN, preferred_element_type=F32
    )
    scan.close()
    put_rows(ax_ref, slice(0, LANES), *sums)
    spread_last(nsum_ref)

    @pl.when(i == nt - 1)
    def _():
        decays = jnp.sum(ax_ref[...], axis=0, keepdims=True)
        wr, wi = win_ref[:, :half].astype(F32), win_ref[:, half:].astype(F32)
        gr, gi = isum_ref[:width, :half], isum_ref[:width, half:]
        re = jnp.sum(wr * gr + wi * gi, axis=0, keepdims=True)
        im = jnp.sum(wr * gi - wi * gr, axis=0, keepdims=True)
        gr, gi = disc_ref[1:2, :half], disc_ref[1:2, half:]
        scale = 1.0 / (gr * gr + gi * gi)
        factors = ((re * gr - im * gi) * scale, (re * gi + im * gr) * scale)
        if last:
            rows = width // BLOCKS
            first = rows + rows // 2
            for b in range(BLOCKS):
                at = b * rows
                sums_ref[b, :rows] = isum_ref[at : at + rows, :width]
                sums_ref[b, rows:first, : states - width] = isum_ref[at : at + rows // 2, width:]
                sums_ref[b, rows:first, states - width :] = isum_ref[
                    at + rows // 2 : at + rows, width:
                ]
                sums_ref[b, first:] = jnp.zeros((SMALL, width), F32)
            small = [nsum_ref[0]] + [ssum_ref[:, cols(c)] for c in range(width // 128)]
            small += [decays[:, cols(c)] for c in range(2 * chunks)]
            small += [v[:, cols(c)] for v in factors for c in range(chunks)]
            small = [v[r : r + 1] for v in small for r in range(v.shape[0])]
            for k, row in enumerate(small):
                at = (k % SMALL, k // SMALL)
                sums_ref[0, first + at[0] : first + at[0] + 1, cols(at[1])] = row
        else:
            sums_ref[width : width + 1] = decays
            sums_ref[width + 1 : width + 2, :half] = factors[0]
            sums_ref[width + 1 : width + 2, half:] = factors[1]


def back_kernel(down, tokens, core, *refs):
    (
        sums_ref, r_ref, up_ref, up_norm_ref, mixed_ref, gate_ref, low_ref, u_ref, norm_ref, wout_ref,
        wgate_ref, disc_ref, jo_ref,
        g_ref, pg_ref, sg_ref, kept_ref, sent_ref, ssum_ref, end_ref, ablk_ref, nsum_ref, bsum_ref, wsum_ref,
        act_ref, logit_ref,
    ) = refs
    i, nt = pl.program_id(0), pl.num_programs(0)
    chunks = chunk_count(sg_ref)
    steps = sg_ref.shape[0] // LANES
    tile = nt - 1 - i if down else i

    @pl.when(i == 0)
    def _():
        nsum_ref[...] = jnp.sum(sums_ref[...], axis=0)
        bsum_ref[0:1], bsum_ref[1:2] = summed(sums_ref)

    zero_first(ablk_ref, wsum_ref, ssum_ref)
    back = GateBackward(
        low_ref, wout_ref, wgate_ref, pg_ref, sg_ref, wsum_ref, ssum_ref, (act_ref, logit_ref)
    )
    decay = disc_row(disc_ref, 0, chunks, conj=True)
    scan = Scan(sg_ref, ablk_ref, decay, jo_ref, tile * steps, down)
    scale = up_norm_ref[2:3] * (-1.0 / tokens)

    def enter(part):
        at = slice(*part)
        standard = (up_ref[at] - up_norm_ref[0:1]) * (scale * up_norm_ref[1:2] * bsum_ref[1:2])
        g = r_ref[at] + (standard + scale * bsum_ref[0:1])
        g_ref[at] = g
        u = u_ref[at].astype(F32)
        normed = (u - norm_ref[0:1]) * norm_ref[2:3] + norm_ref[3:4]
        back.enter(part, g, mixed_ref[at].astype(F32), gate_ref[at].astype(F32), normed)

    in_stages([enter, back.middle, back.leave, scan.run], parts_of(sg_ref.shape[0], down))
    back.sums()
    scan.close()

    @pl.when(i == nt - 1)
    def _():
        zero = [jnp.zeros((1, 128), F32)] * chunks
        power = disc_row(disc_ref, 2, chunks, conj=True)
        cr, ci = chain(ablk_ref, jo_ref, power, (zero, zero), down)
        put_copies(end_ref, cr, ci)
        states, width = wout_ref.shape
        gates, outs = width // BLOCKS, states // BLOCKS
        side = lax.axis_index(core)
        for ref, first in ((kept_ref, side), (sent_ref, 1 - side)):
            for b in range(BLOCKS // 2):
                at = first * (BLOCKS // 2) + b
                ref[b, :gates] = wsum_ref[pl.ds(pl.multiple_of(states + at * gates, 8), gates)]
                ref[b, gates:] = wsum_ref[pl.ds(pl.multiple_of(at * outs, 8), outs)]


def last_kernel(
    tokens, piece_ref, small_ref, out1_ref, gate1_ref, skip1_ref, in1_ref, decay1_ref, norm1_ref,
    disc_ref, rate_ref, step_ref, freq_ref, r_ref, tok_ref, norm_ref,
    grad_in_ref, gain_ref, bias_ref, drate_ref, dstep_ref, dfreq_ref, in_ref, out_ref, skip_ref,
    gate_ref,
):
    gates, width = gate1_ref.shape
    outs = out1_ref.shape[0]
    states = in1_ref.shape[1]
    half = states // 2
    left = states - width
    gate_ref[0], gate_ref[1] = piece_ref[:gates], gate1_ref[...]
    out_ref[0], out_ref[1] = piece_ref[gates : gates + outs], out1_ref[...]
    at = gates + outs
    in_ref[0, :, :width] = piece_ref[at : at + gates]
    at += gates
    in_ref[0, : gates // 2, width:] = piece_ref[at : at + gates // 2, :left]
    in_ref[0, gates // 2 :, width:] = piece_ref[at : at + gates // 2, left:]
    in_ref[1] = in1_ref[...]

    def row(ref, first, count):
        places = [(k % SMALL, k // SMALL) for k in range(first, first + count)]
        return jnp.concatenate([ref[r : r + 1, cols(c)] for r, c in places], axis=1)

    count = width // 128
    bias, gain = row(small_ref, 0, count), row(small_ref, count, count)
    scale = norm_ref[2:3] * (-1.0 / tokens)
    grad_in_ref[...] = r_ref[...] + (
        (tok_ref[...].astype(F32) - norm_ref[0:1]) * (scale * norm_ref[1:2] * gain) + scale * bias
    )

    @pl.when(pl.program_id(0) == 0)
    def _():
        bias_ref[0:1], gain_ref[0:1] = bias, gain
        bias_ref[1:2], gain_ref[1:2] = row(norm1_ref, 0, count), row(norm1_ref, count, count)
        skip_ref[0:1], skip_ref[1:2] = row(small_ref, 2 * count, count), skip1_ref[0:1]
        at = 3 * count
        lanes = half // 128
        for l in range(LAYERS):
            if l == 0:
                ar, ai, sr, si = (row(small_ref, at + k * lanes, lanes) for k in range(4))
            else:
                ar, ai = decay1_ref[0:1, :half], decay1_ref[0:1, half:]
                sr, si = decay1_ref[1:2, :half], decay1_ref[1:2, half:]
            dr, di = disc_ref[l, 0:1, :half], disc_ref[l, 0:1, half:]
            fr, fi = disc_ref[l, 1:2, :half], disc_ref[l, 1:2, half:]
            here = slice(l, l + 1)
            rate, freq, step = rate_ref[here], freq_ref[here], jnp.exp(step_ref[here])
            tr = ar - (fr * sr + fi * si)
            ti = ai - (fr * si - fi * sr)
            size = 1.0 / (dr * dr + di * di)
            gr, gi = (tr * dr - ti * di) * size, (tr * di + ti * dr) * size
            mr, mi = -rate * fr - freq * fi, freq * fr - rate * fi
            size = 1.0 / (rate * rate + freq * freq)
            gr += (-rate * sr - freq * si) * size
            gi += (freq * sr - rate * si) * size
            both = 2.0 * (fr * sr + fi * si)
            gx = gr * dr + gi * di
            gy = gi * dr - gr * di
            drate_ref[here] = (-mr * sr - mi * si - both * rate) * size - step * gx
            dfreq_ref[here] = (mi * sr - mr * si - both * freq) * size + step * gy
            dstep_ref[here] = step * (freq * gy - rate * gx)


def whole(array):
    shape = array.shape
    return pl.BlockSpec(shape, lambda i: (0,) * len(shape))


def tile_spec(rows, width, nt, down):
    if down:
        return pl.BlockSpec((rows, width), lambda i: (nt - 1 - i, 0))
    return pl.BlockSpec((rows, width), lambda i: (i, 0))


def run_spec(steps, width, nt, down):
    if down:
        return pl.BlockSpec((LANES, steps, width), lambda i: (0, nt - 1 - i, 0))
    return pl.BlockSpec((LANES, steps, width), lambda i: (0, i, 0))


def call(kernel, nt, args, outs, scratch, macs, name):
    arrays = [a for a, *_ in args]
    sizes = sum(a.size * a.dtype.itemsize for a in arrays + [a for a, *_ in outs])
    held = [
        a if keep is None else pltpu.with_memory_space_constraint(a, keep)
        for a, _, keep in map(filled, args)
    ]
    return pl.pallas_call(
        kernel,
        grid=(nt,),
        in_specs=[whole(a) if s is None else s for a, s, _ in map(filled, args)],
        out_specs=[whole(a) if s is None else s for a, s, _ in map(filled, outs)],
        out_shape=[
            a if keep is None else keep(a.shape, a.dtype) for a, _, keep in map(filled, outs)
        ],
        scratch_shapes=scratch,
        compiler_params=pltpu.CompilerParams(
            vmem_limit_bytes=VMEM_LIMIT, dimension_semantics=("arbitrary",)
        ),
        cost_estimate=pl.CostEstimate(flops=2 * macs, bytes_accessed=sizes, transcendentals=0),
        name=name,
    )(*held)


def filled(entry):
    return entry if len(entry) == 3 else entry + (pltpu.HBM,)


def shape(*dims, dtype=F32):
    return jax.ShapeDtypeStruct(dims, dtype)


def body(
    axes,
    tokens_in,
    seq_starts,
    norm_gain,
    norm_bias,
    decay_rate,
    step_log,
    frequency,
    in_proj,
    out_proj,
    skip_gain,
    gate_proj,
    grad_out,
):
    rows, width = tokens_in.shape
    states = in_proj.shape[-1]
    devices = 2 ** len(axes)
    tokens = float(rows * devices)
    run = rows // LANES
    steps = min(64, run)
    tile = steps * LANES
    nt = rows // tile
    span = min(32, steps)
    def tiles(array, down):
        return (array, tile_spec(tile, array.shape[-1], nt, down))

    def runs(array, down):
        return (array, run_spec(steps, array.shape[-1], nt, down))

    def full(array):
        return (array, None)

    def of(array, l):
        size = array.shape[1:]
        return (array, pl.BlockSpec((None,) + size, lambda i: (l,) + (0,) * len(size)))

    discs, tables, cuts, order = call(
        functools.partial(prep_kernel, rows, axes), 1,
        [full(seq_starts[None]), full(decay_rate),
         full(step_log), full(frequency)],
        [full(shape(LAYERS, 8, states)), full(shape(2 * LAYERS, 2, devices, 2 * SLOT, 128)),
         full(shape(2, LANES, 128, dtype=jnp.int32)),
         full(shape(span * LANES, span * LANES, dtype=BF16))],
        [], rows * width, "prep",
    )

    def near(entry):
        return entry[:2] + (pltpu.VMEM if rows * states * 4 <= 7 * 2**20 else pltpu.HBM,)

    tokens_run = tokens_in.reshape(LANES, run, width)
    grad_run = grad_out.reshape(LANES, run, width)
    state_scratch = pltpu.VMEM((LANES, states), F32)
    half_scratch = [pltpu.VMEM((tile, width), BF16)] * 2
    cost = rows * width * states

    u0_near, u0, stats = call(
        stats_kernel, nt, [runs(tokens_run, 0), full(order)],
        [near(tiles(shape(rows, width, dtype=BF16), 0)), tiles(shape(rows, width, dtype=BF16), 0),
         near(full(shape(devices, 2 * SLOT, 128)))],
        [], cost // 2, "stats",
    )

    def drive(l, stream, stats):
        down = l % 2
        return call(
            functools.partial(drive_kernel, l, bool(down), tokens), nt,
            [near(full(gather_all(stats, axes))), near(tiles(stream, down)), full(norm_gain), full(norm_bias), full(skip_gain), of(in_proj, l), of(discs, l),
               of(cuts, down)],
            [near(tiles(shape(rows, states), down)), near(full(shape(devices, 2 * SLOT, 128))),
             full(shape(LANES, states)), full(shape(8, width))],
            [], 4 * cost, f"drive_{l}",
        )

    b0, end0, blk0, norm0 = drive(0, u0_near, stats)
    u1_near, u1, low0, mixed0, gate0, stats = call(
        functools.partial(forward_kernel, False), nt,
        [near(full(gather_all(end0, axes))), of(tables, 2 * 0 + 0), near(tiles(b0, 0)), full(blk0), of(discs, 0), of(cuts, 0),
           near(tiles(u0_near, 0)), full(norm0), of(out_proj, 0), of(gate_proj, 0)],
        [near(tiles(shape(rows, width), 0)), tiles(shape(rows, width), 0), tiles(shape(rows, states, dtype=BF16), 0),
         tiles(shape(rows, width, dtype=BF16), 0), tiles(shape(rows, width, dtype=BF16), 0),
         near(full(shape(devices, 2 * SLOT, 128)))],
        [state_scratch], 6 * cost, "forward_0",
    )

    b1, end1, blk1, norm1 = drive(1, u1_near, stats)
    (
        out, low1, g1, pg1, sg1, w_sum1, aend1, ablk1
    ) = call(
        functools.partial(turn_kernel, True), nt,
        [near(full(gather_all(end1, axes))), of(tables, 2 * 1 + 0), near(tiles(b1, 1)), full(blk1), of(discs, 1), of(cuts, 1),
           of(cuts, 0), tiles(u1, 1), full(norm1), of(out_proj, 1), of(gate_proj, 1),
           runs(grad_run, 1), full(order)],
        [runs(shape(LANES, run, width), 1), near(tiles(shape(rows, states, dtype=BF16), 1)),
         near(tiles(shape(rows, width, dtype=BF16), 1)),
         near(tiles(shape(rows, width, dtype=BF16), 1)), near(tiles(shape(rows, states), 1)), full(shape(states + width + 8, width)),
         near(full(shape(devices, 2 * SLOT, 128))), full(shape(LANES, states))],
        [state_scratch, state_scratch] + half_scratch, 16 * cost, "turn_1",
    )

    def adjoint(l, sg, ablk, ends, low, stream, norm, pg, g, skip_sum=None):
        down = 1 - l % 2
        last = l == 0
        held = (lambda entry: entry) if last else near
        args = [
            near(full(ends)), of(tables, 2 * l + 1), held(tiles(sg, down)), full(ablk), of(discs, l),
            of(cuts, down), held(tiles(low, down)), tiles(stream, down),
            full(norm), held(tiles(pg, down)), held(tiles(g, down)), of(in_proj, l), full(order),
        ]
        scratch = [
            state_scratch, pltpu.VMEM((tile, states), BF16), state_scratch,
            pltpu.VMEM((tile, width), BF16),
        ]
        if last:
            args.append(full(skip_sum))
            outs = [
                runs(shape(LANES, run, width), down),
                full(shape(BLOCKS, (width + width // 2) // BLOCKS + SMALL, width)),
            ]
            scratch += [pltpu.VMEM((1, 2 * SLOT, 128), F32), pltpu.VMEM((width, states), F32)]
        else:
            outs = [
                tiles(shape(rows, width), down), full(shape(width + 8, states)),
                near(full(shape(devices, 2 * SLOT, 128))),
            ]
        return call(
            functools.partial(adjoint_kernel, bool(down), last), nt, args, outs, scratch,
            8 * cost, f"adjoint_{l}",
        )

    r1, in_sum1, norm_sum1 = adjoint(
        1, sg1, ablk1, gather_all(aend1, axes), low1, u1, norm1, pg1, g1
    )

    piece = (2 * width + states + width // 2) // BLOCKS + SMALL

    def lower(r1, norm_sum1):
        half = shape(BLOCKS // 2, (states + width) // BLOCKS, width)
        (
            g0, pg0, sg0, kept0, sent0, skip_sum0, aend0, ablk0, small1, _
        ) = call(
            functools.partial(back_kernel, True, tokens, axes[-1]), nt,
            [near(full(gather_all(norm_sum1, axes))), tiles(r1, 1), tiles(u1, 1), full(norm1),
             tiles(mixed0, 1), tiles(gate0, 1), tiles(low0, 1), tiles(u0, 1), full(norm0),
             of(out_proj, 0), of(gate_proj, 0), of(discs, 0), of(cuts, 1)],
            [tiles(shape(rows, width), 1), tiles(shape(rows, width, dtype=BF16), 1),
             tiles(shape(rows, states), 1), full(half), full(half), full(shape(1, width)), near(full(shape(devices, 2 * SLOT, 128))),
             full(shape(LANES, states)), full(shape(2 * SLOT, 128)), full(shape(2, width))],
            [pltpu.VMEM((states + width, width), F32)] + half_scratch, 12 * cost, "back_0",
        )
        core, chips, *others = phases(axes)
        part = kept0 + lax.ppermute(sent0, core[0], [(0, 1), (1, 0)])
        ends, part = lax.optimization_barrier((gather_all(aend0, axes), part))
        part = part.reshape(-1, width)
        part = scatter_sum(part, chips)
        r0, in_sum0 = adjoint(0, sg0, ablk0, ends, low0, u0, norm0, pg0, g0, skip_sum0)
        in_sum0, part = lax.optimization_barrier((in_sum0, part))
        in_part = scatter_sum(scatter_sum(in_sum0.reshape(-1, width), core), chips)
        pad = -piece % (8 * 2 ** len(others[0]))
        part = jnp.concatenate([part, in_part, jnp.zeros((pad, width), F32)], axis=0)
        part = sum_all(part, others)[:piece]
        pieces = gather_rows(gather_rows(part, chips), core)
        return r0.reshape(rows, width), small1, pieces.reshape(BLOCKS, -1, width)

    def nothing(r1, norm_sum1):
        return (
            jnp.zeros((rows, width), F32),
            jnp.zeros((2 * SLOT, 128), F32),
            jnp.zeros((BLOCKS, piece, width), F32),
        )

    w_all1, in_all1 = lax.psum((w_sum1, in_sum1), axes)
    r0, norm_all1, pieces = lax.cond(seq_starts[0] == 0, lower, nothing, r1, norm_sum1)

    gates, outs = width // BLOCKS, states // BLOCKS

    def block(array, *dims, at=lambda i: (i, 0)):
        return (array, pl.BlockSpec(dims, at))

    def flat(array, count):
        return block(array, count, array.shape[1])

    (
        grad_in, gain_grad, bias_grad, rate_grad, step_grad, freq_grad, in_grad, out_grad,
        skip_grad, gate_grad,
    ) = call(
        functools.partial(last_kernel, tokens), BLOCKS,
        [block(pieces, None, piece, width, at=lambda i: (i, 0, 0)) + (None,),
         block(pieces, None, SMALL, width, at=lambda i: (0, piece // SMALL - 1, 0)) + (None,),
         flat(w_all1, outs),
         block(w_all1, gates, width, at=lambda i: (states // gates + i, 0)),
         block(w_all1, 8, width, at=lambda i: ((states + width) // 8, 0)),
         flat(in_all1, gates),
         block(in_all1, 8, states, at=lambda i: (width // 8, 0)),
         full(norm_all1), full(discs), full(decay_rate), full(step_log), full(frequency),
         flat(r0, rows // BLOCKS), flat(tokens_in, rows // BLOCKS), full(norm0)],
        [flat(shape(rows, width), rows // BLOCKS), full(shape(LAYERS, width)),
         full(shape(LAYERS, width)), full(shape(LAYERS, states // 2)),
         full(shape(LAYERS, states // 2)), full(shape(LAYERS, states // 2)),
         block(shape(LAYERS, width, states), LAYERS, gates, states, at=lambda i: (0, i, 0)),
         block(shape(LAYERS, states, width), LAYERS, outs, width, at=lambda i: (0, i, 0)),
         full(shape(LAYERS, width)),
         block(shape(LAYERS, width, width), LAYERS, gates, width, at=lambda i: (0, i, 0))],
        [], cost, "last",
    )
    return (
        out.reshape(rows, width),
        grad_in,
        gain_grad,
        bias_grad,
        rate_grad,
        step_grad,
        freq_grad,
        in_grad,
        out_grad,
        skip_grad,
        gate_grad,
    )


def solution(mesh):
    bits = mesh.devices.size.bit_length() - 1
    axes = tuple("b%d" % k for k in range(bits))
    binary = Mesh(mesh.devices.reshape((2,) * bits), axes)
    rows = P(axes, None)
    return jax.shard_map(
        functools.partial(body, axes),
        mesh=binary,
        in_specs=(rows,) + (P(),) * 10 + (rows,),
        out_specs=(rows, rows) + (P(),) * 9,
        check_vma=False,
    )
```

```python
import functools

import jax
import jax.numpy as jnp
from jax import lax
from jax.experimental import pallas as pl
from jax.experimental.pallas import tpu as pltpu
from jax.sharding import Mesh, PartitionSpec as P

LAYERS = 2
EPSILON = 1e-05
SMALL = 8
BLOCKS = 8
SLOT = 4
LANES = 8
VMEM_LIMIT = 30 * 1024 * 1024
GELU_A = 0.7978845608028654
GELU_B = 0.044715
NT = (((1,), (1,)), ((), ()))
TN = (((0,), (0,)), ((), ()))
F32 = jnp.float32
BF16 = jnp.bfloat16


def gather_all(copies, axes):
    return lax.all_to_all(copies, axes, 0, 0)


def scatter_sum(value, axes):
    count = 2 ** len(axes)
    pieces = value.reshape((count, value.shape[0] // count) + value.shape[1:])
    return jnp.sum(lax.all_to_all(pieces, axes, 0, 0), axis=0)


def gather_rows(value, axes):
    count = 2 ** len(axes)
    copies = jnp.broadcast_to(value, (count,) + value.shape)
    return lax.all_to_all(copies, axes, 0, 0).reshape((count * value.shape[0],) + value.shape[1:])


def phases(axes):
    left, out = list(axes), [(axes[-1],)]
    left = left[:-1]
    while left:
        out.append(tuple(left[-2:]))
        left = left[:-2]
    return out


def sum_all(value, parts):
    for part in parts:
        value = scatter_sum(value, part)
    for part in reversed(parts):
        value = gather_rows(value, part)
    return value


def cols(c):
    return slice(c * 128, (c + 1) * 128)


def chunk_count(ref):
    return ref.shape[-1] // 256


def rows_of(ref, at, chunks):
    half = chunks * 128
    re = [ref[at, c * 128 : (c + 1) * 128] for c in range(chunks)]
    im = [ref[at, half + c * 128 : half + (c + 1) * 128] for c in range(chunks)]
    return re, im


def put_rows(ref, at, re, im):
    chunks = len(re)
    half = chunks * 128
    for c in range(chunks):
        ref[at, c * 128 : (c + 1) * 128] = re[c]
        ref[at, half + c * 128 : half + (c + 1) * 128] = im[c]


def put_copies(ref, re, im):
    ref[0] = jnp.zeros(ref.shape[1:], F32)
    for c in range(len(re)):
        ref[0, c : c + 1] = re[c]
        ref[0, SLOT + c : SLOT + c + 1] = im[c]
    ref[...] = jnp.broadcast_to(ref[0:1], ref.shape)


def wide(rows):
    return [jnp.broadcast_to(v, (LANES, 128)) for v in rows]


def chain(ends_ref, jr_ref, power, carry, down, start_ref=None):
    chunks = len(power[0])
    pr, pi = power
    cr, ci = carry
    order = range(LANES - 1, -1, -1) if down else range(LANES)
    for s in order:
        at = slice(s, s + 1)
        if start_ref is not None:
            put_rows(start_ref, at, cr, ci)
        er, ei = rows_of(ends_ref, at, chunks)
        alive = (jr_ref[at, :] < 0).astype(F32)
        cr, ci = (
            [er[c] + alive * (pr[c] * cr[c] - pi[c] * ci[c]) for c in range(chunks)],
            [ei[c] + alive * (pr[c] * ci[c] + pi[c] * cr[c]) for c in range(chunks)],
        )
    return cr, ci


def carry_in(ends_ref, table_ref, chunks):
    total = jnp.zeros((2 * SLOT, 128), F32)
    for e in range(ends_ref.shape[0]):
        end = ends_ref[e]
        turned = jnp.concatenate([end[SLOT:], end[:SLOT]], axis=0)
        total += table_ref[0, e] * end + table_ref[1, e] * turned
    return (
        [total[c : c + 1] for c in range(chunks)],
        [total[SLOT + c : SLOT + c + 1] for c in range(chunks)],
    )


def in_stages(stages, parts, after={}):
    for turn in range(len(parts) + len(stages) - 1):
        for k, stage in enumerate(stages):
            if 0 <= turn - k < len(parts):
                stage(parts[turn - k])
            if turn - k == len(parts) - 1 and k in after:
                after[k]()


def parts_of(rows, down, count=2):
    size = rows // count
    parts = [(at, at + size) for at in range(0, rows, size)]
    return parts[::-1] if down else parts


class Scan:
    def __init__(self, src_ref, st_ref, decay, jr_ref, first_step, down):
        self.src_ref, self.st_ref, self.down = src_ref, st_ref, down
        self.chunks = chunk_count(src_ref)
        self.dr, self.di = wide(decay[0]), wide(decay[1])
        self.jr, self.first_step = jr_ref[...], first_step
        self.state = rows_of(st_ref, slice(0, LANES), self.chunks)

    def one(self, step):
        br, bi = rows_of(self.src_ref, slice(step * LANES, (step + 1) * LANES), self.chunks)
        live = self.jr != self.first_step + step
        nr, ni = [], []
        for c in range(self.chunks):
            xr = jnp.where(live, self.state[0][c], 0.0)
            xi = jnp.where(live, self.state[1][c], 0.0)
            nr.append(self.dr[c] * xr - self.di[c] * xi + br[c])
            ni.append(self.dr[c] * xi + self.di[c] * xr + bi[c])
        self.state = (nr, ni)
        return nr, ni

    def run(self, part, emit=None):
        low, high = part[0] // LANES, part[1] // LANES
        for n in range(0, high - low, 2):
            step = high - 2 - n if self.down else low + n
            first = self.one(step + 1 if self.down else step)
            second = self.one(step if self.down else step + 1)
            if emit is not None:
                pair = (second, first) if self.down else (first, second)
                emit(slice(step * LANES, (step + 2) * LANES), pair)

    def close(self):
        put_rows(self.st_ref, slice(0, LANES), *self.state)


def store_pair(ref, at, first, second):
    re = [jnp.concatenate([p, q], axis=0).astype(BF16) for p, q in zip(first[0], second[0])]
    im = [jnp.concatenate([p, q], axis=0).astype(BF16) for p, q in zip(first[1], second[1])]
    put_rows(ref, at, re, im)


def disc_row(disc_ref, row, chunks, conj=False):
    re, im = rows_of(disc_ref, slice(row, row + 1), chunks)
    return (re, [-v for v in im]) if conj else (re, im)


def column_sum(value):
    rows, width = value.shape
    return jnp.sum(jnp.sum(value.reshape(rows // 8, 8, width), axis=0), axis=0, keepdims=True)


def permute_in(block_ref, order_ref, part):
    runs, _, width = block_ref.shape
    size = order_ref.shape[0]
    span = size // runs
    out = []
    for k in range(part[0] // size, part[1] // size):
        rows = block_ref[:, k * span : (k + 1) * span, :].reshape(size, width)
        out.append(jnp.dot(order_ref[...], rows, preferred_element_type=F32))
    return out[0] if len(out) == 1 else jnp.concatenate(out, axis=0)


def permute_out(value, order_ref, out_ref, part):
    width = value.shape[1]
    size = order_ref.shape[0]
    span = size // LANES
    high = value.astype(BF16)
    low = (value - high.astype(F32)).astype(BF16)
    for n, k in enumerate(range(part[0] // size, part[1] // size)):
        at = slice(n * size, (n + 1) * size)
        back = lax.dot_general(order_ref[...], high[at], TN, preferred_element_type=F32)
        back += lax.dot_general(order_ref[...], low[at], TN, preferred_element_type=F32)
        out_ref[:, k * span : (k + 1) * span, :] = back.reshape(LANES, span, width)


def expm1(value):
    acc = jnp.full_like(value, 1.0 / 479001600.0)
    for n in (39916800.0, 3628800.0, 362880.0, 40320.0, 5040.0, 720.0, 120.0, 24.0, 6.0, 2.0, 1.0):
        acc = acc * value + 1.0 / n
    return jnp.where(value > -1.0, acc * value, jnp.exp(value) - 1.0)


def prep_kernel(
    rows, axes, starts_ref, rate_ref, step_ref, freq_ref,
    disc_ref, table_ref, cut_ref, order_ref,
):
    devices = 2 ** len(axes)
    total = rows * devices
    run = rows // LANES
    half = rate_ref.shape[-1]
    me = 0
    for axis in axes:
        me = 2 * me + lax.axis_index(axis)
    starts = [starts_ref[:, k : k + 1] for k in range(starts_ref.shape[1])]

    base = me * rows + run * lax.broadcasted_iota(jnp.int32, (LANES, 128), 0)
    up = jnp.full((LANES, 128), -1, jnp.int32)
    down = up
    for begin in starts + [total]:
        rel = begin - base
        up = jnp.maximum(up, jnp.where((rel >= 0) & (rel < run), rel, -1))
        down = jnp.maximum(down, jnp.where((rel >= 1) & (rel <= run), rel - 1, -1))
    cut_ref[0] = up
    cut_ref[1] = down

    size = order_ref.shape[0]
    span = size // LANES
    to = lax.broadcasted_iota(jnp.int32, (size, size), 0)
    back = lax.broadcasted_iota(jnp.int32, (size, size), 1)
    order_ref[...] = ((to % LANES) * span + to // LANES == back).astype(F32).astype(BF16)

    source = lax.broadcasted_iota(jnp.int32, (devices, half), 0)
    for l in range(LAYERS):
        row = slice(l, l + 1)
        rate, freq = rate_ref[row], freq_ref[row]
        step_size = jnp.exp(step_ref[row])
        real_angle = -rate * step_size
        imag_angle = freq * step_size
        magnitude = jnp.exp(real_angle)
        cosine, sine = jnp.cos(imag_angle), jnp.sin(imag_angle)
        minus_real = expm1(real_angle) * cosine - 2.0 * jnp.sin(0.5 * imag_angle) ** 2
        minus_imag = magnitude * sine
        modulus = rate * rate + freq * freq
        disc_ref[l, 0:1, :half] = magnitude * cosine
        disc_ref[l, 0:1, half:] = minus_imag
        disc_ref[l, 1:2, :half] = (-rate * minus_real + freq * minus_imag) / modulus
        disc_ref[l, 1:2, half:] = (-rate * minus_imag - freq * minus_real) / modulus
        magnitude = jnp.exp(real_angle * float(run))
        disc_ref[l, 2:3, :half] = magnitude * jnp.cos(imag_angle * float(run))
        disc_ref[l, 2:3, half:] = magnitude * jnp.sin(imag_angle * float(run))
        disc_ref[l, 3:8] = jnp.zeros((5, 2 * half), F32)
        powers = []
        for bit in range(len(axes)):
            magnitude = jnp.exp(real_angle * float(rows << bit))
            angle = imag_angle * float(rows << bit)
            powers.append((magnitude * jnp.cos(angle), magnitude * jnp.sin(angle)))
        for back in range(2):
            going_down = (l + back) % 2 == 1
            if going_down:
                live, count = source > me, source - me - 1
            else:
                live, count = source < me, me - 1 - source
            for begin in starts:
                if going_down:
                    cut = (begin > (me + 1) * rows) & (source * rows >= begin)
                else:
                    cut = (begin < me * rows) & ((source + 1) * rows <= begin)
                live &= ~cut
            count = jnp.maximum(count, 0)
            real = live.astype(F32)
            imag = jnp.zeros((devices, half), F32)
            for bit, (pr, pi) in enumerate(powers):
                use = (count & (1 << bit)) != 0
                pr, pi = jnp.where(use, pr, 1.0), jnp.where(use, pi, 0.0)
                real, imag = real * pr - imag * pi, real * pi + imag * pr
            imag = -imag if back else imag
            at = 2 * l + back
            table_ref[at] = jnp.zeros(table_ref.shape[1:], F32)
            for c in range(half // 128):
                table_ref[at, 0, :, c, :] = real[:, cols(c)]
                table_ref[at, 0, :, SLOT + c, :] = real[:, cols(c)]
                table_ref[at, 1, :, c, :] = -imag[:, cols(c)]
                table_ref[at, 1, :, SLOT + c, :] = imag[:, cols(c)]


def stats_kernel(tok_ref, order_ref, u_ref, copy_ref, stats_ref):
    value = permute_in(tok_ref, order_ref, (0, u_ref.shape[0]))
    u_ref[...] = value.astype(BF16)
    copy_ref[...] = u_ref[...]
    zero_first(stats_ref)
    add_stats(stats_ref, value)
    spread_last(stats_ref)


def add_stats(stats_ref, value):
    add_rows(stats_ref, column_sum(value), column_sum(value * value))


def add_rows(copies_ref, first, second):
    for c in range(first.shape[1] // 128):
        copies_ref[0, c : c + 1] += first[:, cols(c)]
        copies_ref[0, SLOT + c : SLOT + c + 1] += second[:, cols(c)]


def summed(ref):
    total = jnp.sum(ref[...], axis=0)
    return tuple(
        jnp.concatenate([total[SLOT * k + c : SLOT * k + c + 1] for c in range(SLOT)], axis=1)
        for k in range(2)
    )


def drive_kernel(layer, down, tokens, *refs):
    (
        stat_ref, u_ref, gain_ref, bias_ref, skip_ref, win_ref, disc_ref, jr_ref,
        b_ref, end_ref, blk_ref, norm_ref,
    ) = refs
    i, nt = pl.program_id(0), pl.num_programs(0)
    steps = u_ref.shape[0] // LANES
    chunks = chunk_count(b_ref)
    half = chunks * 128

    @pl.when(i == 0)
    def _():
        total, squares = summed(stat_ref)
        row = slice(layer, layer + 1)
        mean = total / tokens
        inv = lax.rsqrt(squares / tokens - mean * mean + EPSILON)
        norm_ref[0:1] = mean
        norm_ref[1:2] = inv
        norm_ref[2:3] = inv * gain_ref[row]
        norm_ref[3:4] = bias_ref[row]
        norm_ref[4:5] = skip_ref[row]
        norm_ref[5:8] = jnp.zeros((3, norm_ref.shape[1]), F32)
        blk_ref[...] = jnp.zeros_like(blk_ref)

    fr, fi = disc_ref[1:2, :half], disc_ref[1:2, half:]
    tile = nt - 1 - i if down else i
    scan = Scan(b_ref, blk_ref, disc_row(disc_ref, 0, chunks), jr_ref, tile * steps, down)

    def product(part):
        at = slice(*part)
        u = u_ref[at].astype(F32)
        normed = (u - norm_ref[0:1]) * norm_ref[2:3] + norm_ref[3:4]
        drive = jnp.dot(normed.astype(BF16), win_ref[...], preferred_element_type=F32)
        re, im = drive[:, :half], drive[:, half:]
        b_ref[at, :half] = re * fr - im * fi
        b_ref[at, half:] = re * fi + im * fr

    in_stages([product, scan.run], parts_of(b_ref.shape[0], down, 4 if down else 2))
    scan.close()

    @pl.when(i == nt - 1)
    def _():
        zero = [jnp.zeros((1, 128), F32)] * chunks
        cr, ci = chain(blk_ref, jr_ref, disc_row(disc_ref, 2, chunks), (zero, zero), down)
        put_copies(end_ref, cr, ci)


def states_scan(ends_ref, table_ref, b_ref, blk_ref, disc_ref, jr_ref, low_ref, st_ref, down):
    i, nt = pl.program_id(0), pl.num_programs(0)
    chunks = chunk_count(b_ref)
    steps = b_ref.shape[0] // LANES

    @pl.when(i == 0)
    def _():
        carry = carry_in(ends_ref, table_ref, chunks)
        chain(blk_ref, jr_ref, disc_row(disc_ref, 2, chunks), carry, down, st_ref)

    tile = nt - 1 - i if down else i
    scan = Scan(b_ref, st_ref, disc_row(disc_ref, 0, chunks), jr_ref, tile * steps, down)

    def stage(part):
        scan.run(part, lambda at, pair: store_pair(low_ref, at, *pair))

    return scan, stage


def gelu_parts(mixed):
    square = mixed * mixed
    tanh = jnp.tanh(mixed * (GELU_A + (GELU_A * GELU_B) * square))
    half_up = 0.5 + 0.5 * tanh
    return square, tanh, half_up


def gelu_slope(mixed, square, tanh, half_up):
    return half_up + (mixed * (0.5 - 0.5 * tanh * tanh)) * (
        GELU_A + (3.0 * GELU_A * GELU_B) * square
    )


def sigmoid(value):
    return 0.5 + 0.5 * jnp.tanh(0.5 * value)


def forward_kernel(down, *refs):
    (
        ends_ref, table_ref, b_ref, blk_ref, disc_ref, jr_ref, u_ref, norm_ref, wout_ref, wgate_ref,
        next_ref, copy_ref, low_ref, mixed_ref, gate_ref, stats_ref, st_ref,
    ) = refs
    scan, states = states_scan(
        ends_ref, table_ref, b_ref, blk_ref, disc_ref, jr_ref, low_ref, st_ref, down
    )
    zero_first(stats_ref)
    acts = {}

    def mix(part):
        at = slice(*part)
        u = u_ref[at].astype(F32)
        normed = (u - norm_ref[0:1]) * norm_ref[2:3] + norm_ref[3:4]
        mixed = jnp.dot(low_ref[at], wout_ref[...], preferred_element_type=F32)
        mixed += norm_ref[4:5] * normed
        _, _, half_up = gelu_parts(mixed)
        acts[part] = mixed * half_up
        mixed_ref[at] = mixed.astype(BF16)

    def finish(part):
        at = slice(*part)
        act = acts[part]
        gate = sigmoid(jnp.dot(act.astype(BF16), wgate_ref[...], preferred_element_type=F32))
        after = u_ref[at].astype(F32) + act * gate
        next_ref[at] = after
        copy_ref[at] = after
        gate_ref[at] = gate.astype(BF16)
        add_stats(stats_ref, after)

    in_stages([states, mix, finish], parts_of(b_ref.shape[0], down))
    scan.close()
    spread_last(stats_ref)


def zero_first(*refs):
    @pl.when(pl.program_id(0) == 0)
    def _():
        for ref in refs:
            ref[...] = jnp.zeros(ref.shape, ref.dtype)


def spread_last(ref):
    @pl.when(pl.program_id(0) == pl.num_programs(0) - 1)
    def _():
        ref[...] = jnp.broadcast_to(ref[0:1], ref.shape)


class GateBackward:
    def __init__(self, low_ref, wout_ref, wgate_ref, pg_ref, sg_ref, wsum_ref, ssum_ref, acts):
        self.low_ref, self.wout_ref, self.wgate_ref = low_ref, wout_ref, wgate_ref
        self.pg_ref, self.sg_ref = pg_ref, sg_ref
        self.wsum_ref, self.ssum_ref = wsum_ref, ssum_ref
        self.act_ref, self.logit_ref = acts
        self.kept = {}

    def enter(self, part, g, mixed, gate, normed, kept=None):
        at = slice(*part)
        square, tanh, half_up = gelu_parts(mixed) if kept is None else kept
        act = mixed * half_up
        g_gate = g * gate
        if kept is None:
            self.act_ref[at] = act.astype(BF16)
        self.logit_ref[at] = (g_gate * act * (1.0 - gate)).astype(BF16)
        self.kept[part] = (g_gate, gelu_slope(mixed, square, tanh, half_up), normed)

    def middle(self, part):
        at = slice(*part)
        g_gate, slope, normed = self.kept[part]
        act_grad = g_gate + lax.dot_general(
            self.logit_ref[at], self.wgate_ref[...], NT, preferred_element_type=F32
        )
        mixed_grad = act_grad * slope
        self.ssum_ref[...] += column_sum(mixed_grad * normed)
        self.pg_ref[at] = mixed_grad.astype(BF16)

    def leave(self, part):
        at = slice(*part)
        self.sg_ref[at] = lax.dot_general(
            self.pg_ref[at], self.wout_ref[...], NT, preferred_element_type=F32
        )

    def gate_sum(self):
        states, width = self.wout_ref.shape
        self.wsum_ref[states : states + width] += lax.dot_general(
            self.act_ref[...], self.logit_ref[...], TN, preferred_element_type=F32
        )

    def out_sum(self):
        states = self.wout_ref.shape[0]
        self.wsum_ref[:states] += lax.dot_general(
            self.low_ref[...], self.pg_ref[...], TN, preferred_element_type=F32
        )


def turn_kernel(down, *refs):
    (
        ends_ref, table_ref, b_ref, blk_ref, disc_ref, jr_ref, jo_ref, u_ref, norm_ref, wout_ref, wgate_ref,
        gout_ref, order_ref,
        out_ref, low_ref, g_ref, pg_ref, sg_ref, wsum_ref, end_ref, ablk_ref,
        st_ref, w_ref, act_ref, logit_ref,
    ) = refs
    sums = wout_ref.shape[0] + wout_ref.shape[1]
    ssum_ref = wsum_ref.at[sums : sums + 1]
    i, nt = pl.program_id(0), pl.num_programs(0)
    chunks = chunk_count(b_ref)
    half = chunks * 128
    steps = b_ref.shape[0] // LANES
    tile = nt - 1 - i if down else i
    scan, states = states_scan(
        ends_ref, table_ref, b_ref, blk_ref, disc_ref, jr_ref, low_ref, st_ref, down
    )
    back = GateBackward(
        low_ref, wout_ref, wgate_ref, pg_ref, sg_ref, wsum_ref, ssum_ref, (act_ref, logit_ref)
    )

    @pl.when(i == 0)
    def _():
        wsum_ref[...] = jnp.zeros(wsum_ref.shape, F32)
        ablk_ref[...] = jnp.zeros(ablk_ref.shape, F32)
        w_ref[:, :half] = jnp.ones((LANES, half), F32)
        w_ref[:, half:] = jnp.zeros((LANES, half), F32)

    mid = {}

    def mix(part):
        at = slice(*part)
        u = u_ref[at]
        normed = (u - norm_ref[0:1]) * norm_ref[2:3] + norm_ref[3:4]
        mixed = jnp.dot(low_ref[at], wout_ref[...], preferred_element_type=F32)
        mixed += norm_ref[4:5] * normed
        kept = gelu_parts(mixed)
        act_ref[at] = (mixed * kept[2]).astype(BF16)
        mid[part] = (normed, mixed, kept)

    def enter(part):
        at = slice(*part)
        normed, mixed, kept = mid[part]
        gate = sigmoid(jnp.dot(act_ref[at], wgate_ref[...], preferred_element_type=F32))
        permute_out(u_ref[at] + (mixed * kept[2]) * gate, order_ref, out_ref, part)
        g = permute_in(gout_ref, order_ref, part)
        g_ref[at] = g.astype(BF16)
        back.enter(part, g, mixed, gate, normed, kept)

    dr, di = disc_row(disc_ref, 0, chunks, conj=True)
    dr, di = wide(dr), wide(di)
    jo = jo_ref[...]
    live = {
        "w": rows_of(w_ref, slice(0, LANES), chunks),
        "a": rows_of(ablk_ref, slice(0, LANES), chunks),
    }

    def weigh(part):
        (wr, wi), (ar, ai) = (tuple(map(list, live[k])) for k in "wa")
        order = range(part[0] // LANES, part[1] // LANES)
        for step in reversed(order) if down else order:
            sr, si = rows_of(sg_ref, slice(step * LANES, (step + 1) * LANES), chunks)
            keep = jo != tile * steps + step
            for c in range(chunks):
                ar[c] = ar[c] + (wr[c] * sr[c] - wi[c] * si[c])
                ai[c] = ai[c] + (wr[c] * si[c] + wi[c] * sr[c])
                xr = jnp.where(keep, wr[c], 0.0)
                xi = jnp.where(keep, wi[c], 0.0)
                wr[c] = xr * dr[c] - xi * di[c]
                wi[c] = xr * di[c] + xi * dr[c]
        live["w"], live["a"] = (wr, wi), (ar, ai)

    in_stages(
        [states, mix, enter, back.middle, back.leave, weigh], parts_of(b_ref.shape[0], down, 4),
        {2: back.gate_sum, 3: back.out_sum},
    )
    scan.close()
    put_rows(w_ref, slice(0, LANES), *live["w"])
    put_rows(ablk_ref, slice(0, LANES), *live["a"])

    @pl.when(i == nt - 1)
    def _():
        zero = [jnp.zeros((1, 128), F32)] * chunks
        power = disc_row(disc_ref, 2, chunks, conj=True)
        cr, ci = chain(ablk_ref, jo_ref, power, (zero, zero), not down)
        put_copies(end_ref, cr, ci)


def adjoint_kernel(down, last, *refs):
    (
        ends_ref, table_ref, sg_ref, ablk_ref, disc_ref, jr_ref, low_ref, u_ref, norm_ref, pg_ref, g_ref,
        win_ref, order_ref, *refs
    ) = refs
    if last:
        (
            ssum_ref, res_ref, sums_ref, st_ref, dg_ref, ax_ref, low_normed_ref, nsum_ref, isum_ref,
        ) = refs
    else:
        (res_ref, sums_ref, nsum_ref, st_ref, dg_ref, ax_ref, low_normed_ref) = refs
        isum_ref = sums_ref
    width, states = win_ref.shape
    i, nt = pl.program_id(0), pl.num_programs(0)
    chunks = chunk_count(sg_ref)
    half = chunks * 128
    steps = sg_ref.shape[0] // LANES
    tile = nt - 1 - i if down else i

    @pl.when(i == 0)
    def _():
        carry = carry_in(ends_ref, table_ref, chunks)
        power = disc_row(disc_ref, 2, chunks, conj=True)
        chain(ablk_ref, jr_ref, power, carry, down, st_ref)
        ax_ref[...] = jnp.zeros_like(ax_ref)

    zero_first(isum_ref, nsum_ref)
    fr, fi = disc_row(disc_ref, 1, chunks)
    fr, fi = wide(fr), wide(fi)
    decay = disc_row(disc_ref, 0, chunks, conj=True)
    scan = Scan(sg_ref, st_ref, decay, jr_ref, tile * steps, down)
    sums = tuple(map(list, rows_of(ax_ref, slice(0, LANES), chunks)))

    def emit(at, pair):
        xr, xi = rows_of(low_ref, at, chunks)
        xr, xi = [v.astype(F32) for v in xr], [v.astype(F32) for v in xi]
        grads = []
        for which, (ar, ai) in enumerate(pair):
            gr, gi = [], []
            rows = slice(which * LANES, (which + 1) * LANES)
            for c in range(chunks):
                vr, vi = xr[c][rows], xi[c][rows]
                sums[0][c] = sums[0][c] + (ar[c] * vr + ai[c] * vi)
                sums[1][c] = sums[1][c] + (ai[c] * vr - ar[c] * vi)
                gr.append(ar[c] * fr[c] + ai[c] * fi[c])
                gi.append(ai[c] * fr[c] - ar[c] * fi[c])
            grads.append((gr, gi))
        store_pair(dg_ref, at, *grads)

    def finish(part):
        at = slice(*part)
        centered = u_ref[at].astype(F32) - norm_ref[0:1]
        low_normed_ref[at] = (centered * norm_ref[2:3] + norm_ref[3:4]).astype(BF16)
        normed_grad = lax.dot_general(dg_ref[at], win_ref[...], NT, preferred_element_type=F32)
        normed_grad += norm_ref[4:5] * pg_ref[at].astype(F32)
        add_rows(
            nsum_ref, column_sum(normed_grad), column_sum(normed_grad * centered) * norm_ref[1:2]
        )
        result = g_ref[at].astype(F32) + norm_ref[2:3] * normed_grad
        if last:
            permute_out(result, order_ref, res_ref, part)
        else:
            res_ref[at] = result

    in_stages(
        [lambda part: scan.run(part, emit), finish],
        parts_of(sg_ref.shape[0], down, 2 if last else 4),
    )
    isum_ref[:width] += lax.dot_general(
        low_normed_ref[...], dg_ref[...], TN, preferred_element_type=F32
    )
    scan.close()
    put_rows(ax_ref, slice(0, LANES), *sums)
    spread_last(nsum_ref)

    @pl.when(i == nt - 1)
    def _():
        decays = jnp.sum(ax_ref[...], axis=0, keepdims=True)
        wr, wi = win_ref[:, :half].astype(F32), win_ref[:, half:].astype(F32)
        gr, gi = isum_ref[:width, :half], isum_ref[:width, half:]
        re = jnp.sum(wr * gr + wi * gi, axis=0, keepdims=True)
        im = jnp.sum(wr * gi - wi * gr, axis=0, keepdims=True)
        gr, gi = disc_ref[1:2, :half], disc_ref[1:2, half:]
        scale = 1.0 / (gr * gr + gi * gi)
        factors = ((re * gr - im * gi) * scale, (re * gi + im * gr) * scale)
        if last:
            rows = width // BLOCKS
            first = rows + rows // 2
            for b in range(BLOCKS):
                at = b * rows
                sums_ref[b, :rows] = isum_ref[at : at + rows, :width]
                sums_ref[b, rows:first, : states - width] = isum_ref[at : at + rows // 2, width:]
                sums_ref[b, rows:first, states - width :] = isum_ref[
                    at + rows // 2 : at + rows, width:
                ]
                sums_ref[b, first:] = jnp.zeros((SMALL, width), F32)
            small = [nsum_ref[0]] + [ssum_ref[:, cols(c)] for c in range(width // 128)]
            small += [decays[:, cols(c)] for c in range(2 * chunks)]
            small += [v[:, cols(c)] for v in factors for c in range(chunks)]
            small = [v[r : r + 1] for v in small for r in range(v.shape[0])]
            for k, row in enumerate(small):
                at = (k % SMALL, k // SMALL)
                sums_ref[0, first + at[0] : first + at[0] + 1, cols(at[1])] = row
        else:
            sums_ref[width : width + 1] = decays
            sums_ref[width + 1 : width + 2, :half] = factors[0]
            sums_ref[width + 1 : width + 2, half:] = factors[1]


def back_kernel(down, tokens, core, *refs):
    (
        sums_ref, r_ref, up_ref, up_norm_ref, mixed_ref, gate_ref, low_ref, u_ref, norm_ref, wout_ref,
        wgate_ref, disc_ref, jo_ref,
        g_ref, pg_ref, sg_ref, kept_ref, sent_ref, ssum_ref, end_ref, ablk_ref, nsum_ref, bsum_ref, wsum_ref,
        act_ref, logit_ref,
    ) = refs
    i, nt = pl.program_id(0), pl.num_programs(0)
    chunks = chunk_count(sg_ref)
    steps = sg_ref.shape[0] // LANES
    tile = nt - 1 - i if down else i

    @pl.when(i == 0)
    def _():
        nsum_ref[...] = jnp.sum(sums_ref[...], axis=0)
        bsum_ref[0:1], bsum_ref[1:2] = summed(sums_ref)

    zero_first(ablk_ref, wsum_ref, ssum_ref)
    back = GateBackward(
        low_ref, wout_ref, wgate_ref, pg_ref, sg_ref, wsum_ref, ssum_ref, (act_ref, logit_ref)
    )
    decay = disc_row(disc_ref, 0, chunks, conj=True)
    scan = Scan(sg_ref, ablk_ref, decay, jo_ref, tile * steps, down)
    scale = up_norm_ref[2:3] * (-1.0 / tokens)

    def enter(part):
        at = slice(*part)
        standard = (up_ref[at] - up_norm_ref[0:1]) * (scale * up_norm_ref[1:2] * bsum_ref[1:2])
        g = r_ref[at] + (standard + scale * bsum_ref[0:1])
        g_ref[at] = g
        u = u_ref[at].astype(F32)
        normed = (u - norm_ref[0:1]) * norm_ref[2:3] + norm_ref[3:4]
        back.enter(part, g, mixed_ref[at].astype(F32), gate_ref[at].astype(F32), normed)

    in_stages(
        [enter, back.middle, back.leave, scan.run], parts_of(sg_ref.shape[0], down),
        {0: back.gate_sum, 1: back.out_sum},
    )
    scan.close()

    @pl.when(i == nt - 1)
    def _():
        zero = [jnp.zeros((1, 128), F32)] * chunks
        power = disc_row(disc_ref, 2, chunks, conj=True)
        cr, ci = chain(ablk_ref, jo_ref, power, (zero, zero), down)
        put_copies(end_ref, cr, ci)
        states, width = wout_ref.shape
        gates, outs = width // BLOCKS, states // BLOCKS
        side = lax.axis_index(core)
        for ref, first in ((kept_ref, side), (sent_ref, 1 - side)):
            for b in range(BLOCKS // 2):
                at = first * (BLOCKS // 2) + b
                ref[b, :gates] = wsum_ref[pl.ds(pl.multiple_of(states + at * gates, 8), gates)]
                ref[b, gates:] = wsum_ref[pl.ds(pl.multiple_of(at * outs, 8), outs)]


def last_kernel(
    tokens, piece_ref, small_ref, out1_ref, gate1_ref, skip1_ref, in1_ref, decay1_ref, norm1_ref,
    disc_ref, rate_ref, step_ref, freq_ref, r_ref, tok_ref, norm_ref,
    grad_in_ref, gain_ref, bias_ref, drate_ref, dstep_ref, dfreq_ref, in_ref, out_ref, skip_ref,
    gate_ref,
):
    gates, width = gate1_ref.shape
    outs = out1_ref.shape[0]
    states = in1_ref.shape[1]
    half = states // 2
    left = states - width
    gate_ref[0], gate_ref[1] = piece_ref[:gates], gate1_ref[...]
    out_ref[0], out_ref[1] = piece_ref[gates : gates + outs], out1_ref[...]
    at = gates + outs
    in_ref[0, :, :width] = piece_ref[at : at + gates]
    at += gates
    in_ref[0, : gates // 2, width:] = piece_ref[at : at + gates // 2, :left]
    in_ref[0, gates // 2 :, width:] = piece_ref[at : at + gates // 2, left:]
    in_ref[1] = in1_ref[...]

    def row(ref, first, count):
        places = [(k % SMALL, k // SMALL) for k in range(first, first + count)]
        return jnp.concatenate([ref[r : r + 1, cols(c)] for r, c in places], axis=1)

    count = width // 128
    bias, gain = row(small_ref, 0, count), row(small_ref, count, count)
    scale = norm_ref[2:3] * (-1.0 / tokens)
    grad_in_ref[...] = r_ref[...] + (
        (tok_ref[...].astype(F32) - norm_ref[0:1]) * (scale * norm_ref[1:2] * gain) + scale * bias
    )

    @pl.when(pl.program_id(0) == 0)
    def _():
        bias_ref[0:1], gain_ref[0:1] = bias, gain
        bias_ref[1:2], gain_ref[1:2] = row(norm1_ref, 0, count), row(norm1_ref, count, count)
        skip_ref[0:1], skip_ref[1:2] = row(small_ref, 2 * count, count), skip1_ref[0:1]
        at = 3 * count
        lanes = half // 128
        for l in range(LAYERS):
            if l == 0:
                ar, ai, sr, si = (row(small_ref, at + k * lanes, lanes) for k in range(4))
            else:
                ar, ai = decay1_ref[0:1, :half], decay1_ref[0:1, half:]
                sr, si = decay1_ref[1:2, :half], decay1_ref[1:2, half:]
            dr, di = disc_ref[l, 0:1, :half], disc_ref[l, 0:1, half:]
            fr, fi = disc_ref[l, 1:2, :half], disc_ref[l, 1:2, half:]
            here = slice(l, l + 1)
            rate, freq, step = rate_ref[here], freq_ref[here], jnp.exp(step_ref[here])
            tr = ar - (fr * sr + fi * si)
            ti = ai - (fr * si - fi * sr)
            size = 1.0 / (dr * dr + di * di)
            gr, gi = (tr * dr - ti * di) * size, (tr * di + ti * dr) * size
            mr, mi = -rate * fr - freq * fi, freq * fr - rate * fi
            size = 1.0 / (rate * rate + freq * freq)
            gr += (-rate * sr - freq * si) * size
            gi += (freq * sr - rate * si) * size
            both = 2.0 * (fr * sr + fi * si)
            gx = gr * dr + gi * di
            gy = gi * dr - gr * di
            drate_ref[here] = (-mr * sr - mi * si - both * rate) * size - step * gx
            dfreq_ref[here] = (mi * sr - mr * si - both * freq) * size + step * gy
            dstep_ref[here] = step * (freq * gy - rate * gx)


def whole(array):
    shape = array.shape
    return pl.BlockSpec(shape, lambda i: (0,) * len(shape))


def tile_spec(rows, width, nt, down):
    if down:
        return pl.BlockSpec((rows, width), lambda i: (nt - 1 - i, 0))
    return pl.BlockSpec((rows, width), lambda i: (i, 0))


def run_spec(steps, width, nt, down):
    if down:
        return pl.BlockSpec((LANES, steps, width), lambda i: (0, nt - 1 - i, 0))
    return pl.BlockSpec((LANES, steps, width), lambda i: (0, i, 0))


def call(kernel, nt, args, outs, scratch, macs, name):
    arrays = [a for a, *_ in args]
    sizes = sum(a.size * a.dtype.itemsize for a in arrays + [a for a, *_ in outs])
    held = [
        a if keep is None else pltpu.with_memory_space_constraint(a, keep)
        for a, _, keep in map(filled, args)
    ]
    return pl.pallas_call(
        kernel,
        grid=(nt,),
        in_specs=[whole(a) if s is None else s for a, s, _ in map(filled, args)],
        out_specs=[whole(a) if s is None else s for a, s, _ in map(filled, outs)],
        out_shape=[
            a if keep is None else keep(a.shape, a.dtype) for a, _, keep in map(filled, outs)
        ],
        scratch_shapes=scratch,
        compiler_params=pltpu.CompilerParams(
            vmem_limit_bytes=VMEM_LIMIT, dimension_semantics=("arbitrary",)
        ),
        cost_estimate=pl.CostEstimate(flops=2 * macs, bytes_accessed=sizes, transcendentals=0),
        name=name,
    )(*held)


def filled(entry):
    return entry if len(entry) == 3 else entry + (pltpu.HBM,)


def shape(*dims, dtype=F32):
    return jax.ShapeDtypeStruct(dims, dtype)


def body(
    axes,
    tokens_in,
    seq_starts,
    norm_gain,
    norm_bias,
    decay_rate,
    step_log,
    frequency,
    in_proj,
    out_proj,
    skip_gain,
    gate_proj,
    grad_out,
):
    rows, width = tokens_in.shape
    states = in_proj.shape[-1]
    devices = 2 ** len(axes)
    tokens = float(rows * devices)
    run = rows // LANES
    steps = min(64, run)
    tile = steps * LANES
    nt = rows // tile
    span = min(16, steps)
    def tiles(array, down):
        return (array, tile_spec(tile, array.shape[-1], nt, down))

    def runs(array, down):
        return (array, run_spec(steps, array.shape[-1], nt, down))

    def full(array):
        return (array, None)

    def of(array, l):
        size = array.shape[1:]
        return (array, pl.BlockSpec((None,) + size, lambda i: (l,) + (0,) * len(size)))

    discs, tables, cuts, order = call(
        functools.partial(prep_kernel, rows, axes), 1,
        [full(seq_starts[None]), full(decay_rate),
         full(step_log), full(frequency)],
        [full(shape(LAYERS, 8, states)), full(shape(2 * LAYERS, 2, devices, 2 * SLOT, 128)),
         full(shape(2, LANES, 128, dtype=jnp.int32)),
         full(shape(span * LANES, span * LANES, dtype=BF16))],
        [], rows * width, "prep",
    )

    def near(entry):
        return entry[:2] + (pltpu.VMEM if rows * states * 4 <= 7 * 2**20 else pltpu.HBM,)

    tokens_run = tokens_in.reshape(LANES, run, width)
    grad_run = grad_out.reshape(LANES, run, width)
    state_scratch = pltpu.VMEM((LANES, states), F32)
    half_scratch = [pltpu.VMEM((tile, width), BF16)] * 2
    cost = rows * width * states

    u0_near, u0, stats = call(
        stats_kernel, nt, [near(runs(tokens_run, 0)), full(order)],
        [near(tiles(shape(rows, width, dtype=BF16), 0)), tiles(shape(rows, width, dtype=BF16), 0),
         near(full(shape(devices, 2 * SLOT, 128)))],
        [], cost // 2, "stats",
    )

    def drive(l, stream, stats):
        down = l % 2
        return call(
            functools.partial(drive_kernel, l, bool(down), tokens), nt,
            [near(full(gather_all(stats, axes))), near(tiles(stream, down)), full(norm_gain), full(norm_bias), full(skip_gain), of(in_proj, l), of(discs, l),
               of(cuts, down)],
            [near(tiles(shape(rows, states), down)), near(full(shape(devices, 2 * SLOT, 128))),
             full(shape(LANES, states)), full(shape(8, width))],
            [], 4 * cost, f"drive_{l}",
        )

    b0, end0, blk0, norm0 = drive(0, u0_near, stats)
    u1_near, u1, low0, mixed0, gate0, stats = call(
        functools.partial(forward_kernel, False), nt,
        [near(full(gather_all(end0, axes))), of(tables, 2 * 0 + 0), near(tiles(b0, 0)), full(blk0), of(discs, 0), of(cuts, 0),
           near(tiles(u0_near, 0)), full(norm0), of(out_proj, 0), of(gate_proj, 0)],
        [near(tiles(shape(rows, width), 0)), tiles(shape(rows, width), 0), tiles(shape(rows, states, dtype=BF16), 0),
         tiles(shape(rows, width, dtype=BF16), 0), tiles(shape(rows, width, dtype=BF16), 0),
         near(full(shape(devices, 2 * SLOT, 128)))],
        [state_scratch], 6 * cost, "forward_0",
    )

    b1, end1, blk1, norm1 = drive(1, u1_near, stats)
    (
        out, low1, g1, pg1, sg1, w_sum1, aend1, ablk1
    ) = call(
        functools.partial(turn_kernel, True), nt,
        [near(full(gather_all(end1, axes))), of(tables, 2 * 1 + 0), near(tiles(b1, 1)), full(blk1), of(discs, 1), of(cuts, 1),
           of(cuts, 0), tiles(u1, 1), full(norm1), of(out_proj, 1), of(gate_proj, 1),
           runs(grad_run, 1), full(order)],
        [runs(shape(LANES, run, width), 1), near(tiles(shape(rows, states, dtype=BF16), 1)),
         near(tiles(shape(rows, width, dtype=BF16), 1)),
         near(tiles(shape(rows, width, dtype=BF16), 1)), near(tiles(shape(rows, states), 1)), full(shape(states + width + 8, width)),
         near(full(shape(devices, 2 * SLOT, 128))), full(shape(LANES, states))],
        [state_scratch, state_scratch] + half_scratch, 16 * cost, "turn_1",
    )

    def adjoint(l, sg, ablk, ends, low, stream, norm, pg, g, skip_sum=None):
        down = 1 - l % 2
        last = l == 0
        held = (lambda entry: entry) if last else near
        args = [
            near(full(ends)), of(tables, 2 * l + 1), held(tiles(sg, down)), full(ablk), of(discs, l),
            of(cuts, down), held(tiles(low, down)), tiles(stream, down),
            full(norm), held(tiles(pg, down)), held(tiles(g, down)), of(in_proj, l), full(order),
        ]
        scratch = [
            state_scratch, pltpu.VMEM((tile, states), BF16), state_scratch,
            pltpu.VMEM((tile, width), BF16),
        ]
        if last:
            args.append(full(skip_sum))
            outs = [
                runs(shape(LANES, run, width), down),
                full(shape(BLOCKS, (width + width // 2) // BLOCKS + SMALL, width)),
            ]
            scratch += [pltpu.VMEM((1, 2 * SLOT, 128), F32), pltpu.VMEM((width, states), F32)]
        else:
            outs = [
                tiles(shape(rows, width), down), full(shape(width + 8, states)),
                near(full(shape(devices, 2 * SLOT, 128))),
            ]
        return call(
            functools.partial(adjoint_kernel, bool(down), last), nt, args, outs, scratch,
            8 * cost, f"adjoint_{l}",
        )

    r1, in_sum1, norm_sum1 = adjoint(
        1, sg1, ablk1, gather_all(aend1, axes), low1, u1, norm1, pg1, g1
    )

    piece = (2 * width + states + width // 2) // BLOCKS + SMALL

    def lower(r1, norm_sum1):
        half = shape(BLOCKS // 2, (states + width) // BLOCKS, width)
        (
            g0, pg0, sg0, kept0, sent0, skip_sum0, aend0, ablk0, small1, _
        ) = call(
            functools.partial(back_kernel, True, tokens, axes[-1]), nt,
            [near(full(gather_all(norm_sum1, axes))), tiles(r1, 1), tiles(u1, 1), full(norm1),
             tiles(mixed0, 1), tiles(gate0, 1), tiles(low0, 1), tiles(u0, 1), full(norm0),
             of(out_proj, 0), of(gate_proj, 0), of(discs, 0), of(cuts, 1)],
            [tiles(shape(rows, width), 1), tiles(shape(rows, width, dtype=BF16), 1),
             tiles(shape(rows, states), 1), full(half), full(half), full(shape(1, width)), near(full(shape(devices, 2 * SLOT, 128))),
             full(shape(LANES, states)), full(shape(2 * SLOT, 128)), full(shape(2, width))],
            [pltpu.VMEM((states + width, width), F32)] + half_scratch, 12 * cost, "back_0",
        )
        core, chips, *others = phases(axes)
        part = kept0 + lax.ppermute(sent0, core[0], [(0, 1), (1, 0)])
        ends, part = lax.optimization_barrier((gather_all(aend0, axes), part))
        part = part.reshape(-1, width)
        part = scatter_sum(part, chips)
        r0, in_sum0 = adjoint(0, sg0, ablk0, ends, low0, u0, norm0, pg0, g0, skip_sum0)
        in_sum0, part = lax.optimization_barrier((in_sum0, part))
        in_part = scatter_sum(scatter_sum(in_sum0.reshape(-1, width), core), chips)
        pad = -piece % (8 * 2 ** len(others[0]))
        part = jnp.concatenate([part, in_part, jnp.zeros((pad, width), F32)], axis=0)
        part = sum_all(part, others)[:piece]
        pieces = gather_rows(gather_rows(part, chips), core)
        return r0.reshape(rows, width), small1, pieces.reshape(BLOCKS, -1, width)

    def nothing(r1, norm_sum1):
        return (
            jnp.zeros((rows, width), F32),
            jnp.zeros((2 * SLOT, 128), F32),
            jnp.zeros((BLOCKS, piece, width), F32),
        )

    w_all1, in_all1 = lax.psum((w_sum1, in_sum1), axes)
    r0, norm_all1, pieces = lax.cond(seq_starts[0] == 0, lower, nothing, r1, norm_sum1)

    gates, outs = width // BLOCKS, states // BLOCKS

    def block(array, *dims, at=lambda i: (i, 0)):
        return (array, pl.BlockSpec(dims, at))

    def flat(array, count):
        return block(array, count, array.shape[1])

    (
        grad_in, gain_grad, bias_grad, rate_grad, step_grad, freq_grad, in_grad, out_grad,
        skip_grad, gate_grad,
    ) = call(
        functools.partial(last_kernel, tokens), BLOCKS,
        [block(pieces, None, piece, width, at=lambda i: (i, 0, 0)) + (None,),
         block(pieces, None, SMALL, width, at=lambda i: (0, piece // SMALL - 1, 0)) + (None,),
         flat(w_all1, outs),
         block(w_all1, gates, width, at=lambda i: (states // gates + i, 0)),
         block(w_all1, 8, width, at=lambda i: ((states + width) // 8, 0)),
         flat(in_all1, gates),
         block(in_all1, 8, states, at=lambda i: (width // 8, 0)),
         full(norm_all1), full(discs), full(decay_rate), full(step_log), full(frequency),
         flat(r0, rows // BLOCKS), flat(tokens_in, rows // BLOCKS), full(norm0)],
        [flat(shape(rows, width), rows // BLOCKS), full(shape(LAYERS, width)),
         full(shape(LAYERS, width)), full(shape(LAYERS, states // 2)),
         full(shape(LAYERS, states // 2)), full(shape(LAYERS, states // 2)),
         block(shape(LAYERS, width, states), LAYERS, gates, states, at=lambda i: (0, i, 0)),
         block(shape(LAYERS, states, width), LAYERS, outs, width, at=lambda i: (0, i, 0)),
         full(shape(LAYERS, width)),
         block(shape(LAYERS, width, width), LAYERS, gates, width, at=lambda i: (0, i, 0))],
        [], cost, "last",
    )
    return (
        out.reshape(rows, width),
        grad_in,
        gain_grad,
        bias_grad,
        rate_grad,
        step_grad,
        freq_grad,
        in_grad,
        out_grad,
        skip_grad,
        gate_grad,
    )


def solution(mesh):
    bits = mesh.devices.size.bit_length() - 1
    axes = tuple("b%d" % k for k in range(bits))
    binary = Mesh(mesh.devices.reshape((2,) * bits), axes)
    rows = P(axes, None)
    return jax.shard_map(
        functools.partial(body, axes),
        mesh=binary,
        in_specs=(rows,) + (P(),) * 10 + (rows,),
        out_specs=(rows, rows) + (P(),) * 9,
        check_vma=False,
    )
```

```python
import functools

import jax
import jax.numpy as jnp
from jax import lax
from jax.experimental import pallas as pl
from jax.experimental.pallas import tpu as pltpu
from jax.sharding import Mesh, PartitionSpec as P

LAYERS = 2
EPSILON = 1e-05
SMALL = 8
BLOCKS = 8
SLOT = 4
LANES = 8
VMEM_LIMIT = 30 * 1024 * 1024
GELU_A = 0.7978845608028654
GELU_B = 0.044715
NT = (((1,), (1,)), ((), ()))
TN = (((0,), (0,)), ((), ()))
F32 = jnp.float32
BF16 = jnp.bfloat16


def gather_all(copies, axes):
    return lax.all_to_all(copies, axes, 0, 0)


def scatter_sum(value, axes):
    count = 2 ** len(axes)
    pieces = value.reshape((count, value.shape[0] // count) + value.shape[1:])
    return jnp.sum(lax.all_to_all(pieces, axes, 0, 0), axis=0)


def gather_rows(value, axes):
    count = 2 ** len(axes)
    copies = jnp.broadcast_to(value, (count,) + value.shape)
    return lax.all_to_all(copies, axes, 0, 0).reshape((count * value.shape[0],) + value.shape[1:])


def phases(axes):
    left, out = list(axes), [(axes[-1],)]
    left = left[:-1]
    while left:
        out.append(tuple(left[-2:]))
        left = left[:-2]
    return out


def sum_all(value, parts):
    for part in parts:
        value = scatter_sum(value, part)
    for part in reversed(parts):
        value = gather_rows(value, part)
    return value


def cols(c):
    return slice(c * 128, (c + 1) * 128)


def chunk_count(ref):
    return ref.shape[-1] // 256


def rows_of(ref, at, chunks):
    half = chunks * 128
    re = [ref[at, c * 128 : (c + 1) * 128] for c in range(chunks)]
    im = [ref[at, half + c * 128 : half + (c + 1) * 128] for c in range(chunks)]
    return re, im


def put_rows(ref, at, re, im):
    chunks = len(re)
    half = chunks * 128
    for c in range(chunks):
        ref[at, c * 128 : (c + 1) * 128] = re[c]
        ref[at, half + c * 128 : half + (c + 1) * 128] = im[c]


def put_copies(ref, re, im):
    ref[0] = jnp.zeros(ref.shape[1:], F32)
    for c in range(len(re)):
        ref[0, c : c + 1] = re[c]
        ref[0, SLOT + c : SLOT + c + 1] = im[c]
    ref[...] = jnp.broadcast_to(ref[0:1], ref.shape)


def wide(rows):
    return [jnp.broadcast_to(v, (LANES, 128)) for v in rows]


def chain(ends_ref, jr_ref, power, carry, down, start_ref=None):
    chunks = len(power[0])
    pr, pi = power
    cr, ci = carry
    order = range(LANES - 1, -1, -1) if down else range(LANES)
    for s in order:
        at = slice(s, s + 1)
        if start_ref is not None:
            put_rows(start_ref, at, cr, ci)
        er, ei = rows_of(ends_ref, at, chunks)
        alive = (jr_ref[at, :] < 0).astype(F32)
        cr, ci = (
            [er[c] + alive * (pr[c] * cr[c] - pi[c] * ci[c]) for c in range(chunks)],
            [ei[c] + alive * (pr[c] * ci[c] + pi[c] * cr[c]) for c in range(chunks)],
        )
    return cr, ci


def carry_in(ends_ref, table_ref, chunks):
    total = jnp.zeros((2 * SLOT, 128), F32)
    for e in range(ends_ref.shape[0]):
        end = ends_ref[e]
        turned = jnp.concatenate([end[SLOT:], end[:SLOT]], axis=0)
        total += table_ref[0, e] * end + table_ref[1, e] * turned
    return (
        [total[c : c + 1] for c in range(chunks)],
        [total[SLOT + c : SLOT + c + 1] for c in range(chunks)],
    )


def in_stages(stages, parts):
    for turn in range(len(parts) + len(stages) - 1):
        for k, stage in enumerate(stages):
            if 0 <= turn - k < len(parts):
                stage(parts[turn - k])


def parts_of(rows, down, count=2):
    size = rows // count
    parts = [(at, at + size) for at in range(0, rows, size)]
    return parts[::-1] if down else parts


class Scan:
    def __init__(self, src_ref, st_ref, decay, jr_ref, first_step, down):
        self.src_ref, self.st_ref, self.down = src_ref, st_ref, down
        self.chunks = chunk_count(src_ref)
        self.dr, self.di = wide(decay[0]), wide(decay[1])
        self.jr, self.first_step = jr_ref[...], first_step
        self.state = rows_of(st_ref, slice(0, LANES), self.chunks)

    def one(self, step):
        br, bi = rows_of(self.src_ref, slice(step * LANES, (step + 1) * LANES), self.chunks)
        live = self.jr != self.first_step + step
        nr, ni = [], []
        for c in range(self.chunks):
            xr = jnp.where(live, self.state[0][c], 0.0)
            xi = jnp.where(live, self.state[1][c], 0.0)
            nr.append(self.dr[c] * xr - self.di[c] * xi + br[c])
            ni.append(self.dr[c] * xi + self.di[c] * xr + bi[c])
        self.state = (nr, ni)
        return nr, ni

    def run(self, part, emit=None):
        low, high = part[0] // LANES, part[1] // LANES
        for n in range(0, high - low, 2):
            step = high - 2 - n if self.down else low + n
            first = self.one(step + 1 if self.down else step)
            second = self.one(step if self.down else step + 1)
            if emit is not None:
                pair = (second, first) if self.down else (first, second)
                emit(slice(step * LANES, (step + 2) * LANES), pair)

    def close(self):
        put_rows(self.st_ref, slice(0, LANES), *self.state)


def store_pair(ref, at, first, second):
    re = [jnp.concatenate([p, q], axis=0).astype(BF16) for p, q in zip(first[0], second[0])]
    im = [jnp.concatenate([p, q], axis=0).astype(BF16) for p, q in zip(first[1], second[1])]
    put_rows(ref, at, re, im)


def disc_row(disc_ref, row, chunks, conj=False):
    re, im = rows_of(disc_ref, slice(row, row + 1), chunks)
    return (re, [-v for v in im]) if conj else (re, im)


def column_sum(value):
    rows, width = value.shape
    return jnp.sum(jnp.sum(value.reshape(rows // 8, 8, width), axis=0), axis=0, keepdims=True)


def permute_in(block_ref, order_ref, part):
    runs, _, width = block_ref.shape
    size = order_ref.shape[0]
    span = size // runs
    out = []
    for k in range(part[0] // size, part[1] // size):
        rows = block_ref[:, k * span : (k + 1) * span, :].reshape(size, width)
        out.append(jnp.dot(order_ref[...], rows, preferred_element_type=F32))
    return out[0] if len(out) == 1 else jnp.concatenate(out, axis=0)


def permute_out(value, order_ref, out_ref, part):
    width = value.shape[1]
    size = order_ref.shape[0]
    span = size // LANES
    high = value.astype(BF16)
    low = (value - high.astype(F32)).astype(BF16)
    for n, k in enumerate(range(part[0] // size, part[1] // size)):
        at = slice(n * size, (n + 1) * size)
        back = lax.dot_general(order_ref[...], high[at], TN, preferred_element_type=F32)
        back += lax.dot_general(order_ref[...], low[at], TN, preferred_element_type=F32)
        out_ref[:, k * span : (k + 1) * span, :] = back.reshape(LANES, span, width)


def expm1(value):
    acc = jnp.full_like(value, 1.0 / 479001600.0)
    for n in (39916800.0, 3628800.0, 362880.0, 40320.0, 5040.0, 720.0, 120.0, 24.0, 6.0, 2.0, 1.0):
        acc = acc * value + 1.0 / n
    return jnp.where(value > -1.0, acc * value, jnp.exp(value) - 1.0)


def prep_kernel(
    rows, axes, starts_ref, rate_ref, step_ref, freq_ref,
    disc_ref, table_ref, cut_ref,
):
    devices = 2 ** len(axes)
    total = rows * devices
    run = rows // LANES
    half = rate_ref.shape[-1]
    me = 0
    for axis in axes:
        me = 2 * me + lax.axis_index(axis)
    starts = [starts_ref[:, k : k + 1] for k in range(starts_ref.shape[1])]

    base = me * rows + run * lax.broadcasted_iota(jnp.int32, (LANES, 128), 0)
    up = jnp.full((LANES, 128), -1, jnp.int32)
    down = up
    for begin in starts + [total]:
        rel = begin - base
        up = jnp.maximum(up, jnp.where((rel >= 0) & (rel < run), rel, -1))
        down = jnp.maximum(down, jnp.where((rel >= 1) & (rel <= run), rel - 1, -1))
    cut_ref[0] = up
    cut_ref[1] = down

    source = lax.broadcasted_iota(jnp.int32, (devices, half), 0)
    for l in range(LAYERS):
        row = slice(l, l + 1)
        rate, freq = rate_ref[row], freq_ref[row]
        step_size = jnp.exp(step_ref[row])
        real_angle = -rate * step_size
        imag_angle = freq * step_size
        magnitude = jnp.exp(real_angle)
        cosine, sine = jnp.cos(imag_angle), jnp.sin(imag_angle)
        minus_real = expm1(real_angle) * cosine - 2.0 * jnp.sin(0.5 * imag_angle) ** 2
        minus_imag = magnitude * sine
        modulus = rate * rate + freq * freq
        disc_ref[l, 0:1, :half] = magnitude * cosine
        disc_ref[l, 0:1, half:] = minus_imag
        disc_ref[l, 1:2, :half] = (-rate * minus_real + freq * minus_imag) / modulus
        disc_ref[l, 1:2, half:] = (-rate * minus_imag - freq * minus_real) / modulus
        magnitude = jnp.exp(real_angle * float(run))
        disc_ref[l, 2:3, :half] = magnitude * jnp.cos(imag_angle * float(run))
        disc_ref[l, 2:3, half:] = magnitude * jnp.sin(imag_angle * float(run))
        disc_ref[l, 3:8] = jnp.zeros((5, 2 * half), F32)
        powers = []
        for bit in range(len(axes)):
            magnitude = jnp.exp(real_angle * float(rows << bit))
            angle = imag_angle * float(rows << bit)
            powers.append((magnitude * jnp.cos(angle), magnitude * jnp.sin(angle)))
        for back in range(2):
            going_down = (l + back) % 2 == 1
            if going_down:
                live, count = source > me, source - me - 1
            else:
                live, count = source < me, me - 1 - source
            for begin in starts:
                if going_down:
                    cut = (begin > (me + 1) * rows) & (source * rows >= begin)
                else:
                    cut = (begin < me * rows) & ((source + 1) * rows <= begin)
                live &= ~cut
            count = jnp.maximum(count, 0)
            real = live.astype(F32)
            imag = jnp.zeros((devices, half), F32)
            for bit, (pr, pi) in enumerate(powers):
                use = (count & (1 << bit)) != 0
                pr, pi = jnp.where(use, pr, 1.0), jnp.where(use, pi, 0.0)
                real, imag = real * pr - imag * pi, real * pi + imag * pr
            imag = -imag if back else imag
            at = 2 * l + back
            table_ref[at] = jnp.zeros(table_ref.shape[1:], F32)
            for c in range(half // 128):
                table_ref[at, 0, :, c, :] = real[:, cols(c)]
                table_ref[at, 0, :, SLOT + c, :] = real[:, cols(c)]
                table_ref[at, 1, :, c, :] = -imag[:, cols(c)]
                table_ref[at, 1, :, SLOT + c, :] = imag[:, cols(c)]


def stats_kernel(tok_ref, u_ref, copy_ref, order_ref, stats_ref):
    @pl.when(pl.program_id(0) == 0)
    def _():
        size = order_ref.shape[0]
        span = size // LANES
        to = lax.broadcasted_iota(jnp.int32, (size, size), 0)
        back = lax.broadcasted_iota(jnp.int32, (size, size), 1)
        order_ref[...] = ((to % LANES) * span + to // LANES == back).astype(F32).astype(BF16)

    value = permute_in(tok_ref, order_ref, (0, u_ref.shape[0]))
    u_ref[...] = value.astype(BF16)
    copy_ref[...] = u_ref[...]
    zero_first(stats_ref)
    add_stats(stats_ref, value)
    spread_last(stats_ref)


def order_kernel(block_ref, order_ref, out_ref):
    out_ref[...] = permute_in(block_ref, order_ref, (0, out_ref.shape[0])).astype(BF16)


def restore_kernel(tile_ref, order_ref, out_ref):
    permute_out(tile_ref[...], order_ref, out_ref, (0, tile_ref.shape[0]))


def layer_sums_kernel(low_ref, pg_ref, act_ref, logit_ref, ssum_ref, wsum_ref):
    states, width = low_ref.shape[1], act_ref.shape[1]
    zero_first(wsum_ref)
    wsum_ref[:states] += lax.dot_general(
        low_ref[...], pg_ref[...], TN, preferred_element_type=F32
    )
    wsum_ref[states : states + width] += lax.dot_general(
        act_ref[...], logit_ref[...], TN, preferred_element_type=F32
    )

    @pl.when(pl.program_id(0) == pl.num_programs(0) - 1)
    def _():
        wsum_ref[states + width : states + width + 1] = ssum_ref[...]


def drive_sums_kernel(u_ref, norm_ref, dg_ref, win_ref, disc_ref, decays_ref, sums_ref):
    width, states = win_ref.shape
    half = states // 2
    zero_first(sums_ref)
    normed = (u_ref[...] - norm_ref[0:1]) * norm_ref[2:3] + norm_ref[3:4]
    sums_ref[:width] += lax.dot_general(
        normed.astype(BF16), dg_ref[...], TN, preferred_element_type=F32
    )

    @pl.when(pl.program_id(0) == pl.num_programs(0) - 1)
    def _():
        sums_ref[width : width + 1] = decays_ref[...]
        factors = factor_sums(win_ref, sums_ref.at[:width], disc_ref)
        sums_ref[width + 1 : width + 2, :half] = factors[0]
        sums_ref[width + 1 : width + 2, half:] = factors[1]


def factor_sums(win_ref, isum_ref, disc_ref):
    half = win_ref.shape[1] // 2
    wr, wi = win_ref[:, :half].astype(F32), win_ref[:, half:].astype(F32)
    gr, gi = isum_ref[:, :half], isum_ref[:, half:]
    re = jnp.sum(wr * gr + wi * gi, axis=0, keepdims=True)
    im = jnp.sum(wr * gi - wi * gr, axis=0, keepdims=True)
    gr, gi = disc_ref[1:2, :half], disc_ref[1:2, half:]
    scale = 1.0 / (gr * gr + gi * gi)
    return (re * gr - im * gi) * scale, (re * gi + im * gr) * scale


def add_stats(stats_ref, value):
    add_rows(stats_ref, column_sum(value), column_sum(value * value))


def add_rows(copies_ref, first, second):
    for c in range(first.shape[1] // 128):
        copies_ref[0, c : c + 1] += first[:, cols(c)]
        copies_ref[0, SLOT + c : SLOT + c + 1] += second[:, cols(c)]


def summed(ref):
    total = jnp.sum(ref[...], axis=0)
    return tuple(
        jnp.concatenate([total[SLOT * k + c : SLOT * k + c + 1] for c in range(SLOT)], axis=1)
        for k in range(2)
    )


def drive_kernel(layer, down, tokens, *refs):
    (
        stat_ref, u_ref, gain_ref, bias_ref, skip_ref, win_ref, disc_ref, jr_ref,
        b_ref, end_ref, blk_ref, norm_ref,
    ) = refs
    i, nt = pl.program_id(0), pl.num_programs(0)
    steps = u_ref.shape[0] // LANES
    chunks = chunk_count(b_ref)
    half = chunks * 128

    @pl.when(i == 0)
    def _():
        total, squares = summed(stat_ref)
        row = slice(layer, layer + 1)
        mean = total / tokens
        inv = lax.rsqrt(squares / tokens - mean * mean + EPSILON)
        norm_ref[0:1] = mean
        norm_ref[1:2] = inv
        norm_ref[2:3] = inv * gain_ref[row]
        norm_ref[3:4] = bias_ref[row]
        norm_ref[4:5] = skip_ref[row]
        norm_ref[5:8] = jnp.zeros((3, norm_ref.shape[1]), F32)
        blk_ref[...] = jnp.zeros_like(blk_ref)

    fr, fi = disc_ref[1:2, :half], disc_ref[1:2, half:]
    tile = nt - 1 - i if down else i
    scan = Scan(b_ref, blk_ref, disc_row(disc_ref, 0, chunks), jr_ref, tile * steps, down)

    def product(part):
        at = slice(*part)
        u = u_ref[at].astype(F32)
        normed = (u - norm_ref[0:1]) * norm_ref[2:3] + norm_ref[3:4]
        drive = jnp.dot(normed.astype(BF16), win_ref[...], preferred_element_type=F32)
        re, im = drive[:, :half], drive[:, half:]
        b_ref[at, :half] = re * fr - im * fi
        b_ref[at, half:] = re * fi + im * fr

    in_stages([product, scan.run], parts_of(b_ref.shape[0], down, 4))
    scan.close()

    @pl.when(i == nt - 1)
    def _():
        zero = [jnp.zeros((1, 128), F32)] * chunks
        cr, ci = chain(blk_ref, jr_ref, disc_row(disc_ref, 2, chunks), (zero, zero), down)
        put_copies(end_ref, cr, ci)


def states_scan(ends_ref, table_ref, b_ref, blk_ref, disc_ref, jr_ref, low_ref, st_ref, down):
    i, nt = pl.program_id(0), pl.num_programs(0)
    chunks = chunk_count(b_ref)
    steps = b_ref.shape[0] // LANES

    @pl.when(i == 0)
    def _():
        carry = carry_in(ends_ref, table_ref, chunks)
        chain(blk_ref, jr_ref, disc_row(disc_ref, 2, chunks), carry, down, st_ref)

    tile = nt - 1 - i if down else i
    scan = Scan(b_ref, st_ref, disc_row(disc_ref, 0, chunks), jr_ref, tile * steps, down)

    def stage(part):
        scan.run(part, lambda at, pair: store_pair(low_ref, at, *pair))

    return scan, stage


def gelu_parts(mixed):
    square = mixed * mixed
    tanh = jnp.tanh(mixed * (GELU_A + (GELU_A * GELU_B) * square))
    half_up = 0.5 + 0.5 * tanh
    return square, tanh, half_up


def gelu_slope(mixed, square, tanh, half_up):
    return half_up + (mixed * (0.5 - 0.5 * tanh * tanh)) * (
        GELU_A + (3.0 * GELU_A * GELU_B) * square
    )


def sigmoid(value):
    return 0.5 + 0.5 * jnp.tanh(0.5 * value)


def forward_kernel(down, *refs):
    (
        ends_ref, table_ref, b_ref, blk_ref, disc_ref, jr_ref, u_ref, norm_ref, wout_ref, wgate_ref,
        next_ref, copy_ref, low_ref, mixed_ref, gate_ref, stats_ref, st_ref,
    ) = refs
    scan, states = states_scan(
        ends_ref, table_ref, b_ref, blk_ref, disc_ref, jr_ref, low_ref, st_ref, down
    )
    zero_first(stats_ref)
    acts = {}

    def mix(part):
        at = slice(*part)
        u = u_ref[at].astype(F32)
        normed = (u - norm_ref[0:1]) * norm_ref[2:3] + norm_ref[3:4]
        mixed = jnp.dot(low_ref[at], wout_ref[...], preferred_element_type=F32)
        mixed += norm_ref[4:5] * normed
        _, _, half_up = gelu_parts(mixed)
        acts[part] = mixed * half_up
        mixed_ref[at] = mixed.astype(BF16)

    def finish(part):
        at = slice(*part)
        act = acts[part]
        gate = sigmoid(jnp.dot(act.astype(BF16), wgate_ref[...], preferred_element_type=F32))
        after = u_ref[at].astype(F32) + act * gate
        next_ref[at] = after
        copy_ref[at] = after
        gate_ref[at] = gate.astype(BF16)
        add_stats(stats_ref, after)

    in_stages([states, mix, finish], parts_of(b_ref.shape[0], down))
    scan.close()
    spread_last(stats_ref)


def zero_first(*refs):
    @pl.when(pl.program_id(0) == 0)
    def _():
        for ref in refs:
            ref[...] = jnp.zeros(ref.shape, ref.dtype)


def spread_last(ref):
    @pl.when(pl.program_id(0) == pl.num_programs(0) - 1)
    def _():
        ref[...] = jnp.broadcast_to(ref[0:1], ref.shape)


class GateBackward:
    def __init__(self, low_ref, wout_ref, wgate_ref, pg_ref, sg_ref, wsum_ref, ssum_ref, acts):
        self.low_ref, self.wout_ref, self.wgate_ref = low_ref, wout_ref, wgate_ref
        self.pg_ref, self.sg_ref = pg_ref, sg_ref
        self.wsum_ref, self.ssum_ref = wsum_ref, ssum_ref
        self.act_ref, self.logit_ref = acts
        self.kept = {}

    def enter(self, part, g, mixed, gate, normed, kept=None):
        at = slice(*part)
        square, tanh, half_up = gelu_parts(mixed) if kept is None else kept
        act = mixed * half_up
        g_gate = g * gate
        if kept is None:
            self.act_ref[at] = act.astype(BF16)
        self.logit_ref[at] = (g_gate * act * (1.0 - gate)).astype(BF16)
        self.kept[part] = (g_gate, gelu_slope(mixed, square, tanh, half_up), normed)

    def middle(self, part):
        at = slice(*part)
        g_gate, slope, normed = self.kept[part]
        act_grad = g_gate + lax.dot_general(
            self.logit_ref[at], self.wgate_ref[...], NT, preferred_element_type=F32
        )
        mixed_grad = act_grad * slope
        self.ssum_ref[...] += column_sum(mixed_grad * normed)
        self.pg_ref[at] = mixed_grad.astype(BF16)

    def leave(self, part):
        at = slice(*part)
        self.sg_ref[at] = lax.dot_general(
            self.pg_ref[at], self.wout_ref[...], NT, preferred_element_type=F32
        )

    def sums(self):
        states, width = self.wout_ref.shape
        self.wsum_ref[states : states + width] += lax.dot_general(
            self.act_ref[...], self.logit_ref[...], TN, preferred_element_type=F32
        )
        self.wsum_ref[:states] += lax.dot_general(
            self.low_ref[...], self.pg_ref[...], TN, preferred_element_type=F32
        )


def turn_kernel(down, *refs):
    (
        ends_ref, table_ref, b_ref, blk_ref, disc_ref, jr_ref, jo_ref, u_ref, norm_ref, wout_ref, wgate_ref,
        g_ref,
        out_ref, low_ref, pg_ref, sg_ref, act_ref, logit_ref, ssum_ref, end_ref, ablk_ref,
        st_ref, w_ref,
    ) = refs
    i, nt = pl.program_id(0), pl.num_programs(0)
    chunks = chunk_count(b_ref)
    half = chunks * 128
    steps = b_ref.shape[0] // LANES
    tile = nt - 1 - i if down else i
    scan, states = states_scan(
        ends_ref, table_ref, b_ref, blk_ref, disc_ref, jr_ref, low_ref, st_ref, down
    )
    back = GateBackward(
        low_ref, wout_ref, wgate_ref, pg_ref, sg_ref, None, ssum_ref, (act_ref, logit_ref)
    )

    @pl.when(i == 0)
    def _():
        ssum_ref[...] = jnp.zeros(ssum_ref.shape, F32)
        ablk_ref[...] = jnp.zeros(ablk_ref.shape, F32)
        w_ref[:, :half] = jnp.ones((LANES, half), F32)
        w_ref[:, half:] = jnp.zeros((LANES, half), F32)

    mid = {}

    def mix(part):
        at = slice(*part)
        u = u_ref[at]
        normed = (u - norm_ref[0:1]) * norm_ref[2:3] + norm_ref[3:4]
        mixed = jnp.dot(low_ref[at], wout_ref[...], preferred_element_type=F32)
        mixed += norm_ref[4:5] * normed
        kept = gelu_parts(mixed)
        act_ref[at] = (mixed * kept[2]).astype(BF16)
        mid[part] = (normed, mixed, kept)

    def enter(part):
        at = slice(*part)
        normed, mixed, kept = mid[part]
        gate = sigmoid(jnp.dot(act_ref[at], wgate_ref[...], preferred_element_type=F32))
        out_ref[at] = u_ref[at] + (mixed * kept[2]) * gate
        back.enter(part, g_ref[at].astype(F32), mixed, gate, normed, kept)

    dr, di = disc_row(disc_ref, 0, chunks, conj=True)
    dr, di = wide(dr), wide(di)
    jo = jo_ref[...]
    live = {
        "w": rows_of(w_ref, slice(0, LANES), chunks),
        "a": rows_of(ablk_ref, slice(0, LANES), chunks),
    }

    def weigh(part):
        (wr, wi), (ar, ai) = (tuple(map(list, live[k])) for k in "wa")
        order = range(part[0] // LANES, part[1] // LANES)
        for step in reversed(order) if down else order:
            sr, si = rows_of(sg_ref, slice(step * LANES, (step + 1) * LANES), chunks)
            keep = jo != tile * steps + step
            for c in range(chunks):
                ar[c] = ar[c] + (wr[c] * sr[c] - wi[c] * si[c])
                ai[c] = ai[c] + (wr[c] * si[c] + wi[c] * sr[c])
                xr = jnp.where(keep, wr[c], 0.0)
                xi = jnp.where(keep, wi[c], 0.0)
                wr[c] = xr * dr[c] - xi * di[c]
                wi[c] = xr * di[c] + xi * dr[c]
        live["w"], live["a"] = (wr, wi), (ar, ai)

    in_stages(
        [states, mix, enter, back.middle, back.leave, weigh], parts_of(b_ref.shape[0], down)
    )
    scan.close()
    put_rows(w_ref, slice(0, LANES), *live["w"])
    put_rows(ablk_ref, slice(0, LANES), *live["a"])

    @pl.when(i == nt - 1)
    def _():
        zero = [jnp.zeros((1, 128), F32)] * chunks
        power = disc_row(disc_ref, 2, chunks, conj=True)
        cr, ci = chain(ablk_ref, jo_ref, power, (zero, zero), not down)
        put_copies(end_ref, cr, ci)


def adjoint_kernel(down, last, *refs):
    (
        ends_ref, table_ref, sg_ref, ablk_ref, disc_ref, jr_ref, low_ref, u_ref, norm_ref, pg_ref, g_ref,
        win_ref, *refs
    ) = refs
    if last:
        (
            ssum_ref, res_ref, sums_ref, st_ref, dg_ref, ax_ref, low_normed_ref, nsum_ref, isum_ref,
        ) = refs
    else:
        (res_ref, dg_ref, decays_ref, nsum_ref, st_ref, ax_ref) = refs
    width, states = win_ref.shape
    i, nt = pl.program_id(0), pl.num_programs(0)
    chunks = chunk_count(sg_ref)
    half = chunks * 128
    steps = sg_ref.shape[0] // LANES
    tile = nt - 1 - i if down else i

    @pl.when(i == 0)
    def _():
        carry = carry_in(ends_ref, table_ref, chunks)
        power = disc_row(disc_ref, 2, chunks, conj=True)
        chain(ablk_ref, jr_ref, power, carry, down, st_ref)
        ax_ref[...] = jnp.zeros_like(ax_ref)

    zero_first(nsum_ref)
    if last:
        zero_first(isum_ref)
    fr, fi = disc_row(disc_ref, 1, chunks)
    fr, fi = wide(fr), wide(fi)
    decay = disc_row(disc_ref, 0, chunks, conj=True)
    scan = Scan(sg_ref, st_ref, decay, jr_ref, tile * steps, down)
    sums = tuple(map(list, rows_of(ax_ref, slice(0, LANES), chunks)))

    def emit(at, pair):
        xr, xi = rows_of(low_ref, at, chunks)
        xr, xi = [v.astype(F32) for v in xr], [v.astype(F32) for v in xi]
        grads = []
        for which, (ar, ai) in enumerate(pair):
            gr, gi = [], []
            rows = slice(which * LANES, (which + 1) * LANES)
            for c in range(chunks):
                vr, vi = xr[c][rows], xi[c][rows]
                sums[0][c] = sums[0][c] + (ar[c] * vr + ai[c] * vi)
                sums[1][c] = sums[1][c] + (ai[c] * vr - ar[c] * vi)
                gr.append(ar[c] * fr[c] + ai[c] * fi[c])
                gi.append(ai[c] * fr[c] - ar[c] * fi[c])
            grads.append((gr, gi))
        store_pair(dg_ref, at, *grads)

    def finish(part):
        at = slice(*part)
        centered = u_ref[at].astype(F32) - norm_ref[0:1]
        if last:
            low_normed_ref[at] = (centered * norm_ref[2:3] + norm_ref[3:4]).astype(BF16)
        normed_grad = lax.dot_general(dg_ref[at], win_ref[...], NT, preferred_element_type=F32)
        normed_grad += norm_ref[4:5] * pg_ref[at].astype(F32)
        add_rows(
            nsum_ref, column_sum(normed_grad), column_sum(normed_grad * centered) * norm_ref[1:2]
        )
        res_ref[at] = g_ref[at].astype(F32) + norm_ref[2:3] * normed_grad

    in_stages([lambda part: scan.run(part, emit), finish], parts_of(sg_ref.shape[0], down))
    if last:
        isum_ref[...] += lax.dot_general(
            low_normed_ref[...], dg_ref[...], TN, preferred_element_type=F32
        )
    scan.close()
    put_rows(ax_ref, slice(0, LANES), *sums)
    spread_last(nsum_ref)

    @pl.when(i == nt - 1)
    def _():
        decays = jnp.sum(ax_ref[...], axis=0, keepdims=True)
        if last:
            factors = factor_sums(win_ref, isum_ref, disc_ref)
            rows = width // BLOCKS
            first = rows + rows // 2
            for b in range(BLOCKS):
                at = b * rows
                sums_ref[b, :rows] = isum_ref[at : at + rows, :width]
                sums_ref[b, rows:first, : states - width] = isum_ref[at : at + rows // 2, width:]
                sums_ref[b, rows:first, states - width :] = isum_ref[
                    at + rows // 2 : at + rows, width:
                ]
                sums_ref[b, first:] = jnp.zeros((SMALL, width), F32)
            small = [nsum_ref[0]] + [ssum_ref[:, cols(c)] for c in range(width // 128)]
            small += [decays[:, cols(c)] for c in range(2 * chunks)]
            small += [v[:, cols(c)] for v in factors for c in range(chunks)]
            small = [v[r : r + 1] for v in small for r in range(v.shape[0])]
            for k, row in enumerate(small):
                at = (k % SMALL, k // SMALL)
                sums_ref[0, first + at[0] : first + at[0] + 1, cols(at[1])] = row
        else:
            decays_ref[...] = decays


def back_kernel(down, tokens, core, *refs):
    (
        sums_ref, r_ref, up_ref, up_norm_ref, mixed_ref, gate_ref, low_ref, u_ref, norm_ref, wout_ref,
        wgate_ref, disc_ref, jo_ref,
        g_ref, pg_ref, sg_ref, kept_ref, sent_ref, ssum_ref, end_ref, ablk_ref, nsum_ref, bsum_ref, wsum_ref,
        act_ref, logit_ref,
    ) = refs
    i, nt = pl.program_id(0), pl.num_programs(0)
    chunks = chunk_count(sg_ref)
    steps = sg_ref.shape[0] // LANES
    tile = nt - 1 - i if down else i

    @pl.when(i == 0)
    def _():
        nsum_ref[...] = jnp.sum(sums_ref[...], axis=0)
        bsum_ref[0:1], bsum_ref[1:2] = summed(sums_ref)

    zero_first(ablk_ref, wsum_ref, ssum_ref)
    back = GateBackward(
        low_ref, wout_ref, wgate_ref, pg_ref, sg_ref, wsum_ref, ssum_ref, (act_ref, logit_ref)
    )
    decay = disc_row(disc_ref, 0, chunks, conj=True)
    scan = Scan(sg_ref, ablk_ref, decay, jo_ref, tile * steps, down)
    scale = up_norm_ref[2:3] * (-1.0 / tokens)

    def enter(part):
        at = slice(*part)
        standard = (up_ref[at] - up_norm_ref[0:1]) * (scale * up_norm_ref[1:2] * bsum_ref[1:2])
        g = r_ref[at] + (standard + scale * bsum_ref[0:1])
        g_ref[at] = g
        u = u_ref[at].astype(F32)
        normed = (u - norm_ref[0:1]) * norm_ref[2:3] + norm_ref[3:4]
        back.enter(part, g, mixed_ref[at].astype(F32), gate_ref[at].astype(F32), normed)

    in_stages([enter, back.middle, back.leave, scan.run], parts_of(sg_ref.shape[0], down))
    back.sums()
    scan.close()

    @pl.when(i == nt - 1)
    def _():
        zero = [jnp.zeros((1, 128), F32)] * chunks
        power = disc_row(disc_ref, 2, chunks, conj=True)
        cr, ci = chain(ablk_ref, jo_ref, power, (zero, zero), down)
        put_copies(end_ref, cr, ci)
        states, width = wout_ref.shape
        gates, outs = width // BLOCKS, states // BLOCKS
        side = lax.axis_index(core)
        for ref, first in ((kept_ref, side), (sent_ref, 1 - side)):
            for b in range(BLOCKS // 2):
                at = first * (BLOCKS // 2) + b
                ref[b, :gates] = wsum_ref[pl.ds(pl.multiple_of(states + at * gates, 8), gates)]
                ref[b, gates:] = wsum_ref[pl.ds(pl.multiple_of(at * outs, 8), outs)]


def last_kernel(
    tokens, piece_ref, small_ref, out1_ref, gate1_ref, skip1_ref, in1_ref, decay1_ref, norm1_ref,
    disc_ref, rate_ref, step_ref, freq_ref, r_ref, tok_ref, norm_ref,
    grad_in_ref, gain_ref, bias_ref, drate_ref, dstep_ref, dfreq_ref, in_ref, out_ref, skip_ref,
    gate_ref,
):
    gates, width = gate1_ref.shape
    outs = out1_ref.shape[0]
    states = in1_ref.shape[1]
    half = states // 2
    left = states - width
    gate_ref[0], gate_ref[1] = piece_ref[:gates], gate1_ref[...]
    out_ref[0], out_ref[1] = piece_ref[gates : gates + outs], out1_ref[...]
    at = gates + outs
    in_ref[0, :, :width] = piece_ref[at : at + gates]
    at += gates
    in_ref[0, : gates // 2, width:] = piece_ref[at : at + gates // 2, :left]
    in_ref[0, gates // 2 :, width:] = piece_ref[at : at + gates // 2, left:]
    in_ref[1] = in1_ref[...]

    def row(ref, first, count):
        places = [(k % SMALL, k // SMALL) for k in range(first, first + count)]
        return jnp.concatenate([ref[r : r + 1, cols(c)] for r, c in places], axis=1)

    count = width // 128
    bias, gain = row(small_ref, 0, count), row(small_ref, count, count)
    scale = norm_ref[2:3] * (-1.0 / tokens)
    grad_in_ref[...] = r_ref[...] + (
        (tok_ref[...].astype(F32) - norm_ref[0:1]) * (scale * norm_ref[1:2] * gain) + scale * bias
    )

    @pl.when(pl.program_id(0) == 0)
    def _():
        bias_ref[0:1], gain_ref[0:1] = bias, gain
        bias_ref[1:2], gain_ref[1:2] = row(norm1_ref, 0, count), row(norm1_ref, count, count)
        skip_ref[0:1], skip_ref[1:2] = row(small_ref, 2 * count, count), skip1_ref[0:1]
        at = 3 * count
        lanes = half // 128
        for l in range(LAYERS):
            if l == 0:
                ar, ai, sr, si = (row(small_ref, at + k * lanes, lanes) for k in range(4))
            else:
                ar, ai = decay1_ref[0:1, :half], decay1_ref[0:1, half:]
                sr, si = decay1_ref[1:2, :half], decay1_ref[1:2, half:]
            dr, di = disc_ref[l, 0:1, :half], disc_ref[l, 0:1, half:]
            fr, fi = disc_ref[l, 1:2, :half], disc_ref[l, 1:2, half:]
            here = slice(l, l + 1)
            rate, freq, step = rate_ref[here], freq_ref[here], jnp.exp(step_ref[here])
            tr = ar - (fr * sr + fi * si)
            ti = ai - (fr * si - fi * sr)
            size = 1.0 / (dr * dr + di * di)
            gr, gi = (tr * dr - ti * di) * size, (tr * di + ti * dr) * size
            mr, mi = -rate * fr - freq * fi, freq * fr - rate * fi
            size = 1.0 / (rate * rate + freq * freq)
            gr += (-rate * sr - freq * si) * size
            gi += (freq * sr - rate * si) * size
            both = 2.0 * (fr * sr + fi * si)
            gx = gr * dr + gi * di
            gy = gi * dr - gr * di
            drate_ref[here] = (-mr * sr - mi * si - both * rate) * size - step * gx
            dfreq_ref[here] = (mi * sr - mr * si - both * freq) * size + step * gy
            dstep_ref[here] = step * (freq * gy - rate * gx)


def whole(array):
    shape = array.shape
    return pl.BlockSpec(shape, lambda i: (0,) * len(shape))


def tile_spec(rows, width, nt, down):
    if down:
        return pl.BlockSpec((rows, width), lambda i: (nt - 1 - i, 0))
    return pl.BlockSpec((rows, width), lambda i: (i, 0))


def run_spec(steps, width, nt, down):
    if down:
        return pl.BlockSpec((LANES, steps, width), lambda i: (0, nt - 1 - i, 0))
    return pl.BlockSpec((LANES, steps, width), lambda i: (0, i, 0))


def call(kernel, nt, args, outs, scratch, macs, name):
    arrays = [a for a, *_ in args]
    sizes = sum(a.size * a.dtype.itemsize for a in arrays + [a for a, *_ in outs])
    held = [
        a if keep is None else pltpu.with_memory_space_constraint(a, keep)
        for a, _, keep in map(filled, args)
    ]
    return pl.pallas_call(
        kernel,
        grid=(nt,),
        in_specs=[whole(a) if s is None else s for a, s, _ in map(filled, args)],
        out_specs=[whole(a) if s is None else s for a, s, _ in map(filled, outs)],
        out_shape=[
            a if keep is None else keep(a.shape, a.dtype) for a, _, keep in map(filled, outs)
        ],
        scratch_shapes=scratch,
        compiler_params=pltpu.CompilerParams(
            vmem_limit_bytes=VMEM_LIMIT, dimension_semantics=("arbitrary",)
        ),
        cost_estimate=pl.CostEstimate(flops=2 * macs, bytes_accessed=sizes, transcendentals=0),
        name=name,
    )(*held)


def filled(entry):
    return entry if len(entry) == 3 else entry + (pltpu.HBM,)


def shape(*dims, dtype=F32):
    return jax.ShapeDtypeStruct(dims, dtype)


def body(
    axes,
    tokens_in,
    seq_starts,
    norm_gain,
    norm_bias,
    decay_rate,
    step_log,
    frequency,
    in_proj,
    out_proj,
    skip_gain,
    gate_proj,
    grad_out,
):
    rows, width = tokens_in.shape
    states = in_proj.shape[-1]
    devices = 2 ** len(axes)
    tokens = float(rows * devices)
    run = rows // LANES
    steps = min(64, run)
    tile = steps * LANES
    nt = rows // tile
    span = min(32, steps)
    def tiles(array, down):
        return (array, tile_spec(tile, array.shape[-1], nt, down))

    def runs(array, down):
        return (array, run_spec(steps, array.shape[-1], nt, down))

    def full(array):
        return (array, None)

    def of(array, l):
        size = array.shape[1:]
        return (array, pl.BlockSpec((None,) + size, lambda i: (l,) + (0,) * len(size)))

    discs, tables, cuts = call(
        functools.partial(prep_kernel, rows, axes), 1,
        [full(seq_starts[None]), full(decay_rate),
         full(step_log), full(frequency)],
        [full(shape(LAYERS, 8, states)), full(shape(2 * LAYERS, 2, devices, 2 * SLOT, 128)),
         full(shape(2, LANES, 128, dtype=jnp.int32))],
        [], rows * width, "prep",
    )

    def near(entry):
        return entry[:2] + (pltpu.VMEM if rows * states * 4 <= 7 * 2**20 else pltpu.HBM,)

    tokens_run = tokens_in.reshape(LANES, run, width)
    grad_run = grad_out.reshape(LANES, run, width)
    state_scratch = pltpu.VMEM((LANES, states), F32)
    half_scratch = [pltpu.VMEM((tile, width), BF16)] * 2
    cost = rows * width * states

    u0_near, u0, order, stats = call(
        stats_kernel, nt, [runs(tokens_run, 0)],
        [near(tiles(shape(rows, width, dtype=BF16), 0)), tiles(shape(rows, width, dtype=BF16), 0),
         full(shape(span * LANES, span * LANES, dtype=BF16)),
         near(full(shape(devices, 2 * SLOT, 128)))],
        [], cost // 2, "stats",
    )
    (g1,) = call(
        order_kernel, nt, [runs(grad_run, 0), full(order)],
        [tiles(shape(rows, width, dtype=BF16), 0)], [], cost // 2, "order",
    )

    def restored(array, name):
        (out,) = call(
            restore_kernel, nt, [tiles(array, 0), full(order)],
            [runs(shape(LANES, run, width), 0)], [], cost // 2, name,
        )
        return out.reshape(rows, width)


    def drive(l, stream, stats):
        down = l % 2
        return call(
            functools.partial(drive_kernel, l, bool(down), tokens), nt,
            [near(full(gather_all(stats, axes))), near(tiles(stream, down)), full(norm_gain), full(norm_bias), full(skip_gain), of(in_proj, l), of(discs, l),
               of(cuts, down)],
            [near(tiles(shape(rows, states), down)), near(full(shape(devices, 2 * SLOT, 128))),
             full(shape(LANES, states)), full(shape(8, width))],
            [], 4 * cost, f"drive_{l}",
        )

    b0, end0, blk0, norm0 = drive(0, u0_near, stats)
    u1_near, u1, low0, mixed0, gate0, stats = call(
        functools.partial(forward_kernel, False), nt,
        [near(full(gather_all(end0, axes))), of(tables, 2 * 0 + 0), near(tiles(b0, 0)), full(blk0), of(discs, 0), of(cuts, 0),
           near(tiles(u0_near, 0)), full(norm0), of(out_proj, 0), of(gate_proj, 0)],
        [near(tiles(shape(rows, width), 0)), tiles(shape(rows, width), 0), tiles(shape(rows, states, dtype=BF16), 0),
         tiles(shape(rows, width, dtype=BF16), 0), tiles(shape(rows, width, dtype=BF16), 0),
         near(full(shape(devices, 2 * SLOT, 128)))],
        [state_scratch], 6 * cost, "forward_0",
    )

    b1, end1, blk1, norm1 = drive(1, u1_near, stats)
    out, low1, pg1, sg1, act1, logit1, skip_sum1, aend1, ablk1 = call(
        functools.partial(turn_kernel, True), nt,
        [near(full(gather_all(end1, axes))), of(tables, 2), near(tiles(b1, 1)), full(blk1),
         of(discs, 1), of(cuts, 1), of(cuts, 0), tiles(u1, 1), full(norm1), of(out_proj, 1),
         of(gate_proj, 1), tiles(g1, 1)],
        [tiles(shape(rows, width), 1), near(tiles(shape(rows, states, dtype=BF16), 1)),
         near(tiles(shape(rows, width, dtype=BF16), 1)), near(tiles(shape(rows, states), 1)),
         tiles(shape(rows, width, dtype=BF16), 1), tiles(shape(rows, width, dtype=BF16), 1),
         full(shape(1, width)), near(full(shape(devices, 2 * SLOT, 128))),
         full(shape(LANES, states))],
        [state_scratch, state_scratch], 12 * cost, "turn_1",
    )
    out = restored(out, "restore_out")
    (w_sum1,) = call(
        layer_sums_kernel, nt,
        [near(tiles(low1, 0)), near(tiles(pg1, 0)), tiles(act1, 0), tiles(logit1, 0),
         full(skip_sum1)],
        [full(shape(states + width + 8, width))], [], 3 * cost, "layer_sums",
    )

    def adjoint(l, sg, ablk, ends, low, stream, norm, pg, g, skip_sum=None):
        down = 1 - l % 2
        last = l == 0
        held = (lambda entry: entry) if last else near
        args = [
            near(full(ends)), of(tables, 2 * l + 1), held(tiles(sg, down)), full(ablk), of(discs, l),
            of(cuts, down), held(tiles(low, down)), tiles(stream, down),
            full(norm), held(tiles(pg, down)), tiles(g, down), of(in_proj, l),
        ]
        if last:
            args.append(full(skip_sum))
            outs = [
                tiles(shape(rows, width), down),
                full(shape(BLOCKS, (width + width // 2) // BLOCKS + SMALL, width)),
            ]
            scratch = [
                state_scratch, pltpu.VMEM((tile, states), BF16), state_scratch,
                pltpu.VMEM((tile, width), BF16), pltpu.VMEM((1, 2 * SLOT, 128), F32),
                pltpu.VMEM((width, states), F32),
            ]
        else:
            outs = [
                tiles(shape(rows, width), down), near(tiles(shape(rows, states, dtype=BF16), down)),
                full(shape(1, states)), near(full(shape(devices, 2 * SLOT, 128))),
            ]
            scratch = [state_scratch, state_scratch]
        return call(
            functools.partial(adjoint_kernel, bool(down), last), nt, args, outs, scratch,
            8 * cost, f"adjoint_{l}",
        )

    r1, dg1, decays1, norm_sum1 = adjoint(
        1, sg1, ablk1, gather_all(aend1, axes), low1, u1, norm1, pg1, g1
    )
    norm_parts1 = gather_all(norm_sum1, axes)
    (in_sum1,) = call(
        drive_sums_kernel, nt,
        [tiles(u1, 0), full(norm1), near(tiles(dg1, 0)), of(in_proj, 1), of(discs, 1),
         full(decays1)],
        [full(shape(width + 8, states))], [], 2 * cost, "drive_sums",
    )

    piece = (2 * width + states + width // 2) // BLOCKS + SMALL

    def lower(r1, norm_parts1):
        half = shape(BLOCKS // 2, (states + width) // BLOCKS, width)
        (
            g0, pg0, sg0, kept0, sent0, skip_sum0, aend0, ablk0, small1, _
        ) = call(
            functools.partial(back_kernel, True, tokens, axes[-1]), nt,
            [near(full(norm_parts1)), tiles(r1, 1), tiles(u1, 1), full(norm1),
             tiles(mixed0, 1), tiles(gate0, 1), tiles(low0, 1), tiles(u0, 1), full(norm0),
             of(out_proj, 0), of(gate_proj, 0), of(discs, 0), of(cuts, 1)],
            [tiles(shape(rows, width), 1), tiles(shape(rows, width, dtype=BF16), 1),
             tiles(shape(rows, states), 1), full(half), full(half), full(shape(1, width)), near(full(shape(devices, 2 * SLOT, 128))),
             full(shape(LANES, states)), full(shape(2 * SLOT, 128)), full(shape(2, width))],
            [pltpu.VMEM((states + width, width), F32)] + half_scratch, 12 * cost, "back_0",
        )
        core, chips, *others = phases(axes)
        part = kept0 + lax.ppermute(sent0, core[0], [(0, 1), (1, 0)])
        ends, part = lax.optimization_barrier((gather_all(aend0, axes), part))
        part = part.reshape(-1, width)
        part = scatter_sum(part, chips)
        r0, in_sum0 = adjoint(0, sg0, ablk0, ends, low0, u0, norm0, pg0, g0, skip_sum0)
        in_sum0, part = lax.optimization_barrier((in_sum0, part))
        in_part = scatter_sum(scatter_sum(in_sum0.reshape(-1, width), core), chips)
        pad = -piece % (8 * 2 ** len(others[0]))
        part = jnp.concatenate([part, in_part, jnp.zeros((pad, width), F32)], axis=0)
        part = sum_all(part, others)[:piece]
        pieces = gather_rows(gather_rows(part, chips), core)
        return restored(r0, "restore_in"), small1, pieces.reshape(BLOCKS, -1, width)

    def nothing(r1, norm_parts1):
        return (
            jnp.zeros((rows, width), F32),
            jnp.zeros((2 * SLOT, 128), F32),
            jnp.zeros((BLOCKS, piece, width), F32),
        )

    w_all1, in_all1 = lax.psum((w_sum1, in_sum1), axes)
    r0, norm_all1, pieces = lax.cond(seq_starts[0] == 0, lower, nothing, r1, norm_parts1)

    gates, outs = width // BLOCKS, states // BLOCKS

    def block(array, *dims, at=lambda i: (i, 0)):
        return (array, pl.BlockSpec(dims, at))

    def flat(array, count):
        return block(array, count, array.shape[1])

    (
        grad_in, gain_grad, bias_grad, rate_grad, step_grad, freq_grad, in_grad, out_grad,
        skip_grad, gate_grad,
    ) = call(
        functools.partial(last_kernel, tokens), BLOCKS,
        [block(pieces, None, piece, width, at=lambda i: (i, 0, 0)) + (None,),
         block(pieces, None, SMALL, width, at=lambda i: (0, piece // SMALL - 1, 0)) + (None,),
         flat(w_all1, outs),
         block(w_all1, gates, width, at=lambda i: (states // gates + i, 0)),
         block(w_all1, 8, width, at=lambda i: ((states + width) // 8, 0)),
         flat(in_all1, gates),
         block(in_all1, 8, states, at=lambda i: (width // 8, 0)),
         full(norm_all1), full(discs), full(decay_rate), full(step_log), full(frequency),
         flat(r0, rows // BLOCKS), flat(tokens_in, rows // BLOCKS), full(norm0)],
        [flat(shape(rows, width), rows // BLOCKS), full(shape(LAYERS, width)),
         full(shape(LAYERS, width)), full(shape(LAYERS, states // 2)),
         full(shape(LAYERS, states // 2)), full(shape(LAYERS, states // 2)),
         block(shape(LAYERS, width, states), LAYERS, gates, states, at=lambda i: (0, i, 0)),
         block(shape(LAYERS, states, width), LAYERS, outs, width, at=lambda i: (0, i, 0)),
         full(shape(LAYERS, width)),
         block(shape(LAYERS, width, width), LAYERS, gates, width, at=lambda i: (0, i, 0))],
        [], cost, "last",
    )
    return (
        out,
        grad_in,
        gain_grad,
        bias_grad,
        rate_grad,
        step_grad,
        freq_grad,
        in_grad,
        out_grad,
        skip_grad,
        gate_grad,
    )


def solution(mesh):
    bits = mesh.devices.size.bit_length() - 1
    axes = tuple("b%d" % k for k in range(bits))
    binary = Mesh(mesh.devices.reshape((2,) * bits), axes)
    rows = P(axes, None)
    return jax.shard_map(
        functools.partial(body, axes),
        mesh=binary,
        in_specs=(rows,) + (P(),) * 10 + (rows,),
        out_specs=(rows, rows) + (P(),) * 9,
        check_vma=False,
    )
```

```python
import functools

import jax
import jax.numpy as jnp
from jax import lax
from jax.experimental import pallas as pl
from jax.experimental.pallas import tpu as pltpu
from jax.sharding import Mesh, PartitionSpec as P

LAYERS = 2
EPSILON = 1e-05
SMALL = 8
BLOCKS = 8
SLOT = 4
LANES = 8
VMEM_LIMIT = 30 * 1024 * 1024
GELU_A = 0.7978845608028654
GELU_B = 0.044715
NT = (((1,), (1,)), ((), ()))
TN = (((0,), (0,)), ((), ()))
F32 = jnp.float32
BF16 = jnp.bfloat16


def gather_all(copies, axes):
    return lax.all_to_all(copies, axes, 0, 0)


def scatter_sum(value, axes):
    count = 2 ** len(axes)
    pieces = value.reshape((count, value.shape[0] // count) + value.shape[1:])
    return jnp.sum(lax.all_to_all(pieces, axes, 0, 0), axis=0)


def gather_rows(value, axes):
    count = 2 ** len(axes)
    copies = jnp.broadcast_to(value, (count,) + value.shape)
    return lax.all_to_all(copies, axes, 0, 0).reshape((count * value.shape[0],) + value.shape[1:])


def phases(axes):
    left, out = list(axes), [(axes[-1],)]
    left = left[:-1]
    while left:
        out.append(tuple(left[-2:]))
        left = left[:-2]
    return out


def sum_all(value, parts):
    for part in parts:
        value = scatter_sum(value, part)
    for part in reversed(parts):
        value = gather_rows(value, part)
    return value


def cols(c):
    return slice(c * 128, (c + 1) * 128)


def chunk_count(ref):
    return ref.shape[-1] // 256


def rows_of(ref, at, chunks):
    half = chunks * 128
    re = [ref[at, c * 128 : (c + 1) * 128] for c in range(chunks)]
    im = [ref[at, half + c * 128 : half + (c + 1) * 128] for c in range(chunks)]
    return re, im


def put_rows(ref, at, re, im):
    chunks = len(re)
    half = chunks * 128
    for c in range(chunks):
        ref[at, c * 128 : (c + 1) * 128] = re[c]
        ref[at, half + c * 128 : half + (c + 1) * 128] = im[c]


def put_copies(ref, re, im):
    ref[0] = jnp.zeros(ref.shape[1:], F32)
    for c in range(len(re)):
        ref[0, c : c + 1] = re[c]
        ref[0, SLOT + c : SLOT + c + 1] = im[c]
    ref[...] = jnp.broadcast_to(ref[0:1], ref.shape)


def wide(rows):
    return [jnp.broadcast_to(v, (LANES, 128)) for v in rows]


def chain(ends_ref, jr_ref, power, carry, down, start_ref=None):
    chunks = len(power[0])
    pr, pi = power
    cr, ci = carry
    order = range(LANES - 1, -1, -1) if down else range(LANES)
    for s in order:
        at = slice(s, s + 1)
        if start_ref is not None:
            put_rows(start_ref, at, cr, ci)
        er, ei = rows_of(ends_ref, at, chunks)
        alive = (jr_ref[at, :] < 0).astype(F32)
        cr, ci = (
            [er[c] + alive * (pr[c] * cr[c] - pi[c] * ci[c]) for c in range(chunks)],
            [ei[c] + alive * (pr[c] * ci[c] + pi[c] * cr[c]) for c in range(chunks)],
        )
    return cr, ci


def carry_in(ends_ref, table_ref, chunks):
    total = jnp.zeros((2 * SLOT, 128), F32)
    for e in range(ends_ref.shape[0]):
        end = ends_ref[e]
        turned = jnp.concatenate([end[SLOT:], end[:SLOT]], axis=0)
        total += table_ref[0, e] * end + table_ref[1, e] * turned
    return (
        [total[c : c + 1] for c in range(chunks)],
        [total[SLOT + c : SLOT + c + 1] for c in range(chunks)],
    )


def in_stages(stages, parts):
    for turn in range(len(parts) + len(stages) - 1):
        for k, stage in enumerate(stages):
            if 0 <= turn - k < len(parts):
                stage(parts[turn - k])


def parts_of(rows, down, count=2):
    size = rows // count
    parts = [(at, at + size) for at in range(0, rows, size)]
    return parts[::-1] if down else parts


class Scan:
    def __init__(self, src_ref, st_ref, decay, jr_ref, first_step, down):
        self.src_ref, self.st_ref, self.down = src_ref, st_ref, down
        self.chunks = chunk_count(src_ref)
        self.dr, self.di = wide(decay[0]), wide(decay[1])
        self.jr, self.first_step = jr_ref[...], first_step
        self.state = rows_of(st_ref, slice(0, LANES), self.chunks)

    def one(self, step):
        br, bi = rows_of(self.src_ref, slice(step * LANES, (step + 1) * LANES), self.chunks)
        live = self.jr != self.first_step + step
        nr, ni = [], []
        for c in range(self.chunks):
            xr = jnp.where(live, self.state[0][c], 0.0)
            xi = jnp.where(live, self.state[1][c], 0.0)
            nr.append(self.dr[c] * xr - self.di[c] * xi + br[c])
            ni.append(self.dr[c] * xi + self.di[c] * xr + bi[c])
        self.state = (nr, ni)
        return nr, ni

    def run(self, part, emit=None):
        low, high = part[0] // LANES, part[1] // LANES
        for n in range(0, high - low, 2):
            step = high - 2 - n if self.down else low + n
            first = self.one(step + 1 if self.down else step)
            second = self.one(step if self.down else step + 1)
            if emit is not None:
                pair = (second, first) if self.down else (first, second)
                emit(slice(step * LANES, (step + 2) * LANES), pair)

    def close(self):
        put_rows(self.st_ref, slice(0, LANES), *self.state)


def store_pair(ref, at, first, second):
    re = [jnp.concatenate([p, q], axis=0).astype(BF16) for p, q in zip(first[0], second[0])]
    im = [jnp.concatenate([p, q], axis=0).astype(BF16) for p, q in zip(first[1], second[1])]
    put_rows(ref, at, re, im)


def disc_row(disc_ref, row, chunks, conj=False):
    re, im = rows_of(disc_ref, slice(row, row + 1), chunks)
    return (re, [-v for v in im]) if conj else (re, im)


def column_sum(value):
    rows, width = value.shape
    return jnp.sum(jnp.sum(value.reshape(rows // 8, 8, width), axis=0), axis=0, keepdims=True)


def permute_in(block_ref, order_ref, part):
    runs, _, width = block_ref.shape
    size = order_ref.shape[0]
    span = size // runs
    out = []
    for k in range(part[0] // size, part[1] // size):
        rows = block_ref[:, k * span : (k + 1) * span, :].reshape(size, width)
        out.append(jnp.dot(order_ref[...], rows, preferred_element_type=F32))
    return out[0] if len(out) == 1 else jnp.concatenate(out, axis=0)


def permute_out(value, order_ref, out_ref, part):
    width = value.shape[1]
    size = order_ref.shape[0]
    span = size // LANES
    high = value.astype(BF16)
    low = (value - high.astype(F32)).astype(BF16)
    for n, k in enumerate(range(part[0] // size, part[1] // size)):
        at = slice(n * size, (n + 1) * size)
        back = lax.dot_general(order_ref[...], high[at], TN, preferred_element_type=F32)
        back += lax.dot_general(order_ref[...], low[at], TN, preferred_element_type=F32)
        out_ref[:, k * span : (k + 1) * span, :] = back.reshape(LANES, span, width)


def expm1(value):
    acc = jnp.full_like(value, 1.0 / 479001600.0)
    for n in (39916800.0, 3628800.0, 362880.0, 40320.0, 5040.0, 720.0, 120.0, 24.0, 6.0, 2.0, 1.0):
        acc = acc * value + 1.0 / n
    return jnp.where(value > -1.0, acc * value, jnp.exp(value) - 1.0)


def prep_kernel(
    rows, axes, starts_ref, rate_ref, step_ref, freq_ref,
    disc_ref, table_ref, cut_ref,
):
    devices = 2 ** len(axes)
    total = rows * devices
    run = rows // LANES
    half = rate_ref.shape[-1]
    me = 0
    for axis in axes:
        me = 2 * me + lax.axis_index(axis)
    starts = [starts_ref[:, k : k + 1] for k in range(starts_ref.shape[1])]

    base = me * rows + run * lax.broadcasted_iota(jnp.int32, (LANES, 128), 0)
    up = jnp.full((LANES, 128), -1, jnp.int32)
    down = up
    for begin in starts + [total]:
        rel = begin - base
        up = jnp.maximum(up, jnp.where((rel >= 0) & (rel < run), rel, -1))
        down = jnp.maximum(down, jnp.where((rel >= 1) & (rel <= run), rel - 1, -1))
    cut_ref[0] = up
    cut_ref[1] = down

    source = lax.broadcasted_iota(jnp.int32, (devices, half), 0)
    for l in range(LAYERS):
        row = slice(l, l + 1)
        rate, freq = rate_ref[row], freq_ref[row]
        step_size = jnp.exp(step_ref[row])
        real_angle = -rate * step_size
        imag_angle = freq * step_size
        magnitude = jnp.exp(real_angle)
        cosine, sine = jnp.cos(imag_angle), jnp.sin(imag_angle)
        minus_real = expm1(real_angle) * cosine - 2.0 * jnp.sin(0.5 * imag_angle) ** 2
        minus_imag = magnitude * sine
        modulus = rate * rate + freq * freq
        disc_ref[l, 0:1, :half] = magnitude * cosine
        disc_ref[l, 0:1, half:] = minus_imag
        disc_ref[l, 1:2, :half] = (-rate * minus_real + freq * minus_imag) / modulus
        disc_ref[l, 1:2, half:] = (-rate * minus_imag - freq * minus_real) / modulus
        magnitude = jnp.exp(real_angle * float(run))
        disc_ref[l, 2:3, :half] = magnitude * jnp.cos(imag_angle * float(run))
        disc_ref[l, 2:3, half:] = magnitude * jnp.sin(imag_angle * float(run))
        disc_ref[l, 3:8] = jnp.zeros((5, 2 * half), F32)
        powers = []
        for bit in range(len(axes)):
            magnitude = jnp.exp(real_angle * float(rows << bit))
            angle = imag_angle * float(rows << bit)
            powers.append((magnitude * jnp.cos(angle), magnitude * jnp.sin(angle)))
        for back in range(2):
            going_down = (l + back) % 2 == 1
            if going_down:
                live, count = source > me, source - me - 1
            else:
                live, count = source < me, me - 1 - source
            for begin in starts:
                if going_down:
                    cut = (begin > (me + 1) * rows) & (source * rows >= begin)
                else:
                    cut = (begin < me * rows) & ((source + 1) * rows <= begin)
                live &= ~cut
            count = jnp.maximum(count, 0)
            real = live.astype(F32)
            imag = jnp.zeros((devices, half), F32)
            for bit, (pr, pi) in enumerate(powers):
                use = (count & (1 << bit)) != 0
                pr, pi = jnp.where(use, pr, 1.0), jnp.where(use, pi, 0.0)
                real, imag = real * pr - imag * pi, real * pi + imag * pr
            imag = -imag if back else imag
            at = 2 * l + back
            table_ref[at] = jnp.zeros(table_ref.shape[1:], F32)
            for c in range(half // 128):
                table_ref[at, 0, :, c, :] = real[:, cols(c)]
                table_ref[at, 0, :, SLOT + c, :] = real[:, cols(c)]
                table_ref[at, 1, :, c, :] = -imag[:, cols(c)]
                table_ref[at, 1, :, SLOT + c, :] = imag[:, cols(c)]


def stats_kernel(tok_ref, u_ref, copy_ref, order_ref, stats_ref):
    @pl.when(pl.program_id(0) == 0)
    def _():
        size = order_ref.shape[0]
        span = size // LANES
        to = lax.broadcasted_iota(jnp.int32, (size, size), 0)
        back = lax.broadcasted_iota(jnp.int32, (size, size), 1)
        order_ref[...] = ((to % LANES) * span + to // LANES == back).astype(F32).astype(BF16)

    value = permute_in(tok_ref, order_ref, (0, u_ref.shape[0]))
    u_ref[...] = value.astype(BF16)
    copy_ref[...] = u_ref[...]
    zero_first(stats_ref)
    add_stats(stats_ref, value)
    spread_last(stats_ref)


def order_kernel(block_ref, order_ref, out_ref):
    out_ref[...] = permute_in(block_ref, order_ref, (0, out_ref.shape[0])).astype(BF16)


def restore_kernel(tile_ref, order_ref, out_ref):
    permute_out(tile_ref[...], order_ref, out_ref, (0, tile_ref.shape[0]))


def layer_sums_kernel(low_ref, pg_ref, act_ref, logit_ref, ssum_ref, wsum_ref):
    states, width = low_ref.shape[1], act_ref.shape[1]
    zero_first(wsum_ref)
    wsum_ref[:states] += lax.dot_general(
        low_ref[...], pg_ref[...], TN, preferred_element_type=F32
    )
    wsum_ref[states : states + width] += lax.dot_general(
        act_ref[...], logit_ref[...], TN, preferred_element_type=F32
    )

    @pl.when(pl.program_id(0) == pl.num_programs(0) - 1)
    def _():
        wsum_ref[states + width : states + width + 1] = ssum_ref[...]


def drive_sums_kernel(u_ref, norm_ref, dg_ref, win_ref, disc_ref, decays_ref, sums_ref):
    width, states = win_ref.shape
    half = states // 2
    zero_first(sums_ref)
    normed = (u_ref[...] - norm_ref[0:1]) * norm_ref[2:3] + norm_ref[3:4]
    sums_ref[:width] += lax.dot_general(
        normed.astype(BF16), dg_ref[...], TN, preferred_element_type=F32
    )

    @pl.when(pl.program_id(0) == pl.num_programs(0) - 1)
    def _():
        sums_ref[width : width + 1] = decays_ref[...]
        factors = factor_sums(win_ref, sums_ref.at[:width], disc_ref)
        sums_ref[width + 1 : width + 2, :half] = factors[0]
        sums_ref[width + 1 : width + 2, half:] = factors[1]


def factor_sums(win_ref, isum_ref, disc_ref):
    half = win_ref.shape[1] // 2
    wr, wi = win_ref[:, :half].astype(F32), win_ref[:, half:].astype(F32)
    gr, gi = isum_ref[:, :half], isum_ref[:, half:]
    re = jnp.sum(wr * gr + wi * gi, axis=0, keepdims=True)
    im = jnp.sum(wr * gi - wi * gr, axis=0, keepdims=True)
    gr, gi = disc_ref[1:2, :half], disc_ref[1:2, half:]
    scale = 1.0 / (gr * gr + gi * gi)
    return (re * gr - im * gi) * scale, (re * gi + im * gr) * scale


def add_stats(stats_ref, value):
    add_rows(stats_ref, column_sum(value), column_sum(value * value))


def add_rows(copies_ref, first, second):
    for c in range(first.shape[1] // 128):
        copies_ref[0, c : c + 1] += first[:, cols(c)]
        copies_ref[0, SLOT + c : SLOT + c + 1] += second[:, cols(c)]


def summed(ref):
    total = jnp.sum(ref[...], axis=0)
    return tuple(
        jnp.concatenate([total[SLOT * k + c : SLOT * k + c + 1] for c in range(SLOT)], axis=1)
        for k in range(2)
    )


def drive_kernel(layer, down, tokens, *refs):
    (
        stat_ref, u_ref, gain_ref, bias_ref, skip_ref, win_ref, disc_ref, jr_ref,
        b_ref, end_ref, blk_ref, norm_ref,
    ) = refs
    i, nt = pl.program_id(0), pl.num_programs(0)
    steps = u_ref.shape[0] // LANES
    chunks = chunk_count(b_ref)
    half = chunks * 128

    @pl.when(i == 0)
    def _():
        total, squares = summed(stat_ref)
        row = slice(layer, layer + 1)
        mean = total / tokens
        inv = lax.rsqrt(squares / tokens - mean * mean + EPSILON)
        norm_ref[0:1] = mean
        norm_ref[1:2] = inv
        norm_ref[2:3] = inv * gain_ref[row]
        norm_ref[3:4] = bias_ref[row]
        norm_ref[4:5] = skip_ref[row]
        norm_ref[5:8] = jnp.zeros((3, norm_ref.shape[1]), F32)
        blk_ref[...] = jnp.zeros_like(blk_ref)

    fr, fi = disc_ref[1:2, :half], disc_ref[1:2, half:]
    tile = nt - 1 - i if down else i
    scan = Scan(b_ref, blk_ref, disc_row(disc_ref, 0, chunks), jr_ref, tile * steps, down)

    def product(part):
        at = slice(*part)
        u = u_ref[at].astype(F32)
        normed = (u - norm_ref[0:1]) * norm_ref[2:3] + norm_ref[3:4]
        drive = jnp.dot(normed.astype(BF16), win_ref[...], preferred_element_type=F32)
        re, im = drive[:, :half], drive[:, half:]
        b_ref[at, :half] = re * fr - im * fi
        b_ref[at, half:] = re * fi + im * fr

    in_stages([product, scan.run], parts_of(b_ref.shape[0], down, 4))
    scan.close()

    @pl.when(i == nt - 1)
    def _():
        zero = [jnp.zeros((1, 128), F32)] * chunks
        cr, ci = chain(blk_ref, jr_ref, disc_row(disc_ref, 2, chunks), (zero, zero), down)
        put_copies(end_ref, cr, ci)


def states_scan(ends_ref, table_ref, b_ref, blk_ref, disc_ref, jr_ref, low_ref, st_ref, down):
    i, nt = pl.program_id(0), pl.num_programs(0)
    chunks = chunk_count(b_ref)
    steps = b_ref.shape[0] // LANES

    @pl.when(i == 0)
    def _():
        carry = carry_in(ends_ref, table_ref, chunks)
        chain(blk_ref, jr_ref, disc_row(disc_ref, 2, chunks), carry, down, st_ref)

    tile = nt - 1 - i if down else i
    scan = Scan(b_ref, st_ref, disc_row(disc_ref, 0, chunks), jr_ref, tile * steps, down)

    def stage(part):
        scan.run(part, lambda at, pair: store_pair(low_ref, at, *pair))

    return scan, stage


def gelu_parts(mixed):
    square = mixed * mixed
    tanh = jnp.tanh(mixed * (GELU_A + (GELU_A * GELU_B) * square))
    half_up = 0.5 + 0.5 * tanh
    return square, tanh, half_up


def gelu_slope(mixed, square, tanh, half_up):
    return half_up + (mixed * (0.5 - 0.5 * tanh * tanh)) * (
        GELU_A + (3.0 * GELU_A * GELU_B) * square
    )


def sigmoid(value):
    return 0.5 + 0.5 * jnp.tanh(0.5 * value)


def forward_kernel(down, *refs):
    (
        ends_ref, table_ref, b_ref, blk_ref, disc_ref, jr_ref, u_ref, norm_ref, wout_ref, wgate_ref,
        next_ref, copy_ref, low_ref, mixed_ref, gate_ref, stats_ref, st_ref,
    ) = refs
    scan, states = states_scan(
        ends_ref, table_ref, b_ref, blk_ref, disc_ref, jr_ref, low_ref, st_ref, down
    )
    zero_first(stats_ref)
    acts = {}

    def mix(part):
        at = slice(*part)
        u = u_ref[at].astype(F32)
        normed = (u - norm_ref[0:1]) * norm_ref[2:3] + norm_ref[3:4]
        mixed = jnp.dot(low_ref[at], wout_ref[...], preferred_element_type=F32)
        mixed += norm_ref[4:5] * normed
        _, _, half_up = gelu_parts(mixed)
        acts[part] = mixed * half_up
        mixed_ref[at] = mixed.astype(BF16)

    def finish(part):
        at = slice(*part)
        act = acts[part]
        gate = sigmoid(jnp.dot(act.astype(BF16), wgate_ref[...], preferred_element_type=F32))
        after = u_ref[at].astype(F32) + act * gate
        next_ref[at] = after
        copy_ref[at] = after
        gate_ref[at] = gate.astype(BF16)
        add_stats(stats_ref, after)

    in_stages([states, mix, finish], parts_of(b_ref.shape[0], down))
    scan.close()
    spread_last(stats_ref)


def zero_first(*refs):
    @pl.when(pl.program_id(0) == 0)
    def _():
        for ref in refs:
            ref[...] = jnp.zeros(ref.shape, ref.dtype)


def spread_last(ref):
    @pl.when(pl.program_id(0) == pl.num_programs(0) - 1)
    def _():
        ref[...] = jnp.broadcast_to(ref[0:1], ref.shape)


class GateBackward:
    def __init__(self, low_ref, wout_ref, wgate_ref, pg_ref, sg_ref, wsum_ref, ssum_ref, acts):
        self.low_ref, self.wout_ref, self.wgate_ref = low_ref, wout_ref, wgate_ref
        self.pg_ref, self.sg_ref = pg_ref, sg_ref
        self.wsum_ref, self.ssum_ref = wsum_ref, ssum_ref
        self.act_ref, self.logit_ref = acts
        self.kept = {}

    def enter(self, part, g, mixed, gate, normed, kept=None):
        at = slice(*part)
        square, tanh, half_up = gelu_parts(mixed) if kept is None else kept
        act = mixed * half_up
        g_gate = g * gate
        if kept is None:
            self.act_ref[at] = act.astype(BF16)
        self.logit_ref[at] = (g_gate * act * (1.0 - gate)).astype(BF16)
        self.kept[part] = (g_gate, gelu_slope(mixed, square, tanh, half_up), normed)

    def middle(self, part):
        at = slice(*part)
        g_gate, slope, normed = self.kept[part]
        act_grad = g_gate + lax.dot_general(
            self.logit_ref[at], self.wgate_ref[...], NT, preferred_element_type=F32
        )
        mixed_grad = act_grad * slope
        self.ssum_ref[...] += column_sum(mixed_grad * normed)
        self.pg_ref[at] = mixed_grad.astype(BF16)

    def leave(self, part):
        at = slice(*part)
        self.sg_ref[at] = lax.dot_general(
            self.pg_ref[at], self.wout_ref[...], NT, preferred_element_type=F32
        )

    def sums(self):
        states, width = self.wout_ref.shape
        self.wsum_ref[states : states + width] += lax.dot_general(
            self.act_ref[...], self.logit_ref[...], TN, preferred_element_type=F32
        )
        self.wsum_ref[:states] += lax.dot_general(
            self.low_ref[...], self.pg_ref[...], TN, preferred_element_type=F32
        )


def turn_kernel(down, *refs):
    (
        ends_ref, table_ref, b_ref, blk_ref, disc_ref, jr_ref, jo_ref, u_ref, norm_ref, wout_ref, wgate_ref,
        g_ref,
        out_ref, low_ref, pg_ref, sg_ref, act_ref, logit_ref, ssum_ref, end_ref, ablk_ref,
        st_ref, w_ref,
    ) = refs
    i, nt = pl.program_id(0), pl.num_programs(0)
    chunks = chunk_count(b_ref)
    half = chunks * 128
    steps = b_ref.shape[0] // LANES
    tile = nt - 1 - i if down else i
    scan, states = states_scan(
        ends_ref, table_ref, b_ref, blk_ref, disc_ref, jr_ref, low_ref, st_ref, down
    )
    back = GateBackward(
        low_ref, wout_ref, wgate_ref, pg_ref, sg_ref, None, ssum_ref, (act_ref, logit_ref)
    )

    @pl.when(i == 0)
    def _():
        ssum_ref[...] = jnp.zeros(ssum_ref.shape, F32)
        ablk_ref[...] = jnp.zeros(ablk_ref.shape, F32)
        w_ref[:, :half] = jnp.ones((LANES, half), F32)
        w_ref[:, half:] = jnp.zeros((LANES, half), F32)

    mid = {}

    def mix(part):
        at = slice(*part)
        u = u_ref[at]
        normed = (u - norm_ref[0:1]) * norm_ref[2:3] + norm_ref[3:4]
        mixed = jnp.dot(low_ref[at], wout_ref[...], preferred_element_type=F32)
        mixed += norm_ref[4:5] * normed
        kept = gelu_parts(mixed)
        act_ref[at] = (mixed * kept[2]).astype(BF16)
        mid[part] = (normed, mixed, kept)

    def enter(part):
        at = slice(*part)
        normed, mixed, kept = mid[part]
        gate = sigmoid(jnp.dot(act_ref[at], wgate_ref[...], preferred_element_type=F32))
        out_ref[at] = u_ref[at] + (mixed * kept[2]) * gate
        back.enter(part, g_ref[at].astype(F32), mixed, gate, normed, kept)

    dr, di = disc_row(disc_ref, 0, chunks, conj=True)
    dr, di = wide(dr), wide(di)
    jo = jo_ref[...]
    live = {
        "w": rows_of(w_ref, slice(0, LANES), chunks),
        "a": rows_of(ablk_ref, slice(0, LANES), chunks),
    }

    def weigh(part):
        (wr, wi), (ar, ai) = (tuple(map(list, live[k])) for k in "wa")
        order = range(part[0] // LANES, part[1] // LANES)
        for step in reversed(order) if down else order:
            sr, si = rows_of(sg_ref, slice(step * LANES, (step + 1) * LANES), chunks)
            keep = jo != tile * steps + step
            for c in range(chunks):
                ar[c] = ar[c] + (wr[c] * sr[c] - wi[c] * si[c])
                ai[c] = ai[c] + (wr[c] * si[c] + wi[c] * sr[c])
                xr = jnp.where(keep, wr[c], 0.0)
                xi = jnp.where(keep, wi[c], 0.0)
                wr[c] = xr * dr[c] - xi * di[c]
                wi[c] = xr * di[c] + xi * dr[c]
        live["w"], live["a"] = (wr, wi), (ar, ai)

    in_stages(
        [states, mix, enter, back.middle, back.leave, weigh], parts_of(b_ref.shape[0], down)
    )
    scan.close()
    put_rows(w_ref, slice(0, LANES), *live["w"])
    put_rows(ablk_ref, slice(0, LANES), *live["a"])

    @pl.when(i == nt - 1)
    def _():
        zero = [jnp.zeros((1, 128), F32)] * chunks
        power = disc_row(disc_ref, 2, chunks, conj=True)
        cr, ci = chain(ablk_ref, jo_ref, power, (zero, zero), not down)
        put_copies(end_ref, cr, ci)


def adjoint_kernel(down, last, *refs):
    (
        ends_ref, table_ref, sg_ref, ablk_ref, disc_ref, jr_ref, low_ref, u_ref, norm_ref, pg_ref, g_ref,
        win_ref, *refs
    ) = refs
    if last:
        (
            ssum_ref, res_ref, sums_ref, st_ref, dg_ref, ax_ref, low_normed_ref, nsum_ref, isum_ref,
        ) = refs
    else:
        (res_ref, dg_ref, decays_ref, nsum_ref, st_ref, ax_ref) = refs
    width, states = win_ref.shape
    i, nt = pl.program_id(0), pl.num_programs(0)
    chunks = chunk_count(sg_ref)
    half = chunks * 128
    steps = sg_ref.shape[0] // LANES
    tile = nt - 1 - i if down else i

    @pl.when(i == 0)
    def _():
        carry = carry_in(ends_ref, table_ref, chunks)
        power = disc_row(disc_ref, 2, chunks, conj=True)
        chain(ablk_ref, jr_ref, power, carry, down, st_ref)
        ax_ref[...] = jnp.zeros_like(ax_ref)

    zero_first(nsum_ref)
    if last:
        zero_first(isum_ref)
    fr, fi = disc_row(disc_ref, 1, chunks)
    fr, fi = wide(fr), wide(fi)
    decay = disc_row(disc_ref, 0, chunks, conj=True)
    scan = Scan(sg_ref, st_ref, decay, jr_ref, tile * steps, down)
    sums = tuple(map(list, rows_of(ax_ref, slice(0, LANES), chunks)))

    def emit(at, pair):
        xr, xi = rows_of(low_ref, at, chunks)
        xr, xi = [v.astype(F32) for v in xr], [v.astype(F32) for v in xi]
        grads = []
        for which, (ar, ai) in enumerate(pair):
            gr, gi = [], []
            rows = slice(which * LANES, (which + 1) * LANES)
            for c in range(chunks):
                vr, vi = xr[c][rows], xi[c][rows]
                sums[0][c] = sums[0][c] + (ar[c] * vr + ai[c] * vi)
                sums[1][c] = sums[1][c] + (ai[c] * vr - ar[c] * vi)
                gr.append(ar[c] * fr[c] + ai[c] * fi[c])
                gi.append(ai[c] * fr[c] - ar[c] * fi[c])
            grads.append((gr, gi))
        store_pair(dg_ref, at, *grads)

    def finish(part):
        at = slice(*part)
        centered = u_ref[at].astype(F32) - norm_ref[0:1]
        if last:
            low_normed_ref[at] = (centered * norm_ref[2:3] + norm_ref[3:4]).astype(BF16)
        normed_grad = lax.dot_general(dg_ref[at], win_ref[...], NT, preferred_element_type=F32)
        normed_grad += norm_ref[4:5] * pg_ref[at].astype(F32)
        add_rows(
            nsum_ref, column_sum(normed_grad), column_sum(normed_grad * centered) * norm_ref[1:2]
        )
        res_ref[at] = g_ref[at].astype(F32) + norm_ref[2:3] * normed_grad

    in_stages([lambda part: scan.run(part, emit), finish], parts_of(sg_ref.shape[0], down))
    if last:
        isum_ref[...] += lax.dot_general(
            low_normed_ref[...], dg_ref[...], TN, preferred_element_type=F32
        )
    scan.close()
    put_rows(ax_ref, slice(0, LANES), *sums)
    spread_last(nsum_ref)

    @pl.when(i == nt - 1)
    def _():
        decays = jnp.sum(ax_ref[...], axis=0, keepdims=True)
        if last:
            factors = factor_sums(win_ref, isum_ref, disc_ref)
            rows = width // BLOCKS
            first = rows + rows // 2
            for b in range(BLOCKS):
                at = b * rows
                sums_ref[b, :rows] = isum_ref[at : at + rows, :width]
                sums_ref[b, rows:first, : states - width] = isum_ref[at : at + rows // 2, width:]
                sums_ref[b, rows:first, states - width :] = isum_ref[
                    at + rows // 2 : at + rows, width:
                ]
                sums_ref[b, first:] = jnp.zeros((SMALL, width), F32)
            small = [nsum_ref[0]] + [ssum_ref[:, cols(c)] for c in range(width // 128)]
            small += [decays[:, cols(c)] for c in range(2 * chunks)]
            small += [v[:, cols(c)] for v in factors for c in range(chunks)]
            small = [v[r : r + 1] for v in small for r in range(v.shape[0])]
            for k, row in enumerate(small):
                at = (k % SMALL, k // SMALL)
                sums_ref[0, first + at[0] : first + at[0] + 1, cols(at[1])] = row
        else:
            decays_ref[...] = decays


def back_kernel(down, tokens, core, *refs):
    (
        sums_ref, r_ref, up_ref, up_norm_ref, mixed_ref, gate_ref, low_ref, u_ref, norm_ref, wout_ref,
        wgate_ref, disc_ref, jo_ref,
        g_ref, pg_ref, sg_ref, kept_ref, sent_ref, ssum_ref, end_ref, ablk_ref, nsum_ref, bsum_ref, wsum_ref,
        act_ref, logit_ref,
    ) = refs
    i, nt = pl.program_id(0), pl.num_programs(0)
    chunks = chunk_count(sg_ref)
    steps = sg_ref.shape[0] // LANES
    tile = nt - 1 - i if down else i

    @pl.when(i == 0)
    def _():
        nsum_ref[...] = jnp.sum(sums_ref[...], axis=0)
        bsum_ref[0:1], bsum_ref[1:2] = summed(sums_ref)

    zero_first(ablk_ref, wsum_ref, ssum_ref)
    back = GateBackward(
        low_ref, wout_ref, wgate_ref, pg_ref, sg_ref, wsum_ref, ssum_ref, (act_ref, logit_ref)
    )
    decay = disc_row(disc_ref, 0, chunks, conj=True)
    scan = Scan(sg_ref, ablk_ref, decay, jo_ref, tile * steps, down)
    scale = up_norm_ref[2:3] * (-1.0 / tokens)

    def enter(part):
        at = slice(*part)
        standard = (up_ref[at] - up_norm_ref[0:1]) * (scale * up_norm_ref[1:2] * bsum_ref[1:2])
        g = r_ref[at] + (standard + scale * bsum_ref[0:1])
        g_ref[at] = g
        u = u_ref[at].astype(F32)
        normed = (u - norm_ref[0:1]) * norm_ref[2:3] + norm_ref[3:4]
        back.enter(part, g, mixed_ref[at].astype(F32), gate_ref[at].astype(F32), normed)

    in_stages([enter, back.middle, back.leave, scan.run], parts_of(sg_ref.shape[0], down))
    back.sums()
    scan.close()

    @pl.when(i == nt - 1)
    def _():
        zero = [jnp.zeros((1, 128), F32)] * chunks
        power = disc_row(disc_ref, 2, chunks, conj=True)
        cr, ci = chain(ablk_ref, jo_ref, power, (zero, zero), down)
        put_copies(end_ref, cr, ci)
        states, width = wout_ref.shape
        gates, outs = width // BLOCKS, states // BLOCKS
        side = lax.axis_index(core)
        for ref, first in ((kept_ref, side), (sent_ref, 1 - side)):
            for b in range(BLOCKS // 2):
                at = first * (BLOCKS // 2) + b
                ref[b, :gates] = wsum_ref[pl.ds(pl.multiple_of(states + at * gates, 8), gates)]
                ref[b, gates:] = wsum_ref[pl.ds(pl.multiple_of(at * outs, 8), outs)]


def last_kernel(
    tokens, piece_ref, small_ref, out1_ref, gate1_ref, skip1_ref, in1_ref, decay1_ref, norm1_ref,
    disc_ref, rate_ref, step_ref, freq_ref, r_ref, tok_ref, norm_ref,
    grad_in_ref, gain_ref, bias_ref, drate_ref, dstep_ref, dfreq_ref, in_ref, out_ref, skip_ref,
    gate_ref,
):
    gates, width = gate1_ref.shape
    outs = out1_ref.shape[0]
    states = in1_ref.shape[1]
    half = states // 2
    left = states - width
    gate_ref[0], gate_ref[1] = piece_ref[:gates], gate1_ref[...]
    out_ref[0], out_ref[1] = piece_ref[gates : gates + outs], out1_ref[...]
    at = gates + outs
    in_ref[0, :, :width] = piece_ref[at : at + gates]
    at += gates
    in_ref[0, : gates // 2, width:] = piece_ref[at : at + gates // 2, :left]
    in_ref[0, gates // 2 :, width:] = piece_ref[at : at + gates // 2, left:]
    in_ref[1] = in1_ref[...]

    def row(ref, first, count):
        places = [(k % SMALL, k // SMALL) for k in range(first, first + count)]
        return jnp.concatenate([ref[r : r + 1, cols(c)] for r, c in places], axis=1)

    count = width // 128
    bias, gain = row(small_ref, 0, count), row(small_ref, count, count)
    scale = norm_ref[2:3] * (-1.0 / tokens)
    grad_in_ref[...] = r_ref[...] + (
        (tok_ref[...].astype(F32) - norm_ref[0:1]) * (scale * norm_ref[1:2] * gain) + scale * bias
    )

    @pl.when(pl.program_id(0) == 0)
    def _():
        bias_ref[0:1], gain_ref[0:1] = bias, gain
        bias_ref[1:2], gain_ref[1:2] = row(norm1_ref, 0, count), row(norm1_ref, count, count)
        skip_ref[0:1], skip_ref[1:2] = row(small_ref, 2 * count, count), skip1_ref[0:1]
        at = 3 * count
        lanes = half // 128
        for l in range(LAYERS):
            if l == 0:
                ar, ai, sr, si = (row(small_ref, at + k * lanes, lanes) for k in range(4))
            else:
                ar, ai = decay1_ref[0:1, :half], decay1_ref[0:1, half:]
                sr, si = decay1_ref[1:2, :half], decay1_ref[1:2, half:]
            dr, di = disc_ref[l, 0:1, :half], disc_ref[l, 0:1, half:]
            fr, fi = disc_ref[l, 1:2, :half], disc_ref[l, 1:2, half:]
            here = slice(l, l + 1)
            rate, freq, step = rate_ref[here], freq_ref[here], jnp.exp(step_ref[here])
            tr = ar - (fr * sr + fi * si)
            ti = ai - (fr * si - fi * sr)
            size = 1.0 / (dr * dr + di * di)
            gr, gi = (tr * dr - ti * di) * size, (tr * di + ti * dr) * size
            mr, mi = -rate * fr - freq * fi, freq * fr - rate * fi
            size = 1.0 / (rate * rate + freq * freq)
            gr += (-rate * sr - freq * si) * size
            gi += (freq * sr - rate * si) * size
            both = 2.0 * (fr * sr + fi * si)
            gx = gr * dr + gi * di
            gy = gi * dr - gr * di
            drate_ref[here] = (-mr * sr - mi * si - both * rate) * size - step * gx
            dfreq_ref[here] = (mi * sr - mr * si - both * freq) * size + step * gy
            dstep_ref[here] = step * (freq * gy - rate * gx)


def whole(array):
    shape = array.shape
    return pl.BlockSpec(shape, lambda i: (0,) * len(shape))


def tile_spec(rows, width, nt, down):
    if down:
        return pl.BlockSpec((rows, width), lambda i: (nt - 1 - i, 0))
    return pl.BlockSpec((rows, width), lambda i: (i, 0))


def run_spec(steps, width, nt, down):
    if down:
        return pl.BlockSpec((LANES, steps, width), lambda i: (0, nt - 1 - i, 0))
    return pl.BlockSpec((LANES, steps, width), lambda i: (0, i, 0))


def call(kernel, nt, args, outs, scratch, macs, name):
    arrays = [a for a, *_ in args]
    sizes = sum(a.size * a.dtype.itemsize for a in arrays + [a for a, *_ in outs])
    held = [
        a if keep is None else pltpu.with_memory_space_constraint(a, keep)
        for a, _, keep in map(filled, args)
    ]
    return pl.pallas_call(
        kernel,
        grid=(nt,),
        in_specs=[whole(a) if s is None else s for a, s, _ in map(filled, args)],
        out_specs=[whole(a) if s is None else s for a, s, _ in map(filled, outs)],
        out_shape=[
            a if keep is None else keep(a.shape, a.dtype) for a, _, keep in map(filled, outs)
        ],
        scratch_shapes=scratch,
        compiler_params=pltpu.CompilerParams(
            vmem_limit_bytes=VMEM_LIMIT, dimension_semantics=("arbitrary",)
        ),
        cost_estimate=pl.CostEstimate(flops=2 * macs, bytes_accessed=sizes, transcendentals=0),
        name=name,
    )(*held)


def filled(entry):
    return entry if len(entry) == 3 else entry + (pltpu.HBM,)


def shape(*dims, dtype=F32):
    return jax.ShapeDtypeStruct(dims, dtype)


def body(
    axes,
    tokens_in,
    seq_starts,
    norm_gain,
    norm_bias,
    decay_rate,
    step_log,
    frequency,
    in_proj,
    out_proj,
    skip_gain,
    gate_proj,
    grad_out,
):
    rows, width = tokens_in.shape
    states = in_proj.shape[-1]
    devices = 2 ** len(axes)
    tokens = float(rows * devices)
    run = rows // LANES
    steps = min(64, run)
    tile = steps * LANES
    nt = rows // tile
    span = min(32, steps)
    def tiles(array, down):
        return (array, tile_spec(tile, array.shape[-1], nt, down))

    def runs(array, down):
        return (array, run_spec(steps, array.shape[-1], nt, down))

    def full(array):
        return (array, None)

    def of(array, l):
        size = array.shape[1:]
        return (array, pl.BlockSpec((None,) + size, lambda i: (l,) + (0,) * len(size)))

    discs, tables, cuts = call(
        functools.partial(prep_kernel, rows, axes), 1,
        [full(seq_starts[None]), full(decay_rate),
         full(step_log), full(frequency)],
        [full(shape(LAYERS, 8, states)), full(shape(2 * LAYERS, 2, devices, 2 * SLOT, 128)),
         full(shape(2, LANES, 128, dtype=jnp.int32))],
        [], rows * width, "prep",
    )

    def near(entry):
        return entry[:2] + (pltpu.VMEM if rows * states * 4 <= 7 * 2**20 else pltpu.HBM,)

    tokens_run = tokens_in.reshape(LANES, run, width)
    grad_run = grad_out.reshape(LANES, run, width)
    state_scratch = pltpu.VMEM((LANES, states), F32)
    half_scratch = [pltpu.VMEM((tile, width), BF16)] * 2
    cost = rows * width * states

    u0_near, u0, order, stats = call(
        stats_kernel, nt, [runs(tokens_run, 0)],
        [near(tiles(shape(rows, width, dtype=BF16), 0)), tiles(shape(rows, width, dtype=BF16), 0),
         full(shape(span * LANES, span * LANES, dtype=BF16)),
         near(full(shape(devices, 2 * SLOT, 128)))],
        [], cost // 2, "stats",
    )
    (g1,) = call(
        order_kernel, nt, [runs(grad_run, 0), full(order)],
        [tiles(shape(rows, width, dtype=BF16), 0)], [], cost // 2, "order",
    )

    def restored(array, name):
        (out,) = call(
            restore_kernel, nt, [tiles(array, 0), full(order)],
            [runs(shape(LANES, run, width), 0)], [], cost // 2, name,
        )
        return out.reshape(rows, width)


    def drive(l, stream, stats):
        down = l % 2
        return call(
            functools.partial(drive_kernel, l, bool(down), tokens), nt,
            [near(full(stats)), near(tiles(stream, down)), full(norm_gain), full(norm_bias), full(skip_gain), of(in_proj, l), of(discs, l),
               of(cuts, down)],
            [near(tiles(shape(rows, states), down)), near(full(shape(devices, 2 * SLOT, 128))),
             full(shape(LANES, states)), full(shape(8, width))],
            [], 4 * cost, f"drive_{l}",
        )

    stats, g1 = lax.optimization_barrier((gather_all(stats, axes), g1))
    b0, end0, blk0, norm0 = drive(0, u0_near, stats)
    u1_near, u1, low0, mixed0, gate0, stats = call(
        functools.partial(forward_kernel, False), nt,
        [near(full(gather_all(end0, axes))), of(tables, 2 * 0 + 0), near(tiles(b0, 0)), full(blk0), of(discs, 0), of(cuts, 0),
           near(tiles(u0_near, 0)), full(norm0), of(out_proj, 0), of(gate_proj, 0)],
        [near(tiles(shape(rows, width), 0)), tiles(shape(rows, width), 0), tiles(shape(rows, states, dtype=BF16), 0),
         tiles(shape(rows, width, dtype=BF16), 0), tiles(shape(rows, width, dtype=BF16), 0),
         near(full(shape(devices, 2 * SLOT, 128)))],
        [state_scratch], 6 * cost, "forward_0",
    )

    b1, end1, blk1, norm1 = drive(1, u1_near, gather_all(stats, axes))
    out, low1, pg1, sg1, act1, logit1, skip_sum1, aend1, ablk1 = call(
        functools.partial(turn_kernel, True), nt,
        [near(full(gather_all(end1, axes))), of(tables, 2), near(tiles(b1, 1)), full(blk1),
         of(discs, 1), of(cuts, 1), of(cuts, 0), tiles(u1, 1), full(norm1), of(out_proj, 1),
         of(gate_proj, 1), tiles(g1, 1)],
        [tiles(shape(rows, width), 1), tiles(shape(rows, states, dtype=BF16), 1),
         tiles(shape(rows, width, dtype=BF16), 1), tiles(shape(rows, states), 1),
         tiles(shape(rows, width, dtype=BF16), 1), tiles(shape(rows, width, dtype=BF16), 1),
         full(shape(1, width)), near(full(shape(devices, 2 * SLOT, 128))),
         full(shape(LANES, states))],
        [state_scratch, state_scratch], 12 * cost, "turn_1",
    )
    (w_sum1,) = call(
        layer_sums_kernel, nt,
        [tiles(low1, 0), tiles(pg1, 0), tiles(act1, 0), tiles(logit1, 0),
         full(skip_sum1)],
        [full(shape(states + width + 8, width))], [], 3 * cost, "layer_sums",
    )

    def adjoint(l, sg, ablk, ends, low, stream, norm, pg, g, skip_sum=None):
        down = 1 - l % 2
        last = l == 0
        args = [
            near(full(ends)), of(tables, 2 * l + 1), tiles(sg, down), full(ablk), of(discs, l),
            of(cuts, down), tiles(low, down), tiles(stream, down),
            full(norm), tiles(pg, down), tiles(g, down), of(in_proj, l),
        ]
        if last:
            args.append(full(skip_sum))
            outs = [
                tiles(shape(rows, width), down),
                full(shape(BLOCKS, (width + width // 2) // BLOCKS + SMALL, width)),
            ]
            scratch = [
                state_scratch, pltpu.VMEM((tile, states), BF16), state_scratch,
                pltpu.VMEM((tile, width), BF16), pltpu.VMEM((1, 2 * SLOT, 128), F32),
                pltpu.VMEM((width, states), F32),
            ]
        else:
            outs = [
                tiles(shape(rows, width), down), tiles(shape(rows, states, dtype=BF16), down),
                full(shape(1, states)), near(full(shape(devices, 2 * SLOT, 128))),
            ]
            scratch = [state_scratch, state_scratch]
        return call(
            functools.partial(adjoint_kernel, bool(down), last), nt, args, outs, scratch,
            8 * cost, f"adjoint_{l}",
        )

    r1, dg1, decays1, norm_sum1 = adjoint(
        1, sg1, ablk1, gather_all(aend1, axes), low1, u1, norm1, pg1, g1
    )
    norm_parts1 = gather_all(norm_sum1, axes)
    (in_sum1,) = call(
        drive_sums_kernel, nt,
        [tiles(u1, 0), full(norm1), tiles(dg1, 0), of(in_proj, 1), of(discs, 1),
         full(decays1)],
        [full(shape(width + 8, states))], [], 2 * cost, "drive_sums",
    )

    piece = (2 * width + states + width // 2) // BLOCKS + SMALL

    def lower(r1, norm_parts1, out):
        half = shape(BLOCKS // 2, (states + width) // BLOCKS, width)
        (
            g0, pg0, sg0, kept0, sent0, skip_sum0, aend0, ablk0, small1, _
        ) = call(
            functools.partial(back_kernel, True, tokens, axes[-1]), nt,
            [near(full(norm_parts1)), tiles(r1, 1), tiles(u1, 1), full(norm1),
             tiles(mixed0, 1), tiles(gate0, 1), tiles(low0, 1), tiles(u0, 1), full(norm0),
             of(out_proj, 0), of(gate_proj, 0), of(discs, 0), of(cuts, 1)],
            [tiles(shape(rows, width), 1), tiles(shape(rows, width, dtype=BF16), 1),
             tiles(shape(rows, states), 1), full(half), full(half), full(shape(1, width)), near(full(shape(devices, 2 * SLOT, 128))),
             full(shape(LANES, states)), full(shape(2 * SLOT, 128)), full(shape(2, width))],
            [pltpu.VMEM((states + width, width), F32)] + half_scratch, 12 * cost, "back_0",
        )
        core, chips, *others = phases(axes)
        part = kept0 + lax.ppermute(sent0, core[0], [(0, 1), (1, 0)])
        ends, part = lax.optimization_barrier((gather_all(aend0, axes), part))
        part = part.reshape(-1, width)
        part = scatter_sum(part, chips)
        r0, in_sum0 = adjoint(0, sg0, ablk0, ends, low0, u0, norm0, pg0, g0, skip_sum0)
        in_sum0, part = lax.optimization_barrier((in_sum0, part))
        in_part = scatter_sum(scatter_sum(in_sum0.reshape(-1, width), core), chips)
        pad = -piece % (8 * 2 ** len(others[0]))
        part = jnp.concatenate([part, in_part, jnp.zeros((pad, width), F32)], axis=0)
        part = sum_all(part, others)[:piece]
        pieces = gather_rows(gather_rows(part, chips), core)
        return restored(out, "restore_out"), restored(r0, "restore_in"), small1, pieces.reshape(BLOCKS, -1, width)

    def nothing(r1, norm_parts1, out):
        return (
            jnp.zeros((rows, width), F32),
            jnp.zeros((rows, width), F32),
            jnp.zeros((2 * SLOT, 128), F32),
            jnp.zeros((BLOCKS, piece, width), F32),
        )

    w_all1, in_all1 = lax.psum((w_sum1, in_sum1), axes)
    out, r0, norm_all1, pieces = lax.cond(
        seq_starts[0] == 0, lower, nothing, r1, norm_parts1, out
    )

    gates, outs = width // BLOCKS, states // BLOCKS

    def block(array, *dims, at=lambda i: (i, 0)):
        return (array, pl.BlockSpec(dims, at))

    def flat(array, count):
        return block(array, count, array.shape[1])

    (
        grad_in, gain_grad, bias_grad, rate_grad, step_grad, freq_grad, in_grad, out_grad,
        skip_grad, gate_grad,
    ) = call(
        functools.partial(last_kernel, tokens), BLOCKS,
        [block(pieces, None, piece, width, at=lambda i: (i, 0, 0)) + (None,),
         block(pieces, None, SMALL, width, at=lambda i: (0, piece // SMALL - 1, 0)) + (None,),
         flat(w_all1, outs),
         block(w_all1, gates, width, at=lambda i: (states // gates + i, 0)),
         block(w_all1, 8, width, at=lambda i: ((states + width) // 8, 0)),
         flat(in_all1, gates),
         block(in_all1, 8, states, at=lambda i: (width // 8, 0)),
         full(norm_all1), full(discs), full(decay_rate), full(step_log), full(frequency),
         flat(r0, rows // BLOCKS), flat(tokens_in, rows // BLOCKS), full(norm0)],
        [flat(shape(rows, width), rows // BLOCKS), full(shape(LAYERS, width)),
         full(shape(LAYERS, width)), full(shape(LAYERS, states // 2)),
         full(shape(LAYERS, states // 2)), full(shape(LAYERS, states // 2)),
         block(shape(LAYERS, width, states), LAYERS, gates, states, at=lambda i: (0, i, 0)),
         block(shape(LAYERS, states, width), LAYERS, outs, width, at=lambda i: (0, i, 0)),
         full(shape(LAYERS, width)),
         block(shape(LAYERS, width, width), LAYERS, gates, width, at=lambda i: (0, i, 0))],
        [], cost, "last",
    )
    return (
        out,
        grad_in,
        gain_grad,
        bias_grad,
        rate_grad,
        step_grad,
        freq_grad,
        in_grad,
        out_grad,
        skip_grad,
        gate_grad,
    )


def solution(mesh):
    bits = mesh.devices.size.bit_length() - 1
    axes = tuple("b%d" % k for k in range(bits))
    binary = Mesh(mesh.devices.reshape((2,) * bits), axes)
    rows = P(axes, None)
    return jax.shard_map(
        functools.partial(body, axes),
        mesh=binary,
        in_specs=(rows,) + (P(),) * 10 + (rows,),
        out_specs=(rows, rows) + (P(),) * 9,
        check_vma=False,
    )
```

```python
import functools

import jax
import jax.numpy as jnp
from jax import lax
from jax.experimental import pallas as pl
from jax.experimental.pallas import tpu as pltpu
from jax.sharding import Mesh, PartitionSpec as P

LAYERS = 2
EPSILON = 1e-05
SMALL = 8
BLOCKS = 8
SLOT = 4
LANES = 8
VMEM_LIMIT = 30 * 1024 * 1024
GELU_A = 0.7978845608028654
GELU_B = 0.044715
NT = (((1,), (1,)), ((), ()))
TN = (((0,), (0,)), ((), ()))
F32 = jnp.float32
BF16 = jnp.bfloat16


def gather_all(copies, axes):
    return lax.all_to_all(copies, axes, 0, 0)


def scatter_sum(value, axes):
    count = 2 ** len(axes)
    pieces = value.reshape((count, value.shape[0] // count) + value.shape[1:])
    return jnp.sum(lax.all_to_all(pieces, axes, 0, 0), axis=0)


def gather_rows(value, axes):
    count = 2 ** len(axes)
    copies = jnp.broadcast_to(value, (count,) + value.shape)
    return lax.all_to_all(copies, axes, 0, 0).reshape((count * value.shape[0],) + value.shape[1:])


def phases(axes):
    left, out = list(axes), [(axes[-1],)]
    left = left[:-1]
    while left:
        out.append(tuple(left[-2:]))
        left = left[:-2]
    return out


def place_in(axes):
    place = 0
    for axis in axes:
        place = 2 * place + lax.axis_index(axis)
    return place


def traded(value, axes, mask):
    count = 2 ** len(axes)
    return lax.ppermute(value, axes, [(i, i ^ mask) for i in range(count)])


def line_scatter(value, axes):
    count = 2 ** len(axes)
    me = place_in(axes)
    pieces = value.reshape((count, value.shape[0] // count) + value.shape[1:])

    def piece(mask):
        return lax.dynamic_index_in_dim(pieces, me ^ mask, 0, keepdims=False)

    got = [traded(piece(mask), axes, mask) for mask in range(1, count)]
    return functools.reduce(jnp.add, got, piece(0))


def line_gather(value, axes):
    count = 2 ** len(axes)
    me = place_in(axes)
    got = [traded(value, axes, mask) for mask in range(1, count)]
    rows = []
    for j in range(count):
        row = value
        for mask in range(1, count):
            row = jnp.where(me == j ^ mask, got[mask - 1], row)
        rows.append(row)
    return jnp.concatenate(rows, axis=0)


def sum_all(value, parts):
    for part in parts:
        value = scatter_sum(value, part)
    for part in reversed(parts):
        value = gather_rows(value, part)
    return value


def cols(c):
    return slice(c * 128, (c + 1) * 128)


def chunk_count(ref):
    return ref.shape[-1] // 256


def rows_of(ref, at, chunks):
    half = chunks * 128
    re = [ref[at, c * 128 : (c + 1) * 128] for c in range(chunks)]
    im = [ref[at, half + c * 128 : half + (c + 1) * 128] for c in range(chunks)]
    return re, im


def put_rows(ref, at, re, im):
    chunks = len(re)
    half = chunks * 128
    for c in range(chunks):
        ref[at, c * 128 : (c + 1) * 128] = re[c]
        ref[at, half + c * 128 : half + (c + 1) * 128] = im[c]


def put_copies(ref, re, im):
    ref[0] = jnp.zeros(ref.shape[1:], F32)
    for c in range(len(re)):
        ref[0, c : c + 1] = re[c]
        ref[0, SLOT + c : SLOT + c + 1] = im[c]
    ref[...] = jnp.broadcast_to(ref[0:1], ref.shape)


def wide(rows):
    return [jnp.broadcast_to(v, (LANES, 128)) for v in rows]


def chain(ends_ref, jr_ref, power, carry, down, start_ref=None):
    chunks = len(power[0])
    pr, pi = power
    cr, ci = carry
    order = range(LANES - 1, -1, -1) if down else range(LANES)
    for s in order:
        at = slice(s, s + 1)
        if start_ref is not None:
            put_rows(start_ref, at, cr, ci)
        er, ei = rows_of(ends_ref, at, chunks)
        alive = (jr_ref[at, :] < 0).astype(F32)
        cr, ci = (
            [er[c] + alive * (pr[c] * cr[c] - pi[c] * ci[c]) for c in range(chunks)],
            [ei[c] + alive * (pr[c] * ci[c] + pi[c] * cr[c]) for c in range(chunks)],
        )
    return cr, ci


def carry_in(ends_ref, table_ref, chunks):
    total = jnp.zeros((2 * SLOT, 128), F32)
    for e in range(ends_ref.shape[0]):
        end = ends_ref[e]
        turned = jnp.concatenate([end[SLOT:], end[:SLOT]], axis=0)
        total += table_ref[0, e] * end + table_ref[1, e] * turned
    return (
        [total[c : c + 1] for c in range(chunks)],
        [total[SLOT + c : SLOT + c + 1] for c in range(chunks)],
    )


def in_stages(stages, parts):
    for turn in range(len(parts) + len(stages) - 1):
        for k, stage in enumerate(stages):
            if 0 <= turn - k < len(parts):
                stage(parts[turn - k])


def parts_of(rows, down, count=2):
    size = rows // count
    parts = [(at, at + size) for at in range(0, rows, size)]
    return parts[::-1] if down else parts


class Scan:
    def __init__(self, src_ref, st_ref, decay, jr_ref, first_step, down):
        self.src_ref, self.st_ref, self.down = src_ref, st_ref, down
        self.chunks = chunk_count(src_ref)
        self.dr, self.di = wide(decay[0]), wide(decay[1])
        self.jr, self.first_step = jr_ref[...], first_step
        self.state = rows_of(st_ref, slice(0, LANES), self.chunks)

    def one(self, step):
        br, bi = rows_of(self.src_ref, slice(step * LANES, (step + 1) * LANES), self.chunks)
        live = self.jr != self.first_step + step
        nr, ni = [], []
        for c in range(self.chunks):
            xr = jnp.where(live, self.state[0][c], 0.0)
            xi = jnp.where(live, self.state[1][c], 0.0)
            nr.append(self.dr[c] * xr - self.di[c] * xi + br[c])
            ni.append(self.dr[c] * xi + self.di[c] * xr + bi[c])
        self.state = (nr, ni)
        return nr, ni

    def run(self, part, emit=None):
        low, high = part[0] // LANES, part[1] // LANES
        for n in range(0, high - low, 2):
            step = high - 2 - n if self.down else low + n
            first = self.one(step + 1 if self.down else step)
            second = self.one(step if self.down else step + 1)
            if emit is not None:
                pair = (second, first) if self.down else (first, second)
                emit(slice(step * LANES, (step + 2) * LANES), pair)

    def close(self):
        put_rows(self.st_ref, slice(0, LANES), *self.state)


def store_pair(ref, at, first, second):
    re = [jnp.concatenate([p, q], axis=0).astype(BF16) for p, q in zip(first[0], second[0])]
    im = [jnp.concatenate([p, q], axis=0).astype(BF16) for p, q in zip(first[1], second[1])]
    put_rows(ref, at, re, im)


def disc_row(disc_ref, row, chunks, conj=False):
    re, im = rows_of(disc_ref, slice(row, row + 1), chunks)
    return (re, [-v for v in im]) if conj else (re, im)


def column_sum(value):
    rows, width = value.shape
    return jnp.sum(jnp.sum(value.reshape(rows // 8, 8, width), axis=0), axis=0, keepdims=True)


def permute_in(block_ref, order_ref, part):
    runs, _, width = block_ref.shape
    size = order_ref.shape[0]
    span = size // runs
    out = []
    for k in range(part[0] // size, part[1] // size):
        rows = block_ref[:, k * span : (k + 1) * span, :].reshape(size, width)
        out.append(jnp.dot(order_ref[...], rows, preferred_element_type=F32))
    return out[0] if len(out) == 1 else jnp.concatenate(out, axis=0)


def permute_out(value, order_ref, out_ref, part):
    width = value.shape[1]
    size = order_ref.shape[0]
    span = size // LANES
    high = value.astype(BF16)
    low = (value - high.astype(F32)).astype(BF16)
    for n, k in enumerate(range(part[0] // size, part[1] // size)):
        at = slice(n * size, (n + 1) * size)
        back = lax.dot_general(order_ref[...], high[at], TN, preferred_element_type=F32)
        back += lax.dot_general(order_ref[...], low[at], TN, preferred_element_type=F32)
        out_ref[:, k * span : (k + 1) * span, :] = back.reshape(LANES, span, width)


def expm1(value):
    acc = jnp.full_like(value, 1.0 / 479001600.0)
    for n in (39916800.0, 3628800.0, 362880.0, 40320.0, 5040.0, 720.0, 120.0, 24.0, 6.0, 2.0, 1.0):
        acc = acc * value + 1.0 / n
    return jnp.where(value > -1.0, acc * value, jnp.exp(value) - 1.0)


def prep_kernel(
    rows, axes, starts_ref, rate_ref, step_ref, freq_ref,
    disc_ref, table_ref, cut_ref,
):
    devices = 2 ** len(axes)
    total = rows * devices
    run = rows // LANES
    half = rate_ref.shape[-1]
    me = 0
    for axis in axes:
        me = 2 * me + lax.axis_index(axis)
    starts = [starts_ref[:, k : k + 1] for k in range(starts_ref.shape[1])]

    base = me * rows + run * lax.broadcasted_iota(jnp.int32, (LANES, 128), 0)
    up = jnp.full((LANES, 128), -1, jnp.int32)
    down = up
    for begin in starts + [total]:
        rel = begin - base
        up = jnp.maximum(up, jnp.where((rel >= 0) & (rel < run), rel, -1))
        down = jnp.maximum(down, jnp.where((rel >= 1) & (rel <= run), rel - 1, -1))
    cut_ref[0] = up
    cut_ref[1] = down

    source = lax.broadcasted_iota(jnp.int32, (devices, half), 0)
    for l in range(LAYERS):
        row = slice(l, l + 1)
        rate, freq = rate_ref[row], freq_ref[row]
        step_size = jnp.exp(step_ref[row])
        real_angle = -rate * step_size
        imag_angle = freq * step_size
        magnitude = jnp.exp(real_angle)
        cosine, sine = jnp.cos(imag_angle), jnp.sin(imag_angle)
        minus_real = expm1(real_angle) * cosine - 2.0 * jnp.sin(0.5 * imag_angle) ** 2
        minus_imag = magnitude * sine
        modulus = rate * rate + freq * freq
        disc_ref[l, 0:1, :half] = magnitude * cosine
        disc_ref[l, 0:1, half:] = minus_imag
        disc_ref[l, 1:2, :half] = (-rate * minus_real + freq * minus_imag) / modulus
        disc_ref[l, 1:2, half:] = (-rate * minus_imag - freq * minus_real) / modulus
        magnitude = jnp.exp(real_angle * float(run))
        disc_ref[l, 2:3, :half] = magnitude * jnp.cos(imag_angle * float(run))
        disc_ref[l, 2:3, half:] = magnitude * jnp.sin(imag_angle * float(run))
        disc_ref[l, 3:8] = jnp.zeros((5, 2 * half), F32)
        powers = []
        for bit in range(len(axes)):
            magnitude = jnp.exp(real_angle * float(rows << bit))
            angle = imag_angle * float(rows << bit)
            powers.append((magnitude * jnp.cos(angle), magnitude * jnp.sin(angle)))
        for back in range(2):
            going_down = (l + back) % 2 == 1
            if going_down:
                live, count = source > me, source - me - 1
            else:
                live, count = source < me, me - 1 - source
            for begin in starts:
                if going_down:
                    cut = (begin > (me + 1) * rows) & (source * rows >= begin)
                else:
                    cut = (begin < me * rows) & ((source + 1) * rows <= begin)
                live &= ~cut
            count = jnp.maximum(count, 0)
            real = live.astype(F32)
            imag = jnp.zeros((devices, half), F32)
            for bit, (pr, pi) in enumerate(powers):
                use = (count & (1 << bit)) != 0
                pr, pi = jnp.where(use, pr, 1.0), jnp.where(use, pi, 0.0)
                real, imag = real * pr - imag * pi, real * pi + imag * pr
            imag = -imag if back else imag
            at = 2 * l + back
            table_ref[at] = jnp.zeros(table_ref.shape[1:], F32)
            for c in range(half // 128):
                table_ref[at, 0, :, c, :] = real[:, cols(c)]
                table_ref[at, 0, :, SLOT + c, :] = real[:, cols(c)]
                table_ref[at, 1, :, c, :] = -imag[:, cols(c)]
                table_ref[at, 1, :, SLOT + c, :] = imag[:, cols(c)]


def stats_kernel(tok_ref, u_ref, copy_ref, order_ref, stats_ref):
    @pl.when(pl.program_id(0) == 0)
    def _():
        size = order_ref.shape[0]
        span = size // LANES
        to = lax.broadcasted_iota(jnp.int32, (size, size), 0)
        back = lax.broadcasted_iota(jnp.int32, (size, size), 1)
        order_ref[...] = ((to % LANES) * span + to // LANES == back).astype(F32).astype(BF16)

    value = permute_in(tok_ref, order_ref, (0, u_ref.shape[0]))
    u_ref[...] = value.astype(BF16)
    copy_ref[...] = u_ref[...]
    zero_first(stats_ref)
    add_stats(stats_ref, value)
    spread_last(stats_ref)


def order_kernel(block_ref, order_ref, out_ref):
    out_ref[...] = permute_in(block_ref, order_ref, (0, out_ref.shape[0])).astype(BF16)


def restore_kernel(tile_ref, order_ref, out_ref):
    permute_out(tile_ref[...], order_ref, out_ref, (0, tile_ref.shape[0]))


def layer_sums_kernel(low_ref, pg_ref, act_ref, logit_ref, ssum_ref, wsum_ref):
    states, width = low_ref.shape[1], act_ref.shape[1]
    zero_first(wsum_ref)
    wsum_ref[:states] += lax.dot_general(
        low_ref[...], pg_ref[...], TN, preferred_element_type=F32
    )
    wsum_ref[states : states + width] += lax.dot_general(
        act_ref[...], logit_ref[...], TN, preferred_element_type=F32
    )

    @pl.when(pl.program_id(0) == pl.num_programs(0) - 1)
    def _():
        wsum_ref[states + width : states + width + 1] = ssum_ref[...]


def factor_sums(win_ref, isum_ref, disc_ref):
    half = win_ref.shape[1] // 2
    wr, wi = win_ref[:, :half].astype(F32), win_ref[:, half:].astype(F32)
    gr, gi = isum_ref[:, :half], isum_ref[:, half:]
    re = jnp.sum(wr * gr + wi * gi, axis=0, keepdims=True)
    im = jnp.sum(wr * gi - wi * gr, axis=0, keepdims=True)
    gr, gi = disc_ref[1:2, :half], disc_ref[1:2, half:]
    scale = 1.0 / (gr * gr + gi * gi)
    return (re * gr - im * gi) * scale, (re * gi + im * gr) * scale


def add_stats(stats_ref, value):
    add_rows(stats_ref, column_sum(value), column_sum(value * value))


def add_rows(copies_ref, first, second):
    for c in range(first.shape[1] // 128):
        copies_ref[0, c : c + 1] += first[:, cols(c)]
        copies_ref[0, SLOT + c : SLOT + c + 1] += second[:, cols(c)]


def summed(ref):
    total = jnp.sum(ref[...], axis=0)
    return tuple(
        jnp.concatenate([total[SLOT * k + c : SLOT * k + c + 1] for c in range(SLOT)], axis=1)
        for k in range(2)
    )


def drive_kernel(layer, down, tokens, *refs):
    (
        stat_ref, u_ref, gain_ref, bias_ref, skip_ref, win_ref, disc_ref, jr_ref,
        b_ref, end_ref, blk_ref, norm_ref,
    ) = refs
    i, nt = pl.program_id(0), pl.num_programs(0)
    steps = u_ref.shape[0] // LANES
    chunks = chunk_count(b_ref)
    half = chunks * 128

    @pl.when(i == 0)
    def _():
        total, squares = summed(stat_ref)
        row = slice(layer, layer + 1)
        mean = total / tokens
        inv = lax.rsqrt(squares / tokens - mean * mean + EPSILON)
        norm_ref[0:1] = mean
        norm_ref[1:2] = inv
        norm_ref[2:3] = inv * gain_ref[row]
        norm_ref[3:4] = bias_ref[row]
        norm_ref[4:5] = skip_ref[row]
        norm_ref[5:8] = jnp.zeros((3, norm_ref.shape[1]), F32)
        blk_ref[...] = jnp.zeros_like(blk_ref)

    fr, fi = disc_ref[1:2, :half], disc_ref[1:2, half:]
    tile = nt - 1 - i if down else i
    scan = Scan(b_ref, blk_ref, disc_row(disc_ref, 0, chunks), jr_ref, tile * steps, down)

    def product(part):
        at = slice(*part)
        u = u_ref[at].astype(F32)
        normed = (u - norm_ref[0:1]) * norm_ref[2:3] + norm_ref[3:4]
        drive = jnp.dot(normed.astype(BF16), win_ref[...], preferred_element_type=F32)
        re, im = drive[:, :half], drive[:, half:]
        b_ref[at, :half] = re * fr - im * fi
        b_ref[at, half:] = re * fi + im * fr

    in_stages([product, scan.run], parts_of(b_ref.shape[0], down, 4))
    scan.close()

    @pl.when(i == nt - 1)
    def _():
        zero = [jnp.zeros((1, 128), F32)] * chunks
        cr, ci = chain(blk_ref, jr_ref, disc_row(disc_ref, 2, chunks), (zero, zero), down)
        put_copies(end_ref, cr, ci)


def states_scan(ends_ref, table_ref, b_ref, blk_ref, disc_ref, jr_ref, low_ref, st_ref, down):
    i, nt = pl.program_id(0), pl.num_programs(0)
    chunks = chunk_count(b_ref)
    steps = b_ref.shape[0] // LANES

    @pl.when(i == 0)
    def _():
        carry = carry_in(ends_ref, table_ref, chunks)
        chain(blk_ref, jr_ref, disc_row(disc_ref, 2, chunks), carry, down, st_ref)

    tile = nt - 1 - i if down else i
    scan = Scan(b_ref, st_ref, disc_row(disc_ref, 0, chunks), jr_ref, tile * steps, down)

    def stage(part):
        scan.run(part, lambda at, pair: store_pair(low_ref, at, *pair))

    return scan, stage


def gelu_parts(mixed):
    square = mixed * mixed
    tanh = jnp.tanh(mixed * (GELU_A + (GELU_A * GELU_B) * square))
    half_up = 0.5 + 0.5 * tanh
    return square, tanh, half_up


def gelu_slope(mixed, square, tanh, half_up):
    return half_up + (mixed * (0.5 - 0.5 * tanh * tanh)) * (
        GELU_A + (3.0 * GELU_A * GELU_B) * square
    )


def sigmoid(value):
    return 0.5 + 0.5 * jnp.tanh(0.5 * value)


def forward_kernel(down, *refs):
    (
        ends_ref, table_ref, b_ref, blk_ref, disc_ref, jr_ref, u_ref, norm_ref, wout_ref, wgate_ref,
        next_ref, copy_ref, low_ref, mixed_ref, gate_ref, stats_ref, st_ref,
    ) = refs
    scan, states = states_scan(
        ends_ref, table_ref, b_ref, blk_ref, disc_ref, jr_ref, low_ref, st_ref, down
    )
    zero_first(stats_ref)
    acts = {}

    def mix(part):
        at = slice(*part)
        u = u_ref[at].astype(F32)
        normed = (u - norm_ref[0:1]) * norm_ref[2:3] + norm_ref[3:4]
        mixed = jnp.dot(low_ref[at], wout_ref[...], preferred_element_type=F32)
        mixed += norm_ref[4:5] * normed
        _, _, half_up = gelu_parts(mixed)
        acts[part] = mixed * half_up
        mixed_ref[at] = mixed.astype(BF16)

    def finish(part):
        at = slice(*part)
        act = acts[part]
        gate = sigmoid(jnp.dot(act.astype(BF16), wgate_ref[...], preferred_element_type=F32))
        after = u_ref[at].astype(F32) + act * gate
        next_ref[at] = after
        copy_ref[at] = after
        gate_ref[at] = gate.astype(BF16)
        add_stats(stats_ref, after)

    in_stages([states, mix, finish], parts_of(b_ref.shape[0], down))
    scan.close()
    spread_last(stats_ref)


def zero_first(*refs):
    @pl.when(pl.program_id(0) == 0)
    def _():
        for ref in refs:
            ref[...] = jnp.zeros(ref.shape, ref.dtype)


def spread_last(ref):
    @pl.when(pl.program_id(0) == pl.num_programs(0) - 1)
    def _():
        ref[...] = jnp.broadcast_to(ref[0:1], ref.shape)


class GateBackward:
    def __init__(self, low_ref, wout_ref, wgate_ref, pg_ref, sg_ref, wsum_ref, ssum_ref, acts):
        self.low_ref, self.wout_ref, self.wgate_ref = low_ref, wout_ref, wgate_ref
        self.pg_ref, self.sg_ref = pg_ref, sg_ref
        self.wsum_ref, self.ssum_ref = wsum_ref, ssum_ref
        self.act_ref, self.logit_ref = acts
        self.kept = {}

    def enter(self, part, g, mixed, gate, normed, kept=None):
        at = slice(*part)
        square, tanh, half_up = gelu_parts(mixed) if kept is None else kept
        act = mixed * half_up
        g_gate = g * gate
        if kept is None:
            self.act_ref[at] = act.astype(BF16)
        self.logit_ref[at] = (g_gate * act * (1.0 - gate)).astype(BF16)
        self.kept[part] = (g_gate, gelu_slope(mixed, square, tanh, half_up), normed)

    def middle(self, part):
        at = slice(*part)
        g_gate, slope, normed = self.kept[part]
        act_grad = g_gate + lax.dot_general(
            self.logit_ref[at], self.wgate_ref[...], NT, preferred_element_type=F32
        )
        mixed_grad = act_grad * slope
        self.ssum_ref[...] += column_sum(mixed_grad * normed)
        self.pg_ref[at] = mixed_grad.astype(BF16)

    def leave(self, part):
        at = slice(*part)
        self.sg_ref[at] = lax.dot_general(
            self.pg_ref[at], self.wout_ref[...], NT, preferred_element_type=F32
        )

    def sums(self):
        states, width = self.wout_ref.shape
        self.wsum_ref[states : states + width] += lax.dot_general(
            self.act_ref[...], self.logit_ref[...], TN, preferred_element_type=F32
        )
        self.wsum_ref[:states] += lax.dot_general(
            self.low_ref[...], self.pg_ref[...], TN, preferred_element_type=F32
        )


def turn_kernel(down, *refs):
    (
        ends_ref, table_ref, b_ref, blk_ref, disc_ref, jr_ref, jo_ref, u_ref, norm_ref, wout_ref, wgate_ref,
        g_ref,
        out_ref, low_ref, pg_ref, sg_ref, act_ref, logit_ref, ssum_ref, end_ref, ablk_ref,
        st_ref, w_ref,
    ) = refs
    i, nt = pl.program_id(0), pl.num_programs(0)
    chunks = chunk_count(b_ref)
    half = chunks * 128
    steps = b_ref.shape[0] // LANES
    tile = nt - 1 - i if down else i
    scan, states = states_scan(
        ends_ref, table_ref, b_ref, blk_ref, disc_ref, jr_ref, low_ref, st_ref, down
    )
    back = GateBackward(
        low_ref, wout_ref, wgate_ref, pg_ref, sg_ref, None, ssum_ref, (act_ref, logit_ref)
    )

    @pl.when(i == 0)
    def _():
        ssum_ref[...] = jnp.zeros(ssum_ref.shape, F32)
        ablk_ref[...] = jnp.zeros(ablk_ref.shape, F32)
        w_ref[:, :half] = jnp.ones((LANES, half), F32)
        w_ref[:, half:] = jnp.zeros((LANES, half), F32)

    mid = {}

    def mix(part):
        at = slice(*part)
        u = u_ref[at]
        normed = (u - norm_ref[0:1]) * norm_ref[2:3] + norm_ref[3:4]
        mixed = jnp.dot(low_ref[at], wout_ref[...], preferred_element_type=F32)
        mixed += norm_ref[4:5] * normed
        kept = gelu_parts(mixed)
        act_ref[at] = (mixed * kept[2]).astype(BF16)
        mid[part] = (normed, mixed, kept)

    def enter(part):
        at = slice(*part)
        normed, mixed, kept = mid[part]
        gate = sigmoid(jnp.dot(act_ref[at], wgate_ref[...], preferred_element_type=F32))
        out_ref[at] = u_ref[at] + (mixed * kept[2]) * gate
        back.enter(part, g_ref[at].astype(F32), mixed, gate, normed, kept)

    dr, di = disc_row(disc_ref, 0, chunks, conj=True)
    dr, di = wide(dr), wide(di)
    jo = jo_ref[...]
    live = {
        "w": rows_of(w_ref, slice(0, LANES), chunks),
        "a": rows_of(ablk_ref, slice(0, LANES), chunks),
    }

    def weigh(part):
        (wr, wi), (ar, ai) = (tuple(map(list, live[k])) for k in "wa")
        order = range(part[0] // LANES, part[1] // LANES)
        for step in reversed(order) if down else order:
            sr, si = rows_of(sg_ref, slice(step * LANES, (step + 1) * LANES), chunks)
            keep = jo != tile * steps + step
            for c in range(chunks):
                ar[c] = ar[c] + (wr[c] * sr[c] - wi[c] * si[c])
                ai[c] = ai[c] + (wr[c] * si[c] + wi[c] * sr[c])
                xr = jnp.where(keep, wr[c], 0.0)
                xi = jnp.where(keep, wi[c], 0.0)
                wr[c] = xr * dr[c] - xi * di[c]
                wi[c] = xr * di[c] + xi * dr[c]
        live["w"], live["a"] = (wr, wi), (ar, ai)

    in_stages(
        [states, mix, enter, back.middle, back.leave, weigh], parts_of(b_ref.shape[0], down)
    )
    scan.close()
    put_rows(w_ref, slice(0, LANES), *live["w"])
    put_rows(ablk_ref, slice(0, LANES), *live["a"])

    @pl.when(i == nt - 1)
    def _():
        zero = [jnp.zeros((1, 128), F32)] * chunks
        power = disc_row(disc_ref, 2, chunks, conj=True)
        cr, ci = chain(ablk_ref, jo_ref, power, (zero, zero), not down)
        put_copies(end_ref, cr, ci)


def adjoint_kernel(down, last, *refs):
    (
        ends_ref, table_ref, sg_ref, ablk_ref, disc_ref, jr_ref, low_ref, u_ref, norm_ref, pg_ref, g_ref,
        win_ref, *refs
    ) = refs
    if last:
        (
            ssum_ref, res_ref, sums_ref, st_ref, dg_ref, ax_ref, low_normed_ref, nsum_ref, isum_ref,
        ) = refs
    else:
        (res_ref, sums_ref, nsum_ref, st_ref, dg_ref, ax_ref, low_normed_ref) = refs
        isum_ref = sums_ref
    width, states = win_ref.shape
    i, nt = pl.program_id(0), pl.num_programs(0)
    chunks = chunk_count(sg_ref)
    half = chunks * 128
    steps = sg_ref.shape[0] // LANES
    tile = nt - 1 - i if down else i

    @pl.when(i == 0)
    def _():
        carry = carry_in(ends_ref, table_ref, chunks)
        power = disc_row(disc_ref, 2, chunks, conj=True)
        chain(ablk_ref, jr_ref, power, carry, down, st_ref)
        ax_ref[...] = jnp.zeros_like(ax_ref)

    zero_first(isum_ref, nsum_ref)
    fr, fi = disc_row(disc_ref, 1, chunks)
    fr, fi = wide(fr), wide(fi)
    decay = disc_row(disc_ref, 0, chunks, conj=True)
    scan = Scan(sg_ref, st_ref, decay, jr_ref, tile * steps, down)
    sums = tuple(map(list, rows_of(ax_ref, slice(0, LANES), chunks)))

    def emit(at, pair):
        xr, xi = rows_of(low_ref, at, chunks)
        xr, xi = [v.astype(F32) for v in xr], [v.astype(F32) for v in xi]
        grads = []
        for which, (ar, ai) in enumerate(pair):
            gr, gi = [], []
            rows = slice(which * LANES, (which + 1) * LANES)
            for c in range(chunks):
                vr, vi = xr[c][rows], xi[c][rows]
                sums[0][c] = sums[0][c] + (ar[c] * vr + ai[c] * vi)
                sums[1][c] = sums[1][c] + (ai[c] * vr - ar[c] * vi)
                gr.append(ar[c] * fr[c] + ai[c] * fi[c])
                gi.append(ai[c] * fr[c] - ar[c] * fi[c])
            grads.append((gr, gi))
        store_pair(dg_ref, at, *grads)

    def finish(part):
        at = slice(*part)
        centered = u_ref[at].astype(F32) - norm_ref[0:1]
        low_normed_ref[at] = (centered * norm_ref[2:3] + norm_ref[3:4]).astype(BF16)
        normed_grad = lax.dot_general(dg_ref[at], win_ref[...], NT, preferred_element_type=F32)
        normed_grad += norm_ref[4:5] * pg_ref[at].astype(F32)
        add_rows(
            nsum_ref, column_sum(normed_grad), column_sum(normed_grad * centered) * norm_ref[1:2]
        )
        res_ref[at] = g_ref[at].astype(F32) + norm_ref[2:3] * normed_grad

    in_stages([lambda part: scan.run(part, emit), finish], parts_of(sg_ref.shape[0], down))
    isum_ref[:width] += lax.dot_general(
        low_normed_ref[...], dg_ref[...], TN, preferred_element_type=F32
    )
    scan.close()
    put_rows(ax_ref, slice(0, LANES), *sums)
    spread_last(nsum_ref)

    @pl.when(i == nt - 1)
    def _():
        decays = jnp.sum(ax_ref[...], axis=0, keepdims=True)
        factors = factor_sums(win_ref, isum_ref.at[:width], disc_ref)
        if last:
            rows = width // BLOCKS
            first = rows + rows // 2
            for b in range(BLOCKS):
                at = b * rows
                sums_ref[b, :rows] = isum_ref[at : at + rows, :width]
                sums_ref[b, rows:first, : states - width] = isum_ref[at : at + rows // 2, width:]
                sums_ref[b, rows:first, states - width :] = isum_ref[
                    at + rows // 2 : at + rows, width:
                ]
                sums_ref[b, first:] = jnp.zeros((SMALL, width), F32)
            small = [nsum_ref[0]] + [ssum_ref[:, cols(c)] for c in range(width // 128)]
            small += [decays[:, cols(c)] for c in range(2 * chunks)]
            small += [v[:, cols(c)] for v in factors for c in range(chunks)]
            small = [v[r : r + 1] for v in small for r in range(v.shape[0])]
            for k, row in enumerate(small):
                at = (k % SMALL, k // SMALL)
                sums_ref[0, first + at[0] : first + at[0] + 1, cols(at[1])] = row
        else:
            sums_ref[width : width + 1] = decays
            sums_ref[width + 1 : width + 2, :half] = factors[0]
            sums_ref[width + 1 : width + 2, half:] = factors[1]


def back_kernel(down, tokens, core, *refs):
    (
        sums_ref, r_ref, up_ref, up_norm_ref, mixed_ref, gate_ref, low_ref, u_ref, norm_ref, wout_ref,
        wgate_ref, disc_ref, jo_ref,
        g_ref, pg_ref, sg_ref, kept_ref, sent_ref, ssum_ref, end_ref, ablk_ref, nsum_ref, bsum_ref, wsum_ref,
        act_ref, logit_ref,
    ) = refs
    i, nt = pl.program_id(0), pl.num_programs(0)
    chunks = chunk_count(sg_ref)
    steps = sg_ref.shape[0] // LANES
    tile = nt - 1 - i if down else i

    @pl.when(i == 0)
    def _():
        nsum_ref[...] = jnp.sum(sums_ref[...], axis=0)
        bsum_ref[0:1], bsum_ref[1:2] = summed(sums_ref)

    zero_first(ablk_ref, wsum_ref, ssum_ref)
    back = GateBackward(
        low_ref, wout_ref, wgate_ref, pg_ref, sg_ref, wsum_ref, ssum_ref, (act_ref, logit_ref)
    )
    decay = disc_row(disc_ref, 0, chunks, conj=True)
    scan = Scan(sg_ref, ablk_ref, decay, jo_ref, tile * steps, down)
    scale = up_norm_ref[2:3] * (-1.0 / tokens)

    def enter(part):
        at = slice(*part)
        standard = (up_ref[at] - up_norm_ref[0:1]) * (scale * up_norm_ref[1:2] * bsum_ref[1:2])
        g = r_ref[at] + (standard + scale * bsum_ref[0:1])
        g_ref[at] = g
        u = u_ref[at].astype(F32)
        normed = (u - norm_ref[0:1]) * norm_ref[2:3] + norm_ref[3:4]
        back.enter(part, g, mixed_ref[at].astype(F32), gate_ref[at].astype(F32), normed)

    in_stages([enter, back.middle, back.leave, scan.run], parts_of(sg_ref.shape[0], down))
    back.sums()
    scan.close()

    @pl.when(i == nt - 1)
    def _():
        zero = [jnp.zeros((1, 128), F32)] * chunks
        power = disc_row(disc_ref, 2, chunks, conj=True)
        cr, ci = chain(ablk_ref, jo_ref, power, (zero, zero), down)
        put_copies(end_ref, cr, ci)
        states, width = wout_ref.shape
        gates, outs = width // BLOCKS, states // BLOCKS
        side = lax.axis_index(core)
        for ref, first in ((kept_ref, side), (sent_ref, 1 - side)):
            for b in range(BLOCKS // 2):
                at = first * (BLOCKS // 2) + b
                ref[b, :gates] = wsum_ref[pl.ds(pl.multiple_of(states + at * gates, 8), gates)]
                ref[b, gates:] = wsum_ref[pl.ds(pl.multiple_of(at * outs, 8), outs)]


def row_of(ref, first, count):
    places = [(k % SMALL, k // SMALL) for k in range(first, first + count)]
    return jnp.concatenate([ref[r : r + 1, cols(c)] for r, c in places], axis=1)


def lower_kernel(
    tokens, gates, outs, piece_ref, small_ref, r_ref, tok_ref, norm_ref,
    grad_in_ref, in_ref, out_ref, gate_ref,
):
    width = piece_ref.shape[1]
    left = in_ref.shape[1] - width
    gate_ref[...] = piece_ref[:gates]
    out_ref[...] = piece_ref[gates : gates + outs]
    at = gates + outs
    in_ref[:, :width] = piece_ref[at : at + gates]
    at += gates
    in_ref[: gates // 2, width:] = piece_ref[at : at + gates // 2, :left]
    in_ref[gates // 2 :, width:] = piece_ref[at : at + gates // 2, left:]
    count = width // 128
    bias, gain = row_of(small_ref, 0, count), row_of(small_ref, count, count)
    scale = norm_ref[2:3] * (-1.0 / tokens)
    grad_in_ref[...] = r_ref[...] + (
        (tok_ref[...].astype(F32) - norm_ref[0:1]) * (scale * norm_ref[1:2] * gain) + scale * bias
    )


def last_kernel(
    small_ref, out1_ref, gate1_ref, skip1_ref, in1_ref, decay1_ref, norm1_ref, disc_ref,
    rate_ref, step_ref, freq_ref, _in, _out, _gate,
    in_ref, out_ref, gate_ref, gain_ref, bias_ref, drate_ref, dstep_ref, dfreq_ref, skip_ref,
):
    width = gate1_ref.shape[1]
    half = in1_ref.shape[1] // 2
    gate_ref[...] = gate1_ref[...]
    out_ref[...] = out1_ref[...]
    in_ref[...] = in1_ref[...]
    count = width // 128

    @pl.when(pl.program_id(0) == 0)
    def _():
        bias_ref[0:1] = row_of(small_ref, 0, count)
        gain_ref[0:1] = row_of(small_ref, count, count)
        bias_ref[1:2] = row_of(norm1_ref, 0, count)
        gain_ref[1:2] = row_of(norm1_ref, count, count)
        skip_ref[0:1], skip_ref[1:2] = row_of(small_ref, 2 * count, count), skip1_ref[0:1]
        at = 3 * count
        lanes = half // 128
        for l in range(LAYERS):
            if l == 0:
                ar, ai, sr, si = (row_of(small_ref, at + k * lanes, lanes) for k in range(4))
            else:
                ar, ai = decay1_ref[0:1, :half], decay1_ref[0:1, half:]
                sr, si = decay1_ref[1:2, :half], decay1_ref[1:2, half:]
            dr, di = disc_ref[l, 0:1, :half], disc_ref[l, 0:1, half:]
            fr, fi = disc_ref[l, 1:2, :half], disc_ref[l, 1:2, half:]
            here = slice(l, l + 1)
            rate, freq, step = rate_ref[here], freq_ref[here], jnp.exp(step_ref[here])
            tr = ar - (fr * sr + fi * si)
            ti = ai - (fr * si - fi * sr)
            size = 1.0 / (dr * dr + di * di)
            gr, gi = (tr * dr - ti * di) * size, (tr * di + ti * dr) * size
            mr, mi = -rate * fr - freq * fi, freq * fr - rate * fi
            size = 1.0 / (rate * rate + freq * freq)
            gr += (-rate * sr - freq * si) * size
            gi += (freq * sr - rate * si) * size
            both = 2.0 * (fr * sr + fi * si)
            gx = gr * dr + gi * di
            gy = gi * dr - gr * di
            drate_ref[here] = (-mr * sr - mi * si - both * rate) * size - step * gx
            dfreq_ref[here] = (mi * sr - mr * si - both * freq) * size + step * gy
            dstep_ref[here] = step * (freq * gy - rate * gx)


def whole(array):
    shape = array.shape
    return pl.BlockSpec(shape, lambda i: (0,) * len(shape))


def tile_spec(rows, width, nt, down):
    if down:
        return pl.BlockSpec((rows, width), lambda i: (nt - 1 - i, 0))
    return pl.BlockSpec((rows, width), lambda i: (i, 0))


def run_spec(steps, width, nt, down):
    if down:
        return pl.BlockSpec((LANES, steps, width), lambda i: (0, nt - 1 - i, 0))
    return pl.BlockSpec((LANES, steps, width), lambda i: (0, i, 0))


def call(kernel, nt, args, outs, scratch, macs, name, alias=None):
    arrays = [a for a, *_ in args]
    sizes = sum(a.size * a.dtype.itemsize for a in arrays + [a for a, *_ in outs])
    held = [
        a if keep is None else pltpu.with_memory_space_constraint(a, keep)
        for a, _, keep in map(filled, args)
    ]
    return pl.pallas_call(
        kernel,
        grid=(nt,),
        in_specs=[whole(a) if s is None else s for a, s, _ in map(filled, args)],
        out_specs=[whole(a) if s is None else s for a, s, _ in map(filled, outs)],
        out_shape=[
            a if keep is None else keep(a.shape, a.dtype) for a, _, keep in map(filled, outs)
        ],
        scratch_shapes=scratch,
        compiler_params=pltpu.CompilerParams(
            vmem_limit_bytes=VMEM_LIMIT, dimension_semantics=("arbitrary",)
        ),
        cost_estimate=pl.CostEstimate(flops=2 * macs, bytes_accessed=sizes, transcendentals=0),
        input_output_aliases=alias or {},
        name=name,
    )(*held)


def filled(entry):
    return entry if len(entry) == 3 else entry + (pltpu.HBM,)


def shape(*dims, dtype=F32):
    return jax.ShapeDtypeStruct(dims, dtype)


def body(
    axes,
    tokens_in,
    seq_starts,
    norm_gain,
    norm_bias,
    decay_rate,
    step_log,
    frequency,
    in_proj,
    out_proj,
    skip_gain,
    gate_proj,
    grad_out,
):
    rows, width = tokens_in.shape
    states = in_proj.shape[-1]
    devices = 2 ** len(axes)
    tokens = float(rows * devices)
    run = rows // LANES
    steps = min(64, run)
    tile = steps * LANES
    nt = rows // tile
    span = min(32, steps)
    def tiles(array, down):
        return (array, tile_spec(tile, array.shape[-1], nt, down))

    def runs(array, down):
        return (array, run_spec(steps, array.shape[-1], nt, down))

    def full(array):
        return (array, None)

    def of(array, l):
        size = array.shape[1:]
        return (array, pl.BlockSpec((None,) + size, lambda i: (l,) + (0,) * len(size)))

    discs, tables, cuts = call(
        functools.partial(prep_kernel, rows, axes), 1,
        [full(seq_starts[None]), full(decay_rate),
         full(step_log), full(frequency)],
        [full(shape(LAYERS, 8, states)), full(shape(2 * LAYERS, 2, devices, 2 * SLOT, 128)),
         full(shape(2, LANES, 128, dtype=jnp.int32))],
        [], rows * width, "prep",
    )

    def near(entry):
        return entry[:2] + (pltpu.VMEM if rows * states * 4 <= 7 * 2**20 else pltpu.HBM,)

    tokens_run = tokens_in.reshape(LANES, run, width)
    grad_run = grad_out.reshape(LANES, run, width)
    state_scratch = pltpu.VMEM((LANES, states), F32)
    half_scratch = [pltpu.VMEM((tile, width), BF16)] * 2
    cost = rows * width * states

    u0_near, u0, order, stats = call(
        stats_kernel, nt, [runs(tokens_run, 0)],
        [near(tiles(shape(rows, width, dtype=BF16), 0)), tiles(shape(rows, width, dtype=BF16), 0),
         full(shape(span * LANES, span * LANES, dtype=BF16)),
         near(full(shape(devices, 2 * SLOT, 128)))],
        [], cost // 2, "stats",
    )
    (g1,) = call(
        order_kernel, nt, [runs(grad_run, 0), full(order)],
        [tiles(shape(rows, width, dtype=BF16), 0)], [], cost // 2, "order",
    )

    def restored(array, name):
        (out,) = call(
            restore_kernel, nt, [tiles(array, 0), full(order)],
            [runs(shape(LANES, run, width), 0)], [], cost // 2, name,
        )
        return out.reshape(rows, width)


    def drive(l, stream, stats):
        down = l % 2
        return call(
            functools.partial(drive_kernel, l, bool(down), tokens), nt,
            [near(full(stats)), near(tiles(stream, down)), full(norm_gain), full(norm_bias), full(skip_gain), of(in_proj, l), of(discs, l),
               of(cuts, down)],
            [near(tiles(shape(rows, states), down)), near(full(shape(devices, 2 * SLOT, 128))),
             full(shape(LANES, states)), full(shape(8, width))],
            [], 4 * cost, f"drive_{l}",
        )

    stats, g1 = lax.optimization_barrier((gather_all(stats, axes), g1))
    b0, end0, blk0, norm0 = drive(0, u0_near, stats)
    u1_near, u1, low0, mixed0, gate0, stats = call(
        functools.partial(forward_kernel, False), nt,
        [near(full(gather_all(end0, axes))), of(tables, 2 * 0 + 0), near(tiles(b0, 0)), full(blk0), of(discs, 0), of(cuts, 0),
           near(tiles(u0_near, 0)), full(norm0), of(out_proj, 0), of(gate_proj, 0)],
        [near(tiles(shape(rows, width), 0)), tiles(shape(rows, width), 0), tiles(shape(rows, states, dtype=BF16), 0),
         tiles(shape(rows, width, dtype=BF16), 0), tiles(shape(rows, width, dtype=BF16), 0),
         near(full(shape(devices, 2 * SLOT, 128)))],
        [state_scratch], 6 * cost, "forward_0",
    )

    b1, end1, blk1, norm1 = drive(1, u1_near, gather_all(stats, axes))
    out, low1, pg1, sg1, act1, logit1, skip_sum1, aend1, ablk1 = call(
        functools.partial(turn_kernel, True), nt,
        [near(full(gather_all(end1, axes))), of(tables, 2), near(tiles(b1, 1)), full(blk1),
         of(discs, 1), of(cuts, 1), of(cuts, 0), tiles(u1, 1), full(norm1), of(out_proj, 1),
         of(gate_proj, 1), tiles(g1, 1)],
        [tiles(shape(rows, width), 1), tiles(shape(rows, states, dtype=BF16), 1),
         tiles(shape(rows, width, dtype=BF16), 1), tiles(shape(rows, states), 1),
         tiles(shape(rows, width, dtype=BF16), 1), tiles(shape(rows, width, dtype=BF16), 1),
         full(shape(1, width)), near(full(shape(devices, 2 * SLOT, 128))),
         full(shape(LANES, states))],
        [state_scratch, state_scratch], 12 * cost, "turn_1",
    )
    (w_sum1,) = call(
        layer_sums_kernel, nt,
        [tiles(low1, 0), tiles(pg1, 0), tiles(act1, 0), tiles(logit1, 0),
         full(skip_sum1)],
        [full(shape(states + width + 8, width))], [], 3 * cost, "layer_sums",
    )

    def adjoint(l, sg, ablk, ends, low, stream, norm, pg, g, skip_sum=None):
        down = 1 - l % 2
        last = l == 0
        args = [
            near(full(ends)), of(tables, 2 * l + 1), tiles(sg, down), full(ablk), of(discs, l),
            of(cuts, down), tiles(low, down), tiles(stream, down),
            full(norm), tiles(pg, down), tiles(g, down), of(in_proj, l),
        ]
        if last:
            args.append(full(skip_sum))
            outs = [
                tiles(shape(rows, width), down),
                full(shape(BLOCKS, (width + width // 2) // BLOCKS + SMALL, width)),
            ]
            scratch = [
                state_scratch, pltpu.VMEM((tile, states), BF16), state_scratch,
                pltpu.VMEM((tile, width), BF16), pltpu.VMEM((1, 2 * SLOT, 128), F32),
                pltpu.VMEM((width, states), F32),
            ]
        else:
            outs = [
                tiles(shape(rows, width), down), full(shape(width + 8, states)),
                near(full(shape(devices, 2 * SLOT, 128))),
            ]
            scratch = [
                state_scratch, pltpu.VMEM((tile, states), BF16), state_scratch,
                pltpu.VMEM((tile, width), BF16),
            ]
        return call(
            functools.partial(adjoint_kernel, bool(down), last), nt, args, outs, scratch,
            8 * cost, f"adjoint_{l}",
        )

    r1, in_sum1, norm_sum1 = adjoint(
        1, sg1, ablk1, gather_all(aend1, axes), low1, u1, norm1, pg1, g1
    )
    piece = (2 * width + states + width // 2) // BLOCKS + SMALL

    def lower(r1, norm_sum1, out):
        half = shape(BLOCKS // 2, (states + width) // BLOCKS, width)
        (
            g0, pg0, sg0, kept0, sent0, skip_sum0, aend0, ablk0, small1, _
        ) = call(
            functools.partial(back_kernel, True, tokens, axes[-1]), nt,
            [near(full(gather_all(norm_sum1, axes))), tiles(r1, 1), tiles(u1, 1), full(norm1),
             tiles(mixed0, 1), tiles(gate0, 1), tiles(low0, 1), tiles(u0, 1), full(norm0),
             of(out_proj, 0), of(gate_proj, 0), of(discs, 0), of(cuts, 1)],
            [tiles(shape(rows, width), 1), tiles(shape(rows, width, dtype=BF16), 1),
             tiles(shape(rows, states), 1), full(half), full(half), full(shape(1, width)), near(full(shape(devices, 2 * SLOT, 128))),
             full(shape(LANES, states)), full(shape(2 * SLOT, 128)), full(shape(2, width))],
            [pltpu.VMEM((states + width, width), F32)] + half_scratch, 12 * cost, "back_0",
        )
        core, chips, *others = phases(axes)
        part = kept0 + lax.ppermute(sent0, core[0], [(0, 1), (1, 0)])
        ends, part = lax.optimization_barrier((gather_all(aend0, axes), part))
        part = part.reshape(-1, width)
        part = scatter_sum(part, chips)
        r0, in_sum0 = adjoint(0, sg0, ablk0, ends, low0, u0, norm0, pg0, g0, skip_sum0)
        in_sum0, part = lax.optimization_barrier((in_sum0, part))
        in_part = scatter_sum(in_sum0.reshape(-1, width), core)
        share = line_scatter(part, others[0])
        in_part, share = lax.optimization_barrier((in_part, share))
        in_part = scatter_sum(in_part, chips)
        part = line_gather(share, others[0])
        for axes_left in others[1:]:
            part = line_gather(line_scatter(part, axes_left), axes_left)
        in_part, part = lax.optimization_barrier((in_part, part))
        count = in_part.shape[0]
        pad = -count % (8 * 2 ** len(others[0]))
        in_part = jnp.concatenate([in_part, jnp.zeros((pad, width), F32)], axis=0)
        part = jnp.concatenate([part, sum_all(in_part, others)[:count]], axis=0)
        pieces = gather_rows(gather_rows(part, chips), core)
        return restored(out, "restore_out"), restored(r0, "restore_in"), small1, pieces.reshape(BLOCKS, -1, width)

    def nothing(r1, norm_sum1, out):
        return (
            jnp.zeros((rows, width), F32),
            jnp.zeros((rows, width), F32),
            jnp.zeros((2 * SLOT, 128), F32),
            jnp.zeros((BLOCKS, piece, width), F32),
        )

    w_all1, in_all1 = lax.psum((w_sum1, in_sum1), axes)
    out, r0, norm_all1, pieces = lax.cond(
        seq_starts[0] == 0, lower, nothing, r1, norm_sum1, out
    )

    gates, outs = width // BLOCKS, states // BLOCKS

    def block(array, *dims, at=lambda i: (i, 0)):
        return (array, pl.BlockSpec(dims, at))

    def flat(array, count):
        return block(array, count, array.shape[1])

    def layer(l, *dims):
        dims = (LAYERS,) + dims
        return (shape(*dims), pl.BlockSpec((None, dims[1] // BLOCKS, dims[2]), lambda i: (l, i, 0)))

    def gradients(l):
        return [layer(l, width, states), layer(l, states, width), layer(l, width, width)]

    small_part = block(pieces, None, SMALL, width, at=lambda i: (0, piece // SMALL - 1, 0))
    grad_in, *weights = call(
        functools.partial(lower_kernel, tokens, gates, outs), BLOCKS,
        [block(pieces, None, piece, width, at=lambda i: (i, 0, 0)) + (None,),
         small_part + (None,), flat(r0, rows // BLOCKS), flat(tokens_in, rows // BLOCKS),
         full(norm0)],
        [flat(shape(rows, width), rows // BLOCKS)] + gradients(0),
        [], cost // 2, "lower",
    )
    args = [
        small_part + (None,), flat(w_all1, outs),
        block(w_all1, gates, width, at=lambda i: (states // gates + i, 0)),
        block(w_all1, 8, width, at=lambda i: ((states + width) // 8, 0)),
        flat(in_all1, gates), block(in_all1, 8, states, at=lambda i: (width // 8, 0)),
        full(norm_all1), full(discs), full(decay_rate), full(step_log), full(frequency),
    ]
    alias = {len(args) + k: k for k in range(3)}
    args += [(w, pl.BlockSpec(memory_space=pl.ANY), None) for w in weights]
    (
        in_grad, out_grad, gate_grad, gain_grad, bias_grad, rate_grad, step_grad, freq_grad,
        skip_grad,
    ) = call(
        last_kernel, BLOCKS, args,
        [entry + (None,) for entry in gradients(1)]
        + [full(shape(LAYERS, width))] * 2 + [full(shape(LAYERS, states // 2))] * 3
        + [full(shape(LAYERS, width))],
        [], cost // 2, "last", alias,
    )
    return (
        out,
        grad_in,
        gain_grad,
        bias_grad,
        rate_grad,
        step_grad,
        freq_grad,
        in_grad,
        out_grad,
        skip_grad,
        gate_grad,
    )


def solution(mesh):
    bits = mesh.devices.size.bit_length() - 1
    axes = tuple("b%d" % k for k in range(bits))
    binary = Mesh(mesh.devices.reshape((2,) * bits), axes)
    rows = P(axes, None)
    return jax.shard_map(
        functools.partial(body, axes),
        mesh=binary,
        in_specs=(rows,) + (P(),) * 10 + (rows,),
        out_specs=(rows, rows) + (P(),) * 9,
        check_vma=False,
    )
```

```python
import functools

import jax
import jax.numpy as jnp
from jax import lax
from jax.experimental import pallas as pl
from jax.experimental.pallas import tpu as pltpu
from jax.sharding import Mesh, PartitionSpec as P

LAYERS = 2
EPSILON = 1e-05
SMALL = 8
BLOCKS = 8
SLOT = 4
LANES = 8
VMEM_LIMIT = 30 * 1024 * 1024
GELU_A = 0.7978845608028654
GELU_B = 0.044715
NT = (((1,), (1,)), ((), ()))
TN = (((0,), (0,)), ((), ()))
F32 = jnp.float32
BF16 = jnp.bfloat16


def gather_all(copies, axes):
    return lax.all_to_all(copies, axes, 0, 0)


def scatter_sum(value, axes):
    count = 2 ** len(axes)
    pieces = value.reshape((count, value.shape[0] // count) + value.shape[1:])
    return jnp.sum(lax.all_to_all(pieces, axes, 0, 0), axis=0)


def gather_rows(value, axes):
    count = 2 ** len(axes)
    copies = jnp.broadcast_to(value, (count,) + value.shape)
    return lax.all_to_all(copies, axes, 0, 0).reshape((count * value.shape[0],) + value.shape[1:])


def phases(axes):
    left, out = list(axes), [(axes[-1],)]
    left = left[:-1]
    while left:
        out.append(tuple(left[-2:]))
        left = left[:-2]
    return out


def place_in(axes):
    place = 0
    for axis in axes:
        place = 2 * place + lax.axis_index(axis)
    return place


def traded(value, axes, mask):
    count = 2 ** len(axes)
    return lax.ppermute(value, axes, [(i, i ^ mask) for i in range(count)])


def line_scatter(value, axes):
    count = 2 ** len(axes)
    me = place_in(axes)
    pieces = value.reshape((count, value.shape[0] // count) + value.shape[1:])

    def piece(mask):
        return lax.dynamic_index_in_dim(pieces, me ^ mask, 0, keepdims=False)

    got = [traded(piece(mask), axes, mask) for mask in range(1, count)]
    return functools.reduce(jnp.add, got, piece(0))


def line_gather(value, axes):
    count = 2 ** len(axes)
    me = place_in(axes)
    got = [traded(value, axes, mask) for mask in range(1, count)]
    rows = []
    for j in range(count):
        row = value
        for mask in range(1, count):
            row = jnp.where(me == j ^ mask, got[mask - 1], row)
        rows.append(row)
    return jnp.concatenate(rows, axis=0)


def sum_all(value, parts):
    for part in parts:
        value = scatter_sum(value, part)
    for part in reversed(parts):
        value = gather_rows(value, part)
    return value


def cols(c):
    return slice(c * 128, (c + 1) * 128)


def chunk_count(ref):
    return ref.shape[-1] // 256


def rows_of(ref, at, chunks):
    half = chunks * 128
    re = [ref[at, c * 128 : (c + 1) * 128] for c in range(chunks)]
    im = [ref[at, half + c * 128 : half + (c + 1) * 128] for c in range(chunks)]
    return re, im


def put_rows(ref, at, re, im):
    chunks = len(re)
    half = chunks * 128
    for c in range(chunks):
        ref[at, c * 128 : (c + 1) * 128] = re[c]
        ref[at, half + c * 128 : half + (c + 1) * 128] = im[c]


def put_copies(ref, re, im):
    ref[0] = jnp.zeros(ref.shape[1:], F32)
    for c in range(len(re)):
        ref[0, c : c + 1] = re[c]
        ref[0, SLOT + c : SLOT + c + 1] = im[c]
    ref[...] = jnp.broadcast_to(ref[0:1], ref.shape)


def wide(rows):
    return [jnp.broadcast_to(v, (LANES, 128)) for v in rows]


def chain(ends_ref, jr_ref, power, carry, down, start_ref=None):
    chunks = len(power[0])
    pr, pi = power
    cr, ci = carry
    order = range(LANES - 1, -1, -1) if down else range(LANES)
    for s in order:
        at = slice(s, s + 1)
        if start_ref is not None:
            put_rows(start_ref, at, cr, ci)
        er, ei = rows_of(ends_ref, at, chunks)
        alive = (jr_ref[at, :] < 0).astype(F32)
        cr, ci = (
            [er[c] + alive * (pr[c] * cr[c] - pi[c] * ci[c]) for c in range(chunks)],
            [ei[c] + alive * (pr[c] * ci[c] + pi[c] * cr[c]) for c in range(chunks)],
        )
    return cr, ci


def carry_in(ends_ref, table_ref, chunks):
    total = jnp.zeros((2 * SLOT, 128), F32)
    for e in range(ends_ref.shape[0]):
        end = ends_ref[e]
        turned = jnp.concatenate([end[SLOT:], end[:SLOT]], axis=0)
        total += table_ref[0, e] * end + table_ref[1, e] * turned
    return (
        [total[c : c + 1] for c in range(chunks)],
        [total[SLOT + c : SLOT + c + 1] for c in range(chunks)],
    )


def in_stages(stages, parts):
    for turn in range(len(parts) + len(stages) - 1):
        for k, stage in enumerate(stages):
            if 0 <= turn - k < len(parts):
                stage(parts[turn - k])


def parts_of(rows, down, count=2):
    size = rows // count
    parts = [(at, at + size) for at in range(0, rows, size)]
    return parts[::-1] if down else parts


class Scan:
    def __init__(self, src_ref, st_ref, decay, jr_ref, first_step, down):
        self.src_ref, self.st_ref, self.down = src_ref, st_ref, down
        self.chunks = chunk_count(src_ref)
        self.dr, self.di = wide(decay[0]), wide(decay[1])
        self.jr, self.first_step = jr_ref[...], first_step
        self.state = rows_of(st_ref, slice(0, LANES), self.chunks)

    def one(self, step):
        br, bi = rows_of(self.src_ref, slice(step * LANES, (step + 1) * LANES), self.chunks)
        live = self.jr != self.first_step + step
        nr, ni = [], []
        for c in range(self.chunks):
            xr = jnp.where(live, self.state[0][c], 0.0)
            xi = jnp.where(live, self.state[1][c], 0.0)
            nr.append(self.dr[c] * xr - self.di[c] * xi + br[c])
            ni.append(self.dr[c] * xi + self.di[c] * xr + bi[c])
        self.state = (nr, ni)
        return nr, ni

    def run(self, part, emit=None):
        low, high = part[0] // LANES, part[1] // LANES
        for n in range(0, high - low, 2):
            step = high - 2 - n if self.down else low + n
            first = self.one(step + 1 if self.down else step)
            second = self.one(step if self.down else step + 1)
            if emit is not None:
                pair = (second, first) if self.down else (first, second)
                emit(slice(step * LANES, (step + 2) * LANES), pair)

    def close(self):
        put_rows(self.st_ref, slice(0, LANES), *self.state)


def store_pair(ref, at, first, second):
    re = [jnp.concatenate([p, q], axis=0).astype(BF16) for p, q in zip(first[0], second[0])]
    im = [jnp.concatenate([p, q], axis=0).astype(BF16) for p, q in zip(first[1], second[1])]
    put_rows(ref, at, re, im)


def disc_row(disc_ref, row, chunks, conj=False):
    re, im = rows_of(disc_ref, slice(row, row + 1), chunks)
    return (re, [-v for v in im]) if conj else (re, im)


def column_sum(value):
    rows, width = value.shape
    return jnp.sum(jnp.sum(value.reshape(rows // 8, 8, width), axis=0), axis=0, keepdims=True)


def permute_in(block_ref, order_ref, part):
    runs, _, width = block_ref.shape
    size = order_ref.shape[0]
    span = size // runs
    out = []
    for k in range(part[0] // size, part[1] // size):
        rows = block_ref[:, k * span : (k + 1) * span, :].reshape(size, width)
        out.append(jnp.dot(order_ref[...], rows, preferred_element_type=F32))
    return out[0] if len(out) == 1 else jnp.concatenate(out, axis=0)


def permute_out(value, order_ref, out_ref, part):
    width = value.shape[1]
    size = order_ref.shape[0]
    span = size // LANES
    high = value.astype(BF16)
    low = (value - high.astype(F32)).astype(BF16)
    for n, k in enumerate(range(part[0] // size, part[1] // size)):
        at = slice(n * size, (n + 1) * size)
        back = lax.dot_general(order_ref[...], high[at], TN, preferred_element_type=F32)
        back += lax.dot_general(order_ref[...], low[at], TN, preferred_element_type=F32)
        out_ref[:, k * span : (k + 1) * span, :] = back.reshape(LANES, span, width)


def expm1(value):
    acc = jnp.full_like(value, 1.0 / 479001600.0)
    for n in (39916800.0, 3628800.0, 362880.0, 40320.0, 5040.0, 720.0, 120.0, 24.0, 6.0, 2.0, 1.0):
        acc = acc * value + 1.0 / n
    return jnp.where(value > -1.0, acc * value, jnp.exp(value) - 1.0)


def prep_kernel(
    rows, axes, starts_ref, rate_ref, step_ref, freq_ref,
    disc_ref, table_ref, cut_ref,
):
    devices = 2 ** len(axes)
    total = rows * devices
    run = rows // LANES
    half = rate_ref.shape[-1]
    me = 0
    for axis in axes:
        me = 2 * me + lax.axis_index(axis)
    starts = [starts_ref[:, k : k + 1] for k in range(starts_ref.shape[1])]

    base = me * rows + run * lax.broadcasted_iota(jnp.int32, (LANES, 128), 0)
    up = jnp.full((LANES, 128), -1, jnp.int32)
    down = up
    for begin in starts + [total]:
        rel = begin - base
        up = jnp.maximum(up, jnp.where((rel >= 0) & (rel < run), rel, -1))
        down = jnp.maximum(down, jnp.where((rel >= 1) & (rel <= run), rel - 1, -1))
    cut_ref[0] = up
    cut_ref[1] = down

    source = lax.broadcasted_iota(jnp.int32, (devices, half), 0)
    for l in range(LAYERS):
        row = slice(l, l + 1)
        rate, freq = rate_ref[row], freq_ref[row]
        step_size = jnp.exp(step_ref[row])
        real_angle = -rate * step_size
        imag_angle = freq * step_size
        magnitude = jnp.exp(real_angle)
        cosine, sine = jnp.cos(imag_angle), jnp.sin(imag_angle)
        minus_real = expm1(real_angle) * cosine - 2.0 * jnp.sin(0.5 * imag_angle) ** 2
        minus_imag = magnitude * sine
        modulus = rate * rate + freq * freq
        disc_ref[l, 0:1, :half] = magnitude * cosine
        disc_ref[l, 0:1, half:] = minus_imag
        disc_ref[l, 1:2, :half] = (-rate * minus_real + freq * minus_imag) / modulus
        disc_ref[l, 1:2, half:] = (-rate * minus_imag - freq * minus_real) / modulus
        magnitude = jnp.exp(real_angle * float(run))
        disc_ref[l, 2:3, :half] = magnitude * jnp.cos(imag_angle * float(run))
        disc_ref[l, 2:3, half:] = magnitude * jnp.sin(imag_angle * float(run))
        disc_ref[l, 3:8] = jnp.zeros((5, 2 * half), F32)
        powers = []
        for bit in range(len(axes)):
            magnitude = jnp.exp(real_angle * float(rows << bit))
            angle = imag_angle * float(rows << bit)
            powers.append((magnitude * jnp.cos(angle), magnitude * jnp.sin(angle)))
        for back in range(2):
            going_down = (l + back) % 2 == 1
            if going_down:
                live, count = source > me, source - me - 1
            else:
                live, count = source < me, me - 1 - source
            for begin in starts:
                if going_down:
                    cut = (begin > (me + 1) * rows) & (source * rows >= begin)
                else:
                    cut = (begin < me * rows) & ((source + 1) * rows <= begin)
                live &= ~cut
            count = jnp.maximum(count, 0)
            real = live.astype(F32)
            imag = jnp.zeros((devices, half), F32)
            for bit, (pr, pi) in enumerate(powers):
                use = (count & (1 << bit)) != 0
                pr, pi = jnp.where(use, pr, 1.0), jnp.where(use, pi, 0.0)
                real, imag = real * pr - imag * pi, real * pi + imag * pr
            imag = -imag if back else imag
            at = 2 * l + back
            table_ref[at] = jnp.zeros(table_ref.shape[1:], F32)
            for c in range(half // 128):
                table_ref[at, 0, :, c, :] = real[:, cols(c)]
                table_ref[at, 0, :, SLOT + c, :] = real[:, cols(c)]
                table_ref[at, 1, :, c, :] = -imag[:, cols(c)]
                table_ref[at, 1, :, SLOT + c, :] = imag[:, cols(c)]


def stats_kernel(tok_ref, u_ref, copy_ref, order_ref, stats_ref):
    @pl.when(pl.program_id(0) == 0)
    def _():
        size = order_ref.shape[0]
        span = size // LANES
        to = lax.broadcasted_iota(jnp.int32, (size, size), 0)
        back = lax.broadcasted_iota(jnp.int32, (size, size), 1)
        order_ref[...] = ((to % LANES) * span + to // LANES == back).astype(F32).astype(BF16)

    value = permute_in(tok_ref, order_ref, (0, u_ref.shape[0]))
    u_ref[...] = value.astype(BF16)
    copy_ref[...] = u_ref[...]
    zero_first(stats_ref)
    add_stats(stats_ref, value)
    spread_last(stats_ref)


def add_stats(stats_ref, value):
    add_rows(stats_ref, column_sum(value), column_sum(value * value))


def add_rows(copies_ref, first, second):
    for c in range(first.shape[1] // 128):
        copies_ref[0, c : c + 1] += first[:, cols(c)]
        copies_ref[0, SLOT + c : SLOT + c + 1] += second[:, cols(c)]


def summed(ref):
    total = jnp.sum(ref[...], axis=0)
    return tuple(
        jnp.concatenate([total[SLOT * k + c : SLOT * k + c + 1] for c in range(SLOT)], axis=1)
        for k in range(2)
    )


def drive_kernel(layer, down, tokens, *refs):
    (
        stat_ref, u_ref, gain_ref, bias_ref, skip_ref, win_ref, disc_ref, jr_ref,
        b_ref, end_ref, blk_ref, norm_ref,
    ) = refs
    i, nt = pl.program_id(0), pl.num_programs(0)
    steps = u_ref.shape[0] // LANES
    chunks = chunk_count(b_ref)
    half = chunks * 128

    @pl.when(i == 0)
    def _():
        total, squares = summed(stat_ref)
        row = slice(layer, layer + 1)
        mean = total / tokens
        inv = lax.rsqrt(squares / tokens - mean * mean + EPSILON)
        norm_ref[0:1] = mean
        norm_ref[1:2] = inv
        norm_ref[2:3] = inv * gain_ref[row]
        norm_ref[3:4] = bias_ref[row]
        norm_ref[4:5] = skip_ref[row]
        norm_ref[5:8] = jnp.zeros((3, norm_ref.shape[1]), F32)
        blk_ref[...] = jnp.zeros_like(blk_ref)

    fr, fi = disc_ref[1:2, :half], disc_ref[1:2, half:]
    tile = nt - 1 - i if down else i
    scan = Scan(b_ref, blk_ref, disc_row(disc_ref, 0, chunks), jr_ref, tile * steps, down)

    def product(part):
        at = slice(*part)
        u = u_ref[at].astype(F32)
        normed = (u - norm_ref[0:1]) * norm_ref[2:3] + norm_ref[3:4]
        drive = jnp.dot(normed.astype(BF16), win_ref[...], preferred_element_type=F32)
        re, im = drive[:, :half], drive[:, half:]
        b_ref[at, :half] = re * fr - im * fi
        b_ref[at, half:] = re * fi + im * fr

    in_stages([product, scan.run], parts_of(b_ref.shape[0], down, 4))
    scan.close()

    @pl.when(i == nt - 1)
    def _():
        zero = [jnp.zeros((1, 128), F32)] * chunks
        cr, ci = chain(blk_ref, jr_ref, disc_row(disc_ref, 2, chunks), (zero, zero), down)
        put_copies(end_ref, cr, ci)


def states_scan(ends_ref, table_ref, b_ref, blk_ref, disc_ref, jr_ref, low_ref, st_ref, down):
    i, nt = pl.program_id(0), pl.num_programs(0)
    chunks = chunk_count(b_ref)
    steps = b_ref.shape[0] // LANES

    @pl.when(i == 0)
    def _():
        carry = carry_in(ends_ref, table_ref, chunks)
        chain(blk_ref, jr_ref, disc_row(disc_ref, 2, chunks), carry, down, st_ref)

    tile = nt - 1 - i if down else i
    scan = Scan(b_ref, st_ref, disc_row(disc_ref, 0, chunks), jr_ref, tile * steps, down)

    def stage(part):
        scan.run(part, lambda at, pair: store_pair(low_ref, at, *pair))

    return scan, stage


def gelu_parts(mixed):
    square = mixed * mixed
    tanh = jnp.tanh(mixed * (GELU_A + (GELU_A * GELU_B) * square))
    half_up = 0.5 + 0.5 * tanh
    return square, tanh, half_up


def gelu_slope(mixed, square, tanh, half_up):
    return half_up + (mixed * (0.5 - 0.5 * tanh * tanh)) * (
        GELU_A + (3.0 * GELU_A * GELU_B) * square
    )


def sigmoid(value):
    return 0.5 + 0.5 * jnp.tanh(0.5 * value)


def forward_kernel(down, *refs):
    (
        ends_ref, table_ref, b_ref, blk_ref, disc_ref, jr_ref, u_ref, norm_ref, wout_ref, wgate_ref,
        next_ref, copy_ref, low_ref, mixed_ref, gate_ref, stats_ref, st_ref,
    ) = refs
    scan, states = states_scan(
        ends_ref, table_ref, b_ref, blk_ref, disc_ref, jr_ref, low_ref, st_ref, down
    )
    zero_first(stats_ref)
    acts = {}

    def mix(part):
        at = slice(*part)
        u = u_ref[at].astype(F32)
        normed = (u - norm_ref[0:1]) * norm_ref[2:3] + norm_ref[3:4]
        mixed = jnp.dot(low_ref[at], wout_ref[...], preferred_element_type=F32)
        mixed += norm_ref[4:5] * normed
        _, _, half_up = gelu_parts(mixed)
        acts[part] = mixed * half_up
        mixed_ref[at] = mixed.astype(BF16)

    def finish(part):
        at = slice(*part)
        act = acts[part]
        gate = sigmoid(jnp.dot(act.astype(BF16), wgate_ref[...], preferred_element_type=F32))
        after = u_ref[at].astype(F32) + act * gate
        next_ref[at] = after
        copy_ref[at] = after
        gate_ref[at] = gate.astype(BF16)
        add_stats(stats_ref, after)

    in_stages([states, mix, finish], parts_of(b_ref.shape[0], down))
    scan.close()
    spread_last(stats_ref)


def zero_first(*refs):
    @pl.when(pl.program_id(0) == 0)
    def _():
        for ref in refs:
            ref[...] = jnp.zeros(ref.shape, ref.dtype)


def spread_last(ref):
    @pl.when(pl.program_id(0) == pl.num_programs(0) - 1)
    def _():
        ref[...] = jnp.broadcast_to(ref[0:1], ref.shape)


class GateBackward:
    def __init__(self, low_ref, wout_ref, wgate_ref, pg_ref, sg_ref, wsum_ref, ssum_ref, acts):
        self.low_ref, self.wout_ref, self.wgate_ref = low_ref, wout_ref, wgate_ref
        self.pg_ref, self.sg_ref = pg_ref, sg_ref
        self.wsum_ref, self.ssum_ref = wsum_ref, ssum_ref
        self.act_ref, self.logit_ref = acts
        self.kept = {}

    def enter(self, part, g, mixed, gate, normed, kept=None):
        at = slice(*part)
        square, tanh, half_up = gelu_parts(mixed) if kept is None else kept
        act = mixed * half_up
        g_gate = g * gate
        if kept is None:
            self.act_ref[at] = act.astype(BF16)
        self.logit_ref[at] = (g_gate * act * (1.0 - gate)).astype(BF16)
        self.kept[part] = (g_gate, gelu_slope(mixed, square, tanh, half_up), normed)

    def middle(self, part):
        at = slice(*part)
        g_gate, slope, normed = self.kept[part]
        act_grad = g_gate + lax.dot_general(
            self.logit_ref[at], self.wgate_ref[...], NT, preferred_element_type=F32
        )
        mixed_grad = act_grad * slope
        self.ssum_ref[...] += column_sum(mixed_grad * normed)
        self.pg_ref[at] = mixed_grad.astype(BF16)

    def leave(self, part):
        at = slice(*part)
        self.sg_ref[at] = lax.dot_general(
            self.pg_ref[at], self.wout_ref[...], NT, preferred_element_type=F32
        )

    def sums(self):
        states, width = self.wout_ref.shape
        self.wsum_ref[states : states + width] += lax.dot_general(
            self.act_ref[...], self.logit_ref[...], TN, preferred_element_type=F32
        )
        self.wsum_ref[:states] += lax.dot_general(
            self.low_ref[...], self.pg_ref[...], TN, preferred_element_type=F32
        )


def turn_kernel(down, *refs):
    (
        ends_ref, table_ref, b_ref, blk_ref, disc_ref, jr_ref, jo_ref, u_ref, norm_ref, wout_ref, wgate_ref,
        gout_ref, order_ref,
        out_ref, low_ref, g_ref, pg_ref, sg_ref, wsum_ref, end_ref, ablk_ref,
        st_ref, w_ref, act_ref, logit_ref,
    ) = refs
    sums = wout_ref.shape[0] + wout_ref.shape[1]
    ssum_ref = wsum_ref.at[sums : sums + 1]
    i, nt = pl.program_id(0), pl.num_programs(0)
    chunks = chunk_count(b_ref)
    half = chunks * 128
    steps = b_ref.shape[0] // LANES
    tile = nt - 1 - i if down else i
    scan, states = states_scan(
        ends_ref, table_ref, b_ref, blk_ref, disc_ref, jr_ref, low_ref, st_ref, down
    )
    back = GateBackward(
        low_ref, wout_ref, wgate_ref, pg_ref, sg_ref, wsum_ref, ssum_ref, (act_ref, logit_ref)
    )

    @pl.when(i == 0)
    def _():
        wsum_ref[...] = jnp.zeros(wsum_ref.shape, F32)
        ablk_ref[...] = jnp.zeros(ablk_ref.shape, F32)
        w_ref[:, :half] = jnp.ones((LANES, half), F32)
        w_ref[:, half:] = jnp.zeros((LANES, half), F32)

    mid = {}

    def mix(part):
        at = slice(*part)
        u = u_ref[at]
        normed = (u - norm_ref[0:1]) * norm_ref[2:3] + norm_ref[3:4]
        mixed = jnp.dot(low_ref[at], wout_ref[...], preferred_element_type=F32)
        mixed += norm_ref[4:5] * normed
        kept = gelu_parts(mixed)
        act_ref[at] = (mixed * kept[2]).astype(BF16)
        mid[part] = (normed, mixed, kept)

    def enter(part):
        at = slice(*part)
        normed, mixed, kept = mid[part]
        gate = sigmoid(jnp.dot(act_ref[at], wgate_ref[...], preferred_element_type=F32))
        permute_out(u_ref[at] + (mixed * kept[2]) * gate, order_ref, out_ref, part)
        g = permute_in(gout_ref, order_ref, part)
        g_ref[at] = g.astype(BF16)
        back.enter(part, g, mixed, gate, normed, kept)

    dr, di = disc_row(disc_ref, 0, chunks, conj=True)
    dr, di = wide(dr), wide(di)
    jo = jo_ref[...]
    live = {
        "w": rows_of(w_ref, slice(0, LANES), chunks),
        "a": rows_of(ablk_ref, slice(0, LANES), chunks),
    }

    def weigh(part):
        (wr, wi), (ar, ai) = (tuple(map(list, live[k])) for k in "wa")
        order = range(part[0] // LANES, part[1] // LANES)
        for step in reversed(order) if down else order:
            sr, si = rows_of(sg_ref, slice(step * LANES, (step + 1) * LANES), chunks)
            keep = jo != tile * steps + step
            for c in range(chunks):
                ar[c] = ar[c] + (wr[c] * sr[c] - wi[c] * si[c])
                ai[c] = ai[c] + (wr[c] * si[c] + wi[c] * sr[c])
                xr = jnp.where(keep, wr[c], 0.0)
                xi = jnp.where(keep, wi[c], 0.0)
                wr[c] = xr * dr[c] - xi * di[c]
                wi[c] = xr * di[c] + xi * dr[c]
        live["w"], live["a"] = (wr, wi), (ar, ai)

    in_stages(
        [states, mix, enter, back.middle, back.leave, weigh], parts_of(b_ref.shape[0], down)
    )
    back.sums()
    scan.close()
    put_rows(w_ref, slice(0, LANES), *live["w"])
    put_rows(ablk_ref, slice(0, LANES), *live["a"])

    @pl.when(i == nt - 1)
    def _():
        zero = [jnp.zeros((1, 128), F32)] * chunks
        power = disc_row(disc_ref, 2, chunks, conj=True)
        cr, ci = chain(ablk_ref, jo_ref, power, (zero, zero), not down)
        put_copies(end_ref, cr, ci)


def adjoint_kernel(down, last, *refs):
    (
        ends_ref, table_ref, sg_ref, ablk_ref, disc_ref, jr_ref, low_ref, u_ref, norm_ref, pg_ref, g_ref,
        win_ref, order_ref, *refs
    ) = refs
    if last:
        (
            ssum_ref, res_ref, sums_ref, st_ref, dg_ref, ax_ref, low_normed_ref, nsum_ref, isum_ref,
        ) = refs
    else:
        (res_ref, sums_ref, nsum_ref, st_ref, dg_ref, ax_ref, low_normed_ref) = refs
        isum_ref = sums_ref
    width, states = win_ref.shape
    i, nt = pl.program_id(0), pl.num_programs(0)
    chunks = chunk_count(sg_ref)
    half = chunks * 128
    steps = sg_ref.shape[0] // LANES
    tile = nt - 1 - i if down else i

    @pl.when(i == 0)
    def _():
        carry = carry_in(ends_ref, table_ref, chunks)
        power = disc_row(disc_ref, 2, chunks, conj=True)
        chain(ablk_ref, jr_ref, power, carry, down, st_ref)
        ax_ref[...] = jnp.zeros_like(ax_ref)

    zero_first(isum_ref, nsum_ref)
    fr, fi = disc_row(disc_ref, 1, chunks)
    fr, fi = wide(fr), wide(fi)
    decay = disc_row(disc_ref, 0, chunks, conj=True)
    scan = Scan(sg_ref, st_ref, decay, jr_ref, tile * steps, down)
    sums = tuple(map(list, rows_of(ax_ref, slice(0, LANES), chunks)))

    def emit(at, pair):
        xr, xi = rows_of(low_ref, at, chunks)
        xr, xi = [v.astype(F32) for v in xr], [v.astype(F32) for v in xi]
        grads = []
        for which, (ar, ai) in enumerate(pair):
            gr, gi = [], []
            rows = slice(which * LANES, (which + 1) * LANES)
            for c in range(chunks):
                vr, vi = xr[c][rows], xi[c][rows]
                sums[0][c] = sums[0][c] + (ar[c] * vr + ai[c] * vi)
                sums[1][c] = sums[1][c] + (ai[c] * vr - ar[c] * vi)
                gr.append(ar[c] * fr[c] + ai[c] * fi[c])
                gi.append(ai[c] * fr[c] - ar[c] * fi[c])
            grads.append((gr, gi))
        store_pair(dg_ref, at, *grads)

    def finish(part):
        at = slice(*part)
        centered = u_ref[at].astype(F32) - norm_ref[0:1]
        low_normed_ref[at] = (centered * norm_ref[2:3] + norm_ref[3:4]).astype(BF16)
        normed_grad = lax.dot_general(dg_ref[at], win_ref[...], NT, preferred_element_type=F32)
        normed_grad += norm_ref[4:5] * pg_ref[at].astype(F32)
        add_rows(
            nsum_ref, column_sum(normed_grad), column_sum(normed_grad * centered) * norm_ref[1:2]
        )
        result = g_ref[at].astype(F32) + norm_ref[2:3] * normed_grad
        if last:
            permute_out(result, order_ref, res_ref, part)
        else:
            res_ref[at] = result

    in_stages([lambda part: scan.run(part, emit), finish], parts_of(sg_ref.shape[0], down))
    isum_ref[:width] += lax.dot_general(
        low_normed_ref[...], dg_ref[...], TN, preferred_element_type=F32
    )
    scan.close()
    put_rows(ax_ref, slice(0, LANES), *sums)
    spread_last(nsum_ref)

    @pl.when(i == nt - 1)
    def _():
        decays = jnp.sum(ax_ref[...], axis=0, keepdims=True)
        wr, wi = win_ref[:, :half].astype(F32), win_ref[:, half:].astype(F32)
        gr, gi = isum_ref[:width, :half], isum_ref[:width, half:]
        re = jnp.sum(wr * gr + wi * gi, axis=0, keepdims=True)
        im = jnp.sum(wr * gi - wi * gr, axis=0, keepdims=True)
        gr, gi = disc_ref[1:2, :half], disc_ref[1:2, half:]
        scale = 1.0 / (gr * gr + gi * gi)
        factors = ((re * gr - im * gi) * scale, (re * gi + im * gr) * scale)
        if last:
            rows = width // BLOCKS
            first = rows + rows // 2
            for b in range(BLOCKS):
                at = b * rows
                sums_ref[b, :rows] = isum_ref[at : at + rows, :width]
                sums_ref[b, rows:first, : states - width] = isum_ref[at : at + rows // 2, width:]
                sums_ref[b, rows:first, states - width :] = isum_ref[
                    at + rows // 2 : at + rows, width:
                ]
                sums_ref[b, first:] = jnp.zeros((SMALL, width), F32)
            small = [nsum_ref[0]] + [ssum_ref[:, cols(c)] for c in range(width // 128)]
            small += [decays[:, cols(c)] for c in range(2 * chunks)]
            small += [v[:, cols(c)] for v in factors for c in range(chunks)]
            small = [v[r : r + 1] for v in small for r in range(v.shape[0])]
            for k, row in enumerate(small):
                at = (k % SMALL, k // SMALL)
                sums_ref[0, first + at[0] : first + at[0] + 1, cols(at[1])] = row
        else:
            sums_ref[width : width + 1] = decays
            sums_ref[width + 1 : width + 2, :half] = factors[0]
            sums_ref[width + 1 : width + 2, half:] = factors[1]


def back_kernel(down, tokens, core, *refs):
    (
        sums_ref, r_ref, up_ref, up_norm_ref, mixed_ref, gate_ref, low_ref, u_ref, norm_ref, wout_ref,
        wgate_ref, disc_ref, jo_ref,
        g_ref, pg_ref, sg_ref, kept_ref, sent_ref, ssum_ref, end_ref, ablk_ref, nsum_ref, bsum_ref, wsum_ref,
        act_ref, logit_ref,
    ) = refs
    i, nt = pl.program_id(0), pl.num_programs(0)
    chunks = chunk_count(sg_ref)
    steps = sg_ref.shape[0] // LANES
    tile = nt - 1 - i if down else i

    @pl.when(i == 0)
    def _():
        nsum_ref[...] = jnp.sum(sums_ref[...], axis=0)
        bsum_ref[0:1], bsum_ref[1:2] = summed(sums_ref)

    zero_first(ablk_ref, wsum_ref, ssum_ref)
    back = GateBackward(
        low_ref, wout_ref, wgate_ref, pg_ref, sg_ref, wsum_ref, ssum_ref, (act_ref, logit_ref)
    )
    decay = disc_row(disc_ref, 0, chunks, conj=True)
    scan = Scan(sg_ref, ablk_ref, decay, jo_ref, tile * steps, down)
    scale = up_norm_ref[2:3] * (-1.0 / tokens)

    def enter(part):
        at = slice(*part)
        standard = (up_ref[at] - up_norm_ref[0:1]) * (scale * up_norm_ref[1:2] * bsum_ref[1:2])
        g = r_ref[at] + (standard + scale * bsum_ref[0:1])
        g_ref[at] = g
        u = u_ref[at].astype(F32)
        normed = (u - norm_ref[0:1]) * norm_ref[2:3] + norm_ref[3:4]
        back.enter(part, g, mixed_ref[at].astype(F32), gate_ref[at].astype(F32), normed)

    in_stages([enter, back.middle, back.leave, scan.run], parts_of(sg_ref.shape[0], down))
    back.sums()
    scan.close()

    @pl.when(i == nt - 1)
    def _():
        zero = [jnp.zeros((1, 128), F32)] * chunks
        power = disc_row(disc_ref, 2, chunks, conj=True)
        cr, ci = chain(ablk_ref, jo_ref, power, (zero, zero), down)
        put_copies(end_ref, cr, ci)
        states, width = wout_ref.shape
        gates, outs = width // BLOCKS, states // BLOCKS
        side = lax.axis_index(core)
        for ref, first in ((kept_ref, side), (sent_ref, 1 - side)):
            for b in range(BLOCKS // 2):
                at = first * (BLOCKS // 2) + b
                ref[b, :gates] = wsum_ref[pl.ds(pl.multiple_of(states + at * gates, 8), gates)]
                ref[b, gates:] = wsum_ref[pl.ds(pl.multiple_of(at * outs, 8), outs)]


def last_kernel(
    tokens, piece_ref, small_ref, out1_ref, gate1_ref, skip1_ref, in1_ref, decay1_ref, norm1_ref,
    disc_ref, rate_ref, step_ref, freq_ref, r_ref, tok_ref, norm_ref,
    grad_in_ref, gain_ref, bias_ref, drate_ref, dstep_ref, dfreq_ref, in_ref, out_ref, skip_ref,
    gate_ref,
):
    gates, width = gate1_ref.shape
    outs = out1_ref.shape[0]
    states = in1_ref.shape[1]
    half = states // 2
    left = states - width
    gate_ref[0], gate_ref[1] = piece_ref[:gates], gate1_ref[...]
    out_ref[0], out_ref[1] = piece_ref[gates : gates + outs], out1_ref[...]
    at = gates + outs
    in_ref[0, :, :width] = piece_ref[at : at + gates]
    at += gates
    in_ref[0, : gates // 2, width:] = piece_ref[at : at + gates // 2, :left]
    in_ref[0, gates // 2 :, width:] = piece_ref[at : at + gates // 2, left:]
    in_ref[1] = in1_ref[...]

    def row(ref, first, count):
        places = [(k % SMALL, k // SMALL) for k in range(first, first + count)]
        return jnp.concatenate([ref[r : r + 1, cols(c)] for r, c in places], axis=1)

    count = width // 128
    bias, gain = row(small_ref, 0, count), row(small_ref, count, count)
    scale = norm_ref[2:3] * (-1.0 / tokens)
    grad_in_ref[...] = r_ref[...] + (
        (tok_ref[...].astype(F32) - norm_ref[0:1]) * (scale * norm_ref[1:2] * gain) + scale * bias
    )

    @pl.when(pl.program_id(0) == 0)
    def _():
        bias_ref[0:1], gain_ref[0:1] = bias, gain
        bias_ref[1:2], gain_ref[1:2] = row(norm1_ref, 0, count), row(norm1_ref, count, count)
        skip_ref[0:1], skip_ref[1:2] = row(small_ref, 2 * count, count), skip1_ref[0:1]
        at = 3 * count
        lanes = half // 128
        for l in range(LAYERS):
            if l == 0:
                ar, ai, sr, si = (row(small_ref, at + k * lanes, lanes) for k in range(4))
            else:
                ar, ai = decay1_ref[0:1, :half], decay1_ref[0:1, half:]
                sr, si = decay1_ref[1:2, :half], decay1_ref[1:2, half:]
            dr, di = disc_ref[l, 0:1, :half], disc_ref[l, 0:1, half:]
            fr, fi = disc_ref[l, 1:2, :half], disc_ref[l, 1:2, half:]
            here = slice(l, l + 1)
            rate, freq, step = rate_ref[here], freq_ref[here], jnp.exp(step_ref[here])
            tr = ar - (fr * sr + fi * si)
            ti = ai - (fr * si - fi * sr)
            size = 1.0 / (dr * dr + di * di)
            gr, gi = (tr * dr - ti * di) * size, (tr * di + ti * dr) * size
            mr, mi = -rate * fr - freq * fi, freq * fr - rate * fi
            size = 1.0 / (rate * rate + freq * freq)
            gr += (-rate * sr - freq * si) * size
            gi += (freq * sr - rate * si) * size
            both = 2.0 * (fr * sr + fi * si)
            gx = gr * dr + gi * di
            gy = gi * dr - gr * di
            drate_ref[here] = (-mr * sr - mi * si - both * rate) * size - step * gx
            dfreq_ref[here] = (mi * sr - mr * si - both * freq) * size + step * gy
            dstep_ref[here] = step * (freq * gy - rate * gx)


def whole(array):
    shape = array.shape
    return pl.BlockSpec(shape, lambda i: (0,) * len(shape))


def tile_spec(rows, width, nt, down):
    if down:
        return pl.BlockSpec((rows, width), lambda i: (nt - 1 - i, 0))
    return pl.BlockSpec((rows, width), lambda i: (i, 0))


def run_spec(steps, width, nt, down):
    if down:
        return pl.BlockSpec((LANES, steps, width), lambda i: (0, nt - 1 - i, 0))
    return pl.BlockSpec((LANES, steps, width), lambda i: (0, i, 0))


def call(kernel, nt, args, outs, scratch, macs, name):
    arrays = [a for a, *_ in args]
    sizes = sum(a.size * a.dtype.itemsize for a in arrays + [a for a, *_ in outs])
    held = [
        a if keep is None else pltpu.with_memory_space_constraint(a, keep)
        for a, _, keep in map(filled, args)
    ]
    return pl.pallas_call(
        kernel,
        grid=(nt,),
        in_specs=[whole(a) if s is None else s for a, s, _ in map(filled, args)],
        out_specs=[whole(a) if s is None else s for a, s, _ in map(filled, outs)],
        out_shape=[
            a if keep is None else keep(a.shape, a.dtype) for a, _, keep in map(filled, outs)
        ],
        scratch_shapes=scratch,
        compiler_params=pltpu.CompilerParams(
            vmem_limit_bytes=VMEM_LIMIT, dimension_semantics=("arbitrary",)
        ),
        cost_estimate=pl.CostEstimate(flops=2 * macs, bytes_accessed=sizes, transcendentals=0),
        name=name,
    )(*held)


def filled(entry):
    return entry if len(entry) == 3 else entry + (pltpu.HBM,)


def shape(*dims, dtype=F32):
    return jax.ShapeDtypeStruct(dims, dtype)


def body(
    axes,
    tokens_in,
    seq_starts,
    norm_gain,
    norm_bias,
    decay_rate,
    step_log,
    frequency,
    in_proj,
    out_proj,
    skip_gain,
    gate_proj,
    grad_out,
):
    rows, width = tokens_in.shape
    states = in_proj.shape[-1]
    devices = 2 ** len(axes)
    tokens = float(rows * devices)
    run = rows // LANES
    steps = min(64, run)
    tile = steps * LANES
    nt = rows // tile
    span = min(32, steps)
    def tiles(array, down):
        return (array, tile_spec(tile, array.shape[-1], nt, down))

    def runs(array, down):
        return (array, run_spec(steps, array.shape[-1], nt, down))

    def full(array):
        return (array, None)

    def of(array, l):
        size = array.shape[1:]
        return (array, pl.BlockSpec((None,) + size, lambda i: (l,) + (0,) * len(size)))

    discs, tables, cuts = call(
        functools.partial(prep_kernel, rows, axes), 1,
        [full(seq_starts[None]), full(decay_rate),
         full(step_log), full(frequency)],
        [full(shape(LAYERS, 8, states)), full(shape(2 * LAYERS, 2, devices, 2 * SLOT, 128)),
         full(shape(2, LANES, 128, dtype=jnp.int32))],
        [], rows * width, "prep",
    )

    def near(entry):
        return entry[:2] + (pltpu.VMEM if rows * states * 4 <= 7 * 2**20 else pltpu.HBM,)

    tokens_run = tokens_in.reshape(LANES, run, width)
    grad_run = grad_out.reshape(LANES, run, width)
    state_scratch = pltpu.VMEM((LANES, states), F32)
    half_scratch = [pltpu.VMEM((tile, width), BF16)] * 2
    cost = rows * width * states

    u0_near, u0, order, stats = call(
        stats_kernel, nt, [runs(tokens_run, 0)],
        [near(tiles(shape(rows, width, dtype=BF16), 0)), tiles(shape(rows, width, dtype=BF16), 0),
         full(shape(span * LANES, span * LANES, dtype=BF16)),
         near(full(shape(devices, 2 * SLOT, 128)))],
        [], cost // 2, "stats",
    )

    def drive(l, stream, stats):
        down = l % 2
        return call(
            functools.partial(drive_kernel, l, bool(down), tokens), nt,
            [near(full(gather_all(stats, axes))), near(tiles(stream, down)), full(norm_gain), full(norm_bias), full(skip_gain), of(in_proj, l), of(discs, l),
               of(cuts, down)],
            [near(tiles(shape(rows, states), down)), near(full(shape(devices, 2 * SLOT, 128))),
             full(shape(LANES, states)), full(shape(8, width))],
            [], 4 * cost, f"drive_{l}",
        )

    b0, end0, blk0, norm0 = drive(0, u0_near, stats)
    u1_near, u1, low0, mixed0, gate0, stats = call(
        functools.partial(forward_kernel, False), nt,
        [near(full(gather_all(end0, axes))), of(tables, 2 * 0 + 0), near(tiles(b0, 0)), full(blk0), of(discs, 0), of(cuts, 0),
           near(tiles(u0_near, 0)), full(norm0), of(out_proj, 0), of(gate_proj, 0)],
        [near(tiles(shape(rows, width), 0)), tiles(shape(rows, width), 0), tiles(shape(rows, states, dtype=BF16), 0),
         tiles(shape(rows, width, dtype=BF16), 0), tiles(shape(rows, width, dtype=BF16), 0),
         near(full(shape(devices, 2 * SLOT, 128)))],
        [state_scratch], 6 * cost, "forward_0",
    )

    b1, end1, blk1, norm1 = drive(1, u1_near, stats)
    (
        out, low1, g1, pg1, sg1, w_sum1, aend1, ablk1
    ) = call(
        functools.partial(turn_kernel, True), nt,
        [near(full(gather_all(end1, axes))), of(tables, 2 * 1 + 0), near(tiles(b1, 1)), full(blk1), of(discs, 1), of(cuts, 1),
           of(cuts, 0), tiles(u1, 1), full(norm1), of(out_proj, 1), of(gate_proj, 1),
           runs(grad_run, 1), full(order)],
        [runs(shape(LANES, run, width), 1), near(tiles(shape(rows, states, dtype=BF16), 1)),
         near(tiles(shape(rows, width, dtype=BF16), 1)),
         near(tiles(shape(rows, width, dtype=BF16), 1)), near(tiles(shape(rows, states), 1)), full(shape(states + width + 8, width)),
         near(full(shape(devices, 2 * SLOT, 128))), full(shape(LANES, states))],
        [state_scratch, state_scratch] + half_scratch, 16 * cost, "turn_1",
    )

    def adjoint(l, sg, ablk, ends, low, stream, norm, pg, g, skip_sum=None):
        down = 1 - l % 2
        last = l == 0
        held = (lambda entry: entry) if last else near
        args = [
            near(full(ends)), of(tables, 2 * l + 1), held(tiles(sg, down)), full(ablk), of(discs, l),
            of(cuts, down), held(tiles(low, down)), tiles(stream, down),
            full(norm), held(tiles(pg, down)), held(tiles(g, down)), of(in_proj, l), full(order),
        ]
        scratch = [
            state_scratch, pltpu.VMEM((tile, states), BF16), state_scratch,
            pltpu.VMEM((tile, width), BF16),
        ]
        if last:
            args.append(full(skip_sum))
            outs = [
                runs(shape(LANES, run, width), down),
                full(shape(BLOCKS, (width + width // 2) // BLOCKS + SMALL, width)),
            ]
            scratch += [pltpu.VMEM((1, 2 * SLOT, 128), F32), pltpu.VMEM((width, states), F32)]
        else:
            outs = [
                tiles(shape(rows, width), down), full(shape(width + 8, states)),
                near(full(shape(devices, 2 * SLOT, 128))),
            ]
        return call(
            functools.partial(adjoint_kernel, bool(down), last), nt, args, outs, scratch,
            8 * cost, f"adjoint_{l}",
        )

    r1, in_sum1, norm_sum1 = adjoint(
        1, sg1, ablk1, gather_all(aend1, axes), low1, u1, norm1, pg1, g1
    )

    piece = (2 * width + states + width // 2) // BLOCKS + SMALL

    def lower(r1, norm_sum1):
        half = shape(BLOCKS // 2, (states + width) // BLOCKS, width)
        (
            g0, pg0, sg0, kept0, sent0, skip_sum0, aend0, ablk0, small1, _
        ) = call(
            functools.partial(back_kernel, True, tokens, axes[-1]), nt,
            [near(full(gather_all(norm_sum1, axes))), tiles(r1, 1), tiles(u1, 1), full(norm1),
             tiles(mixed0, 1), tiles(gate0, 1), tiles(low0, 1), tiles(u0, 1), full(norm0),
             of(out_proj, 0), of(gate_proj, 0), of(discs, 0), of(cuts, 1)],
            [tiles(shape(rows, width), 1), tiles(shape(rows, width, dtype=BF16), 1),
             tiles(shape(rows, states), 1), full(half), full(half), full(shape(1, width)), near(full(shape(devices, 2 * SLOT, 128))),
             full(shape(LANES, states)), full(shape(2 * SLOT, 128)), full(shape(2, width))],
            [pltpu.VMEM((states + width, width), F32)] + half_scratch, 12 * cost, "back_0",
        )
        core, chips, *others = phases(axes)
        part = kept0 + lax.ppermute(sent0, core[0], [(0, 1), (1, 0)])
        ends, part = lax.optimization_barrier((gather_all(aend0, axes), part))
        part = part.reshape(-1, width)
        part = scatter_sum(part, chips)
        r0, in_sum0 = adjoint(0, sg0, ablk0, ends, low0, u0, norm0, pg0, g0, skip_sum0)
        in_sum0, part = lax.optimization_barrier((in_sum0, part))
        in_part = scatter_sum(in_sum0.reshape(-1, width), core)
        share = line_scatter(part, others[0])
        in_part, share = lax.optimization_barrier((in_part, share))
        in_part = scatter_sum(in_part, chips)
        part = line_gather(share, others[0])
        for axes_left in others[1:]:
            part = line_gather(line_scatter(part, axes_left), axes_left)
        in_part, part = lax.optimization_barrier((in_part, part))
        count = in_part.shape[0]
        pad = -count % (8 * 2 ** len(others[0]))
        in_part = jnp.concatenate([in_part, jnp.zeros((pad, width), F32)], axis=0)
        part = jnp.concatenate([part, sum_all(in_part, others)[:count]], axis=0)
        pieces = gather_rows(gather_rows(part, chips), core)
        return r0.reshape(rows, width), small1, pieces.reshape(BLOCKS, -1, width)

    def nothing(r1, norm_sum1):
        return (
            jnp.zeros((rows, width), F32),
            jnp.zeros((2 * SLOT, 128), F32),
            jnp.zeros((BLOCKS, piece, width), F32),
        )

    w_all1, in_all1 = lax.psum((w_sum1, in_sum1), axes)
    r0, norm_all1, pieces = lax.cond(seq_starts[0] == 0, lower, nothing, r1, norm_sum1)

    gates, outs = width // BLOCKS, states // BLOCKS

    def block(array, *dims, at=lambda i: (i, 0)):
        return (array, pl.BlockSpec(dims, at))

    def flat(array, count):
        return block(array, count, array.shape[1])

    (
        grad_in, gain_grad, bias_grad, rate_grad, step_grad, freq_grad, in_grad, out_grad,
        skip_grad, gate_grad,
    ) = call(
        functools.partial(last_kernel, tokens), BLOCKS,
        [block(pieces, None, piece, width, at=lambda i: (i, 0, 0)) + (None,),
         block(pieces, None, SMALL, width, at=lambda i: (0, piece // SMALL - 1, 0)) + (None,),
         flat(w_all1, outs),
         block(w_all1, gates, width, at=lambda i: (states // gates + i, 0)),
         block(w_all1, 8, width, at=lambda i: ((states + width) // 8, 0)),
         flat(in_all1, gates),
         block(in_all1, 8, states, at=lambda i: (width // 8, 0)),
         full(norm_all1), full(discs), full(decay_rate), full(step_log), full(frequency),
         flat(r0, rows // BLOCKS), flat(tokens_in, rows // BLOCKS), full(norm0)],
        [flat(shape(rows, width), rows // BLOCKS), full(shape(LAYERS, width)),
         full(shape(LAYERS, width)), full(shape(LAYERS, states // 2)),
         full(shape(LAYERS, states // 2)), full(shape(LAYERS, states // 2)),
         block(shape(LAYERS, width, states), LAYERS, gates, states, at=lambda i: (0, i, 0)),
         block(shape(LAYERS, states, width), LAYERS, outs, width, at=lambda i: (0, i, 0)),
         full(shape(LAYERS, width)),
         block(shape(LAYERS, width, width), LAYERS, gates, width, at=lambda i: (0, i, 0))],
        [], cost, "last",
    )
    return (
        out.reshape(rows, width),
        grad_in,
        gain_grad,
        bias_grad,
        rate_grad,
        step_grad,
        freq_grad,
        in_grad,
        out_grad,
        skip_grad,
        gate_grad,
    )


def solution(mesh):
    bits = mesh.devices.size.bit_length() - 1
    axes = tuple("b%d" % k for k in range(bits))
    binary = Mesh(mesh.devices.reshape((2,) * bits), axes)
    rows = P(axes, None)
    return jax.shard_map(
        functools.partial(body, axes),
        mesh=binary,
        in_specs=(rows,) + (P(),) * 10 + (rows,),
        out_specs=(rows, rows) + (P(),) * 9,
        check_vma=False,
    )
```

```python
import functools

import jax
import jax.numpy as jnp
from jax import lax
from jax.experimental import pallas as pl
from jax.experimental.pallas import tpu as pltpu
from jax.sharding import Mesh, PartitionSpec as P

LAYERS = 2
EPSILON = 1e-05
SMALL = 8
BLOCKS = 8
SLOT = 4
LANES = 8
VMEM_LIMIT = 30 * 1024 * 1024
GELU_A = 0.7978845608028654
GELU_B = 0.044715
NT = (((1,), (1,)), ((), ()))
TN = (((0,), (0,)), ((), ()))
F32 = jnp.float32
BF16 = jnp.bfloat16


def gather_all(copies, axes):
    return lax.all_to_all(copies, axes, 0, 0)


def scatter_sum(value, axes):
    count = 2 ** len(axes)
    pieces = value.reshape((count, value.shape[0] // count) + value.shape[1:])
    return jnp.sum(lax.all_to_all(pieces, axes, 0, 0), axis=0)


def gather_rows(value, axes):
    count = 2 ** len(axes)
    copies = jnp.broadcast_to(value, (count,) + value.shape)
    return lax.all_to_all(copies, axes, 0, 0).reshape((count * value.shape[0],) + value.shape[1:])


def phases(axes):
    left, out = list(axes), [(axes[-1],)]
    left = left[:-1]
    while left:
        out.append(tuple(left[-2:]))
        left = left[:-2]
    return out


def place_in(axes):
    place = 0
    for axis in axes:
        place = 2 * place + lax.axis_index(axis)
    return place


def traded(value, axes, mask):
    count = 2 ** len(axes)
    return lax.ppermute(value, axes, [(i, i ^ mask) for i in range(count)])


def line_scatter(value, axes):
    count = 2 ** len(axes)
    me = place_in(axes)
    pieces = value.reshape((count, value.shape[0] // count) + value.shape[1:])

    def piece(mask):
        return lax.dynamic_index_in_dim(pieces, me ^ mask, 0, keepdims=False)

    got = [traded(piece(mask), axes, mask) for mask in range(1, count)]
    return functools.reduce(jnp.add, got, piece(0))


def line_gather(value, axes):
    count = 2 ** len(axes)
    me = place_in(axes)
    got = [traded(value, axes, mask) for mask in range(1, count)]
    rows = []
    for j in range(count):
        row = value
        for mask in range(1, count):
            row = jnp.where(me == j ^ mask, got[mask - 1], row)
        rows.append(row)
    return jnp.concatenate(rows, axis=0)


def cols(c):
    return slice(c * 128, (c + 1) * 128)


def chunk_count(ref):
    return ref.shape[-1] // 256


def rows_of(ref, at, chunks):
    half = chunks * 128
    re = [ref[at, c * 128 : (c + 1) * 128] for c in range(chunks)]
    im = [ref[at, half + c * 128 : half + (c + 1) * 128] for c in range(chunks)]
    return re, im


def put_rows(ref, at, re, im):
    chunks = len(re)
    half = chunks * 128
    for c in range(chunks):
        ref[at, c * 128 : (c + 1) * 128] = re[c]
        ref[at, half + c * 128 : half + (c + 1) * 128] = im[c]


def put_copies(ref, re, im):
    ref[0] = jnp.zeros(ref.shape[1:], F32)
    for c in range(len(re)):
        ref[0, c : c + 1] = re[c]
        ref[0, SLOT + c : SLOT + c + 1] = im[c]
    ref[...] = jnp.broadcast_to(ref[0:1], ref.shape)


def wide(rows):
    return [jnp.broadcast_to(v, (LANES, 128)) for v in rows]


def chain(ends_ref, jr_ref, power, carry, down, start_ref=None):
    chunks = len(power[0])
    pr, pi = power
    cr, ci = carry
    order = range(LANES - 1, -1, -1) if down else range(LANES)
    for s in order:
        at = slice(s, s + 1)
        if start_ref is not None:
            put_rows(start_ref, at, cr, ci)
        er, ei = rows_of(ends_ref, at, chunks)
        alive = (jr_ref[at, :] < 0).astype(F32)
        cr, ci = (
            [er[c] + alive * (pr[c] * cr[c] - pi[c] * ci[c]) for c in range(chunks)],
            [ei[c] + alive * (pr[c] * ci[c] + pi[c] * cr[c]) for c in range(chunks)],
        )
    return cr, ci


def carry_in(ends_ref, table_ref, chunks):
    total = jnp.zeros((2 * SLOT, 128), F32)
    for e in range(ends_ref.shape[0]):
        end = ends_ref[e]
        turned = jnp.concatenate([end[SLOT:], end[:SLOT]], axis=0)
        total += table_ref[0, e] * end + table_ref[1, e] * turned
    return (
        [total[c : c + 1] for c in range(chunks)],
        [total[SLOT + c : SLOT + c + 1] for c in range(chunks)],
    )


def in_stages(stages, parts):
    for turn in range(len(parts) + len(stages) - 1):
        for k, stage in enumerate(stages):
            if 0 <= turn - k < len(parts):
                stage(parts[turn - k])


def parts_of(rows, down, count=2):
    size = rows // count
    parts = [(at, at + size) for at in range(0, rows, size)]
    return parts[::-1] if down else parts


class Scan:
    def __init__(self, src_ref, st_ref, decay, jr_ref, first_step, down):
        self.src_ref, self.st_ref, self.down = src_ref, st_ref, down
        self.chunks = chunk_count(src_ref)
        self.dr, self.di = wide(decay[0]), wide(decay[1])
        self.jr, self.first_step = jr_ref[...], first_step
        self.state = rows_of(st_ref, slice(0, LANES), self.chunks)

    def one(self, step):
        br, bi = rows_of(self.src_ref, slice(step * LANES, (step + 1) * LANES), self.chunks)
        live = self.jr != self.first_step + step
        nr, ni = [], []
        for c in range(self.chunks):
            xr = jnp.where(live, self.state[0][c], 0.0)
            xi = jnp.where(live, self.state[1][c], 0.0)
            nr.append(self.dr[c] * xr - self.di[c] * xi + br[c])
            ni.append(self.dr[c] * xi + self.di[c] * xr + bi[c])
        self.state = (nr, ni)
        return nr, ni

    def run(self, part, emit=None):
        low, high = part[0] // LANES, part[1] // LANES
        for n in range(0, high - low, 2):
            step = high - 2 - n if self.down else low + n
            first = self.one(step + 1 if self.down else step)
            second = self.one(step if self.down else step + 1)
            if emit is not None:
                pair = (second, first) if self.down else (first, second)
                emit(slice(step * LANES, (step + 2) * LANES), pair)

    def close(self):
        put_rows(self.st_ref, slice(0, LANES), *self.state)


def store_pair(ref, at, first, second):
    re = [jnp.concatenate([p, q], axis=0).astype(BF16) for p, q in zip(first[0], second[0])]
    im = [jnp.concatenate([p, q], axis=0).astype(BF16) for p, q in zip(first[1], second[1])]
    put_rows(ref, at, re, im)


def disc_row(disc_ref, row, chunks, conj=False):
    re, im = rows_of(disc_ref, slice(row, row + 1), chunks)
    return (re, [-v for v in im]) if conj else (re, im)


def column_sum(value):
    rows, width = value.shape
    return jnp.sum(jnp.sum(value.reshape(rows // 8, 8, width), axis=0), axis=0, keepdims=True)


def permute_in(block_ref, order_ref, part):
    runs, _, width = block_ref.shape
    size = order_ref.shape[0]
    span = size // runs
    out = []
    for k in range(part[0] // size, part[1] // size):
        rows = block_ref[:, k * span : (k + 1) * span, :].reshape(size, width)
        out.append(jnp.dot(order_ref[...], rows, preferred_element_type=F32))
    return out[0] if len(out) == 1 else jnp.concatenate(out, axis=0)


def permute_out(value, order_ref, out_ref, part):
    width = value.shape[1]
    size = order_ref.shape[0]
    span = size // LANES
    high = value.astype(BF16)
    low = (value - high.astype(F32)).astype(BF16)
    for n, k in enumerate(range(part[0] // size, part[1] // size)):
        at = slice(n * size, (n + 1) * size)
        back = lax.dot_general(order_ref[...], high[at], TN, preferred_element_type=F32)
        back += lax.dot_general(order_ref[...], low[at], TN, preferred_element_type=F32)
        out_ref[:, k * span : (k + 1) * span, :] = back.reshape(LANES, span, width)


def expm1(value):
    acc = jnp.full_like(value, 1.0 / 479001600.0)
    for n in (39916800.0, 3628800.0, 362880.0, 40320.0, 5040.0, 720.0, 120.0, 24.0, 6.0, 2.0, 1.0):
        acc = acc * value + 1.0 / n
    return jnp.where(value > -1.0, acc * value, jnp.exp(value) - 1.0)


def prep_kernel(
    rows, axes, starts_ref, rate_ref, step_ref, freq_ref,
    disc_ref, table_ref, cut_ref,
):
    devices = 2 ** len(axes)
    total = rows * devices
    run = rows // LANES
    half = rate_ref.shape[-1]
    me = 0
    for axis in axes:
        me = 2 * me + lax.axis_index(axis)
    starts = [starts_ref[:, k : k + 1] for k in range(starts_ref.shape[1])]

    base = me * rows + run * lax.broadcasted_iota(jnp.int32, (LANES, 128), 0)
    up = jnp.full((LANES, 128), -1, jnp.int32)
    down = up
    for begin in starts + [total]:
        rel = begin - base
        up = jnp.maximum(up, jnp.where((rel >= 0) & (rel < run), rel, -1))
        down = jnp.maximum(down, jnp.where((rel >= 1) & (rel <= run), rel - 1, -1))
    cut_ref[0] = up
    cut_ref[1] = down

    source = lax.broadcasted_iota(jnp.int32, (devices, half), 0)
    for l in range(LAYERS):
        row = slice(l, l + 1)
        rate, freq = rate_ref[row], freq_ref[row]
        step_size = jnp.exp(step_ref[row])
        real_angle = -rate * step_size
        imag_angle = freq * step_size
        magnitude = jnp.exp(real_angle)
        cosine, sine = jnp.cos(imag_angle), jnp.sin(imag_angle)
        minus_real = expm1(real_angle) * cosine - 2.0 * jnp.sin(0.5 * imag_angle) ** 2
        minus_imag = magnitude * sine
        modulus = rate * rate + freq * freq
        disc_ref[l, 0:1, :half] = magnitude * cosine
        disc_ref[l, 0:1, half:] = minus_imag
        disc_ref[l, 1:2, :half] = (-rate * minus_real + freq * minus_imag) / modulus
        disc_ref[l, 1:2, half:] = (-rate * minus_imag - freq * minus_real) / modulus
        magnitude = jnp.exp(real_angle * float(run))
        disc_ref[l, 2:3, :half] = magnitude * jnp.cos(imag_angle * float(run))
        disc_ref[l, 2:3, half:] = magnitude * jnp.sin(imag_angle * float(run))
        disc_ref[l, 3:8] = jnp.zeros((5, 2 * half), F32)
        powers = []
        for bit in range(len(axes)):
            magnitude = jnp.exp(real_angle * float(rows << bit))
            angle = imag_angle * float(rows << bit)
            powers.append((magnitude * jnp.cos(angle), magnitude * jnp.sin(angle)))
        for back in range(2):
            going_down = (l + back) % 2 == 1
            if going_down:
                live, count = source > me, source - me - 1
            else:
                live, count = source < me, me - 1 - source
            for begin in starts:
                if going_down:
                    cut = (begin > (me + 1) * rows) & (source * rows >= begin)
                else:
                    cut = (begin < me * rows) & ((source + 1) * rows <= begin)
                live &= ~cut
            count = jnp.maximum(count, 0)
            real = live.astype(F32)
            imag = jnp.zeros((devices, half), F32)
            for bit, (pr, pi) in enumerate(powers):
                use = (count & (1 << bit)) != 0
                pr, pi = jnp.where(use, pr, 1.0), jnp.where(use, pi, 0.0)
                real, imag = real * pr - imag * pi, real * pi + imag * pr
            imag = -imag if back else imag
            at = 2 * l + back
            table_ref[at] = jnp.zeros(table_ref.shape[1:], F32)
            for c in range(half // 128):
                table_ref[at, 0, :, c, :] = real[:, cols(c)]
                table_ref[at, 0, :, SLOT + c, :] = real[:, cols(c)]
                table_ref[at, 1, :, c, :] = -imag[:, cols(c)]
                table_ref[at, 1, :, SLOT + c, :] = imag[:, cols(c)]


def stats_kernel(tok_ref, u_ref, copy_ref, order_ref, stats_ref):
    @pl.when(pl.program_id(0) == 0)
    def _():
        size = order_ref.shape[0]
        span = size // LANES
        to = lax.broadcasted_iota(jnp.int32, (size, size), 0)
        back = lax.broadcasted_iota(jnp.int32, (size, size), 1)
        order_ref[...] = ((to % LANES) * span + to // LANES == back).astype(F32).astype(BF16)

    value = permute_in(tok_ref, order_ref, (0, u_ref.shape[0]))
    u_ref[...] = value.astype(BF16)
    copy_ref[...] = u_ref[...]
    zero_first(stats_ref)
    add_stats(stats_ref, value)
    spread_last(stats_ref)


def add_stats(stats_ref, value):
    add_rows(stats_ref, column_sum(value), column_sum(value * value))


def add_rows(copies_ref, first, second):
    for c in range(first.shape[1] // 128):
        copies_ref[0, c : c + 1] += first[:, cols(c)]
        copies_ref[0, SLOT + c : SLOT + c + 1] += second[:, cols(c)]


def summed(ref):
    total = jnp.sum(ref[...], axis=0)
    return tuple(
        jnp.concatenate([total[SLOT * k + c : SLOT * k + c + 1] for c in range(SLOT)], axis=1)
        for k in range(2)
    )


def drive_kernel(layer, down, tokens, *refs):
    (
        stat_ref, u_ref, gain_ref, bias_ref, skip_ref, win_ref, disc_ref, jr_ref,
        b_ref, end_ref, blk_ref, norm_ref,
    ) = refs
    i, nt = pl.program_id(0), pl.num_programs(0)
    steps = u_ref.shape[0] // LANES
    chunks = chunk_count(b_ref)
    half = chunks * 128

    @pl.when(i == 0)
    def _():
        total, squares = summed(stat_ref)
        row = slice(layer, layer + 1)
        mean = total / tokens
        inv = lax.rsqrt(squares / tokens - mean * mean + EPSILON)
        norm_ref[0:1] = mean
        norm_ref[1:2] = inv
        norm_ref[2:3] = inv * gain_ref[row]
        norm_ref[3:4] = bias_ref[row]
        norm_ref[4:5] = skip_ref[row]
        norm_ref[5:8] = jnp.zeros((3, norm_ref.shape[1]), F32)
        blk_ref[...] = jnp.zeros_like(blk_ref)

    fr, fi = disc_ref[1:2, :half], disc_ref[1:2, half:]
    tile = nt - 1 - i if down else i
    scan = Scan(b_ref, blk_ref, disc_row(disc_ref, 0, chunks), jr_ref, tile * steps, down)

    def product(part):
        at = slice(*part)
        u = u_ref[at].astype(F32)
        normed = (u - norm_ref[0:1]) * norm_ref[2:3] + norm_ref[3:4]
        drive = jnp.dot(normed.astype(BF16), win_ref[...], preferred_element_type=F32)
        re, im = drive[:, :half], drive[:, half:]
        b_ref[at, :half] = re * fr - im * fi
        b_ref[at, half:] = re * fi + im * fr

    in_stages([product, scan.run], parts_of(b_ref.shape[0], down, 4))
    scan.close()

    @pl.when(i == nt - 1)
    def _():
        zero = [jnp.zeros((1, 128), F32)] * chunks
        cr, ci = chain(blk_ref, jr_ref, disc_row(disc_ref, 2, chunks), (zero, zero), down)
        put_copies(end_ref, cr, ci)


def states_scan(ends_ref, table_ref, b_ref, blk_ref, disc_ref, jr_ref, low_ref, st_ref, down):
    i, nt = pl.program_id(0), pl.num_programs(0)
    chunks = chunk_count(b_ref)
    steps = b_ref.shape[0] // LANES

    @pl.when(i == 0)
    def _():
        carry = carry_in(ends_ref, table_ref, chunks)
        chain(blk_ref, jr_ref, disc_row(disc_ref, 2, chunks), carry, down, st_ref)

    tile = nt - 1 - i if down else i
    scan = Scan(b_ref, st_ref, disc_row(disc_ref, 0, chunks), jr_ref, tile * steps, down)

    def stage(part):
        scan.run(part, lambda at, pair: store_pair(low_ref, at, *pair))

    return scan, stage


def gelu_parts(mixed):
    square = mixed * mixed
    tanh = jnp.tanh(mixed * (GELU_A + (GELU_A * GELU_B) * square))
    half_up = 0.5 + 0.5 * tanh
    return square, tanh, half_up


def gelu_slope(mixed, square, tanh, half_up):
    return half_up + (mixed * (0.5 - 0.5 * tanh * tanh)) * (
        GELU_A + (3.0 * GELU_A * GELU_B) * square
    )


def sigmoid(value):
    return 0.5 + 0.5 * jnp.tanh(0.5 * value)


def forward_kernel(down, *refs):
    (
        ends_ref, table_ref, b_ref, blk_ref, disc_ref, jr_ref, u_ref, norm_ref, wout_ref, wgate_ref,
        next_ref, copy_ref, low_ref, mixed_ref, gate_ref, stats_ref, st_ref,
    ) = refs
    scan, states = states_scan(
        ends_ref, table_ref, b_ref, blk_ref, disc_ref, jr_ref, low_ref, st_ref, down
    )
    zero_first(stats_ref)
    acts = {}

    def mix(part):
        at = slice(*part)
        u = u_ref[at].astype(F32)
        normed = (u - norm_ref[0:1]) * norm_ref[2:3] + norm_ref[3:4]
        mixed = jnp.dot(low_ref[at], wout_ref[...], preferred_element_type=F32)
        mixed += norm_ref[4:5] * normed
        _, _, half_up = gelu_parts(mixed)
        acts[part] = mixed * half_up
        mixed_ref[at] = mixed.astype(BF16)

    def finish(part):
        at = slice(*part)
        act = acts[part]
        gate = sigmoid(jnp.dot(act.astype(BF16), wgate_ref[...], preferred_element_type=F32))
        after = u_ref[at].astype(F32) + act * gate
        next_ref[at] = after
        copy_ref[at] = after
        gate_ref[at] = gate.astype(BF16)
        add_stats(stats_ref, after)

    in_stages([states, mix, finish], parts_of(b_ref.shape[0], down))
    scan.close()
    spread_last(stats_ref)


def zero_first(*refs):
    @pl.when(pl.program_id(0) == 0)
    def _():
        for ref in refs:
            ref[...] = jnp.zeros(ref.shape, ref.dtype)


def spread_last(ref):
    @pl.when(pl.program_id(0) == pl.num_programs(0) - 1)
    def _():
        ref[...] = jnp.broadcast_to(ref[0:1], ref.shape)


class GateBackward:
    def __init__(self, low_ref, wout_ref, wgate_ref, pg_ref, sg_ref, wsum_ref, ssum_ref, acts):
        self.low_ref, self.wout_ref, self.wgate_ref = low_ref, wout_ref, wgate_ref
        self.pg_ref, self.sg_ref = pg_ref, sg_ref
        self.wsum_ref, self.ssum_ref = wsum_ref, ssum_ref
        self.act_ref, self.logit_ref = acts
        self.kept = {}

    def enter(self, part, g, mixed, gate, normed, kept=None):
        at = slice(*part)
        square, tanh, half_up = gelu_parts(mixed) if kept is None else kept
        act = mixed * half_up
        g_gate = g * gate
        if kept is None:
            self.act_ref[at] = act.astype(BF16)
        self.logit_ref[at] = (g_gate * act * (1.0 - gate)).astype(BF16)
        self.kept[part] = (g_gate, gelu_slope(mixed, square, tanh, half_up), normed)

    def middle(self, part):
        at = slice(*part)
        g_gate, slope, normed = self.kept[part]
        act_grad = g_gate + lax.dot_general(
            self.logit_ref[at], self.wgate_ref[...], NT, preferred_element_type=F32
        )
        mixed_grad = act_grad * slope
        self.ssum_ref[...] += column_sum(mixed_grad * normed)
        self.pg_ref[at] = mixed_grad.astype(BF16)

    def leave(self, part):
        at = slice(*part)
        self.sg_ref[at] = lax.dot_general(
            self.pg_ref[at], self.wout_ref[...], NT, preferred_element_type=F32
        )

    def sums(self):
        states, width = self.wout_ref.shape
        self.wsum_ref[states : states + width] += lax.dot_general(
            self.act_ref[...], self.logit_ref[...], TN, preferred_element_type=F32
        )
        self.wsum_ref[:states] += lax.dot_general(
            self.low_ref[...], self.pg_ref[...], TN, preferred_element_type=F32
        )


def turn_kernel(down, *refs):
    (
        ends_ref, table_ref, b_ref, blk_ref, disc_ref, jr_ref, jo_ref, u_ref, norm_ref, wout_ref, wgate_ref,
        gout_ref, order_ref,
        out_ref, low_ref, g_ref, pg_ref, sg_ref, wsum_ref, end_ref, ablk_ref,
        st_ref, w_ref, act_ref, logit_ref,
    ) = refs
    sums = wout_ref.shape[0] + wout_ref.shape[1]
    ssum_ref = wsum_ref.at[sums : sums + 1]
    i, nt = pl.program_id(0), pl.num_programs(0)
    chunks = chunk_count(b_ref)
    half = chunks * 128
    steps = b_ref.shape[0] // LANES
    tile = nt - 1 - i if down else i
    scan, states = states_scan(
        ends_ref, table_ref, b_ref, blk_ref, disc_ref, jr_ref, low_ref, st_ref, down
    )
    back = GateBackward(
        low_ref, wout_ref, wgate_ref, pg_ref, sg_ref, wsum_ref, ssum_ref, (act_ref, logit_ref)
    )

    @pl.when(i == 0)
    def _():
        wsum_ref[...] = jnp.zeros(wsum_ref.shape, F32)
        ablk_ref[...] = jnp.zeros(ablk_ref.shape, F32)
        w_ref[:, :half] = jnp.ones((LANES, half), F32)
        w_ref[:, half:] = jnp.zeros((LANES, half), F32)

    mid = {}

    def mix(part):
        at = slice(*part)
        u = u_ref[at]
        normed = (u - norm_ref[0:1]) * norm_ref[2:3] + norm_ref[3:4]
        mixed = jnp.dot(low_ref[at], wout_ref[...], preferred_element_type=F32)
        mixed += norm_ref[4:5] * normed
        kept = gelu_parts(mixed)
        act_ref[at] = (mixed * kept[2]).astype(BF16)
        mid[part] = (normed, mixed, kept)

    def enter(part):
        at = slice(*part)
        normed, mixed, kept = mid[part]
        gate = sigmoid(jnp.dot(act_ref[at], wgate_ref[...], preferred_element_type=F32))
        permute_out(u_ref[at] + (mixed * kept[2]) * gate, order_ref, out_ref, part)
        g = permute_in(gout_ref, order_ref, part)
        g_ref[at] = g.astype(BF16)
        back.enter(part, g, mixed, gate, normed, kept)

    dr, di = disc_row(disc_ref, 0, chunks, conj=True)
    dr, di = wide(dr), wide(di)
    jo = jo_ref[...]
    live = {
        "w": rows_of(w_ref, slice(0, LANES), chunks),
        "a": rows_of(ablk_ref, slice(0, LANES), chunks),
    }

    def weigh(part):
        (wr, wi), (ar, ai) = (tuple(map(list, live[k])) for k in "wa")
        order = range(part[0] // LANES, part[1] // LANES)
        for step in reversed(order) if down else order:
            sr, si = rows_of(sg_ref, slice(step * LANES, (step + 1) * LANES), chunks)
            keep = jo != tile * steps + step
            for c in range(chunks):
                ar[c] = ar[c] + (wr[c] * sr[c] - wi[c] * si[c])
                ai[c] = ai[c] + (wr[c] * si[c] + wi[c] * sr[c])
                xr = jnp.where(keep, wr[c], 0.0)
                xi = jnp.where(keep, wi[c], 0.0)
                wr[c] = xr * dr[c] - xi * di[c]
                wi[c] = xr * di[c] + xi * dr[c]
        live["w"], live["a"] = (wr, wi), (ar, ai)

    in_stages(
        [states, mix, enter, back.middle, back.leave, weigh], parts_of(b_ref.shape[0], down)
    )
    back.sums()
    scan.close()
    put_rows(w_ref, slice(0, LANES), *live["w"])
    put_rows(ablk_ref, slice(0, LANES), *live["a"])

    @pl.when(i == nt - 1)
    def _():
        zero = [jnp.zeros((1, 128), F32)] * chunks
        power = disc_row(disc_ref, 2, chunks, conj=True)
        cr, ci = chain(ablk_ref, jo_ref, power, (zero, zero), not down)
        put_copies(end_ref, cr, ci)


def adjoint_kernel(down, last, *refs):
    (
        ends_ref, table_ref, sg_ref, ablk_ref, disc_ref, jr_ref, low_ref, u_ref, norm_ref, pg_ref, g_ref,
        win_ref, order_ref, *refs
    ) = refs
    if last:
        (
            ssum_ref, res_ref, sums_ref, st_ref, dg_ref, ax_ref, low_normed_ref, nsum_ref, isum_ref,
        ) = refs
    else:
        (res_ref, sums_ref, nsum_ref, st_ref, dg_ref, ax_ref, low_normed_ref) = refs
        isum_ref = sums_ref
    width, states = win_ref.shape
    i, nt = pl.program_id(0), pl.num_programs(0)
    chunks = chunk_count(sg_ref)
    half = chunks * 128
    steps = sg_ref.shape[0] // LANES
    tile = nt - 1 - i if down else i

    @pl.when(i == 0)
    def _():
        carry = carry_in(ends_ref, table_ref, chunks)
        power = disc_row(disc_ref, 2, chunks, conj=True)
        chain(ablk_ref, jr_ref, power, carry, down, st_ref)
        ax_ref[...] = jnp.zeros_like(ax_ref)

    zero_first(isum_ref, nsum_ref)
    fr, fi = disc_row(disc_ref, 1, chunks)
    fr, fi = wide(fr), wide(fi)
    decay = disc_row(disc_ref, 0, chunks, conj=True)
    scan = Scan(sg_ref, st_ref, decay, jr_ref, tile * steps, down)
    sums = tuple(map(list, rows_of(ax_ref, slice(0, LANES), chunks)))

    def emit(at, pair):
        xr, xi = rows_of(low_ref, at, chunks)
        xr, xi = [v.astype(F32) for v in xr], [v.astype(F32) for v in xi]
        grads = []
        for which, (ar, ai) in enumerate(pair):
            gr, gi = [], []
            rows = slice(which * LANES, (which + 1) * LANES)
            for c in range(chunks):
                vr, vi = xr[c][rows], xi[c][rows]
                sums[0][c] = sums[0][c] + (ar[c] * vr + ai[c] * vi)
                sums[1][c] = sums[1][c] + (ai[c] * vr - ar[c] * vi)
                gr.append(ar[c] * fr[c] + ai[c] * fi[c])
                gi.append(ai[c] * fr[c] - ar[c] * fi[c])
            grads.append((gr, gi))
        store_pair(dg_ref, at, *grads)

    def finish(part):
        at = slice(*part)
        centered = u_ref[at].astype(F32) - norm_ref[0:1]
        low_normed_ref[at] = (centered * norm_ref[2:3] + norm_ref[3:4]).astype(BF16)
        normed_grad = lax.dot_general(dg_ref[at], win_ref[...], NT, preferred_element_type=F32)
        normed_grad += norm_ref[4:5] * pg_ref[at].astype(F32)
        add_rows(
            nsum_ref, column_sum(normed_grad), column_sum(normed_grad * centered) * norm_ref[1:2]
        )
        result = g_ref[at].astype(F32) + norm_ref[2:3] * normed_grad
        if last:
            permute_out(result, order_ref, res_ref, part)
        else:
            res_ref[at] = result

    in_stages([lambda part: scan.run(part, emit), finish], parts_of(sg_ref.shape[0], down))
    isum_ref[:width] += lax.dot_general(
        low_normed_ref[...], dg_ref[...], TN, preferred_element_type=F32
    )
    scan.close()
    put_rows(ax_ref, slice(0, LANES), *sums)
    spread_last(nsum_ref)

    @pl.when(i == nt - 1)
    def _():
        decays = jnp.sum(ax_ref[...], axis=0, keepdims=True)
        wr, wi = win_ref[:, :half].astype(F32), win_ref[:, half:].astype(F32)
        gr, gi = isum_ref[:width, :half], isum_ref[:width, half:]
        re = jnp.sum(wr * gr + wi * gi, axis=0, keepdims=True)
        im = jnp.sum(wr * gi - wi * gr, axis=0, keepdims=True)
        gr, gi = disc_ref[1:2, :half], disc_ref[1:2, half:]
        scale = 1.0 / (gr * gr + gi * gi)
        factors = ((re * gr - im * gi) * scale, (re * gi + im * gr) * scale)
        if last:
            rows = width // BLOCKS
            first = rows + rows // 2
            for b in range(BLOCKS):
                at = b * rows
                sums_ref[b, :rows] = isum_ref[at : at + rows, :width]
                sums_ref[b, rows:first, : states - width] = isum_ref[at : at + rows // 2, width:]
                sums_ref[b, rows:first, states - width :] = isum_ref[
                    at + rows // 2 : at + rows, width:
                ]
                sums_ref[b, first:] = jnp.zeros((SMALL, width), F32)
            small = [nsum_ref[0]] + [ssum_ref[:, cols(c)] for c in range(width // 128)]
            small += [decays[:, cols(c)] for c in range(2 * chunks)]
            small += [v[:, cols(c)] for v in factors for c in range(chunks)]
            small = [v[r : r + 1] for v in small for r in range(v.shape[0])]
            for k, row in enumerate(small):
                at = (k % SMALL, k // SMALL)
                sums_ref[0, first + at[0] : first + at[0] + 1, cols(at[1])] = row
        else:
            sums_ref[width : width + 1] = decays
            sums_ref[width + 1 : width + 2, :half] = factors[0]
            sums_ref[width + 1 : width + 2, half:] = factors[1]


def back_kernel(down, tokens, core, *refs):
    (
        sums_ref, r_ref, up_ref, up_norm_ref, mixed_ref, gate_ref, low_ref, u_ref, norm_ref, wout_ref,
        wgate_ref, disc_ref, jo_ref,
        g_ref, pg_ref, sg_ref, kept_ref, sent_ref, ssum_ref, end_ref, ablk_ref, nsum_ref, bsum_ref, wsum_ref,
        act_ref, logit_ref,
    ) = refs
    i, nt = pl.program_id(0), pl.num_programs(0)
    chunks = chunk_count(sg_ref)
    steps = sg_ref.shape[0] // LANES
    tile = nt - 1 - i if down else i

    @pl.when(i == 0)
    def _():
        nsum_ref[...] = jnp.sum(sums_ref[...], axis=0)
        bsum_ref[0:1], bsum_ref[1:2] = summed(sums_ref)

    zero_first(ablk_ref, wsum_ref, ssum_ref)
    back = GateBackward(
        low_ref, wout_ref, wgate_ref, pg_ref, sg_ref, wsum_ref, ssum_ref, (act_ref, logit_ref)
    )
    decay = disc_row(disc_ref, 0, chunks, conj=True)
    scan = Scan(sg_ref, ablk_ref, decay, jo_ref, tile * steps, down)
    scale = up_norm_ref[2:3] * (-1.0 / tokens)

    def enter(part):
        at = slice(*part)
        standard = (up_ref[at] - up_norm_ref[0:1]) * (scale * up_norm_ref[1:2] * bsum_ref[1:2])
        g = r_ref[at] + (standard + scale * bsum_ref[0:1])
        g_ref[at] = g
        u = u_ref[at].astype(F32)
        normed = (u - norm_ref[0:1]) * norm_ref[2:3] + norm_ref[3:4]
        back.enter(part, g, mixed_ref[at].astype(F32), gate_ref[at].astype(F32), normed)

    in_stages([enter, back.middle, back.leave, scan.run], parts_of(sg_ref.shape[0], down))
    back.sums()
    scan.close()

    @pl.when(i == nt - 1)
    def _():
        zero = [jnp.zeros((1, 128), F32)] * chunks
        power = disc_row(disc_ref, 2, chunks, conj=True)
        cr, ci = chain(ablk_ref, jo_ref, power, (zero, zero), down)
        put_copies(end_ref, cr, ci)
        states, width = wout_ref.shape
        gates, outs = width // BLOCKS, states // BLOCKS
        side = lax.axis_index(core)
        for ref, first in ((kept_ref, side), (sent_ref, 1 - side)):
            for b in range(BLOCKS // 2):
                at = first * (BLOCKS // 2) + b
                ref[b, :gates] = wsum_ref[pl.ds(pl.multiple_of(states + at * gates, 8), gates)]
                ref[b, gates:] = wsum_ref[pl.ds(pl.multiple_of(at * outs, 8), outs)]


def last_kernel(
    tokens, piece_ref, small_ref, out1_ref, gate1_ref, skip1_ref, in1_ref, decay1_ref, norm1_ref,
    disc_ref, rate_ref, step_ref, freq_ref, r_ref, tok_ref, norm_ref,
    grad_in_ref, gain_ref, bias_ref, drate_ref, dstep_ref, dfreq_ref, in_ref, out_ref, skip_ref,
    gate_ref,
):
    gates, width = gate1_ref.shape
    outs = out1_ref.shape[0]
    states = in1_ref.shape[1]
    half = states // 2
    left = states - width
    gate_ref[0], gate_ref[1] = piece_ref[:gates], gate1_ref[...]
    out_ref[0], out_ref[1] = piece_ref[gates : gates + outs], out1_ref[...]
    at = gates + outs
    in_ref[0, :, :width] = piece_ref[at : at + gates]
    at += gates
    in_ref[0, : gates // 2, width:] = piece_ref[at : at + gates // 2, :left]
    in_ref[0, gates // 2 :, width:] = piece_ref[at : at + gates // 2, left:]
    in_ref[1] = in1_ref[...]

    def row(ref, first, count):
        places = [(k % SMALL, k // SMALL) for k in range(first, first + count)]
        return jnp.concatenate([ref[r : r + 1, cols(c)] for r, c in places], axis=1)

    count = width // 128
    bias, gain = row(small_ref, 0, count), row(small_ref, count, count)
    scale = norm_ref[2:3] * (-1.0 / tokens)
    grad_in_ref[...] = r_ref[...] + (
        (tok_ref[...].astype(F32) - norm_ref[0:1]) * (scale * norm_ref[1:2] * gain) + scale * bias
    )

    @pl.when(pl.program_id(0) == 0)
    def _():
        bias_ref[0:1], gain_ref[0:1] = bias, gain
        bias_ref[1:2], gain_ref[1:2] = row(norm1_ref, 0, count), row(norm1_ref, count, count)
        skip_ref[0:1], skip_ref[1:2] = row(small_ref, 2 * count, count), skip1_ref[0:1]
        at = 3 * count
        lanes = half // 128
        for l in range(LAYERS):
            if l == 0:
                ar, ai, sr, si = (row(small_ref, at + k * lanes, lanes) for k in range(4))
            else:
                ar, ai = decay1_ref[0:1, :half], decay1_ref[0:1, half:]
                sr, si = decay1_ref[1:2, :half], decay1_ref[1:2, half:]
            dr, di = disc_ref[l, 0:1, :half], disc_ref[l, 0:1, half:]
            fr, fi = disc_ref[l, 1:2, :half], disc_ref[l, 1:2, half:]
            here = slice(l, l + 1)
            rate, freq, step = rate_ref[here], freq_ref[here], jnp.exp(step_ref[here])
            tr = ar - (fr * sr + fi * si)
            ti = ai - (fr * si - fi * sr)
            size = 1.0 / (dr * dr + di * di)
            gr, gi = (tr * dr - ti * di) * size, (tr * di + ti * dr) * size
            mr, mi = -rate * fr - freq * fi, freq * fr - rate * fi
            size = 1.0 / (rate * rate + freq * freq)
            gr += (-rate * sr - freq * si) * size
            gi += (freq * sr - rate * si) * size
            both = 2.0 * (fr * sr + fi * si)
            gx = gr * dr + gi * di
            gy = gi * dr - gr * di
            drate_ref[here] = (-mr * sr - mi * si - both * rate) * size - step * gx
            dfreq_ref[here] = (mi * sr - mr * si - both * freq) * size + step * gy
            dstep_ref[here] = step * (freq * gy - rate * gx)


def whole(array):
    shape = array.shape
    return pl.BlockSpec(shape, lambda i: (0,) * len(shape))


def tile_spec(rows, width, nt, down):
    if down:
        return pl.BlockSpec((rows, width), lambda i: (nt - 1 - i, 0))
    return pl.BlockSpec((rows, width), lambda i: (i, 0))


def run_spec(steps, width, nt, down):
    if down:
        return pl.BlockSpec((LANES, steps, width), lambda i: (0, nt - 1 - i, 0))
    return pl.BlockSpec((LANES, steps, width), lambda i: (0, i, 0))


def call(kernel, nt, args, outs, scratch, macs, name):
    arrays = [a for a, *_ in args]
    sizes = sum(a.size * a.dtype.itemsize for a in arrays + [a for a, *_ in outs])
    held = [
        a if keep is None else pltpu.with_memory_space_constraint(a, keep)
        for a, _, keep in map(filled, args)
    ]
    return pl.pallas_call(
        kernel,
        grid=(nt,),
        in_specs=[whole(a) if s is None else s for a, s, _ in map(filled, args)],
        out_specs=[whole(a) if s is None else s for a, s, _ in map(filled, outs)],
        out_shape=[
            a if keep is None else keep(a.shape, a.dtype) for a, _, keep in map(filled, outs)
        ],
        scratch_shapes=scratch,
        compiler_params=pltpu.CompilerParams(
            vmem_limit_bytes=VMEM_LIMIT, dimension_semantics=("arbitrary",)
        ),
        cost_estimate=pl.CostEstimate(flops=2 * macs, bytes_accessed=sizes, transcendentals=0),
        name=name,
    )(*held)


def filled(entry):
    return entry if len(entry) == 3 else entry + (pltpu.HBM,)


def shape(*dims, dtype=F32):
    return jax.ShapeDtypeStruct(dims, dtype)


def body(
    axes,
    tokens_in,
    seq_starts,
    norm_gain,
    norm_bias,
    decay_rate,
    step_log,
    frequency,
    in_proj,
    out_proj,
    skip_gain,
    gate_proj,
    grad_out,
):
    rows, width = tokens_in.shape
    states = in_proj.shape[-1]
    devices = 2 ** len(axes)
    tokens = float(rows * devices)
    run = rows // LANES
    steps = min(64, run)
    tile = steps * LANES
    nt = rows // tile
    span = min(32, steps)
    def tiles(array, down):
        return (array, tile_spec(tile, array.shape[-1], nt, down))

    def runs(array, down):
        return (array, run_spec(steps, array.shape[-1], nt, down))

    def full(array):
        return (array, None)

    def of(array, l):
        size = array.shape[1:]
        return (array, pl.BlockSpec((None,) + size, lambda i: (l,) + (0,) * len(size)))

    discs, tables, cuts = call(
        functools.partial(prep_kernel, rows, axes), 1,
        [full(seq_starts[None]), full(decay_rate),
         full(step_log), full(frequency)],
        [full(shape(LAYERS, 8, states)), full(shape(2 * LAYERS, 2, devices, 2 * SLOT, 128)),
         full(shape(2, LANES, 128, dtype=jnp.int32))],
        [], rows * width, "prep",
    )

    def near(entry):
        return entry[:2] + (pltpu.VMEM if rows * states * 4 <= 7 * 2**20 else pltpu.HBM,)

    tokens_run = tokens_in.reshape(LANES, run, width)
    grad_run = grad_out.reshape(LANES, run, width)
    state_scratch = pltpu.VMEM((LANES, states), F32)
    half_scratch = [pltpu.VMEM((tile, width), BF16)] * 2
    cost = rows * width * states

    u0_near, u0, order, stats = call(
        stats_kernel, nt, [runs(tokens_run, 0)],
        [near(tiles(shape(rows, width, dtype=BF16), 0)), tiles(shape(rows, width, dtype=BF16), 0),
         full(shape(span * LANES, span * LANES, dtype=BF16)),
         near(full(shape(devices, 2 * SLOT, 128)))],
        [], cost // 2, "stats",
    )

    def drive(l, stream, stats):
        down = l % 2
        return call(
            functools.partial(drive_kernel, l, bool(down), tokens), nt,
            [near(full(gather_all(stats, axes))), near(tiles(stream, down)), full(norm_gain), full(norm_bias), full(skip_gain), of(in_proj, l), of(discs, l),
               of(cuts, down)],
            [near(tiles(shape(rows, states), down)), near(full(shape(devices, 2 * SLOT, 128))),
             full(shape(LANES, states)), full(shape(8, width))],
            [], 4 * cost, f"drive_{l}",
        )

    b0, end0, blk0, norm0 = drive(0, u0_near, stats)
    u1_near, u1, low0, mixed0, gate0, stats = call(
        functools.partial(forward_kernel, False), nt,
        [near(full(gather_all(end0, axes))), of(tables, 2 * 0 + 0), near(tiles(b0, 0)), full(blk0), of(discs, 0), of(cuts, 0),
           near(tiles(u0_near, 0)), full(norm0), of(out_proj, 0), of(gate_proj, 0)],
        [near(tiles(shape(rows, width), 0)), tiles(shape(rows, width), 0), tiles(shape(rows, states, dtype=BF16), 0),
         tiles(shape(rows, width, dtype=BF16), 0), tiles(shape(rows, width, dtype=BF16), 0),
         near(full(shape(devices, 2 * SLOT, 128)))],
        [state_scratch], 6 * cost, "forward_0",
    )

    b1, end1, blk1, norm1 = drive(1, u1_near, stats)
    (
        out, low1, g1, pg1, sg1, w_sum1, aend1, ablk1
    ) = call(
        functools.partial(turn_kernel, True), nt,
        [near(full(gather_all(end1, axes))), of(tables, 2 * 1 + 0), near(tiles(b1, 1)), full(blk1), of(discs, 1), of(cuts, 1),
           of(cuts, 0), tiles(u1, 1), full(norm1), of(out_proj, 1), of(gate_proj, 1),
           runs(grad_run, 1), full(order)],
        [runs(shape(LANES, run, width), 1), near(tiles(shape(rows, states, dtype=BF16), 1)),
         near(tiles(shape(rows, width, dtype=BF16), 1)),
         near(tiles(shape(rows, width, dtype=BF16), 1)), near(tiles(shape(rows, states), 1)), full(shape(states + width + 8, width)),
         near(full(shape(devices, 2 * SLOT, 128))), full(shape(LANES, states))],
        [state_scratch, state_scratch] + half_scratch, 16 * cost, "turn_1",
    )

    def adjoint(l, sg, ablk, ends, low, stream, norm, pg, g, skip_sum=None):
        down = 1 - l % 2
        last = l == 0
        held = (lambda entry: entry) if last else near
        args = [
            near(full(ends)), of(tables, 2 * l + 1), held(tiles(sg, down)), full(ablk), of(discs, l),
            of(cuts, down), held(tiles(low, down)), tiles(stream, down),
            full(norm), held(tiles(pg, down)), held(tiles(g, down)), of(in_proj, l), full(order),
        ]
        scratch = [
            state_scratch, pltpu.VMEM((tile, states), BF16), state_scratch,
            pltpu.VMEM((tile, width), BF16),
        ]
        if last:
            args.append(full(skip_sum))
            outs = [
                runs(shape(LANES, run, width), down),
                full(shape(BLOCKS, (width + width // 2) // BLOCKS + SMALL, width)),
            ]
            scratch += [pltpu.VMEM((1, 2 * SLOT, 128), F32), pltpu.VMEM((width, states), F32)]
        else:
            outs = [
                tiles(shape(rows, width), down), full(shape(width + 8, states)),
                near(full(shape(devices, 2 * SLOT, 128))),
            ]
        return call(
            functools.partial(adjoint_kernel, bool(down), last), nt, args, outs, scratch,
            8 * cost, f"adjoint_{l}",
        )

    r1, in_sum1, norm_sum1 = adjoint(
        1, sg1, ablk1, gather_all(aend1, axes), low1, u1, norm1, pg1, g1
    )

    piece = (2 * width + states + width // 2) // BLOCKS + SMALL

    def lower(r1, norm_sum1):
        half = shape(BLOCKS // 2, (states + width) // BLOCKS, width)
        (
            g0, pg0, sg0, kept0, sent0, skip_sum0, aend0, ablk0, small1, _
        ) = call(
            functools.partial(back_kernel, True, tokens, axes[-1]), nt,
            [near(full(gather_all(norm_sum1, axes))), tiles(r1, 1), tiles(u1, 1), full(norm1),
             tiles(mixed0, 1), tiles(gate0, 1), tiles(low0, 1), tiles(u0, 1), full(norm0),
             of(out_proj, 0), of(gate_proj, 0), of(discs, 0), of(cuts, 1)],
            [tiles(shape(rows, width), 1), tiles(shape(rows, width, dtype=BF16), 1),
             tiles(shape(rows, states), 1), full(half), full(half), full(shape(1, width)), near(full(shape(devices, 2 * SLOT, 128))),
             full(shape(LANES, states)), full(shape(2 * SLOT, 128)), full(shape(2, width))],
            [pltpu.VMEM((states + width, width), F32)] + half_scratch, 12 * cost, "back_0",
        )
        core, chips, *others = phases(axes)
        part = kept0 + lax.ppermute(sent0, core[0], [(0, 1), (1, 0)])
        ends, part = lax.optimization_barrier((gather_all(aend0, axes), part))
        part = part.reshape(-1, width)
        part = scatter_sum(part, chips)
        r0, in_sum0 = adjoint(0, sg0, ablk0, ends, low0, u0, norm0, pg0, g0, skip_sum0)
        in_sum0, part = lax.optimization_barrier((in_sum0, part))
        in_part = scatter_sum(in_sum0.reshape(-1, width), core)
        share = line_scatter(part, others[0])
        in_part, share = lax.optimization_barrier((in_part, share))
        in_part = scatter_sum(in_part, chips)
        part = line_gather(share, others[0])
        for axes_left in others[1:]:
            part = line_gather(line_scatter(part, axes_left), axes_left)
        in_part, part = lax.optimization_barrier((in_part, part))
        count = in_part.shape[0]
        pad = -count % (8 * 2 ** len(others[0]))
        in_part = jnp.concatenate([in_part, jnp.zeros((pad, width), F32)], axis=0)
        for axes_left in others:
            in_part = line_gather(line_scatter(in_part, axes_left), axes_left)
        part = jnp.concatenate([part, in_part[:count]], axis=0)
        pieces = gather_rows(gather_rows(part, chips), core)
        return r0.reshape(rows, width), small1, pieces.reshape(BLOCKS, -1, width)

    def nothing(r1, norm_sum1):
        return (
            jnp.zeros((rows, width), F32),
            jnp.zeros((2 * SLOT, 128), F32),
            jnp.zeros((BLOCKS, piece, width), F32),
        )

    w_all1, in_all1 = lax.psum((w_sum1, in_sum1), axes)
    r0, norm_all1, pieces = lax.cond(seq_starts[0] == 0, lower, nothing, r1, norm_sum1)

    gates, outs = width // BLOCKS, states // BLOCKS

    def block(array, *dims, at=lambda i: (i, 0)):
        return (array, pl.BlockSpec(dims, at))

    def flat(array, count):
        return block(array, count, array.shape[1])

    (
        grad_in, gain_grad, bias_grad, rate_grad, step_grad, freq_grad, in_grad, out_grad,
        skip_grad, gate_grad,
    ) = call(
        functools.partial(last_kernel, tokens), BLOCKS,
        [block(pieces, None, piece, width, at=lambda i: (i, 0, 0)) + (None,),
         block(pieces, None, SMALL, width, at=lambda i: (0, piece // SMALL - 1, 0)) + (None,),
         flat(w_all1, outs),
         block(w_all1, gates, width, at=lambda i: (states // gates + i, 0)),
         block(w_all1, 8, width, at=lambda i: ((states + width) // 8, 0)),
         flat(in_all1, gates),
         block(in_all1, 8, states, at=lambda i: (width // 8, 0)),
         full(norm_all1), full(discs), full(decay_rate), full(step_log), full(frequency),
         flat(r0, rows // BLOCKS), flat(tokens_in, rows // BLOCKS), full(norm0)],
        [flat(shape(rows, width), rows // BLOCKS), full(shape(LAYERS, width)),
         full(shape(LAYERS, width)), full(shape(LAYERS, states // 2)),
         full(shape(LAYERS, states // 2)), full(shape(LAYERS, states // 2)),
         block(shape(LAYERS, width, states), LAYERS, gates, states, at=lambda i: (0, i, 0)),
         block(shape(LAYERS, states, width), LAYERS, outs, width, at=lambda i: (0, i, 0)),
         full(shape(LAYERS, width)),
         block(shape(LAYERS, width, width), LAYERS, gates, width, at=lambda i: (0, i, 0))],
        [], cost, "last",
    )
    return (
        out.reshape(rows, width),
        grad_in,
        gain_grad,
        bias_grad,
        rate_grad,
        step_grad,
        freq_grad,
        in_grad,
        out_grad,
        skip_grad,
        gate_grad,
    )


def solution(mesh):
    bits = mesh.devices.size.bit_length() - 1
    axes = tuple("b%d" % k for k in range(bits))
    binary = Mesh(mesh.devices.reshape((2,) * bits), axes)
    rows = P(axes, None)
    return jax.shard_map(
        functools.partial(body, axes),
        mesh=binary,
        in_specs=(rows,) + (P(),) * 10 + (rows,),
        out_specs=(rows, rows) + (P(),) * 9,
        check_vma=False,
    )
```
